32 devices in a mesh: rep: 4 (over y, x), fsdp: 8 (over z, core).
Axes of the slice: x: 2, y: 2, z: 4, core: 2. Of those that a mesh axis runs over, the one named last changes fastest.
Arguments:
- images: bfloat16 [32, 12, 16, 512], P(('rep', 'fsdp')), may hold values from -6 to 6
- enc_first: bfloat16 [4608, 512], P('fsdp'), may hold values from -0.09375 to 0.09375
- enc_second: bfloat16 [4608, 512], P('fsdp'), may hold values from -0.09375 to 0.09375
- dec_first: bfloat16 [4608, 512], P('fsdp'), may hold values from -0.09375 to 0.09375
- dec_second: bfloat16 [4608, 512], P('fsdp'), may hold values from -0.09375 to 0.09375
- head_conv: bfloat16 [4608, 64], P('fsdp'), may hold values from -0.09375 to 0.09375
- head_out: bfloat16 [64, 17], P('fsdp'), may hold values from -0.75 to 0.75
- norm_gain: float32 [4, 512], replicated, may hold values from 0.1 to 1.9
- norm_bias: float32 [4, 512], replicated, may hold values from -3 to 3
- head_bias: float32 [64], replicated, may hold values from -3 to 3
- out_bias: float32 [17], replicated, may hold values from -3 to 3
- task_weights: float32 [3], replicated, may hold values from 0.5 to 2
- pool_index: int32 [32, 48], P(('rep', 'fsdp')), may hold values from 0 to 3
- labels: int32 [32, 192], P(('rep', 'fsdp')), may hold values from 0 to 12
- task_masks: int32 [32, 3, 192], P(('rep', 'fsdp')), may hold values from 0 to 1, as said below
- targets: float32 [32, 4, 192], P(('rep', 'fsdp')), may hold values from -6 to 6
Outputs:
- grad_images: float32 [32, 12, 16, 512], P(('rep', 'fsdp'))
- grad_enc_first: float32 [4608, 512], P('fsdp')
- grad_enc_second: float32 [4608, 512], P('fsdp')
- grad_dec_first: float32 [4608, 512], P('fsdp')
- grad_dec_second: float32 [4608, 512], P('fsdp')
- grad_head_conv: float32 [4608, 64], P('fsdp')
- grad_head_out: float32 [64, 17], P('fsdp')
- grad_norm_gain: float32 [4, 512], replicated
- grad_norm_bias: float32 [4, 512], replicated
- grad_head_bias: float32 [64], replicated
- grad_out_bias: float32 [17], replicated
The draws below stay inside these ranges and needn't reach their ends.
Inputs may be any that keep to these rules, and one draw needn't show every extreme that they name: `pool_index`: position of the pooled value in its 2x2 window, 2 times row plus column. `task_masks`: 1 where a pixel counts for a task; each image has its own share for each task, from about an eighth to all of its pixels; pixel 0 of every image counts for every task.
All inputs are finite; a program needn't handle non-finite values.
Results may differ from the reference program's by a relative error of at most 0.02.
Values may be sent and summed in bfloat16 or wider, within the bound.
A program may use at most 192 MiB of HBM per device.

```python
import math
import jax
import jax.numpy as jnp
from jax import lax

CH = 512
HEAD_CH = 64
CLASSES = 13
IMG_H = 12
IMG_W = 16
NORMS = 4
BATCH = 32
PIX = 192
PIX_POOL = 48
PATCH = 4608
OUT_CH = 17
PIXELS = 6144


def draw_task_masks(key, part):
    key = jax.random.fold_in(key, 7)
    level_key, roll_key = jax.random.split(key)
    levels = jax.random.randint(level_key, (BATCH, 3, 1), 1, 9)
    rolled = jax.random.randint(roll_key, (BATCH, 3, PIX), 0, 8)
    leading = jnp.arange(PIX, dtype=jnp.int32)[None, None, :] == 0
    return jnp.where((rolled < levels) | leading, 1, 0).astype(jnp.int32)


def with_ends(values, rng, least, high):
    longest = values.shape.index(max(values.shape))
    spots = []
    for shift in (0, 1):
        where = [jax.random.randint(jax.random.fold_in(rng, axis), (), 0, length) for axis, length in enumerate(values.shape)]
        where[longest] = (where[longest] + shift) % values.shape[longest]
        spots.append(tuple(where))
    return values.at[spots[0]].set(least).at[spots[1]].set(high)


def steps_of(own_key, dims, cuts, low, high):
    gain, own = 1.0, jax.random.fold_in(own_key, 6)
    for dim, shards_of in cuts:
        steps = jnp.exp(jax.random.uniform(jax.random.fold_in(own, dim), (shards_of,), jnp.float32, low / len(cuts), high / len(cuts)))
        gain = gain * jnp.repeat(steps, dims[dim] // shards_of).reshape([-1 if axis == dim else 1 for axis in range(len(dims))])
    return gain


def centred(own_key, extent, scale, limit, cuts=(), kind=jnp.bfloat16):
    entries = scale * jax.random.normal(own_key, extent, jnp.float32)
    if cuts:
        entries = entries * steps_of(own_key, extent, cuts, -0.22, 0.18)
    return jnp.clip(entries, -limit, limit).astype(kind)


def setup_inputs(seed: int = 0) -> dict:
    key_list = jax.random.split(jax.random.key(seed), 17)
    images = centred(key_list[0], (BATCH, IMG_H, IMG_W, CH), 1.0, 6.0, ((0, 32),))
    enc_first = centred(key_list[1], (PATCH, CH), PATCH ** -0.5, 0.09375, ((0, 8),))
    enc_second = centred(key_list[2], (PATCH, CH), PATCH ** -0.5, 0.09375, ((0, 8),))
    dec_first = centred(key_list[3], (PATCH, CH), PATCH ** -0.5, 0.09375, ((0, 8),))
    dec_second = centred(key_list[4], (PATCH, CH), PATCH ** -0.5, 0.09375, ((0, 8),))
    head_conv = centred(key_list[5], (PATCH, HEAD_CH), PATCH ** -0.5, 0.09375, ((0, 8),))
    head_out = centred(key_list[6], (HEAD_CH, OUT_CH), HEAD_CH ** -0.5, 0.75, ((0, 8),))
    norm_gain = jnp.clip(1.0 + 0.18 * jax.random.normal(key_list[7], (NORMS, CH), jnp.float32), 0.1, 1.9)
    norm_bias = centred(key_list[8], (NORMS, CH), 0.5, 3.0, (), jnp.float32)
    head_bias = centred(key_list[9], (HEAD_CH,), 0.5, 3.0, (), jnp.float32)
    out_bias = centred(key_list[10], (OUT_CH,), 0.5, 3.0, (), jnp.float32)
    task_weights = jnp.clip(jnp.exp(jax.random.uniform(key_list[11], (3,), jnp.float32, math.log(0.5), math.log(2.0))), 0.5, 2.0)
    pool_index = with_ends(jax.random.randint(key_list[12], (BATCH, PIX_POOL), 0, 4), jax.random.fold_in(key_list[12], 1), 0, 3).astype(jnp.int32)
    labels = with_ends(jax.random.randint(key_list[13], (BATCH, PIX), 0, CLASSES), jax.random.fold_in(key_list[13], 1), 0, CLASSES - 1).astype(jnp.int32)
    task_masks = draw_task_masks(jax.random.fold_in(key_list[16], 71), 0)
    targets = centred(key_list[15], (BATCH, 4, PIX), 1.0, 6.0, ((0, 32),), jnp.float32)
    return dict(images=images, enc_first=enc_first, enc_second=enc_second, dec_first=dec_first, dec_second=dec_second, head_conv=head_conv, head_out=head_out, norm_gain=norm_gain, norm_bias=norm_bias, head_bias=head_bias, out_bias=out_bias, task_weights=task_weights, pool_index=pool_index, labels=labels, task_masks=task_masks, targets=targets)


eps = 1e-05

@jax.custom_vjp
def low(v):
    return lax.optimization_barrier(v.astype(jnp.bfloat16)).astype(jnp.float32)

@jax.custom_vjp
def low_back(v):
    return v

def low_keep(v):
    return (low(v), None)

def low_pass(kept, grad):
    return (grad,)

def back_keep(v):
    return (v, None)

def back_low(kept, grad):
    return (low(grad),)
low.defvjp(low_keep, low_pass)
low_back.defvjp(back_keep, back_low)

def conv_same(source, weight):
    channels = source.shape[3]
    kernel = weight.reshape(3, 3, channels, weight.shape[1])
    return lax.conv_general_dilated(source, kernel, (1, 1), ((1, 1), (1, 1)), dimension_numbers=('NHWC', 'HWIO', 'NHWC'), precision=lax.Precision.HIGHEST)

def norm_silu(conv_out, gain_row, bias_row):
    mean_val = lax.optimization_barrier(jnp.mean(conv_out, axis=(0, 1, 2)))
    spread = lax.optimization_barrier(jnp.mean(jnp.square(conv_out - mean_val), axis=(0, 1, 2)))
    normed = (conv_out - mean_val) * lax.rsqrt(spread + eps)
    return jax.nn.silu(normed * gain_row + bias_row)

def pool_unpool(hidden, pool_index):
    images_n, height, breadth, channels = hidden.shape
    pooled = lax.optimization_barrier(jnp.mean(hidden.reshape(images_n, height // 2, 2, breadth // 2, 2, channels), axis=(2, 4)))
    picks = (pool_index.reshape(images_n, height // 2, breadth // 2, 1) == jnp.arange(4, dtype=jnp.int32)).astype(jnp.float32)
    placed = pooled[:, :, :, None, :] * picks[:, :, :, :, None]
    placed = placed.reshape(images_n, height // 2, breadth // 2, 2, 2, channels)
    return jnp.transpose(placed, (0, 1, 3, 2, 4, 5)).reshape(images_n, height, breadth, channels)

def objective(params, task_weights, pool_index, labels, task_masks, targets):
    images, enc_first, enc_second, dec_first, dec_second, head_conv, head_out, norm_gain, norm_bias, head_bias, out_bias = params
    kernels = (enc_first, enc_second, dec_first, dec_second)
    hidden = images
    for number in range(4):
        if number == 2:
            hidden = pool_unpool(hidden, pool_index)
        conv_out = low_back(conv_same(low(hidden), kernels[number]))
        hidden = norm_silu(conv_out, norm_gain[number], norm_bias[number])
    head_raw = low_back(conv_same(low(hidden), head_conv) + head_bias)
    head_act = jax.nn.silu(head_raw)
    outputs = jnp.einsum('nhwc,cd->nhwd', head_act, head_out, precision=lax.Precision.HIGHEST) + out_bias
    outputs = outputs.reshape(outputs.shape[0], -1, outputs.shape[3])
    logits = outputs[:, :, :CLASSES]
    picked = lax.optimization_barrier(jnp.sum(logits * jax.nn.one_hot(labels, CLASSES, dtype=jnp.float32), axis=-1))
    seg_term = jax.nn.logsumexp(logits, axis=-1) - picked
    misfit = outputs[:, :, CLASSES] - targets[:, 0]
    depth_term = jnp.sqrt(misfit * misfit + 1.0) - 1.0
    predicted = outputs[:, :, CLASSES + 1:]
    wanted = jnp.transpose(targets[:, 1:], (0, 2, 1))
    radius = jnp.sqrt(lax.optimization_barrier(jnp.sum(predicted * predicted, axis=-1)) + 1.0)
    normal_term = 1.0 - lax.optimization_barrier(jnp.sum(predicted * wanted, axis=-1)) / radius
    terms = jnp.stack([seg_term, depth_term, normal_term], axis=1)
    mask_float = task_masks.astype(jnp.float32)
    counts = lax.optimization_barrier(jnp.sum(mask_float, axis=(0, 2)))
    task_loss = lax.optimization_barrier(jnp.sum(mask_float * terms, axis=(0, 2))) / counts
    return PIXELS * jnp.sum(task_weights * task_loss)

def reference(images, enc_first, enc_second, dec_first, dec_second, head_conv, head_out, norm_gain, norm_bias, head_bias, out_bias, task_weights, pool_index, labels, task_masks, targets):
    params = (images.astype(jnp.float32), enc_first.astype(jnp.float32), enc_second.astype(jnp.float32), dec_first.astype(jnp.float32), dec_second.astype(jnp.float32), head_conv.astype(jnp.float32), head_out.astype(jnp.float32), norm_gain, norm_bias, head_bias, out_bias)

    def closed(params_in):
        return objective(params_in, task_weights, pool_index, labels, task_masks, targets)
    objective_value, pullback = jax.vjp(closed, params)
    gradients, = pullback(jnp.ones_like(objective_value))
    root_pop = jnp.sqrt(jnp.float32(PIXELS))
    return (gradients[0], gradients[1] / root_pop, gradients[2] / root_pop, gradients[3] / root_pop, gradients[4] / root_pop, gradients[5] / root_pop, gradients[6] / root_pop, gradients[7] / root_pop, gradients[8] / root_pop, gradients[9] / root_pop, gradients[10] / root_pop)
```

```python
import functools
import math
import types

import jax
import jax.numpy as jnp
from jax import lax
from jax.experimental import pallas as pl
from jax.experimental.pallas import tpu as pltpu
from jax.sharding import PartitionSpec as P

MESH = pl.DeviceIdType.MESH
F32, BF16 = jnp.float32, jnp.bfloat16
EPS = 1e-05
LANES = 128
EXACT = lax.Precision.HIGHEST

GROUPS = (
    ["images", "start", "head_out", "a2a", "pool", "dh3", "rs3", "rs2", "rs1", "rs0", "norms", "small_rep", "small_all"]
    + [f"ag{i}" for i in (0, 2)]
    + [f"stat{i}" for i in range(8)]
    + [f"core{i}" for i in range(5)]
    + [f"z{i}" for i in range(5)]
    + [f"rows{i}" for i in range(5)]
    + [f"own{i}" for i in range(5)]
    + ["own_image"]
)
GROUP = {name: number for number, name in enumerate(GROUPS)}


def kernel(d, *refs):
    it = iter(refs)
    take = lambda count: [next(it) for _ in range(count)]
    images, w0, w1, w2, w3, hw, ho, gain, shift, hb, ob, tw, pidx, lab, msk, tgt = take(16)
    gi, gw0, gw1, gw2, gw3, ghc, gnorm, gsmall = take(8)
    (s, s4, wf, y, zb, zhat, d9, u_sel, ut_sel, a2a_s, a2a_r, rs_s, rs_r, pool_own, pool_all, ps_s, ps_r, gi_s, gi_r) = take(19)
    (gf, cr, zr, hr, hw_s, st_s, st_r, start_s, start_r, ho_s, ho_r, rep_s, rep_r, all_s, all_r, norm_s, feat) = take(17)
    ssem, rsem, wsz, wrz, wsf, wrf = take(6)
    w_in, gw = (w0, w1, w2, w3, hw_s), (gw0, gw1, gw2, gw3)
    R, F, Z, rows, C, CR, W, PIX, PD, M, PW = d.R, d.F, d.Z, d.rows, d.C, d.CR, d.W, d.PIX, d.PD, d.M, d.PW
    total = float(M * F)
    root = math.sqrt(total)

    r, f = lax.axis_index("rep"), lax.axis_index("fsdp")
    zc, core = f // 2, f % 2
    sib = (r, zc * 2 + (1 - core))
    rep_peer = lambda k: ((r + k) % R, f)
    z_peer = lambda k: (r, ((zc + k) % Z) * 2 + core)
    my_lanes = pl.ds(pl.multiple_of(r * CR, CR), CR)

    def block(owner):
        return pl.ds(pl.multiple_of(owner * rows, d.row_tile), rows)

    def send(src, dst, to, group):
        g = GROUP[group]
        pltpu.make_async_remote_copy(
            src_ref=src, dst_ref=dst, send_sem=ssem.at[g], recv_sem=rsem.at[g], device_id=to, device_id_type=MESH
        ).start()

    def wait_recv(ref, group):
        pltpu.make_async_copy(ref, ref, rsem.at[GROUP[group]]).wait()

    def wait_send(ref, group):
        pltpu.make_async_copy(ref, ref, ssem.at[GROUP[group]]).wait()

    def over(count, body, first=0):
        def step(i, carry):
            body(i)
            return carry

        lax.fori_loop(first, count, step, 0)

    barrier = pltpu.get_barrier_semaphore()
    over(R, lambda k: pl.semaphore_signal(barrier, inc=1, device_id=rep_peer(k), device_id_type=MESH), 1)
    over(F, lambda k: pl.semaphore_signal(barrier, inc=1, device_id=(r, (f + k) % F), device_id_type=MESH), 1)
    pl.semaphore_wait(barrier, R + F - 2)

    def w_copy(l, src, owner, to, send_sem, recv_sem):
        return pltpu.make_async_remote_copy(
            src_ref=src, dst_ref=wf.at[l, block(owner)], send_sem=send_sem, recv_sem=recv_sem, device_id=to, device_id_type=MESH
        )

    def w_push(l):
        src = w_in[l].at[:, my_lanes] if l < 4 else w_in[l]
        over(Z, lambda k: w_copy(l, src, f, z_peer(k), wsz.at[l, k], wrz.at[l, k]).start(), 1)
        w_copy(l, src, f, sib, wsf.at[l, 0], wrf.at[l, 0]).start()
        pltpu.make_async_copy(src, wf.at[l, block(f)], rsem.at[GROUP[f"own{l}"]]).start()

    def w_relay(l):
        def step(k):
            owner = ((zc + Z - k) % Z) * 2 + core
            here = wf.at[l, block(owner)]
            pltpu.make_async_copy(here, here, wrz.at[l, k]).wait()
            w_copy(l, here, owner, sib, wsf.at[l, k], wrf.at[l, k]).start()

        over(Z, step, 1)

    def w_finish(l):
        over(Z, lambda k: pltpu.make_async_copy(wf.at[l, block(f)], wf.at[l, block(f)], wrf.at[l, k]).wait())
        wait_recv(wf.at[l, block(f)], f"own{l}")

    w_push(0)
    over(R, lambda k: send(images, s.at[0, pl.ds(pl.multiple_of(r * PD, PD), PD)], rep_peer(k), "images"), 1)
    own_rows = s.at[0, pl.ds(pl.multiple_of(r * PD, PD), PD)]
    pltpu.make_async_copy(images, own_rows, rsem.at[GROUP["own_image"]]).start()

    start_s[...] = jnp.zeros_like(start_s)
    counted = jnp.sum(msk[...].astype(F32), axis=1, keepdims=True)
    lane = lax.broadcasted_iota(jnp.int32, (1, LANES), 1)
    start_s[0:1, :] = sum(jnp.where(lane == t, counted[t : t + 1, :], 0.0) for t in range(3))
    start_s[1:2, 0 : PW // R] = pidx[...].astype(F32)
    over(R, lambda k: send(start_s, start_r.at[r], rep_peer(k), "start"), 1)
    start_r[r] = start_s[...]
    ho_s[...] = jnp.zeros_like(ho_s)
    ho_s[0 : d.q, 0 : d.OC] = ho[...].astype(F32)
    over(F, lambda k: send(ho_s, ho_r.at[f], (r, (f + k) % F), "head_out"), 1)
    ho_r[f] = ho_s[...]
    hw_s[...] = jnp.zeros_like(hw_s)
    hw_s[:, 0 : d.HC] = hw[...]

    feat[...] = jnp.zeros_like(feat)
    feat[0:1, 0:PD] = lab[...].astype(F32)
    feat[1:4, 0:PD] = msk[...].astype(F32)
    feat[4:8, 0:PD] = tgt[...]
    columns = jnp.transpose(feat[...])[0:PD, :]

    wait_recv(start_r.at[pl.ds(0, R - 1)], "start")
    feat[...] = jnp.zeros_like(feat)
    for i in range(R):
        feat[0:1, i * (PW // R) : (i + 1) * (PW // R)] = start_r[i, 1:2, 0 : PW // R]
    picked_row = feat[0:1, 0:PW]
    picked_col = jnp.transpose(feat[...])[0:PW, 0:1]
    bits = W.bit_length() - 1

    def places(axis, shape):
        q = lax.broadcasted_iota(jnp.int32, shape, axis)
        image = jnp.zeros(shape, jnp.int32)
        for i in range(1, M // PIX):
            image = image + jnp.where(q >= i * PIX, 1, 0)
        q = q - image * PIX
        window = image * (PIX // 4) + (q >> (bits + 1)) * (W // 2) + ((q & (W - 1)) >> 1)
        position = 2 * ((q >> bits) & 1) + (q & 1)
        return window, position.astype(F32)

    def windows(rows_first):
        shape = (M, PW) if rows_first else (PW, M)
        window, position = places(0 if rows_first else 1, shape)
        other = lax.broadcasted_iota(jnp.int32, shape, 1 if rows_first else 0)
        return window == other, position

    inside, position = windows(True)
    u_sel[...] = jnp.where(inside & (position == picked_row), 1.0, 0.0).astype(BF16)
    inside, position = windows(False)
    ut_sel[...] = jnp.where(inside & (position == picked_col), 1.0, 0.0).astype(BF16)

    def image_rows(i):
        return pl.ds(pl.multiple_of(i * PIX, PIX), PIX)

    def per_image(count, body, init):
        return lax.fori_loop(0, count, body, init)

    def column_of(shape):
        return lax.broadcasted_iota(jnp.int32, shape, 0) & (W - 1)

    blank = jnp.zeros((W, CR), F32)

    def conv(src, count, l, out):
        height = count * PIX
        for kx in range(3):
            taps = [wf[l, (3 * ky + kx) * C : (3 * ky + kx + 1) * C, :].astype(BF16) for ky in range(3)]
            y[0:height, kx * 3 * CR : (kx + 1) * 3 * CR] = jnp.dot(
                src[...], jnp.concatenate(taps, axis=1), preferred_element_type=F32
            )

        def body(i, summed):
            at = image_rows(i)
            col = column_of((PIX, CR))
            parts = []
            for kx in range(3):
                up, mid, down = (y[at, (kx * 3 + ky) * CR : (kx * 3 + ky + 1) * CR] for ky in range(3))
                parts.append(
                    mid
                    + jnp.concatenate([blank, up[: PIX - W]], axis=0)
                    + jnp.concatenate([down[W:], blank], axis=0)
                )
            z = (
                parts[1]
                + jnp.where(col > 0, pltpu.roll(parts[0], 1, 0), 0.0)
                + jnp.where(col < W - 1, pltpu.roll(parts[2], PIX - 1, 0), 0.0)
            )
            out[at, :] = z
            return summed + jnp.sum(z, axis=0, keepdims=True)

        return per_image(count, body, jnp.zeros((1, CR), F32))

    def spread_taps(i, grad):
        at = image_rows(i)
        col = column_of((PIX, CR))
        moved = (
            jnp.where(col < W - 1, pltpu.roll(grad, PIX - 1, 0), 0.0),
            grad,
            jnp.where(col > 0, pltpu.roll(grad, 1, 0), 0.0),
        )
        low_blank = blank.astype(BF16)
        for kx in range(3):
            low = moved[kx].astype(BF16)
            nine = (
                jnp.concatenate([low[W:], low_blank], axis=0),
                low,
                jnp.concatenate([low_blank, low[: PIX - W]], axis=0),
            )
            for ky in range(3):
                d9[at, (kx * 3 + ky) * CR : (kx * 3 + ky + 1) * CR] = nine[ky]

    def data_grad(l, height, write):
        step = 2 * CR
        for half in range(C // step):
            taps = [
                wf[l, t * C + half * step : t * C + (half + 1) * step, :].astype(BF16)
                for t in (3 * ky + kx for kx in range(3) for ky in range(3))
            ]
            part = lax.dot_general(
                d9[0:height, :],
                jnp.concatenate(taps, axis=1),
                (((1,), (1,)), ((), ())),
                preferred_element_type=F32,
            )
            write(half, part)

    def weight_grad(l, src, height):
        for kx in range(3):
            part = lax.dot_general(
                src[...],
                d9[0:height, kx * 3 * CR : (kx + 1) * 3 * CR],
                (((0,), (0,)), ((), ())),
                preferred_element_type=F32,
            )
            for ky in range(3):
                t = 3 * ky + kx
                gf[l, t * C : (t + 1) * C, :] = part[:, ky * CR : (ky + 1) * CR].astype(gf.dtype)
        over(Z, lambda k: send(gf.at[l, block(2 * k + 1 - core)], cr.at[l, k], sib, f"core{l}"))

    def core_sum(l):
        wait_recv(cr.at[l], f"core{l}")

        def step(k):
            to = (zc + k) % Z
            at = block(2 * to + core)
            gf[l, at, :] = (gf[l, at, :].astype(F32) + cr[l, to].astype(F32)).astype(gf.dtype)

        def push(k):
            to = (zc + k) % Z
            step(k)
            send(gf.at[l, block(2 * to + core)], zr.at[l, zc], (r, 2 * to + core), f"z{l}")

        over(Z, push, 1)
        step(0)

    def z_sum(l):
        wait_recv(zr.at[l, pl.ds(0, Z - 1)], f"z{l}")
        summed = lax.fori_loop(
            1, Z, lambda k, so_far: so_far + zr[l, (zc + k) % Z].astype(F32), gf[l, block(f), :].astype(F32)
        )
        summed = summed * (1.0 / root)
        if l < 4:
            gw[l][:, my_lanes] = summed.astype(gw[l].dtype)
            here = gw[l].at[:, my_lanes]
            over(R, lambda k: send(here, here, rep_peer(k), f"rows{l}"), 1)
        else:
            hr[r] = summed.astype(hr.dtype)
            over(R, lambda k: send(hr.at[r], hr.at[r], rep_peer(k), "rows4"), 1)

    def rows_done(l):
        if l < 4:
            wait_recv(gw[l].at[:, pl.ds(0, (R - 1) * CR)], f"rows{l}")
        else:
            wait_recv(hr.at[pl.ds(0, R - 1)], "rows4")
            ghc[...] = sum(hr[i].astype(F32) for i in range(R))

    def exchange(e):
        over(F, lambda k: send(st_s.at[e], st_r.at[e, f], (r, (f + k) % F), f"stat{e}"), 1)
        st_r[e, f] = st_s[e]

    def exchanged(e):
        wait_recv(st_r.at[e, pl.ds(0, F - 1)], f"stat{e}")
        return st_r[e]

    st_s[...] = jnp.zeros_like(st_s)
    w_relay(0)
    w_push(1)
    wait_recv(s.at[0, pl.ds(0, (R - 1) * PD)], "images")
    wait_recv(own_rows, "own_image")

    inverse_of, counts = [], None
    for l in range(4):
        w_finish(l)
        if l == 2:
            wait_recv(pool_all.at[:, pl.ds(0, (R - 1) * CR)], "pool")
            s[2] = jnp.dot(u_sel[...], pool_all[...], preferred_element_type=F32).astype(BF16)
        elif l:
            wait_recv(s.at[l, :, pl.ds(0, (R - 1) * CR)], f"ag{l - 1}")
        first = conv(s.at[l], M // PIX, l, zb)
        mean_here = first * (1.0 / M)

        def squares(i, so_far):
            return so_far + jnp.sum(jnp.square(zb[image_rows(i), :] - mean_here), axis=0, keepdims=True)

        st_s[l, 0:1, :] = first
        st_s[l, 1:2, :] = per_image(M // PIX, squares, jnp.zeros((1, CR), F32))
        if l == 0:
            st_s[l, 2:3, :] = sum(start_r[i, 0:1, :] for i in range(R))
        exchange(l)
        parts = exchanged(l)
        tot = jnp.sum(parts, axis=0)
        mean = tot[0:1] * (1.0 / total)
        apart = jnp.sum(jnp.square(parts * (1.0 / M) - mean[None]), axis=0)[0:1] * float(M)
        inverse = lax.rsqrt((tot[1:2] + apart) * (1.0 / total) + EPS)
        inverse_of.append(inverse)
        if l == 0:
            counts = tot[2:3]
        g_row, b_row = gain[l : l + 1, my_lanes], shift[l : l + 1, my_lanes]

        def activate(i, carry):
            at = image_rows(i)
            normed = (zb[at, :] - mean) * inverse
            zhat[l, at, :] = normed
            shaped = normed * g_row + b_row
            hidden = shaped * jax.nn.sigmoid(shaped)
            if l == 1:
                zb[at, :] = hidden
            elif l == 3:
                a2a_s[i] = hidden.astype(BF16)
            else:
                s[l + 1, at, my_lanes] = hidden.astype(BF16)
            return carry

        per_image(M // PIX, activate, 0)
        if l == 1:
            inside, unused = windows(False)
            pooled = jnp.dot(
                jnp.where(inside, 0.25, 0.0), zb[...], precision=EXACT, preferred_element_type=F32
            )
            pool_own[...] = pooled.astype(BF16)
            pool_all[:, my_lanes] = pooled.astype(BF16)
            over(R, lambda k: send(pool_own, pool_all.at[:, my_lanes], rep_peer(k), "pool"), 1)
        elif l == 3:
            over(R, lambda k: send(a2a_s.at[(r + k) % R], s4.at[:, my_lanes], rep_peer(k), "a2a"), 1)
            s4[:, my_lanes] = a2a_s[r]
        else:
            here = s.at[l + 1, :, my_lanes]
            over(R, lambda k: send(here, here, rep_peer(k), f"ag{l}"), 1)
        w_relay(l + 1)
        if l < 3:
            w_push(l + 2)

    w_finish(4)
    wait_recv(s4.at[:, pl.ds(0, (R - 1) * CR)], "a2a")
    wait_recv(ho_r.at[pl.ds(0, F - 1)], "head_out")
    conv(s4, PD // PIX, 4, zb)
    head_bias = jnp.concatenate([hb[...], jnp.zeros((1, CR - d.HC), F32)], axis=1)
    out_bias = jnp.concatenate([ob[...], jnp.zeros((1, CR - d.OC), F32)], axis=1)
    head_raw = zb[0:PD, :] + head_bias
    squashed = jax.nn.sigmoid(head_raw)
    head_act = head_raw * squashed
    project = jnp.concatenate([ho_r[i][0 : d.q] for i in range(F)] + [jnp.zeros((LANES - d.HC, LANES), F32)], axis=0)
    out = jnp.dot(head_act, project, precision=EXACT, preferred_element_type=F32) + out_bias
    lane = lax.broadcasted_iota(jnp.int32, (PD, LANES), 1)
    classes = d.OC - 4
    factor = total * jnp.concatenate([tw[...], jnp.zeros((1, LANES - 3), F32)], axis=1) / jnp.maximum(counts, 1.0)
    pixel = [columns[:, i : i + 1] for i in range(8)]
    is_class = lane < classes
    top = jnp.max(jnp.where(is_class, out, -jnp.inf), axis=1, keepdims=True)
    grown = jnp.where(is_class, jnp.exp(jnp.where(is_class, out - top, 0.0)), 0.0)
    likely = grown / jnp.sum(grown, axis=1, keepdims=True)
    onehot = jnp.where(lane.astype(F32) == pixel[0], 1.0, 0.0)
    grad_class = factor[:, 0:1] * pixel[1] * (likely - onehot)
    misfit = out - pixel[4]
    grad_depth = factor[:, 1:2] * pixel[2] * misfit / jnp.sqrt(misfit * misfit + 1.0)
    is_normal = (lane > classes) & (lane < d.OC)
    predicted = jnp.where(is_normal, out, 0.0)
    wanted = sum(jnp.where(lane == classes + 1 + i, pixel[5 + i], 0.0) for i in range(3))
    radius = jnp.sqrt(jnp.sum(predicted * predicted, axis=1, keepdims=True) + 1.0)
    aligned = jnp.sum(predicted * wanted, axis=1, keepdims=True)
    grad_normal = -(factor[:, 2:3] * pixel[3]) * (wanted / radius - aligned / (radius * radius * radius) * predicted)
    grad_out = jnp.where(
        is_class, grad_class, jnp.where(lane == classes, grad_depth, jnp.where(is_normal, grad_normal, 0.0))
    )
    grad_act = lax.dot_general(
        grad_out, project, (((1,), (1,)), ((), ())), precision=EXACT, preferred_element_type=F32
    )
    grad_head = (grad_act * (squashed + head_raw * squashed * (1.0 - squashed))).astype(BF16).astype(F32)
    zb[0:PD, :] = grad_head
    y[0:PD, 0:CR] = head_act
    y[0:PD, CR : 2 * CR] = grad_out

    def spread_head(i, carry):
        spread_taps(i, zb[image_rows(i), :])
        return carry

    per_image(PD // PIX, spread_head, 0)

    def write_dh3(half, part):
        a2a_s[2 * half] = part[:, 0:CR].astype(BF16)
        a2a_s[2 * half + 1] = part[:, CR : 2 * CR].astype(BF16)

    wait_send(a2a_r.at[pl.ds(0, R - 1)], "a2a")
    data_grad(4, PD, write_dh3)
    over(R, lambda k: send(a2a_s.at[(r + k) % R], a2a_r.at[r], rep_peer(k), "dh3"), 1)
    a2a_r[r] = a2a_s[r]
    weight_grad(4, s4, PD)
    head_act, grad_out = y[0:PD, 0:CR], y[0:PD, CR : 2 * CR]
    pad = jnp.zeros((2 * LANES - PD, LANES), F32)
    act_t = jnp.transpose(jnp.concatenate([head_act, pad], axis=0))[:, 0:PD]
    rep_s[0 : d.HC, :] = jnp.dot(act_t, grad_out, precision=EXACT, preferred_element_type=F32)[0 : d.HC]
    rep_s[d.HC : d.HC + 8, :] = jnp.zeros((8, LANES), F32)
    rep_s[d.HC : d.HC + 1, :] = jnp.sum(zb[0:PD, :], axis=0, keepdims=True)
    rep_s[d.HC + 1 : d.HC + 2, :] = jnp.sum(grad_out, axis=0, keepdims=True)
    over(R, lambda k: send(rep_s, rep_r.at[r], rep_peer(k), "small_rep"), 1)
    rep_r[r] = rep_s[...]

    def head_small():
        wait_recv(rep_r.at[pl.ds(0, R - 1)], "small_rep")
        summed = sum(rep_r[i] for i in range(R))
        for i in range(F):
            all_s[i, 0 : d.q, :] = summed[i * d.q : (i + 1) * d.q]
            if d.q < 8:
                all_s[i, d.q : 8, :] = jnp.zeros((8 - d.q, LANES), F32)
            all_s[i, 8:16, :] = summed[d.HC : d.HC + 8]
        over(F, lambda k: send(all_s.at[(f + k) % F], all_r.at[f], (r, (f + k) % F), "small_all"), 1)
        all_r[f] = all_s[f]

    for l in (3, 2, 1, 0):
        e = 7 - l
        g_row, b_row = gain[l : l + 1, my_lanes], shift[l : l + 1, my_lanes]
        if l == 3:
            wait_recv(a2a_r.at[pl.ds(0, R - 1)], "dh3")
            entering = lambda i, at: a2a_r[i].astype(F32)
        elif l == 1:
            wait_recv(ps_r.at[pl.ds(0, R - 1)], "rs2")
            pooled = sum(ps_r[i].astype(F32) for i in range(R))
            inside, unused = windows(True)
            zb[...] = jnp.dot(jnp.where(inside, 0.25, 0.0), pooled, precision=EXACT, preferred_element_type=F32)
            entering = lambda i, at: zb[at, :]
        else:
            slot = 0 if l == 2 else 1
            wait_recv(rs_r.at[slot, pl.ds(0, R - 1)], f"rs{l + 1}")
            entering = lambda i, at: sum(rs_r[slot, j, at, :].astype(F32) for j in range(R))

        def slopes(i, so_far):
            at = image_rows(i)
            normed = zhat[l, at, :]
            shaped = normed * g_row + b_row
            squashed = jax.nn.sigmoid(shaped)
            grad = entering(i, at) * (squashed + shaped * squashed * (1.0 - squashed))
            zb[at, :] = grad
            return (
                so_far[0] + jnp.sum(grad, axis=0, keepdims=True),
                so_far[1] + jnp.sum(grad * normed, axis=0, keepdims=True),
            )

        none = jnp.zeros((1, CR), F32)
        part_bias, part_gain = per_image(M // PIX, slopes, (none, none))
        st_s[e, 0:1, :] = part_bias
        st_s[e, 1:2, :] = part_gain
        exchange(e)
        if l == 3:
            core_sum(4)
            head_small()
        else:
            z_sum(l + 2)
        tot = jnp.sum(exchanged(e), axis=0)
        bias_sum, gain_sum = tot[0:1], tot[1:2]
        norm_s[l : l + 1, :] = gain_sum * (1.0 / root)
        norm_s[4 + l : 5 + l, :] = bias_sum * (1.0 / root)
        scale = inverse_of[l] * g_row

        def through_norm(i, carry):
            at = image_rows(i)
            spread_taps(
                i, scale * (zb[at, :] - bias_sum * (1.0 / total) - zhat[l, at, :] * (gain_sum * (1.0 / total)))
            )
            return carry

        per_image(M // PIX, through_norm, 0)
        if l == 2:

            def write(half, part):
                chosen = jnp.dot(ut_sel[...], part.astype(BF16), preferred_element_type=F32).astype(BF16)
                ps_s[2 * half] = chosen[:, 0:CR]
                ps_s[2 * half + 1] = chosen[:, CR : 2 * CR]

            data_grad(l, M, write)
            over(R, lambda k: send(ps_s.at[(r + k) % R], ps_r.at[r], rep_peer(k), "rs2"), 1)
            ps_r[r] = ps_s[r]
            weight_grad(l, s.at[l], M)
            core_sum(l)
        elif l == 0:
            weight_grad(l, s.at[l], M)

            def write(half, part):
                for i in range(R):
                    gi_s[i, :, half * 2 * CR : (half + 1) * 2 * CR] = part[i * PD : (i + 1) * PD].astype(BF16)

            data_grad(l, M, write)
            over(R, lambda k: send(gi_s.at[(r + k) % R], gi_r.at[r], rep_peer(k), "rs0"), 1)
            gi_r[r] = gi_s[r]
            core_sum(l)
        else:
            slot = 0 if l == 3 else 1

            def write(half, part):
                rs_s[slot, 2 * half] = part[:, 0:CR].astype(BF16)
                rs_s[slot, 2 * half + 1] = part[:, CR : 2 * CR].astype(BF16)

            data_grad(l, M, write)
            over(R, lambda k: send(rs_s.at[slot, (r + k) % R], rs_r.at[slot, r], rep_peer(k), f"rs{l}"), 1)
            rs_r[slot, r] = rs_s[slot, r]
            weight_grad(l, s.at[l], M)
            core_sum(l)

    gnorm[:, my_lanes] = norm_s[...]
    over(R, lambda k: send(norm_s, gnorm.at[:, my_lanes], rep_peer(k), "norms"), 1)
    z_sum(1)
    wait_recv(all_r.at[pl.ds(0, F - 1)], "small_all")
    gsmall[...] = jnp.sum(all_r[...], axis=0) * (1.0 / root)
    rows_done(4)
    rows_done(3)
    rows_done(2)
    wait_recv(gi_r.at[pl.ds(0, R - 1)], "rs0")
    gi[...] = sum(gi_r[i].astype(F32) for i in range(R))
    z_sum(0)
    wait_recv(gnorm.at[:, pl.ds(0, (R - 1) * CR)], "norms")
    rows_done(1)
    rows_done(0)

    wait_send(s.at[0, pl.ds(0, (R - 1) * PD)], "images")
    wait_send(start_r.at[pl.ds(0, R - 1)], "start")
    wait_send(ho_r.at[pl.ds(0, F - 1)], "head_out")
    wait_send(pool_all.at[:, pl.ds(0, (R - 1) * CR)], "pool")
    for i in (0, 2):
        wait_send(s.at[i + 1, :, pl.ds(0, (R - 1) * CR)], f"ag{i}")
    wait_send(a2a_r.at[pl.ds(0, R - 1)], "dh3")
    wait_send(rs_r.at[0, pl.ds(0, R - 1)], "rs3")
    wait_send(ps_r.at[pl.ds(0, R - 1)], "rs2")
    wait_send(rs_r.at[1, pl.ds(0, R - 1)], "rs1")
    wait_send(gi_r.at[pl.ds(0, R - 1)], "rs0")
    wait_send(gnorm.at[:, pl.ds(0, (R - 1) * CR)], "norms")
    wait_send(rep_r.at[pl.ds(0, R - 1)], "small_rep")
    wait_send(all_r.at[pl.ds(0, F - 1)], "small_all")
    for e in range(8):
        wait_send(st_r.at[e, pl.ds(0, F - 1)], f"stat{e}")
    for l in range(5):
        wait_send(cr.at[l], f"core{l}")
        wait_send(zr.at[l, pl.ds(0, Z - 1)], f"z{l}")
        wait_send(gw[l].at[:, pl.ds(0, (R - 1) * CR)] if l < 4 else hr.at[pl.ds(0, R - 1)], f"rows{l}")
        one = wf.at[l, block(f)]
        over(Z, lambda k: pltpu.make_async_copy(one, one, wsf.at[l, k]).wait())
        over(Z, lambda k: pltpu.make_async_copy(one, one, wsz.at[l, k]).wait(), 1)


def per_device(
    R, F,
    images, enc_first, enc_second, dec_first, dec_second, head_conv, head_out, norm_gain, norm_bias, head_bias, out_bias,
    task_weights, pool_index, labels, task_masks, targets,
):
    n, height, breadth, channels = images.shape
    rows, hidden = head_conv.shape
    q, out_ch = head_out.shape
    d = types.SimpleNamespace(
        R=R, F=F, Z=F // 2, rows=rows, C=channels, CR=channels // R, W=breadth, PIX=height * breadth,
        PD=n * height * breadth, HC=hidden, OC=out_ch, q=q,
    )
    d.M = R * d.PD
    d.PW = d.M // 4
    wire = BF16 if rows % 16 == 0 else F32
    d.row_tile = 16 if rows % 16 == 0 else 8
    vm = pltpu.VMEM
    patch = 9 * channels
    scratch = [
        vm((4, d.M, d.C), BF16),
        vm((d.PD, d.C), BF16),
        vm((5, patch, d.CR), wire),
        vm((d.M, 9 * d.CR), F32),
        vm((d.M, d.CR), F32),
        vm((4, d.M, d.CR), F32),
        vm((d.M, 9 * d.CR), BF16),
        vm((d.M, d.PW), BF16),
        vm((d.PW, d.M), BF16),
        vm((R, d.PD, d.CR), BF16),
        vm((R, d.PD, d.CR), BF16),
        vm((2, R, d.M, d.CR), BF16),
        vm((2, R, d.M, d.CR), BF16),
        vm((d.PW, d.CR), BF16),
        vm((d.PW, d.C), BF16),
        vm((R, d.PW, d.CR), BF16),
        vm((R, d.PW, d.CR), BF16),
        vm((R, d.PD, d.C), BF16),
        vm((R, d.PD, d.C), BF16),
        vm((5, patch, d.CR), wire),
        vm((5, d.Z, rows, d.CR), wire),
        vm((5, d.Z, rows, d.CR), wire),
        vm((R, rows, d.CR), wire),
        vm((rows, LANES), wire),
        vm((8, 8, LANES), F32),
        vm((8, F, 8, LANES), F32),
        vm((8, LANES), F32),
        vm((R, 8, LANES), F32),
        vm((8, LANES), F32),
        vm((F, 8, LANES), F32),
        vm((hidden + 8, LANES), F32),
        vm((R, hidden + 8, LANES), F32),
        vm((F, 16, LANES), F32),
        vm((F, 16, LANES), F32),
        vm((8, LANES), F32),
        vm((LANES, 2 * LANES), F32),
        pltpu.SemaphoreType.DMA((len(GROUPS),)),
        pltpu.SemaphoreType.DMA((len(GROUPS),)),
        pltpu.SemaphoreType.DMA((5, d.Z)),
        pltpu.SemaphoreType.DMA((5, d.Z)),
        pltpu.SemaphoreType.DMA((5, d.Z)),
        pltpu.SemaphoreType.DMA((5, d.Z)),
    ]
    here, there = pl.BlockSpec(memory_space=pltpu.VMEM), pl.BlockSpec(memory_space=pl.ANY)
    row_type = BF16 if rows % 16 == 0 else F32
    shape = jax.ShapeDtypeStruct
    gi, gw0, gw1, gw2, gw3, ghc, gnorm, gsmall = pl.pallas_call(
        functools.partial(kernel, d),
        out_shape=[shape((d.PD, d.C), F32)]
        + [shape((rows, d.C), row_type)] * 4
        + [shape((rows, LANES), F32), shape((8, d.C), F32), shape((16, LANES), F32)],
        in_specs=[there] * 5 + [here] * 11,
        out_specs=[here] * 8,
        scratch_shapes=scratch,
        compiler_params=pltpu.CompilerParams(collective_id=0, has_side_effects=True, vmem_limit_bytes=60 * 2**20),
    )(
        images.reshape(d.PD, channels),
        *(w.astype(wire) for w in (enc_first, enc_second, dec_first, dec_second, head_conv)),
        head_out, norm_gain, norm_bias, head_bias.reshape(1, hidden), out_bias.reshape(1, out_ch),
        task_weights.reshape(1, 3), pool_index.reshape(1, -1), labels.reshape(1, -1),
        jnp.transpose(task_masks, (1, 0, 2)).reshape(3, -1), jnp.transpose(targets, (1, 0, 2)).reshape(4, -1),
    )
    return (
        gi.reshape(images.shape), gw0.astype(F32), gw1.astype(F32), gw2.astype(F32), gw3.astype(F32), ghc[:, :hidden],
        gsmall[:q, :out_ch], gnorm[0:4], gnorm[4:8], gsmall[8, :hidden], gsmall[9, :out_ch],
    )


def solution(mesh):
    split = ("rep", "fsdp")
    rows = P("fsdp", None)
    return jax.shard_map(
        functools.partial(per_device, mesh.shape["rep"], mesh.shape["fsdp"]),
        mesh=mesh,
        in_specs=(P(split, None, None, None),)
        + (rows,) * 6
        + (P(),) * 5
        + (P(split, None), P(split, None), P(split, None, None), P(split, None, None)),
        out_specs=(P(split, None, None, None),) + (rows,) * 6 + (P(),) * 4,
        check_vma=False,
    )
```

```python
import functools
import math
import types

import jax
import jax.numpy as jnp
from jax import lax
from jax.experimental import pallas as pl
from jax.experimental.pallas import tpu as pltpu
from jax.sharding import PartitionSpec as P

MESH = pl.DeviceIdType.MESH
F32, BF16 = jnp.float32, jnp.bfloat16
EPS = 1e-05
LANES = 128
EXACT = lax.Precision.HIGHEST

GROUPS = (
    ["images", "start", "head_out", "a2a", "pool", "dh3", "rs3", "rs2", "rs1", "rs0", "norms", "small_rep", "small_all"]
    + [f"ag{i}" for i in (0, 2)]
    + [f"stat{i}" for i in range(8)]
    + [f"core{i}" for i in range(5)]
    + [f"z{i}" for i in range(5)]
    + [f"mid{i}" for i in range(5)]
    + [f"rows{i}" for i in range(5)]
    + [f"own{i}" for i in range(5)]
    + ["own_image"]
)
GROUP = {name: number for number, name in enumerate(GROUPS)}


def kernel(d, *refs):
    it = iter(refs)
    take = lambda count: [next(it) for _ in range(count)]
    images, w0, w1, w2, w3, hw, ho, gain, shift, hb, ob, tw, pidx, lab, msk, tgt = take(16)
    gi, gw0, gw1, gw2, gw3, ghc, gnorm, gsmall = take(8)
    (s, s4, wf, y, zb, zhat, d9, u_sel, ut_sel, a2a_s, a2a_r, rs_s, rs_r, pool_own, pool_all, ps_s, ps_r, gi_s, gi_r) = take(19)
    (gf, cr, zr, hw_s, hp, hg, hcr, hzr, hr, st_s, st_r, start_s, start_r, ho_s, ho_r, rep_s, rep_r, all_s, all_r, norm_s, feat) = take(21)
    ssem, rsem, wsz, wrz, wsf, wrf = take(6)
    w_in, gw = (w0, w1, w2, w3, hw_s), (gw0, gw1, gw2, gw3)
    R, F, Z, rows, half, C, CR, W, PIX, PD, M, PW = d.R, d.F, d.Z, d.rows, d.half, d.C, d.CR, d.W, d.PIX, d.PD, d.M, d.PW
    total = float(M * F)
    root = math.sqrt(total)

    r, f = lax.axis_index("rep"), lax.axis_index("fsdp")
    zc, core = f // 2, f % 2
    sib = (r, zc * 2 + (1 - core))
    rep_peer = lambda k: ((r + k) % R, f)
    z_peer = lambda k: (r, ((zc + k) % Z) * 2 + core)
    line = Z == 4
    is_end = (zc == 0) | (zc == Z - 1)
    is_far = lambda k: (zc + k) % Z - zc == Z - 1
    is_far_back = lambda k: zc - (zc + k) % Z == Z - 1
    ends_apart = lambda k: is_far(k) | is_far_back(k)
    my_lanes = pl.ds(pl.multiple_of(r * CR, CR), CR)

    def block(owner):
        return pl.ds(pl.multiple_of(owner * rows, d.row_tile), rows)

    arriving, leaving = {}, {}

    def first_of(ref, count):
        return lambda: ref.at[pl.ds(0, count)]

    volume = {
        "images": first_of(s.at[0], (R - 1) * PD),
        "own_image": first_of(s.at[0], PD),
        "start": first_of(start_r, R - 1),
        "head_out": first_of(ho_r, F - 1),
        "a2a": lambda: s4.at[:, pl.ds(0, (R - 1) * CR)],
        "pool": lambda: pool_all.at[:, pl.ds(0, (R - 1) * CR)],
        "dh3": first_of(a2a_r, R - 1),
        "rs3": first_of(rs_r.at[0], R - 1),
        "rs2": first_of(ps_r, R - 1),
        "rs1": first_of(rs_r.at[1], R - 1),
        "rs0": first_of(gi_r, R - 1),
        "norms": lambda: gnorm.at[:, pl.ds(0, (R - 1) * CR)],
        "small_rep": first_of(rep_r, R - 1),
        "small_all": first_of(all_r, F - 1),
        "rows4": first_of(hr, R - 1),
        "core4": lambda: hcr,
        "mid4": lambda: hzr.at[0],
    }
    for l in (0, 2):
        volume[f"ag{l}"] = lambda l=l: s.at[l + 1, :, pl.ds(0, (R - 1) * CR)]
    for e in range(8):
        volume[f"stat{e}"] = first_of(st_r.at[e], F - 1)
    for l in range(4):
        volume[f"core{l}"] = lambda l=l: cr.at[l]
        volume[f"mid{l}"] = lambda l=l: zr.at[l, 0]
        volume[f"rows{l}"] = lambda l=l: gw[l].at[:, pl.ds(0, (R - 1) * CR)]

    def wait_for(ref, sem):
        pltpu.make_async_copy(ref, ref, sem).wait()

    def wait_recv(group):
        arriving.pop(group)()

    def wait_send(group):
        leaving.pop(group)()

    def copy_here(src, dst, group):
        g = GROUP[group]
        arriving[group] = lambda: wait_for(dst, rsem.at[g])
        pltpu.make_async_copy(src, dst, rsem.at[g]).start()

    def send(src, dst, to, group):
        g = GROUP[group]
        if group in volume:
            arriving[group] = lambda: wait_for(volume[group](), rsem.at[g])
            leaving[group] = lambda: wait_for(volume[group](), ssem.at[g])
        pltpu.make_async_remote_copy(
            src_ref=src, dst_ref=dst, send_sem=ssem.at[g], recv_sem=rsem.at[g], device_id=to, device_id_type=MESH
        ).start()

    def over(count, body, first=0):
        if count <= 8:
            for i in range(first, count):
                body(i)
            return

        def step(i, carry):
            body(i)
            return carry

        lax.fori_loop(first, count, step, 0)

    def when(condition, body):
        pl.when(condition)(body)

    def direct(k, body):
        if line and k in (1, Z - 1):
            when(jnp.logical_not(ends_apart(k)), body)
        else:
            body()

    def drain():
        for waits in (arriving, leaving):
            for wait in list(waits.values()):
                wait()

    barrier = pltpu.get_barrier_semaphore()
    over(R, lambda k: pl.semaphore_signal(barrier, inc=1, device_id=rep_peer(k), device_id_type=MESH), 1)
    over(F, lambda k: pl.semaphore_signal(barrier, inc=1, device_id=(r, (f + k) % F), device_id_type=MESH), 1)
    pl.semaphore_wait(barrier, R + F - 2)

    def w_block(l, owner):
        return wf.at[l, block(owner)] if l < 4 else hp.at[owner]

    def w_copy(l, src, owner, to, send_sem, recv_sem):
        return pltpu.make_async_remote_copy(
            src_ref=src, dst_ref=w_block(l, owner), send_sem=send_sem, recv_sem=recv_sem, device_id=to, device_id_type=MESH
        )

    def w_src(l):
        return w_in[l].at[:, my_lanes] if l < 4 else hw_s

    def w_send(l, k):
        arriving["near" if k in (1, Z - 1) else "rest", l, k] = lambda: direct(Z - k, lambda: w_wait(l, wrz.at[l, k]))
        leaving["w", l, k] = lambda: direct(k, lambda: w_wait(l, wsz.at[l, k]))
        direct(k, lambda: w_copy(l, w_src(l), f, z_peer(k), wsz.at[l, k], wrz.at[l, k]).start())

    def w_push_near(l):
        for k in sorted({1, Z - 1}):
            w_send(l, k)
        w_copy(l, w_src(l), f, sib, wsf.at[l, 0], wrf.at[l, 0]).start()
        arriving["core", l, 0] = lambda: w_wait(l, wrf.at[l, 0])
        leaving["core", l, 0] = lambda: w_wait(l, wsf.at[l, 0])
        copy_here(w_src(l), w_block(l, f), f"own{l}")

    def w_push_rest(l):
        for k in range(2, Z - 1):
            w_send(l, k)

    def w_wait(l, sem):
        pltpu.make_async_copy(w_block(l, f), w_block(l, f), sem).wait()

    def w_arrived(l, k):
        owner = ((zc + Z - k) % Z) * 2 + core
        w_wait(l, wrz.at[l, k])
        w_copy(l, w_block(l, owner), owner, sib, wsf.at[l, k], wrf.at[l, k]).start()

    def w_relayed(l, k):
        arriving["core", l, k] = lambda: w_wait(l, wrf.at[l, k])
        leaving["core", l, k] = lambda: w_wait(l, wsf.at[l, k])

    def w_relay_rest(l):
        for k in range(2, Z - 1):
            arriving.pop(("rest", l, k))
            w_arrived(l, k)
            w_relayed(l, k)
        if line:

            def hand_on():
                to = (Z - 1) * (zc - 1)
                owner = (Z - 1 - to) * 2 + core
                slot = jnp.where(zc == 1, 1, Z - 1)
                w_copy(l, w_block(l, owner), owner, (r, to * 2 + core), wsz.at[l, 0], wrz.at[l, slot]).start()

            when(jnp.logical_not(is_end), hand_on)
            leaving["far", l] = lambda: when(jnp.logical_not(is_end), lambda: w_wait(l, wsz.at[l, 0]))

    def w_relay_near(l):
        for k in sorted({1, Z - 1}):
            arriving.pop(("near", l, k))
            direct(Z - k, lambda: w_arrived(l, k))
            if not line:
                w_relayed(l, k)

    def w_far(l):
        if line:
            for k in (1, Z - 1):
                w_relayed(l, k)
            when(zc == 0, lambda: w_arrived(l, 1))
            when(zc == Z - 1, lambda: w_arrived(l, Z - 1))

    def w_finish(l):
        for k in range(Z):
            wait_recv(("core", l, k))
        wait_recv(f"own{l}")

    w_push_rest(0)
    w_push_near(0)
    over(R, lambda k: send(images, s.at[0, pl.ds(pl.multiple_of(r * PD, PD), PD)], rep_peer(k), "images"), 1)
    own_rows = s.at[0, pl.ds(pl.multiple_of(r * PD, PD), PD)]
    copy_here(images, own_rows, "own_image")

    start_s[...] = jnp.zeros_like(start_s)
    masks = jnp.concatenate([msk[:, i, :] for i in range(d.n)], axis=1).astype(F32)
    labels = jnp.concatenate([lab[i : i + 1, :] for i in range(d.n)], axis=1).astype(F32)
    wanted = jnp.concatenate([tgt[i] for i in range(d.n)], axis=1)
    pools = jnp.concatenate([pidx[i : i + 1, :] for i in range(d.n)], axis=1).astype(F32)
    counted = jnp.sum(masks, axis=1, keepdims=True)
    lane = lax.broadcasted_iota(jnp.int32, (1, LANES), 1)
    start_s[0:1, :] = sum(jnp.where(lane == t, counted[t : t + 1, :], 0.0) for t in range(3))
    start_s[1:2, 0 : PW // R] = pools
    over(R, lambda k: send(start_s, start_r.at[r], rep_peer(k), "start"), 1)
    start_r[r] = start_s[...]
    ho_s[...] = jnp.zeros_like(ho_s)
    ho_s[0 : d.q, 0 : d.OC] = ho[...].astype(F32)
    over(F, lambda k: send(ho_s, ho_r.at[f], (r, (f + k) % F), "head_out"), 1)
    ho_r[f] = ho_s[...]
    wide = -(-rows // LANES) * LANES
    tall = jnp.concatenate([hw[...].astype(F32), jnp.zeros((LANES - d.HC, rows), F32)], axis=0)
    if wide > rows:
        tall = jnp.concatenate([tall, jnp.zeros((LANES, wide - rows), F32)], axis=1)
    tall = jnp.transpose(tall)
    if wide < 2 * half:
        tall = jnp.concatenate([tall, jnp.zeros((2 * half - wide, LANES), F32)], axis=0)
    hw_s[...] = (tall[0:half] + pltpu.roll(tall[half : 2 * half], d.HC, 1)).astype(hw_s.dtype)

    feat[...] = jnp.zeros_like(feat)
    feat[0:1, 0:PD] = labels
    feat[1:4, 0:PD] = masks
    feat[4:8, 0:PD] = wanted
    columns = jnp.transpose(feat[...])[0:PD, :]

    wait_recv("start")
    feat[...] = jnp.zeros_like(feat)
    for i in range(R):
        feat[0:1, i * (PW // R) : (i + 1) * (PW // R)] = start_r[i, 1:2, 0 : PW // R]
    picked_row = feat[0:1, 0:PW]
    picked_col = jnp.transpose(feat[...])[0:PW, 0:1]
    bits = W.bit_length() - 1

    def places(axis, shape):
        q = lax.broadcasted_iota(jnp.int32, shape, axis)
        image = jnp.zeros(shape, jnp.int32)
        for i in range(1, M // PIX):
            image = image + jnp.where(q >= i * PIX, 1, 0)
        q = q - image * PIX
        window = image * (PIX // 4) + (q >> (bits + 1)) * (W // 2) + ((q & (W - 1)) >> 1)
        position = 2 * ((q >> bits) & 1) + (q & 1)
        return window, position.astype(F32)

    def windows(rows_first):
        shape = (M, PW) if rows_first else (PW, M)
        window, position = places(0 if rows_first else 1, shape)
        other = lax.broadcasted_iota(jnp.int32, shape, 1 if rows_first else 0)
        return window == other, position

    inside, position = windows(True)
    u_sel[...] = jnp.where(inside & (position == picked_row), 1.0, 0.0).astype(BF16)
    inside, position = windows(False)
    ut_sel[...] = jnp.where(inside & (position == picked_col), 1.0, 0.0).astype(BF16)

    def image_rows(i):
        return pl.ds(pl.multiple_of(i * PIX, PIX), PIX)

    def per_image(count, body, init):
        return lax.fori_loop(0, count, body, init)

    def column_of(shape):
        return lax.broadcasted_iota(jnp.int32, shape, 0) & (W - 1)

    blank = jnp.zeros((W, CR), F32)

    def conv(src, count, l, out):
        height = count * PIX
        for kx in range(3):
            taps = [wf[l, (3 * ky + kx) * C : (3 * ky + kx + 1) * C, :].astype(BF16) for ky in range(3)]
            y[0:height, kx * 3 * CR : (kx + 1) * 3 * CR] = jnp.dot(
                src[...], jnp.concatenate(taps, axis=1), preferred_element_type=F32
            )

        def body(i, summed):
            at = image_rows(i)
            col = column_of((PIX, CR))
            parts = []
            for kx in range(3):
                up, mid, down = (y[at, (kx * 3 + ky) * CR : (kx * 3 + ky + 1) * CR] for ky in range(3))
                parts.append(
                    mid
                    + jnp.concatenate([blank, up[: PIX - W]], axis=0)
                    + jnp.concatenate([down[W:], blank], axis=0)
                )
            z = (
                parts[1]
                + jnp.where(col > 0, pltpu.roll(parts[0], 1, 0), 0.0)
                + jnp.where(col < W - 1, pltpu.roll(parts[2], PIX - 1, 0), 0.0)
            )
            out[at, :] = z
            return summed + jnp.sum(z, axis=0, keepdims=True)

        return per_image(count, body, jnp.zeros((1, CR), F32))

    def spread_taps(i, grad):
        at = image_rows(i)
        col = column_of((PIX, CR))
        moved = (
            jnp.where(col < W - 1, pltpu.roll(grad, PIX - 1, 0), 0.0),
            grad,
            jnp.where(col > 0, pltpu.roll(grad, 1, 0), 0.0),
        )
        low_blank = blank.astype(BF16)
        for kx in range(3):
            low = moved[kx].astype(BF16)
            nine = (
                jnp.concatenate([low[W:], low_blank], axis=0),
                low,
                jnp.concatenate([low_blank, low[: PIX - W]], axis=0),
            )
            for ky in range(3):
                d9[at, (kx * 3 + ky) * CR : (kx * 3 + ky + 1) * CR] = nine[ky]

    def data_grad(l, height, write):
        step = 2 * CR
        for half in range(C // step):
            taps = [
                wf[l, t * C + half * step : t * C + (half + 1) * step, :].astype(BF16)
                for t in (3 * ky + kx for kx in range(3) for ky in range(3))
            ]
            part = lax.dot_general(
                d9[0:height, :],
                jnp.concatenate(taps, axis=1),
                (((1,), (1,)), ((), ())),
                preferred_element_type=F32,
            )
            write(half, part)

    def g_block(l, owner):
        return gf.at[l, block(owner)] if l < 4 else hg.at[owner]

    def from_core(l):
        return cr.at[l] if l < 4 else hcr

    def from_z(l):
        return zr.at[l] if l < 4 else hzr

    def weight_grad(l, src, height):
        for kx in range(3):
            part = lax.dot_general(
                src[...],
                d9[0:height, kx * 3 * CR : (kx + 1) * 3 * CR],
                (((0,), (0,)), ((), ())),
                preferred_element_type=F32,
            )
            for ky in range(3):
                t = 3 * ky + kx
                gf[l % 4, t * C : (t + 1) * C, :] = part[:, ky * CR : (ky + 1) * CR].astype(gf.dtype)
        if l == 4:

            def pack(i, carry):
                at = i * rows
                low = gf[0, pl.ds(pl.multiple_of(at, d.row_tile), half), :].astype(F32)
                high = gf[0, pl.ds(pl.multiple_of(at + half, d.row_tile), rows - half), :].astype(F32)
                if rows < 2 * half:
                    high = jnp.concatenate([high, jnp.zeros((2 * half - rows, CR), F32)], axis=0)
                hg[i] = (low + pltpu.roll(high, d.HC, 1)).astype(hg.dtype)
                return carry

            lax.fori_loop(0, F, pack, 0)
        over(Z, lambda k: send(g_block(l, 2 * k + 1 - core), from_core(l).at[k], sib, f"core{l}"))

    def core_sum(l):
        wait_recv(f"core{l}")

        def step(k):
            ref = g_block(l, 2 * k + core)
            ref[...] = (ref[...].astype(F32) + from_core(l)[k].astype(F32)).astype(ref.dtype)

        over(Z, step)

    def z_push(l):
        def push(k):
            to = (zc + k) % Z
            send(g_block(l, 2 * to + core), from_z(l).at[zc], (r, 2 * to + core), f"z{l}")

        if line:

            def to_middle():
                through, owner = jnp.where(zc == 0, 1, Z - 2), Z - 1 - zc
                send(g_block(l, 2 * owner + core), from_z(l).at[through], (r, 2 * through + core), f"mid{l}")

            when(is_end, to_middle)
            middle, outside = arriving.pop(f"mid{l}"), leaving.pop(f"mid{l}")
            arriving[f"mid{l}"] = lambda: when(jnp.logical_not(is_end), middle)
            leaving[f"mid{l}"] = lambda: when(is_end, outside)
        for k in range(1, Z) if Z <= 8 else ():
            if line and k == 2:
                when(is_end, lambda: push(2))
            else:
                direct(k, lambda: push(k))
        if Z > 8:
            over(Z, push, 1)
        arriving[f"z{l}"] = lambda: z_wait(l, rsem.at[GROUP[f"z{l}"]])
        leaving[f"z{l}"] = lambda: z_wait(l, ssem.at[GROUP[f"z{l}"]])

    def z_middle(l):
        if line:
            wait_recv(f"mid{l}")

            def hand_on():
                owner = (Z - 1) * (Z - 2 - zc)
                ref = g_block(l, 2 * owner + core)
                ref[...] = (ref[...].astype(F32) + from_z(l)[zc].astype(F32)).astype(ref.dtype)
                send(ref, from_z(l).at[zc], (r, 2 * owner + core), f"z{l}")

            when(jnp.logical_not(is_end), hand_on)

    def z_wait(l, sem):
        if line:
            when(is_end, lambda: wait_for(from_z(l).at[pl.ds(0, Z - 2)], sem))
            when(jnp.logical_not(is_end), lambda: wait_for(from_z(l).at[pl.ds(0, Z - 1)], sem))
        else:
            wait_for(from_z(l).at[pl.ds(0, Z - 1)], sem)

    def z_sum(l):
        wait_recv(f"z{l}")
        summed = g_block(l, f)[...].astype(F32)
        if line:
            one_side = jnp.where(zc == 0, 1, jnp.where(zc == Z - 1, Z - 2, zc - 1))
            other_side = jnp.where(zc == 0, 2, jnp.where(zc == Z - 1, 1, zc + 1))
            summed = summed + from_z(l)[one_side].astype(F32) + from_z(l)[other_side].astype(F32)
            opposite = jnp.where(zc == 1, Z - 1, 0)
            third = from_z(l)[opposite].astype(F32)
            summed = summed + jnp.where(is_end, 0.0, third)
        else:
            summed = lax.fori_loop(1, Z, lambda k, so_far: so_far + from_z(l)[(zc + k) % Z].astype(F32), summed)
        summed = summed * (1.0 / root)
        if l < 4:
            gw[l][:, my_lanes] = summed.astype(gw[l].dtype)
            here = gw[l].at[:, my_lanes]
            over(R, lambda k: send(here, here, rep_peer(k), f"rows{l}"), 1)
        else:
            hr[r] = summed.astype(hr.dtype)
            over(R, lambda k: send(hr.at[r], hr.at[r], rep_peer(k), "rows4"), 1)

    def rows_done(l):
        if l < 4:
            wait_recv(f"rows{l}")
        else:
            wait_recv("rows4")
            summed = sum(hr[i].astype(F32) for i in range(R))
            wide = -(-half // LANES) * LANES
            if wide > half:
                summed = jnp.concatenate([summed, jnp.zeros((wide - half, LANES), F32)], axis=0)
            summed = jnp.transpose(summed)
            ghc[:, 0:half] = summed[0 : d.HC, 0:half]
            ghc[:, half:rows] = summed[d.HC : 2 * d.HC, 0 : rows - half]

    def exchange(e):
        over(F, lambda k: send(st_s.at[e], st_r.at[e, f], (r, (f + k) % F), f"stat{e}"), 1)
        st_r[e, f] = st_s[e]

    def exchanged(e):
        wait_recv(f"stat{e}")
        return st_r[e]

    st_s[...] = jnp.zeros_like(st_s)
    w_relay_rest(0)
    w_relay_near(0)
    w_far(0)
    wait_recv("images")
    wait_recv("own_image")

    inverse_of, counts = [], None
    for l in range(4):
        w_finish(l)
        if l == 2:
            wait_recv("pool")
            s[2] = jnp.dot(u_sel[...], pool_all[...], preferred_element_type=F32).astype(BF16)
        elif l:
            wait_recv(f"ag{l - 1}")
        first = conv(s.at[l], M // PIX, l, zb)
        mean_here = first * (1.0 / M)

        def squares(i, so_far):
            return so_far + jnp.sum(jnp.square(zb[image_rows(i), :] - mean_here), axis=0, keepdims=True)

        st_s[l, 0:1, :] = first
        st_s[l, 1:2, :] = per_image(M // PIX, squares, jnp.zeros((1, CR), F32))
        if l == 0:
            st_s[l, 2:3, :] = sum(start_r[i, 0:1, :] for i in range(R))
        exchange(l)
        if l != 1:
            w_push_rest(l + 1)
        w_push_near(l + 1)
        parts = exchanged(l)
        tot = jnp.sum(parts, axis=0)
        mean = tot[0:1] * (1.0 / total)
        apart = jnp.sum(jnp.square(parts * (1.0 / M) - mean[None]), axis=0)[0:1] * float(M)
        inverse = lax.rsqrt((tot[1:2] + apart) * (1.0 / total) + EPS)
        inverse_of.append(inverse)
        if l == 0:
            counts = tot[2:3]
        g_row, b_row = gain[l : l + 1, my_lanes], shift[l : l + 1, my_lanes]

        def activate(i, carry):
            at = image_rows(i)
            normed = (zb[at, :] - mean) * inverse
            zhat[l, at, :] = normed
            shaped = normed * g_row + b_row
            hidden = shaped * jax.nn.sigmoid(shaped)
            if l == 1:
                zb[at, :] = hidden
            elif l == 3:
                a2a_s[i] = hidden.astype(BF16)
            else:
                s[l + 1, at, my_lanes] = hidden.astype(BF16)
            return carry

        per_image(M // PIX, activate, 0)
        if l == 1:
            inside, unused = windows(False)
            pooled = jnp.dot(
                jnp.where(inside, 0.25, 0.0), zb[...], precision=EXACT, preferred_element_type=F32
            )
            pool_own[...] = pooled.astype(BF16)
            pool_all[:, my_lanes] = pooled.astype(BF16)
            over(R, lambda k: send(pool_own, pool_all.at[:, my_lanes], rep_peer(k), "pool"), 1)
        elif l == 3:
            over(R, lambda k: send(a2a_s.at[(r + k) % R], s4.at[:, my_lanes], rep_peer(k), "a2a"), 1)
            s4[:, my_lanes] = a2a_s[r]
        else:
            here = s.at[l + 1, :, my_lanes]
            over(R, lambda k: send(here, here, rep_peer(k), f"ag{l}"), 1)
        w_relay_rest(l + 1)
        w_relay_near(l + 1)
        if l == 0:
            w_push_rest(2)
        w_far(l + 1)

    w_finish(4)
    low_lanes = lax.broadcasted_iota(jnp.int32, (half, LANES), 1) < d.HC

    def unpack(i, carry):
        both = hp[i].astype(F32)
        at = i * rows
        wf[4, pl.ds(pl.multiple_of(at, d.row_tile), half), :] = jnp.where(low_lanes, both, 0.0).astype(wf.dtype)
        high = jnp.where(low_lanes, pltpu.roll(both, d.HC, 1), 0.0).astype(wf.dtype)
        wf[4, pl.ds(pl.multiple_of(at + half, d.row_tile), rows - half), :] = high[0 : rows - half]
        return carry

    lax.fori_loop(0, F, unpack, 0)
    wait_recv("a2a")
    wait_recv("head_out")
    conv(s4, PD // PIX, 4, zb)
    head_bias = jnp.concatenate([hb[...], jnp.zeros((1, CR - d.HC), F32)], axis=1)
    out_bias = jnp.concatenate([ob[...], jnp.zeros((1, CR - d.OC), F32)], axis=1)
    head_raw = zb[0:PD, :] + head_bias
    squashed = jax.nn.sigmoid(head_raw)
    head_act = head_raw * squashed
    project = jnp.concatenate([ho_r[i][0 : d.q] for i in range(F)] + [jnp.zeros((LANES - d.HC, LANES), F32)], axis=0)
    out = jnp.dot(head_act, project, precision=EXACT, preferred_element_type=F32) + out_bias
    lane = lax.broadcasted_iota(jnp.int32, (PD, LANES), 1)
    classes = d.OC - 4
    factor = total * jnp.concatenate([tw[...], jnp.zeros((1, LANES - 3), F32)], axis=1) / jnp.maximum(counts, 1.0)
    pixel = [columns[:, i : i + 1] for i in range(8)]
    is_class = lane < classes
    top = jnp.max(jnp.where(is_class, out, -jnp.inf), axis=1, keepdims=True)
    grown = jnp.where(is_class, jnp.exp(jnp.where(is_class, out - top, 0.0)), 0.0)
    likely = grown / jnp.sum(grown, axis=1, keepdims=True)
    onehot = jnp.where(lane.astype(F32) == pixel[0], 1.0, 0.0)
    grad_class = factor[:, 0:1] * pixel[1] * (likely - onehot)
    misfit = out - pixel[4]
    grad_depth = factor[:, 1:2] * pixel[2] * misfit / jnp.sqrt(misfit * misfit + 1.0)
    is_normal = (lane > classes) & (lane < d.OC)
    predicted = jnp.where(is_normal, out, 0.0)
    wanted = sum(jnp.where(lane == classes + 1 + i, pixel[5 + i], 0.0) for i in range(3))
    radius = jnp.sqrt(jnp.sum(predicted * predicted, axis=1, keepdims=True) + 1.0)
    aligned = jnp.sum(predicted * wanted, axis=1, keepdims=True)
    grad_normal = -(factor[:, 2:3] * pixel[3]) * (wanted / radius - aligned / (radius * radius * radius) * predicted)
    grad_out = jnp.where(
        is_class, grad_class, jnp.where(lane == classes, grad_depth, jnp.where(is_normal, grad_normal, 0.0))
    )
    grad_act = lax.dot_general(
        grad_out, project, (((1,), (1,)), ((), ())), precision=EXACT, preferred_element_type=F32
    )
    grad_head = (grad_act * (squashed + head_raw * squashed * (1.0 - squashed))).astype(BF16).astype(F32)
    zb[0:PD, :] = grad_head
    y[0:PD, 0:CR] = head_act
    y[0:PD, CR : 2 * CR] = grad_out

    def spread_head(i, carry):
        spread_taps(i, zb[image_rows(i), :])
        return carry

    per_image(PD // PIX, spread_head, 0)

    def write_dh3(half, part):
        a2a_s[2 * half] = part[:, 0:CR].astype(BF16)
        a2a_s[2 * half + 1] = part[:, CR : 2 * CR].astype(BF16)

    wait_send("a2a")
    data_grad(4, PD, write_dh3)
    over(R, lambda k: send(a2a_s.at[(r + k) % R], a2a_r.at[r], rep_peer(k), "dh3"), 1)
    a2a_r[r] = a2a_s[r]
    weight_grad(4, s4, PD)
    head_act, grad_out = y[0:PD, 0:CR], y[0:PD, CR : 2 * CR]
    pad = jnp.zeros((2 * LANES - PD, LANES), F32)
    act_t = jnp.transpose(jnp.concatenate([head_act, pad], axis=0))[:, 0:PD]
    rep_s[0 : d.HC, :] = jnp.dot(act_t, grad_out, precision=EXACT, preferred_element_type=F32)[0 : d.HC]
    rep_s[d.HC : d.HC + 8, :] = jnp.zeros((8, LANES), F32)
    rep_s[d.HC : d.HC + 1, :] = jnp.sum(zb[0:PD, :], axis=0, keepdims=True)
    rep_s[d.HC + 1 : d.HC + 2, :] = jnp.sum(grad_out, axis=0, keepdims=True)
    over(R, lambda k: send(rep_s, rep_r.at[r], rep_peer(k), "small_rep"), 1)
    rep_r[r] = rep_s[...]

    def head_small():
        wait_recv("small_rep")
        summed = sum(rep_r[i] for i in range(R))
        for i in range(F):
            all_s[i, 0 : d.q, :] = summed[i * d.q : (i + 1) * d.q]
            if d.q < 8:
                all_s[i, d.q : 8, :] = jnp.zeros((8 - d.q, LANES), F32)
            all_s[i, 8:16, :] = summed[d.HC : d.HC + 8]
        over(F, lambda k: send(all_s.at[(f + k) % F], all_r.at[f], (r, (f + k) % F), "small_all"), 1)
        all_r[f] = all_s[f]

    for l in (3, 2, 1, 0):
        e = 7 - l
        g_row, b_row = gain[l : l + 1, my_lanes], shift[l : l + 1, my_lanes]
        if l == 3:
            wait_recv("dh3")
            entering = lambda i, at: a2a_r[i].astype(F32)
        elif l == 1:
            wait_recv("rs2")
            pooled = sum(ps_r[i].astype(F32) for i in range(R))
            inside, unused = windows(True)
            zb[...] = jnp.dot(jnp.where(inside, 0.25, 0.0), pooled, precision=EXACT, preferred_element_type=F32)
            entering = lambda i, at: zb[at, :]
        else:
            slot = 0 if l == 2 else 1
            wait_recv(f"rs{l + 1}")
            entering = lambda i, at: sum(rs_r[slot, j, at, :].astype(F32) for j in range(R))

        def slopes(i, so_far):
            at = image_rows(i)
            normed = zhat[l, at, :]
            shaped = normed * g_row + b_row
            squashed = jax.nn.sigmoid(shaped)
            grad = entering(i, at) * (squashed + shaped * squashed * (1.0 - squashed))
            zb[at, :] = grad
            return (
                so_far[0] + jnp.sum(grad, axis=0, keepdims=True),
                so_far[1] + jnp.sum(grad * normed, axis=0, keepdims=True),
            )

        none = jnp.zeros((1, CR), F32)
        part_bias, part_gain = per_image(M // PIX, slopes, (none, none))
        st_s[e, 0:1, :] = part_bias
        st_s[e, 1:2, :] = part_gain
        exchange(e)
        core_sum(l + 1)
        z_push(l + 1)
        if l == 3:
            head_small()
        else:
            z_sum(l + 2)
        tot = jnp.sum(exchanged(e), axis=0)
        bias_sum, gain_sum = tot[0:1], tot[1:2]
        norm_s[l : l + 1, :] = gain_sum * (1.0 / root)
        norm_s[4 + l : 5 + l, :] = bias_sum * (1.0 / root)
        scale = inverse_of[l] * g_row

        def through_norm(i, carry):
            at = image_rows(i)
            spread_taps(
                i, scale * (zb[at, :] - bias_sum * (1.0 / total) - zhat[l, at, :] * (gain_sum * (1.0 / total)))
            )
            return carry

        per_image(M // PIX, through_norm, 0)
        if l == 2:

            def write(half, part):
                chosen = jnp.dot(ut_sel[...], part.astype(BF16), preferred_element_type=F32).astype(BF16)
                ps_s[2 * half] = chosen[:, 0:CR]
                ps_s[2 * half + 1] = chosen[:, CR : 2 * CR]

            data_grad(l, M, write)
            over(R, lambda k: send(ps_s.at[(r + k) % R], ps_r.at[r], rep_peer(k), "rs2"), 1)
            ps_r[r] = ps_s[r]
            weight_grad(l, s.at[l], M)
            z_middle(l + 1)
        elif l == 0:
            weight_grad(l, s.at[l], M)

            def write(half, part):
                for i in range(R):
                    gi_s[i, :, half * 2 * CR : (half + 1) * 2 * CR] = part[i * PD : (i + 1) * PD].astype(BF16)

            data_grad(l, M, write)
            over(R, lambda k: send(gi_s.at[(r + k) % R], gi_r.at[r], rep_peer(k), "rs0"), 1)
            gi_r[r] = gi_s[r]
            z_middle(1)
            core_sum(0)
            z_push(0)
        else:
            slot = 0 if l == 3 else 1

            def write(half, part):
                rs_s[slot, 2 * half] = part[:, 0:CR].astype(BF16)
                rs_s[slot, 2 * half + 1] = part[:, CR : 2 * CR].astype(BF16)

            data_grad(l, M, write)
            over(R, lambda k: send(rs_s.at[slot, (r + k) % R], rs_r.at[slot, r], rep_peer(k), f"rs{l}"), 1)
            rs_r[slot, r] = rs_s[slot, r]
            weight_grad(l, s.at[l], M)
            z_middle(l + 1)

    gnorm[:, my_lanes] = norm_s[...]
    over(R, lambda k: send(norm_s, gnorm.at[:, my_lanes], rep_peer(k), "norms"), 1)
    z_middle(0)
    z_sum(1)
    wait_recv("small_all")
    gsmall[...] = jnp.sum(all_r[...], axis=0) * (1.0 / root)
    rows_done(4)
    rows_done(3)
    rows_done(2)
    wait_recv("rs0")
    gi[...] = sum(gi_r[i].astype(F32) for i in range(R))
    z_sum(0)
    wait_recv("norms")
    rows_done(1)
    rows_done(0)

    drain()


def finish(gi, gw0, gw1, gw2, gw3, ghc, gnorm, gsmall, *outs):
    out_gi, out0, out1, out2, out3, out_hc, out_ho, out_gain, out_bias, out_hb, out_ob = outs
    out_gi[...] = gi[...]
    for src, dst in ((gw0, out0), (gw1, out1), (gw2, out2), (gw3, out3)):
        dst[...] = src[...].astype(F32)

    @pl.when(pl.program_id(0) == 0)
    def _():
        out_hc[...] = ghc[...]
        out_ho[...] = gsmall[0 : out_ho.shape[0], 0 : out_ho.shape[1]]
        out_gain[...] = gnorm[0:4, :]
        out_bias[...] = gnorm[4:8, :]
        out_hb[...] = gsmall[8:9, 0 : out_hb.shape[1]]
        out_ob[...] = gsmall[9:10, 0 : out_ob.shape[1]]


def per_device(
    R, F,
    images, enc_first, enc_second, dec_first, dec_second, head_conv, head_out, norm_gain, norm_bias, head_bias, out_bias,
    task_weights, pool_index, labels, task_masks, targets,
):
    n, height, breadth, channels = images.shape
    rows, hidden = head_conv.shape
    q, out_ch = head_out.shape
    d = types.SimpleNamespace(
        n=n, R=R, F=F, Z=F // 2, rows=rows, C=channels, CR=channels // R, W=breadth, PIX=height * breadth,
        PD=n * height * breadth, HC=hidden, OC=out_ch, q=q,
    )
    d.M = R * d.PD
    d.PW = d.M // 4
    wire = BF16 if rows % 16 == 0 else F32
    d.row_tile = 16 if rows % 16 == 0 else 8
    d.half = -(-rows // (2 * d.row_tile)) * d.row_tile
    vm = pltpu.VMEM
    patch = 9 * channels
    scratch = [
        vm((4, d.M, d.C), BF16),
        vm((d.PD, d.C), BF16),
        vm((5, patch, d.CR), wire),
        vm((d.M, 9 * d.CR), F32),
        vm((d.M, d.CR), F32),
        vm((4, d.M, d.CR), F32),
        vm((d.M, 9 * d.CR), BF16),
        vm((d.M, d.PW), BF16),
        vm((d.PW, d.M), BF16),
        vm((R, d.PD, d.CR), BF16),
        vm((R, d.PD, d.CR), BF16),
        vm((2, R, d.M, d.CR), BF16),
        vm((2, R, d.M, d.CR), BF16),
        vm((d.PW, d.CR), BF16),
        vm((d.PW, d.C), BF16),
        vm((R, d.PW, d.CR), BF16),
        vm((R, d.PW, d.CR), BF16),
        vm((R, d.PD, d.C), BF16),
        vm((R, d.PD, d.C), BF16),
        vm((4, patch, d.CR), wire),
        vm((4, d.Z, rows, d.CR), wire),
        vm((4, d.Z, rows, d.CR), wire),
        vm((d.half, LANES), wire),
        vm((F, d.half, LANES), wire),
        vm((F, d.half, LANES), wire),
        vm((d.Z, d.half, LANES), wire),
        vm((d.Z, d.half, LANES), wire),
        vm((R, d.half, LANES), wire),
        vm((8, 8, LANES), F32),
        vm((8, F, 8, LANES), F32),
        vm((8, LANES), F32),
        vm((R, 8, LANES), F32),
        vm((8, LANES), F32),
        vm((F, 8, LANES), F32),
        vm((hidden + 8, LANES), F32),
        vm((R, hidden + 8, LANES), F32),
        vm((F, 16, LANES), F32),
        vm((F, 16, LANES), F32),
        vm((8, LANES), F32),
        vm((LANES, 2 * LANES), F32),
        pltpu.SemaphoreType.DMA((len(GROUPS),)),
        pltpu.SemaphoreType.DMA((len(GROUPS),)),
        pltpu.SemaphoreType.DMA((5, d.Z)),
        pltpu.SemaphoreType.DMA((5, d.Z)),
        pltpu.SemaphoreType.DMA((5, d.Z)),
        pltpu.SemaphoreType.DMA((5, d.Z)),
    ]
    here, there = pl.BlockSpec(memory_space=pltpu.VMEM), pl.BlockSpec(memory_space=pl.ANY)
    shape = jax.ShapeDtypeStruct
    kept = pl.pallas_call(
        functools.partial(kernel, d),
        out_shape=[shape((d.PD, d.C), F32)]
        + [shape((rows, d.C), wire)] * 4
        + [shape((hidden, rows), F32), shape((8, d.C), F32), shape((16, LANES), F32)],
        in_specs=[there] * 5 + [here] * 11,
        out_specs=[here] * 8,
        scratch_shapes=scratch,
        compiler_params=pltpu.CompilerParams(collective_id=0, has_side_effects=True, vmem_limit_bytes=60 * 2**20),
    )(
        images.reshape(d.PD, channels),
        *(w.astype(wire) for w in (enc_first, enc_second, dec_first, dec_second)),
        head_conv.T, head_out, norm_gain, norm_bias, head_bias.reshape(1, hidden), out_bias.reshape(1, out_ch),
        task_weights.reshape(1, 3), pool_index, labels, jnp.transpose(task_masks, (1, 0, 2)), targets,
    )
    steps = next(count for count in (4, 3, 2, 1) if rows % (count * d.row_tile) == 0 and d.PD % (count * 8) == 0)
    part = lambda height, width: pl.BlockSpec((height // steps, width), lambda i: (i, 0))
    all_of = lambda height, width: pl.BlockSpec((height, width), lambda i: (0, 0))
    rest = ((q, out_ch), (4, channels), (4, channels), (1, hidden), (1, out_ch))
    gi, gw0, gw1, gw2, gw3, ghc, gq, gain, bias, ghb, gob = pl.pallas_call(
        finish,
        grid=(steps,),
        out_shape=[shape((d.PD, channels), F32)]
        + [shape((rows, channels), F32)] * 4
        + [shape((hidden, rows), F32)]
        + [shape(size, F32) for size in rest],
        in_specs=[part(d.PD, channels)]
        + [part(rows, channels)] * 4
        + [all_of(hidden, rows), all_of(8, channels), all_of(16, LANES)],
        out_specs=[part(d.PD, channels)]
        + [part(rows, channels)] * 4
        + [all_of(hidden, rows)]
        + [all_of(*size) for size in rest],
    )(*kept)
    return (
        gi.reshape(images.shape), gw0, gw1, gw2, gw3, ghc.T, gq, gain, bias, ghb.reshape(hidden), gob.reshape(out_ch),
    )


def solution(mesh):
    split = ("rep", "fsdp")
    rows = P("fsdp", None)
    return jax.shard_map(
        functools.partial(per_device, mesh.shape["rep"], mesh.shape["fsdp"]),
        mesh=mesh,
        in_specs=(P(split, None, None, None),)
        + (rows,) * 6
        + (P(),) * 5
        + (P(split, None), P(split, None), P(split, None, None), P(split, None, None)),
        out_specs=(P(split, None, None, None),) + (rows,) * 6 + (P(),) * 4,
        check_vma=False,
    )
```

```python
import functools
import math
import types

import jax
import jax.numpy as jnp
from jax import lax
from jax.experimental import pallas as pl
from jax.experimental.pallas import tpu as pltpu
from jax.sharding import PartitionSpec as P

MESH = pl.DeviceIdType.MESH
F32, BF16 = jnp.float32, jnp.bfloat16
EPS = 1e-05
LANES = 128
EXACT = lax.Precision.HIGHEST

GROUPS = (
    ["images", "start", "head_out", "a2a", "pool", "dh3", "rs2", "norms", "small_rep", "small_all"]
    + [f"sums{i}" for i in range(2)]
    + [f"norm{i}" for i in range(2)]
    + [
        f"{name}{way}"
        for name in ("ag0", "ag2", "rs3", "rs1", "rs0", "rows0", "rows1", "rows2", "rows3")
        for way in ("x0", "x1", "y0", "y1", "f0", "f1")
    ]
    + [f"stat{i}" for i in range(8)]
    + [f"core{i}" for i in range(5)]
    + [f"z{i}" for i in range(5)]
    + [f"mid{i}" for i in range(5)]
    + ["rows4"]
    + [f"own{i}" for i in range(5)]
    + [f"out{i}" for i in range(4)]
    + ["own_image"]
)
GROUP = {name: number for number, name in enumerate(GROUPS)}


def kernel(d, *refs):
    it = iter(refs)
    take = lambda count: [next(it) for _ in range(count)]
    images, w0, w1, w2, w3, hw, ho, gain, shift, hb, ob, tw, pidx, lab, msk, tgt = take(16)
    gi, gw0, gw1, gw2, gw3, ghc, gnorm, gsmall = take(8)
    gather, columns_s = take(2)
    (s, s4, wf, y, zb, zhat, d9, u_sel, ut_sel, a2a_s, a2a_r, rs_s, rs_l, pool_own, pool_all, ps_s, ps_r, gi_s, gi_l) = take(19)
    (zg, slope, slope_z, nrm_s, nrm_r, sums_s, sums_r) = take(7)
    (gf, cr, zr, hw_s, hp, hg, hcr, hzr, hr, st_s, st_r, start_s, start_r, ho_s, ho_r, rep_s, rep_r, all_s, all_r, norm_s, feat) = take(21)
    ssem, rsem, wsz, wrz, wsf, wrf = take(6)
    w_in, gw = (w0, w1, w2, w3, hw_s), (gw0, gw1, gw2, gw3)
    R, F, Z, rows, half, C, CR, W, PIX, PD, M, PW = d.R, d.F, d.Z, d.rows, d.half, d.C, d.CR, d.W, d.PIX, d.PD, d.M, d.PW
    total = float(M * F)
    root = math.sqrt(total)

    r, f = lax.axis_index("rep"), lax.axis_index("fsdp")
    zc, core = f // 2, f % 2
    sib = (r, zc * 2 + (1 - core))
    rep_peer = lambda k: ((r + k) % R, f)
    one, two = r + 1 - 2 * (r % 2), (r + 2) % R
    both = (one + 2) % R
    at_one, at_two = (one, f), (two, f)
    z_peer = lambda k: (r, ((zc + k) % Z) * 2 + core)
    line = Z == 4
    is_end = (zc == 0) | (zc == Z - 1)
    is_far = lambda k: (zc + k) % Z - zc == Z - 1
    is_far_back = lambda k: zc - (zc + k) % Z == Z - 1
    ends_apart = lambda k: is_far(k) | is_far_back(k)
    my_lanes = pl.ds(pl.multiple_of(r * CR, CR), CR)

    def block(owner):
        return pl.ds(pl.multiple_of(owner * rows, d.row_tile), rows)

    arriving, leaving = {}, {}

    def first_of(ref, count):
        return lambda: ref.at[pl.ds(0, count)]

    volume = {
        "images": first_of(s.at[0], (R - 1) * PD),
        "own_image": first_of(s.at[0], PD),
        "start": first_of(start_r, R - 1),
        "head_out": first_of(ho_r, F - 1),
        "a2a": lambda: s4.at[:, pl.ds(0, (R - 1) * CR)],
        "pool": lambda: pool_all.at[:, pl.ds(0, (R - 1) * CR)],
        "dh3": first_of(a2a_r, R - 1),
        "rs2": first_of(ps_r, R - 1),
        "norms": lambda: gnorm.at[:, pl.ds(0, (R - 1) * CR)],
        "small_rep": first_of(rep_r, R - 1),
        "small_all": first_of(all_r, F - 1),
        "rows4": first_of(hr, R - 1),
        "core4": lambda: hcr,
        "mid4": lambda: hzr.at[0],
    }
    for way in ("x", "y", "f"):
        for h in range(2):
            for j in range(2):
                volume[f"ag{2 * j}{way}{h}"] = lambda j=j: zg.at[j, pl.ds(0, M // 2), pl.ds(0, CR)]
                volume[f"rs{2 * j + 1}{way}{h}"] = lambda j=j: rs_l.at[j, 0]
            volume[f"rs0{way}{h}"] = lambda: gi_l.at[0]
            size = half if h == 0 else rows - half
            for l in range(4):
                volume[f"rows{l}{way}{h}"] = lambda l=l, size=size: gather.at[l, pl.ds(0, size), pl.ds(0, CR)]
    for j in range(2):
        volume[f"sums{j}"] = first_of(sums_r.at[j], R - 1)
        volume[f"norm{j}"] = first_of(nrm_r.at[j], R - 1)
    for e in range(8):
        volume[f"stat{e}"] = first_of(st_r.at[e], F - 1)
    for l in range(4):
        volume[f"core{l}"] = lambda l=l: cr.at[l]
        volume[f"mid{l}"] = lambda l=l: zr.at[l, 0]

    def wait_for(ref, sem):
        pltpu.make_async_copy(ref, ref, sem).wait()

    def wait_recv(group):
        arriving.pop(group)()

    def wait_send(group):
        leaving.pop(group)()

    def copy_here(src, dst, group):
        g = GROUP[group]
        arriving[group] = lambda: wait_for(dst, rsem.at[g])
        pltpu.make_async_copy(src, dst, rsem.at[g]).start()

    def send(src, dst, to, group):
        g = GROUP[group]
        if group in volume:
            arriving[group] = lambda: wait_for(volume[group](), rsem.at[g])
            leaving[group] = lambda: wait_for(volume[group](), ssem.at[g])
        pltpu.make_async_remote_copy(
            src_ref=src, dst_ref=dst, send_sem=ssem.at[g], recv_sem=rsem.at[g], device_id=to, device_id_type=MESH
        ).start()

    def over(count, body, first=0):
        if count <= 8:
            for i in range(first, count):
                body(i)
            return

        def step(i, carry):
            body(i)
            return carry

        lax.fori_loop(first, count, step, 0)

    def when(condition, body):
        pl.when(condition)(body)

    def direct(k, body):
        if line and k in (1, Z - 1):
            when(jnp.logical_not(ends_apart(k)), body)
        else:
            body()

    def drain():
        for waits in (arriving, leaving):
            for wait in list(waits.values()):
                wait()

    barrier = pltpu.get_barrier_semaphore()
    over(R, lambda k: pl.semaphore_signal(barrier, inc=1, device_id=rep_peer(k), device_id_type=MESH), 1)
    over(F, lambda k: pl.semaphore_signal(barrier, inc=1, device_id=(r, (f + k) % F), device_id_type=MESH), 1)
    pl.semaphore_wait(barrier, R + F - 2)

    def w_block(l, owner):
        return wf.at[l, block(owner)] if l < 4 else hp.at[owner]

    def w_copy(l, src, owner, to, send_sem, recv_sem):
        return pltpu.make_async_remote_copy(
            src_ref=src, dst_ref=w_block(l, owner), send_sem=send_sem, recv_sem=recv_sem, device_id=to, device_id_type=MESH
        )

    def w_src(l):
        return w_in[l].at[:, my_lanes] if l < 4 else hw_s

    def w_send(l, k):
        arriving["near" if k in (1, Z - 1) else "rest", l, k] = lambda: direct(Z - k, lambda: w_wait(l, wrz.at[l, k]))
        leaving["w", l, k] = lambda: direct(k, lambda: w_wait(l, wsz.at[l, k]))
        direct(k, lambda: w_copy(l, w_src(l), f, z_peer(k), wsz.at[l, k], wrz.at[l, k]).start())

    def w_push_near(l):
        for k in sorted({1, Z - 1}):
            w_send(l, k)
        w_copy(l, w_src(l), f, sib, wsf.at[l, 0], wrf.at[l, 0]).start()
        arriving["core", l, 0] = lambda: w_wait(l, wrf.at[l, 0])
        leaving["core", l, 0] = lambda: w_wait(l, wsf.at[l, 0])
        copy_here(w_src(l), w_block(l, f), f"own{l}")

    def w_push_rest(l):
        for k in range(2, Z - 1):
            w_send(l, k)

    def w_wait(l, sem):
        pltpu.make_async_copy(w_block(l, f), w_block(l, f), sem).wait()

    def w_arrived(l, k):
        owner = ((zc + Z - k) % Z) * 2 + core
        w_wait(l, wrz.at[l, k])
        w_copy(l, w_block(l, owner), owner, sib, wsf.at[l, k], wrf.at[l, k]).start()

    def w_relayed(l, k):
        arriving["core", l, k] = lambda: w_wait(l, wrf.at[l, k])
        leaving["core", l, k] = lambda: w_wait(l, wsf.at[l, k])

    def w_relay_rest(l):
        for k in range(2, Z - 1):
            arriving.pop(("rest", l, k))
            w_arrived(l, k)
            w_relayed(l, k)
        if line:

            def hand_on():
                to = (Z - 1) * (zc - 1)
                owner = (Z - 1 - to) * 2 + core
                slot = jnp.where(zc == 1, 1, Z - 1)
                w_copy(l, w_block(l, owner), owner, (r, to * 2 + core), wsz.at[l, 0], wrz.at[l, slot]).start()

            when(jnp.logical_not(is_end), hand_on)
            leaving["far", l] = lambda: when(jnp.logical_not(is_end), lambda: w_wait(l, wsz.at[l, 0]))

    def w_relay_near(l):
        for k in sorted({1, Z - 1}):
            arriving.pop(("near", l, k))
            direct(Z - k, lambda: w_arrived(l, k))
            if not line:
                w_relayed(l, k)

    def w_far(l):
        if line:
            for k in (1, Z - 1):
                w_relayed(l, k)
            when(zc == 0, lambda: w_arrived(l, 1))
            when(zc == Z - 1, lambda: w_arrived(l, Z - 1))

    def w_finish(l):
        for k in range(Z):
            wait_recv(("core", l, k))
        wait_recv(f"own{l}")

    w_push_rest(0)
    w_push_near(0)
    over(R, lambda k: send(images, s.at[0, pl.ds(pl.multiple_of(r * PD, PD), PD)], rep_peer(k), "images"), 1)
    own_rows = s.at[0, pl.ds(pl.multiple_of(r * PD, PD), PD)]
    copy_here(images, own_rows, "own_image")

    start_s[...] = jnp.zeros_like(start_s)
    masks = jnp.concatenate([msk[:, i, :] for i in range(d.n)], axis=1).astype(F32)
    labels = jnp.concatenate([lab[i : i + 1, :] for i in range(d.n)], axis=1).astype(F32)
    wanted = jnp.concatenate([tgt[i] for i in range(d.n)], axis=1)
    pools = jnp.concatenate([pidx[i : i + 1, :] for i in range(d.n)], axis=1).astype(F32)
    counted = jnp.sum(masks, axis=1, keepdims=True)
    lane = lax.broadcasted_iota(jnp.int32, (1, LANES), 1)
    start_s[0:1, :] = sum(jnp.where(lane == t, counted[t : t + 1, :], 0.0) for t in range(3))
    start_s[1:2, 0 : PW // R] = pools
    over(R, lambda k: send(start_s, start_r.at[r], rep_peer(k), "start"), 1)
    start_r[r] = start_s[...]
    ho_s[...] = jnp.zeros_like(ho_s)
    ho_s[0 : d.q, 0 : d.OC] = ho[...].astype(F32)
    over(F, lambda k: send(ho_s, ho_r.at[f], (r, (f + k) % F), "head_out"), 1)
    ho_r[f] = ho_s[...]
    def pack_head():
        wide = -(-rows // LANES) * LANES
        tall = jnp.concatenate([hw[...].astype(F32), jnp.zeros((LANES - d.HC, rows), F32)], axis=0)
        if wide > rows:
            tall = jnp.concatenate([tall, jnp.zeros((LANES, wide - rows), F32)], axis=1)
        tall = jnp.transpose(tall)
        if wide < 2 * half:
            tall = jnp.concatenate([tall, jnp.zeros((2 * half - wide, LANES), F32)], axis=0)
        hw_s[...] = (tall[0:half] + pltpu.roll(tall[half : 2 * half], d.HC, 1)).astype(hw_s.dtype)

    bits = W.bit_length() - 1

    def places(axis, shape):
        q = lax.broadcasted_iota(jnp.int32, shape, axis)
        image = jnp.zeros(shape, jnp.int32)
        for i in range(1, M // PIX):
            image = image + jnp.where(q >= i * PIX, 1, 0)
        q = q - image * PIX
        window = image * (PIX // 4) + (q >> (bits + 1)) * (W // 2) + ((q & (W - 1)) >> 1)
        position = 2 * ((q >> bits) & 1) + (q & 1)
        return window, position.astype(F32)

    def windows(rows_first):
        shape = (M, PW) if rows_first else (PW, M)
        window, position = places(0 if rows_first else 1, shape)
        other = lax.broadcasted_iota(jnp.int32, shape, 1 if rows_first else 0)
        return window == other, position

    def pixel_columns():
        feat[...] = jnp.zeros_like(feat)
        feat[0:1, 0:PD] = labels
        feat[1:4, 0:PD] = masks
        feat[4:8, 0:PD] = wanted
        columns_s[...] = jnp.transpose(feat[...])[0:PD, 0:LANES]

    def pool_matrices():
        feat[...] = jnp.zeros_like(feat)
        for i in range(R):
            feat[0:1, i * (PW // R) : (i + 1) * (PW // R)] = start_r[i, 1:2, 0 : PW // R]
        picked_row = feat[0:1, 0:PW]
        picked_col = jnp.transpose(feat[...])[0:PW, 0:1]
        inside, position = windows(True)
        u_sel[...] = jnp.where(inside & (position == picked_row), 1.0, 0.0).astype(BF16)
        inside, position = windows(False)
        ut_sel[...] = jnp.where(inside & (position == picked_col), 1.0, 0.0).astype(BF16)

    def image_rows(i):
        return pl.ds(pl.multiple_of(i * PIX, PIX), PIX)

    def per_image(count, body, init):
        return lax.fori_loop(0, count, body, init)

    def column_of(shape):
        return lax.broadcasted_iota(jnp.int32, shape, 0) & (W - 1)

    blank = jnp.zeros((W, CR), F32)

    def conv(src, count, l, out):
        height = count * PIX
        for kx in range(3):
            taps = [wf[l, (3 * ky + kx) * C : (3 * ky + kx + 1) * C, :].astype(BF16) for ky in range(3)]
            y[0:height, kx * 3 * CR : (kx + 1) * 3 * CR] = jnp.dot(
                src[...], jnp.concatenate(taps, axis=1), preferred_element_type=F32
            )

        def body(i, summed):
            at = image_rows(i)
            col = column_of((PIX, CR))
            parts = []
            for kx in range(3):
                up, mid, down = (y[at, (kx * 3 + ky) * CR : (kx * 3 + ky + 1) * CR] for ky in range(3))
                parts.append(
                    mid
                    + jnp.concatenate([blank, up[: PIX - W]], axis=0)
                    + jnp.concatenate([down[W:], blank], axis=0)
                )
            z = (
                parts[1]
                + jnp.where(col > 0, pltpu.roll(parts[0], 1, 0), 0.0)
                + jnp.where(col < W - 1, pltpu.roll(parts[2], PIX - 1, 0), 0.0)
            )
            out[at, :] = z
            return summed + jnp.sum(z, axis=0, keepdims=True)

        return per_image(count, body, jnp.zeros((1, CR), F32))

    def spread_taps(i, grad):
        at = image_rows(i)
        col = column_of((PIX, CR))
        moved = (
            jnp.where(col < W - 1, pltpu.roll(grad, PIX - 1, 0), 0.0),
            grad,
            jnp.where(col > 0, pltpu.roll(grad, 1, 0), 0.0),
        )
        low_blank = blank.astype(BF16)
        for kx in range(3):
            low = moved[kx].astype(BF16)
            nine = (
                jnp.concatenate([low[W:], low_blank], axis=0),
                low,
                jnp.concatenate([low_blank, low[: PIX - W]], axis=0),
            )
            for ky in range(3):
                d9[at, (kx * 3 + ky) * CR : (kx * 3 + ky + 1) * CR] = nine[ky]

    def data_grad(l, height, write):
        step = 2 * CR
        for half in range(C // step):
            taps = [
                wf[l, t * C + half * step : t * C + (half + 1) * step, :].astype(BF16)
                for t in (3 * ky + kx for kx in range(3) for ky in range(3))
            ]
            part = lax.dot_general(
                d9[0:height, :],
                jnp.concatenate(taps, axis=1),
                (((1,), (1,)), ((), ())),
                preferred_element_type=F32,
            )
            write(half, part)

    def lanes_of(owner):
        return pl.ds(pl.multiple_of(owner * CR, CR), CR)

    def gather_start(name, piece):
        send(piece(r, 0), piece(r, 0), at_one, f"{name}x0")
        send(piece(r, 1), piece(r, 1), at_two, f"{name}y1")
        send(piece(r, 1), piece(r, 1), at_one, f"{name}x1")
        send(piece(r, 0), piece(r, 0), at_two, f"{name}y0")

    def gather_forward(name, piece):
        wait_recv(f"{name}x0")
        send(piece(one, 0), piece(one, 0), at_two, f"{name}f0")
        wait_recv(f"{name}y1")
        send(piece(two, 1), piece(two, 1), at_one, f"{name}f1")

    def await_rest(name):
        for way in ("x1", "y0", "f0", "f1"):
            wait_recv(f"{name}{way}")

    def scatter_start(name, piece, land):
        send(piece(both, 0), land(0), at_one, f"{name}x0")
        send(piece(both, 1), land(2), at_two, f"{name}y1")
        send(piece(one, 0), land(1), at_one, f"{name}x1")
        send(piece(two, 1), land(3), at_two, f"{name}y0")

    def scatter_forward(name, piece, land):
        for way, ref, came, dst, to, group in (
            ("x0", piece(two, 0), land(0), land(4), at_two, "f0"),
            ("y1", piece(one, 1), land(2), land(5), at_one, "f1"),
        ):
            wait_recv(f"{name}{way}")
            ref[...] = (ref[...].astype(F32) + came[...].astype(F32)).astype(ref.dtype)
            send(ref, dst, to, f"{name}{group}")

    def ag_piece(j):
        return lambda owner, h: zg.at[j, pl.ds(h * (M // 2), M // 2), lanes_of(owner)]

    def rows_piece(l):
        return lambda owner, h: gather.at[l, pl.ds(h * half, half if h == 0 else rows - half), lanes_of(owner)]

    def rs_piece(j):
        return lambda owner, h: rs_s.at[j, owner, pl.ds(h * (M // 2), M // 2)]

    def rs_land(j):
        return lambda i: rs_l.at[j, i]

    def gi_piece(owner, h):
        return gi_s.at[owner, pl.ds(h * (PD // 2), PD // 2)]

    def gi_land(i):
        return gi_l.at[i]

    def sigmoid(v):
        return 0.5 * jnp.tanh(0.5 * v) + 0.5

    def g_block(l, owner):
        return gf.at[l, block(owner)] if l < 4 else hg.at[owner]

    def from_core(l):
        return cr.at[l] if l < 4 else hcr

    def from_z(l):
        return zr.at[l] if l < 4 else hzr

    def weight_grad(l, src, height):
        for kx in range(3):
            part = lax.dot_general(
                src[...],
                d9[0:height, kx * 3 * CR : (kx + 1) * 3 * CR],
                (((0,), (0,)), ((), ())),
                preferred_element_type=F32,
            )
            for ky in range(3):
                t = 3 * ky + kx
                gf[l % 4, t * C : (t + 1) * C, :] = part[:, ky * CR : (ky + 1) * CR].astype(gf.dtype)
        if l == 4:

            def pack(i, carry):
                at = i * rows
                low = gf[0, pl.ds(pl.multiple_of(at, d.row_tile), half), :].astype(F32)
                high = gf[0, pl.ds(pl.multiple_of(at + half, d.row_tile), rows - half), :].astype(F32)
                if rows < 2 * half:
                    high = jnp.concatenate([high, jnp.zeros((2 * half - rows, CR), F32)], axis=0)
                hg[i] = (low + pltpu.roll(high, d.HC, 1)).astype(hg.dtype)
                return carry

            lax.fori_loop(0, F, pack, 0)
        over(Z, lambda k: send(g_block(l, 2 * k + 1 - core), from_core(l).at[k], sib, f"core{l}"))

    def core_sum(l):
        wait_recv(f"core{l}")

        def step(k):
            ref = g_block(l, 2 * k + core)
            ref[...] = (ref[...].astype(F32) + from_core(l)[k].astype(F32)).astype(ref.dtype)

        over(Z, step)

    def z_push(l):
        def push(k):
            to = (zc + k) % Z
            send(g_block(l, 2 * to + core), from_z(l).at[zc], (r, 2 * to + core), f"z{l}")

        if line:

            def to_middle():
                through, owner = jnp.where(zc == 0, 1, Z - 2), Z - 1 - zc
                send(g_block(l, 2 * owner + core), from_z(l).at[through], (r, 2 * through + core), f"mid{l}")

            when(is_end, to_middle)
            middle, outside = arriving.pop(f"mid{l}"), leaving.pop(f"mid{l}")
            arriving[f"mid{l}"] = lambda: when(jnp.logical_not(is_end), middle)
            leaving[f"mid{l}"] = lambda: when(is_end, outside)
        for k in range(1, Z) if Z <= 8 else ():
            if line and k == 2:
                when(is_end, lambda: push(2))
            else:
                direct(k, lambda: push(k))
        if Z > 8:
            over(Z, push, 1)
        arriving[f"z{l}"] = lambda: z_wait(l, rsem.at[GROUP[f"z{l}"]])
        leaving[f"z{l}"] = lambda: z_wait(l, ssem.at[GROUP[f"z{l}"]])

    def z_middle(l):
        if line:
            wait_recv(f"mid{l}")

            def hand_on():
                owner = (Z - 1) * (Z - 2 - zc)
                ref = g_block(l, 2 * owner + core)
                ref[...] = (ref[...].astype(F32) + from_z(l)[zc].astype(F32)).astype(ref.dtype)
                send(ref, from_z(l).at[zc], (r, 2 * owner + core), f"z{l}")

            when(jnp.logical_not(is_end), hand_on)

    def z_wait(l, sem):
        if line:
            when(is_end, lambda: wait_for(from_z(l).at[pl.ds(0, Z - 2)], sem))
            when(jnp.logical_not(is_end), lambda: wait_for(from_z(l).at[pl.ds(0, Z - 1)], sem))
        else:
            wait_for(from_z(l).at[pl.ds(0, Z - 1)], sem)

    def z_sum(l):
        wait_recv(f"z{l}")
        summed = g_block(l, f)[...].astype(F32)
        if line:
            one_side = jnp.where(zc == 0, 1, jnp.where(zc == Z - 1, Z - 2, zc - 1))
            other_side = jnp.where(zc == 0, 2, jnp.where(zc == Z - 1, 1, zc + 1))
            summed = summed + from_z(l)[one_side].astype(F32) + from_z(l)[other_side].astype(F32)
            opposite = jnp.where(zc == 1, Z - 1, 0)
            third = from_z(l)[opposite].astype(F32)
            summed = summed + jnp.where(is_end, 0.0, third)
        else:
            summed = lax.fori_loop(1, Z, lambda k, so_far: so_far + from_z(l)[(zc + k) % Z].astype(F32), summed)
        summed = summed * (1.0 / root)
        if l < 4:
            gather[l, :, my_lanes] = summed.astype(gather.dtype)
            gather_start(f"rows{l}", rows_piece(l))
        else:
            hr[r] = summed.astype(hr.dtype)
            over(R, lambda k: send(hr.at[r], hr.at[r], rep_peer(k), "rows4"), 1)

    def rows_done(l):
        if l < 4:
            await_rest(f"rows{l}")
            copy_here(gather.at[l], gw[l], f"out{l}")
        else:
            wait_recv("rows4")
            summed = sum(hr[i].astype(F32) for i in range(R))
            wide = -(-half // LANES) * LANES
            if wide > half:
                summed = jnp.concatenate([summed, jnp.zeros((wide - half, LANES), F32)], axis=0)
            summed = jnp.transpose(summed)
            ghc[:, 0:half] = summed[0 : d.HC, 0:half]
            ghc[:, half:rows] = summed[d.HC : 2 * d.HC, 0 : rows - half]

    def exchange(e):
        over(F, lambda k: send(st_s.at[e], st_r.at[e, f], (r, (f + k) % F), f"stat{e}"), 1)
        st_r[e, f] = st_s[e]

    def exchanged(e):
        wait_recv(f"stat{e}")
        return st_r[e]

    st_s[...] = jnp.zeros_like(st_s)
    w_relay_rest(0)
    w_relay_near(0)
    w_far(0)
    wait_recv("images")
    wait_recv("own_image")
    wait_recv("start")

    rep_all = lambda src, dst, group: over(R, lambda k: send(src, dst, rep_peer(k), group), 1)
    images_here = M // PIX
    inverse_of, counts = [], None

    def w_relay(l):
        w_relay_rest(l)
        w_relay_near(l)

    def widened(j, i, b):
        value = zg[j, image_rows(i), b * CR : (b + 1) * CR].astype(F32)
        return value, [nrm_r[j, b, k : k + 1, :] for k in range(4)]

    def slopes_of(j):
        def body(i, carry):
            for b in range(R):
                value, (a, o, inverse, off) = widened(j, i, b)
                shaped = value * a + o
                squashed = sigmoid(shaped)
                steep = squashed + shaped * squashed * (1.0 - squashed)
                slope[j, image_rows(i), b * CR : (b + 1) * CR] = steep.astype(BF16)
                slope_z[j, image_rows(i), b * CR : (b + 1) * CR] = (steep * (value * inverse + off)).astype(BF16)
            return carry

        per_image(images_here, body, 0)

    for l in range(4):
        w_finish(l)
        if l == 2:
            wait_recv("pool")
            s[2] = jnp.dot(u_sel[...], pool_all[...], preferred_element_type=F32).astype(BF16)
        first = conv(s.at[l], images_here, l, zb)
        mean_here = first * (1.0 / M)
        j = l // 2
        gathers = l in (0, 2)

        def squares(i, so_far):
            apart = zb[image_rows(i), :] - mean_here
            if gathers:
                zg[j, image_rows(i), my_lanes] = apart.astype(BF16)
            return so_far + jnp.sum(jnp.square(apart), axis=0, keepdims=True)

        squared = per_image(images_here, squares, jnp.zeros((1, CR), F32))
        if gathers:
            gather_start(f"ag{l}", ag_piece(j))
        st_s[l, 0:1, :] = first
        st_s[l, 1:2, :] = squared
        if l == 0:
            st_s[l, 2:3, :] = sum(start_r[i, 0:1, :] for i in range(R))
        exchange(l)
        if l != 1:
            w_push_rest(l + 1)
        w_push_near(l + 1)
        if gathers:
            gather_forward(f"ag{l}", ag_piece(j))
        elif l == 1:
            pixel_columns()
        else:
            slopes_of(1)
        parts = exchanged(l)
        tot = jnp.sum(parts, axis=0)
        mean = tot[0:1] * (1.0 / total)
        apart = jnp.sum(jnp.square(parts * (1.0 / M) - mean[None]), axis=0)[0:1] * float(M)
        inverse = lax.rsqrt((tot[1:2] + apart) * (1.0 / total) + EPS)
        inverse_of.append(inverse)
        if l == 0:
            counts = tot[2:3]
        g_row, b_row = gain[l : l + 1, my_lanes], shift[l : l + 1, my_lanes]
        if gathers:
            off = (mean_here - mean) * inverse
            nrm_s[j, 0:1, :] = inverse * g_row
            nrm_s[j, 1:2, :] = off * g_row + b_row
            nrm_s[j, 2:3, :] = inverse
            nrm_s[j, 3:4, :] = off
            rep_all(nrm_s.at[j], nrm_r.at[j, r], f"norm{j}")
            nrm_r[j, r] = nrm_s[j]

        def activate(i, carry):
            at = image_rows(i)
            normed = (zb[at, :] - mean) * inverse
            zhat[l, at, :] = normed
            shaped = normed * g_row + b_row
            hidden = shaped * sigmoid(shaped)
            if l == 1:
                zb[at, :] = hidden
            else:
                a2a_s[i] = hidden.astype(BF16)
            return carry

        def keep_normed(i, carry):
            zhat[l, image_rows(i), :] = (zb[image_rows(i), :] - mean) * inverse
            return carry

        def activate_all(i, carry):
            for b in range(R):
                value, (a, o, unused, also) = widened(j, i, b)
                shaped = value * a + o
                s[l + 1, image_rows(i), b * CR : (b + 1) * CR] = (shaped * sigmoid(shaped)).astype(BF16)
            return carry

        per_image(images_here, keep_normed if gathers else activate, 0)
        if l == 1:
            inside, unused = windows(False)
            pooled = jnp.dot(
                jnp.where(inside, 0.25, 0.0), zb[...], precision=EXACT, preferred_element_type=F32
            )
            pool_own[...] = pooled.astype(BF16)
            pool_all[:, my_lanes] = pooled.astype(BF16)
            rep_all(pool_own, pool_all.at[:, my_lanes], "pool")
            slopes_of(0)
        elif l == 3:
            over(R, lambda k: send(a2a_s.at[(r + k) % R], s4.at[:, my_lanes], rep_peer(k), "a2a"), 1)
            s4[:, my_lanes] = a2a_s[r]
        elif l == 0:
            pool_matrices()
        else:
            pack_head()
        w_relay(l + 1)
        if l == 0:
            w_push_rest(2)
        if gathers:
            wait_recv(f"norm{j}")
            await_rest(f"ag{l}")
            per_image(images_here, activate_all, 0)
        w_far(l + 1)

    w_finish(4)
    low_lanes = lax.broadcasted_iota(jnp.int32, (half, LANES), 1) < d.HC

    def unpack(i, carry):
        both = hp[i].astype(F32)
        at = i * rows
        wf[4, pl.ds(pl.multiple_of(at, d.row_tile), half), :] = jnp.where(low_lanes, both, 0.0).astype(wf.dtype)
        high = jnp.where(low_lanes, pltpu.roll(both, d.HC, 1), 0.0).astype(wf.dtype)
        wf[4, pl.ds(pl.multiple_of(at + half, d.row_tile), rows - half), :] = high[0 : rows - half]
        return carry

    lax.fori_loop(0, F, unpack, 0)
    wait_recv("a2a")
    wait_recv("head_out")
    conv(s4, PD // PIX, 4, zb)
    head_bias = jnp.concatenate([hb[...], jnp.zeros((1, CR - d.HC), F32)], axis=1)
    out_bias = jnp.concatenate([ob[...], jnp.zeros((1, CR - d.OC), F32)], axis=1)
    head_raw = zb[0:PD, :] + head_bias
    squashed = sigmoid(head_raw)
    head_act = head_raw * squashed
    project = jnp.concatenate([ho_r[i][0 : d.q] for i in range(F)] + [jnp.zeros((LANES - d.HC, LANES), F32)], axis=0)
    out = jnp.dot(head_act, project, precision=EXACT, preferred_element_type=F32) + out_bias
    lane = lax.broadcasted_iota(jnp.int32, (PD, LANES), 1)
    classes = d.OC - 4
    factor = total * jnp.concatenate([tw[...], jnp.zeros((1, LANES - 3), F32)], axis=1) / jnp.maximum(counts, 1.0)
    pixel = [columns_s[:, i : i + 1] for i in range(8)]
    is_class = lane < classes
    top = jnp.max(jnp.where(is_class, out, -jnp.inf), axis=1, keepdims=True)
    grown = jnp.where(is_class, jnp.exp(jnp.where(is_class, out - top, 0.0)), 0.0)
    likely = grown / jnp.sum(grown, axis=1, keepdims=True)
    onehot = jnp.where(lane.astype(F32) == pixel[0], 1.0, 0.0)
    grad_class = factor[:, 0:1] * pixel[1] * (likely - onehot)
    misfit = out - pixel[4]
    grad_depth = factor[:, 1:2] * pixel[2] * misfit / jnp.sqrt(misfit * misfit + 1.0)
    is_normal = (lane > classes) & (lane < d.OC)
    predicted = jnp.where(is_normal, out, 0.0)
    wanted = sum(jnp.where(lane == classes + 1 + i, pixel[5 + i], 0.0) for i in range(3))
    radius = jnp.sqrt(jnp.sum(predicted * predicted, axis=1, keepdims=True) + 1.0)
    aligned = jnp.sum(predicted * wanted, axis=1, keepdims=True)
    grad_normal = -(factor[:, 2:3] * pixel[3]) * (wanted / radius - aligned / (radius * radius * radius) * predicted)
    grad_out = jnp.where(
        is_class, grad_class, jnp.where(lane == classes, grad_depth, jnp.where(is_normal, grad_normal, 0.0))
    )
    grad_act = lax.dot_general(
        grad_out, project, (((1,), (1,)), ((), ())), precision=EXACT, preferred_element_type=F32
    )
    grad_head = (grad_act * (squashed + head_raw * squashed * (1.0 - squashed))).astype(BF16).astype(F32)
    zb[0:PD, :] = grad_head
    y[0:PD, 0:CR] = head_act
    y[0:PD, CR : 2 * CR] = grad_out

    def spread_head(i, carry):
        spread_taps(i, zb[image_rows(i), :])
        return carry

    per_image(PD // PIX, spread_head, 0)

    def write_dh3(half, part):
        a2a_s[2 * half] = part[:, 0:CR].astype(BF16)
        a2a_s[2 * half + 1] = part[:, CR : 2 * CR].astype(BF16)

    wait_send("a2a")
    data_grad(4, PD, write_dh3)
    over(R, lambda k: send(a2a_s.at[(r + k) % R], a2a_r.at[r], rep_peer(k), "dh3"), 1)
    a2a_r[r] = a2a_s[r]
    weight_grad(4, s4, PD)
    head_act, grad_out = y[0:PD, 0:CR], y[0:PD, CR : 2 * CR]
    pad = jnp.zeros((2 * LANES - PD, LANES), F32)
    act_t = jnp.transpose(jnp.concatenate([head_act, pad], axis=0))[:, 0:PD]
    rep_s[0 : d.HC, :] = jnp.dot(act_t, grad_out, precision=EXACT, preferred_element_type=F32)[0 : d.HC]
    rep_s[d.HC : d.HC + 8, :] = jnp.zeros((8, LANES), F32)
    rep_s[d.HC : d.HC + 1, :] = jnp.sum(zb[0:PD, :], axis=0, keepdims=True)
    rep_s[d.HC + 1 : d.HC + 2, :] = jnp.sum(grad_out, axis=0, keepdims=True)
    over(R, lambda k: send(rep_s, rep_r.at[r], rep_peer(k), "small_rep"), 1)
    rep_r[r] = rep_s[...]

    def head_small():
        wait_recv("small_rep")
        summed = sum(rep_r[i] for i in range(R))
        for i in range(F):
            all_s[i, 0 : d.q, :] = summed[i * d.q : (i + 1) * d.q]
            if d.q < 8:
                all_s[i, d.q : 8, :] = jnp.zeros((8 - d.q, LANES), F32)
            all_s[i, 8:16, :] = summed[d.HC : d.HC + 8]
        over(F, lambda k: send(all_s.at[(f + k) % F], all_r.at[f], (r, (f + k) % F), "small_all"), 1)
        all_r[f] = all_s[f]

    def rows_of(l):
        return gain[l : l + 1, my_lanes], shift[l : l + 1, my_lanes]

    def slope_here(l, at):
        g_row, b_row = rows_of(l)
        normed = zhat[l, at, :]
        shaped = normed * g_row + b_row
        squashed = sigmoid(shaped)
        return normed, squashed + shaped * squashed * (1.0 - squashed)

    def enter(l, entering):
        def body(i, so_far):
            at = image_rows(i)
            normed, steep = slope_here(l, at)
            grad = entering(i, at) * steep
            zb[at, :] = grad
            return (
                so_far[0] + jnp.sum(grad, axis=0, keepdims=True),
                so_far[1] + jnp.sum(grad * normed, axis=0, keepdims=True),
            )

        none = jnp.zeros((1, CR), F32)
        part_bias, part_gain = per_image(images_here, body, (none, none))
        st_s[7 - l, 0:1, :] = part_bias
        st_s[7 - l, 1:2, :] = part_gain
        exchange(7 - l)

    def through_norm(l, grad_of):
        tot = jnp.sum(exchanged(7 - l), axis=0)
        bias_sum, gain_sum = tot[0:1], tot[1:2]
        norm_s[l : l + 1, :] = gain_sum * (1.0 / root)
        norm_s[4 + l : 5 + l, :] = bias_sum * (1.0 / root)
        scale = inverse_of[l] * rows_of(l)[0]
        if l in (0, 2):
            await_rest(f"rs{l + 1}")

        def body(i, carry):
            at = image_rows(i)
            normed, grad = grad_of(i, at)
            spread_taps(i, scale * (grad - bias_sum * (1.0 / total) - normed * (gain_sum * (1.0 / total))))
            return carry

        per_image(images_here, body, 0)

    def from_zb(l):
        return lambda i, at: (zhat[l, at, :], zb[at, :])

    def from_scatter(l):
        j = l // 2
        here = images_here // 2

        def grad_of(i, at):
            normed, steep = slope_here(l, at)
            h = i // here
            local = image_rows(i - h * here)
            grad = (
                rs_s[j, r, at, :].astype(F32)
                + rs_l[j, 1 + 2 * h, local, :].astype(F32)
                + rs_l[j, 4 + h, local, :].astype(F32)
            )
            return normed, grad * steep

        return grad_of

    def layer_down(l):
        j = (l - 1) // 2

        def write(part_at, part):
            for b in range(2):
                n = 2 * part_at + b
                grad = part[:, b * CR : (b + 1) * CR]
                rs_s[j, n] = grad.astype(BF16)
                cols = slice(n * CR, (n + 1) * CR)
                sums_s[j, n, 0:1, :] = jnp.sum(grad * slope[j, :, cols].astype(F32), axis=0, keepdims=True)
                sums_s[j, n, 1:2, :] = jnp.sum(grad * slope_z[j, :, cols].astype(F32), axis=0, keepdims=True)

        data_grad(l, M, write)
        over(R, lambda k: send(sums_s.at[j, (r + k) % R], sums_r.at[j, r], rep_peer(k), f"sums{j}"), 1)
        scatter_start(f"rs{l}", rs_piece(j), rs_land(j))
        sums_r[j, r] = sums_s[j, r]
        weight_grad(l, s.at[l], M)
        wait_recv(f"sums{j}")
        e = 7 - (l - 1)
        st_s[e, 0:2, :] = sum(sums_r[j, i, 0:2, :] for i in range(R))
        exchange(e)
        scatter_forward(f"rs{l}", rs_piece(j), rs_land(j))

    wait_recv("dh3")
    enter(3, lambda i, at: a2a_r[i].astype(F32))
    core_sum(4)
    z_push(4)
    head_small()
    through_norm(3, from_zb(3))
    layer_down(3)
    z_middle(4)
    core_sum(3)
    z_push(3)

    through_norm(2, from_scatter(2))

    def write_pooled(part_at, part):
        chosen = jnp.dot(ut_sel[...], part.astype(BF16), preferred_element_type=F32).astype(BF16)
        ps_s[2 * part_at] = chosen[:, 0:CR]
        ps_s[2 * part_at + 1] = chosen[:, CR : 2 * CR]

    data_grad(2, M, write_pooled)
    over(R, lambda k: send(ps_s.at[(r + k) % R], ps_r.at[r], rep_peer(k), "rs2"), 1)
    ps_r[r] = ps_s[r]
    weight_grad(2, s.at[2], M)
    z_middle(3)
    wait_recv("rs2")
    pooled = sum(ps_r[i].astype(F32) for i in range(R))
    inside, unused = windows(True)
    zb[...] = jnp.dot(jnp.where(inside, 0.25, 0.0), pooled, precision=EXACT, preferred_element_type=F32)
    enter(1, lambda i, at: zb[at, :])
    core_sum(2)
    z_push(2)
    z_sum(4)
    z_sum(3)
    through_norm(1, from_zb(1))
    gather_forward("rows3", rows_piece(3))
    layer_down(1)
    z_middle(2)
    core_sum(1)
    z_push(1)

    through_norm(0, from_scatter(0))
    weight_grad(0, s.at[0], M)
    z_sum(2)

    def write_images(part_at, part):
        for i in range(R):
            gi_s[i, :, part_at * 2 * CR : (part_at + 1) * 2 * CR] = part[i * PD : (i + 1) * PD].astype(BF16)

    data_grad(0, M, write_images)
    scatter_start("rs0", gi_piece, gi_land)
    gather_forward("rows2", rows_piece(2))
    z_middle(1)
    core_sum(0)
    z_push(0)

    gnorm[:, my_lanes] = norm_s[...]
    rep_all(norm_s, gnorm.at[:, my_lanes], "norms")
    z_middle(0)
    scatter_forward("rs0", gi_piece, gi_land)
    z_sum(1)
    wait_recv("small_all")
    gsmall[...] = jnp.sum(all_r[...], axis=0) * (1.0 / root)
    rows_done(4)
    rows_done(3)
    gather_forward("rows1", rows_piece(1))
    rows_done(2)
    await_rest("rs0")
    for h in range(2):
        at = slice(h * (PD // 2), (h + 1) * (PD // 2))
        gi[at, :] = gi_s[r, at, :].astype(F32) + gi_l[1 + 2 * h].astype(F32) + gi_l[4 + h].astype(F32)
    z_sum(0)
    wait_recv("norms")
    rows_done(1)
    gather_forward("rows0", rows_piece(0))
    rows_done(0)

    drain()


def finish(gi, gw0, gw1, gw2, gw3, ghc, gnorm, gsmall, *outs):
    out_gi, out0, out1, out2, out3, out_hc, out_ho, out_gain, out_bias, out_hb, out_ob = outs
    out_gi[...] = gi[...]
    for src, dst in ((gw0, out0), (gw1, out1), (gw2, out2), (gw3, out3)):
        dst[...] = src[...].astype(F32)

    @pl.when(pl.program_id(0) == 0)
    def _():
        out_hc[...] = ghc[...]
        out_ho[...] = gsmall[0 : out_ho.shape[0], 0 : out_ho.shape[1]]
        out_gain[...] = gnorm[0:4, :]
        out_bias[...] = gnorm[4:8, :]
        out_hb[...] = gsmall[8:9, 0 : out_hb.shape[1]]
        out_ob[...] = gsmall[9:10, 0 : out_ob.shape[1]]


def per_device(
    R, F,
    images, enc_first, enc_second, dec_first, dec_second, head_conv, head_out, norm_gain, norm_bias, head_bias, out_bias,
    task_weights, pool_index, labels, task_masks, targets,
):
    n, height, breadth, channels = images.shape
    rows, hidden = head_conv.shape
    q, out_ch = head_out.shape
    d = types.SimpleNamespace(
        n=n, R=R, F=F, Z=F // 2, rows=rows, C=channels, CR=channels // R, W=breadth, PIX=height * breadth,
        PD=n * height * breadth, HC=hidden, OC=out_ch, q=q,
    )
    d.M = R * d.PD
    d.PW = d.M // 4
    wire = BF16 if rows % 16 == 0 else F32
    d.row_tile = 16 if rows % 16 == 0 else 8
    d.half = -(-rows // (2 * d.row_tile)) * d.row_tile
    vm = pltpu.VMEM
    patch = 9 * channels
    scratch = [
        vm((4, rows, d.C), wire),
        vm((d.PD, LANES), F32),
        vm((4, d.M, d.C), BF16),
        vm((d.PD, d.C), BF16),
        vm((5, patch, d.CR), wire),
        vm((d.M, 9 * d.CR), F32),
        vm((d.M, d.CR), F32),
        vm((4, d.M, d.CR), F32),
        vm((d.M, 9 * d.CR), BF16),
        vm((d.M, d.PW), BF16),
        vm((d.PW, d.M), BF16),
        vm((R, d.PD, d.CR), BF16),
        vm((R, d.PD, d.CR), BF16),
        vm((2, R, d.M, d.CR), BF16),
        vm((2, 6, d.M // 2, d.CR), BF16),
        vm((d.PW, d.CR), BF16),
        vm((d.PW, d.C), BF16),
        vm((R, d.PW, d.CR), BF16),
        vm((R, d.PW, d.CR), BF16),
        vm((R, d.PD, d.C), BF16),
        vm((6, d.PD // 2, d.C), BF16),
        vm((2, d.M, d.C), BF16),
        vm((2, d.M, d.C), BF16),
        vm((2, d.M, d.C), BF16),
        vm((2, 8, LANES), F32),
        vm((2, R, 8, LANES), F32),
        vm((2, R, 8, LANES), F32),
        vm((2, R, 8, LANES), F32),
        vm((4, patch, d.CR), wire),
        vm((4, d.Z, rows, d.CR), wire),
        vm((4, d.Z, rows, d.CR), wire),
        vm((d.half, LANES), wire),
        vm((F, d.half, LANES), wire),
        vm((F, d.half, LANES), wire),
        vm((d.Z, d.half, LANES), wire),
        vm((d.Z, d.half, LANES), wire),
        vm((R, d.half, LANES), wire),
        vm((8, 8, LANES), F32),
        vm((8, F, 8, LANES), F32),
        vm((8, LANES), F32),
        vm((R, 8, LANES), F32),
        vm((8, LANES), F32),
        vm((F, 8, LANES), F32),
        vm((hidden + 8, LANES), F32),
        vm((R, hidden + 8, LANES), F32),
        vm((F, 16, LANES), F32),
        vm((F, 16, LANES), F32),
        vm((8, LANES), F32),
        vm((LANES, 2 * LANES), F32),
        pltpu.SemaphoreType.DMA((len(GROUPS),)),
        pltpu.SemaphoreType.DMA((len(GROUPS),)),
        pltpu.SemaphoreType.DMA((5, d.Z)),
        pltpu.SemaphoreType.DMA((5, d.Z)),
        pltpu.SemaphoreType.DMA((5, d.Z)),
        pltpu.SemaphoreType.DMA((5, d.Z)),
    ]
    here, there = pl.BlockSpec(memory_space=pltpu.VMEM), pl.BlockSpec(memory_space=pl.ANY)
    shape = jax.ShapeDtypeStruct
    kept = pl.pallas_call(
        functools.partial(kernel, d),
        out_shape=[shape((d.PD, d.C), F32)]
        + [shape((rows, d.C), wire)] * 4
        + [shape((hidden, rows), F32), shape((8, d.C), F32), shape((16, LANES), F32)],
        in_specs=[there] * 5 + [here] * 11,
        out_specs=[here] + [there] * 4 + [here] * 3,
        scratch_shapes=scratch,
        compiler_params=pltpu.CompilerParams(collective_id=0, has_side_effects=True, vmem_limit_bytes=60 * 2**20),
    )(
        images.reshape(d.PD, channels),
        *(w.astype(wire) for w in (enc_first, enc_second, dec_first, dec_second)),
        head_conv.T, head_out, norm_gain, norm_bias, head_bias.reshape(1, hidden), out_bias.reshape(1, out_ch),
        task_weights.reshape(1, 3), pool_index, labels, jnp.transpose(task_masks, (1, 0, 2)), targets,
    )
    steps = next(count for count in (2, 1) if rows % (count * d.row_tile) == 0 and d.PD % (count * 8) == 0)
    part = lambda height, width: pl.BlockSpec((height // steps, width), lambda i: (i, 0))
    all_of = lambda height, width: pl.BlockSpec((height, width), lambda i: (0, 0))
    rest = ((q, out_ch), (4, channels), (4, channels), (1, hidden), (1, out_ch))
    gi, gw0, gw1, gw2, gw3, ghc, gq, gain, bias, ghb, gob = pl.pallas_call(
        finish,
        grid=(steps,),
        out_shape=[shape((d.PD, channels), F32)]
        + [shape((rows, channels), F32)] * 4
        + [shape((hidden, rows), F32)]
        + [shape(size, F32) for size in rest],
        in_specs=[part(d.PD, channels)]
        + [part(rows, channels)] * 4
        + [all_of(hidden, rows), all_of(8, channels), all_of(16, LANES)],
        out_specs=[part(d.PD, channels)]
        + [part(rows, channels)] * 4
        + [all_of(hidden, rows)]
        + [all_of(*size) for size in rest],
    )(*kept)
    return (
        gi.reshape(images.shape), gw0, gw1, gw2, gw3, ghc.T, gq, gain, bias, ghb.reshape(hidden), gob.reshape(out_ch),
    )


def solution(mesh):
    split = ("rep", "fsdp")
    rows = P("fsdp", None)
    return jax.shard_map(
        functools.partial(per_device, mesh.shape["rep"], mesh.shape["fsdp"]),
        mesh=mesh,
        in_specs=(P(split, None, None, None),)
        + (rows,) * 6
        + (P(),) * 5
        + (P(split, None), P(split, None), P(split, None, None), P(split, None, None)),
        out_specs=(P(split, None, None, None),) + (rows,) * 6 + (P(),) * 4,
        check_vma=False,
    )
```

```python
import functools
import math
import types

import jax
import jax.numpy as jnp
from jax import lax
from jax.experimental import pallas as pl
from jax.experimental.pallas import tpu as pltpu
from jax.sharding import PartitionSpec as P

MESH = pl.DeviceIdType.MESH
F32, BF16 = jnp.float32, jnp.bfloat16
EPS = 1e-05
LANES = 128
EXACT = lax.Precision.HIGHEST

GROUPS = (
    ["images", "start", "head_out", "a2a", "pool", "dh3", "rs2", "norms", "small_rep", "small_all"]
    + [f"sums{i}" for i in range(2)]
    + [f"norm{i}" for i in range(2)]
    + [
        f"{name}{way}"
        for name in ("ag0", "ag2", "rs3", "rs1", "rs0", "rows0", "rows1", "rows2", "rows3")
        for way in ("x0", "x1", "y0", "y1", "f0", "f1")
    ]
    + [f"stat{i}" for i in range(8)]
    + [f"core{i}" for i in range(5)]
    + [f"z{i}.{h}" for i in range(5) for h in range(2)]
    + [f"mid{i}.{h}" for i in range(5) for h in range(2)]
    + ["rows4"]
    + [f"own{i}" for i in range(5)]
    + [f"out{i}" for i in range(4)]
    + ["own_image"]
)
GROUP = {name: number for number, name in enumerate(GROUPS)}


def kernel(d, *refs):
    it = iter(refs)
    take = lambda count: [next(it) for _ in range(count)]
    images, w0, w1, w2, w3, hw, ho, gain, shift, hb, ob, tw, pidx, lab, msk, tgt = take(16)
    gi, gw0, gw1, gw2, gw3, ghc, gnorm, gsmall = take(8)
    gather, columns_s = take(2)
    (s, s4, wf, y, zb, zhat, d9, u_sel, ut_sel, a2a_s, a2a_r, rs_s, rs_l, pool_own, pool_all, ps_s, ps_r, gi_s, gi_l) = take(19)
    (zg, slope, slope_z, nrm_s, nrm_r, sums_s, sums_r) = take(7)
    (gf, cr, zr, hw_s, hp, hg, hcr, hzr, hr, st_s, st_r, start_s, start_r, ho_s, ho_r, rep_s, rep_r, all_s, all_r, norm_s, feat) = take(21)
    ssem, rsem, wsz, wrz, wsf, wrf = take(6)
    w_in, gw = (w0, w1, w2, w3, hw_s), (gw0, gw1, gw2, gw3)
    R, F, Z, rows, half, C, CR, W, PIX, PD, M, PW = d.R, d.F, d.Z, d.rows, d.half, d.C, d.CR, d.W, d.PIX, d.PD, d.M, d.PW
    total = float(M * F)
    root = math.sqrt(total)

    r, f = lax.axis_index("rep"), lax.axis_index("fsdp")
    zc, core = f // 2, f % 2
    sib = (r, zc * 2 + (1 - core))
    rep_peer = lambda k: ((r + k) % R, f)
    one, two = r + 1 - 2 * (r % 2), (r + 2) % R
    both = (one + 2) % R
    at_one, at_two = (one, f), (two, f)
    z_peer = lambda k: (r, ((zc + k) % Z) * 2 + core)
    line = Z == 4
    is_end = (zc == 0) | (zc == Z - 1)
    is_far = lambda k: (zc + k) % Z - zc == Z - 1
    is_far_back = lambda k: zc - (zc + k) % Z == Z - 1
    ends_apart = lambda k: is_far(k) | is_far_back(k)
    my_lanes = pl.ds(pl.multiple_of(r * CR, CR), CR)

    def block(owner):
        return pl.ds(pl.multiple_of(owner * rows, d.row_tile), rows)

    arriving, leaving = {}, {}

    def first_of(ref, count):
        return lambda: ref.at[pl.ds(0, count)]

    volume = {
        "images": first_of(s.at[0], (R - 1) * PD),
        "own_image": first_of(s.at[0], PD),
        "start": first_of(start_r, R - 1),
        "head_out": first_of(ho_r, F - 1),
        "a2a": lambda: s4.at[:, pl.ds(0, (R - 1) * CR)],
        "pool": lambda: pool_all.at[:, pl.ds(0, (R - 1) * CR)],
        "dh3": first_of(a2a_r, R - 1),
        "rs2": first_of(ps_r, R - 1),
        "norms": lambda: gnorm.at[:, pl.ds(0, (R - 1) * CR)],
        "small_rep": first_of(rep_r, R - 1),
        "small_all": first_of(all_r, F - 1),
        "rows4": first_of(hr, R - 1),
        "core4": lambda: hcr,
    }
    for way in ("x", "y", "f"):
        for h in range(2):
            for j in range(2):
                volume[f"ag{2 * j}{way}{h}"] = lambda j=j: zg.at[j, pl.ds(0, M // 2), pl.ds(0, CR)]
                volume[f"rs{2 * j + 1}{way}{h}"] = lambda j=j: rs_l.at[j, 0]
            volume[f"rs0{way}{h}"] = lambda: gi_l.at[0]
            size = half if h == 0 else rows - half
            for l in range(4):
                volume[f"rows{l}{way}{h}"] = lambda l=l, size=size: gather.at[l, pl.ds(0, size), pl.ds(0, CR)]
    for j in range(2):
        volume[f"sums{j}"] = first_of(sums_r.at[j], R - 1)
        volume[f"norm{j}"] = first_of(nrm_r.at[j], R - 1)
    for e in range(8):
        volume[f"stat{e}"] = first_of(st_r.at[e], F - 1)
    for l in range(4):
        volume[f"core{l}"] = lambda l=l: cr.at[l]

    def wait_for(ref, sem):
        pltpu.make_async_copy(ref, ref, sem).wait()

    def wait_recv(group):
        arriving.pop(group)()

    def wait_send(group):
        leaving.pop(group)()

    def copy_here(src, dst, group):
        g = GROUP[group]
        arriving[group] = lambda: wait_for(dst, rsem.at[g])
        pltpu.make_async_copy(src, dst, rsem.at[g]).start()

    def send(src, dst, to, group):
        g = GROUP[group]
        if group in volume:
            arriving[group] = lambda: wait_for(volume[group](), rsem.at[g])
            leaving[group] = lambda: wait_for(volume[group](), ssem.at[g])
        pltpu.make_async_remote_copy(
            src_ref=src, dst_ref=dst, send_sem=ssem.at[g], recv_sem=rsem.at[g], device_id=to, device_id_type=MESH
        ).start()

    def over(count, body, first=0):
        if count <= 8:
            for i in range(first, count):
                body(i)
            return

        def step(i, carry):
            body(i)
            return carry

        lax.fori_loop(first, count, step, 0)

    def when(condition, body):
        pl.when(condition)(body)

    def direct(k, body):
        if line and k in (1, Z - 1):
            when(jnp.logical_not(ends_apart(k)), body)
        else:
            body()

    def drain():
        for waits in (arriving, leaving):
            for wait in list(waits.values()):
                wait()

    barrier = pltpu.get_barrier_semaphore()
    over(R, lambda k: pl.semaphore_signal(barrier, inc=1, device_id=rep_peer(k), device_id_type=MESH), 1)
    over(F, lambda k: pl.semaphore_signal(barrier, inc=1, device_id=(r, (f + k) % F), device_id_type=MESH), 1)
    pl.semaphore_wait(barrier, R + F - 2)

    pieces = range(d.pieces)

    def cut(l, h):
        size = rows if l < 4 else half
        first = -(-size // (d.pieces * d.row_tile)) * d.row_tile
        return (0, first) if h == 0 else (first, size - first)

    def cut_at(l, h):
        first, size = cut(l, h)
        return pl.ds(first, size)

    near = sorted({1, Z - 1})
    beyond = list(range(2, Z - 1))

    def w_block(l, owner, h):
        first, size = cut(l, h)
        if l < 4:
            return wf.at[l, pl.ds(pl.multiple_of(owner * rows + first, d.row_tile), size)]
        return hp.at[owner, pl.ds(first, size)]

    def w_copy(l, h, src, owner, to, send_sem, recv_sem):
        return pltpu.make_async_remote_copy(
            src_ref=src, dst_ref=w_block(l, owner, h), send_sem=send_sem, recv_sem=recv_sem, device_id=to, device_id_type=MESH
        )

    def w_src(l, h):
        return w_in[l].at[cut_at(l, h), my_lanes] if l < 4 else hw_s.at[cut_at(l, h)]

    def w_wait(l, h, sem):
        wait_for(w_block(l, f, h), sem)

    def w_send(l, h, k, who=lambda body: body()):
        u = l * d.pieces + h
        arriving["z", l, h, k] = lambda: direct(Z - k, lambda: w_wait(l, h, wrz.at[u, k]))
        leaving["z", l, h, k] = lambda: direct(k, lambda: w_wait(l, h, wsz.at[u, k]))
        start = lambda: w_copy(l, h, w_src(l, h), f, z_peer(k), wsz.at[u, k], wrz.at[u, k]).start()
        who(lambda: direct(k, start))

    def w_relayed(l, h, k):
        u = l * d.pieces + h
        arriving["core", l, h, k] = lambda: w_wait(l, h, wrf.at[u, k])
        leaving["core", l, h, k] = lambda: w_wait(l, h, wsf.at[u, k])

    def w_push_near(l):
        for h in pieces:
            u = l * d.pieces + h
            for k in near:
                w_send(l, h, k)
            w_copy(l, h, w_src(l, h), f, sib, wsf.at[u, 0], wrf.at[u, 0]).start()
            w_relayed(l, h, 0)
        copy_here(w_in[l].at[:, my_lanes] if l < 4 else hw_s, wf.at[l, block(f)] if l < 4 else hp.at[f], f"own{l}")

    def w_push_rest(l, hs=pieces, who=lambda body: body()):
        for h in hs:
            for k in beyond:
                w_send(l, h, k, who)

    def at_ends(body):
        if line:
            when(is_end, body)
        else:
            body()

    def between(body):
        if line:
            when(jnp.logical_not(is_end), body)

    def w_arrived(l, h, k):
        u = l * d.pieces + h
        owner = ((zc + Z - k) % Z) * 2 + core
        w_wait(l, h, wrz.at[u, k])
        w_copy(l, h, w_block(l, owner, h), owner, sib, wsf.at[u, k], wrf.at[u, k]).start()

    def w_relay_rest(l, hs=pieces):
        for h in hs:
            u = l * d.pieces + h
            for k in beyond:
                arriving.pop(("z", l, h, k))
                w_arrived(l, h, k)
                w_relayed(l, h, k)
            if line:

                def hand_on():
                    to = (Z - 1) * (zc - 1)
                    owner = (Z - 1 - to) * 2 + core
                    slot = jnp.where(zc == 1, 1, Z - 1)
                    w_copy(
                        l, h, w_block(l, owner, h), owner, (r, to * 2 + core), wsz.at[u, 0], wrz.at[u, slot]
                    ).start()

                when(jnp.logical_not(is_end), hand_on)
                leaving["far", l, h] = lambda u=u, h=h: when(
                    jnp.logical_not(is_end), lambda: w_wait(l, h, wsz.at[u, 0])
                )

    def w_relay_near(l):
        for h in pieces:
            for k in near:
                arriving.pop(("z", l, h, k))
                direct(Z - k, lambda: w_arrived(l, h, k))
                if not line:
                    w_relayed(l, h, k)

    def w_far(l):
        if line:
            for h in pieces:
                for k in near:
                    w_relayed(l, h, k)
                when(zc == 0, lambda: w_arrived(l, h, 1))
                when(zc == Z - 1, lambda: w_arrived(l, h, Z - 1))

    def w_finish(l):
        for h in pieces:
            for k in range(Z):
                wait_recv(("core", l, h, k))
        wait_recv(f"own{l}")

    w_push_rest(0)
    w_push_near(0)
    over(R, lambda k: send(images, s.at[0, pl.ds(pl.multiple_of(r * PD, PD), PD)], rep_peer(k), "images"), 1)
    own_rows = s.at[0, pl.ds(pl.multiple_of(r * PD, PD), PD)]
    copy_here(images, own_rows, "own_image")

    start_s[...] = jnp.zeros_like(start_s)
    masks = jnp.concatenate([msk[:, i, :] for i in range(d.n)], axis=1).astype(F32)
    labels = jnp.concatenate([lab[i : i + 1, :] for i in range(d.n)], axis=1).astype(F32)
    wanted = jnp.concatenate([tgt[i] for i in range(d.n)], axis=1)
    pools = jnp.concatenate([pidx[i : i + 1, :] for i in range(d.n)], axis=1).astype(F32)
    counted = jnp.sum(masks, axis=1, keepdims=True)
    lane = lax.broadcasted_iota(jnp.int32, (1, LANES), 1)
    start_s[0:1, :] = sum(jnp.where(lane == t, counted[t : t + 1, :], 0.0) for t in range(3))
    start_s[1:2, 0 : PW // R] = pools
    over(R, lambda k: send(start_s, start_r.at[r], rep_peer(k), "start"), 1)
    start_r[r] = start_s[...]
    ho_s[...] = jnp.zeros_like(ho_s)
    ho_s[0 : d.q, 0 : d.OC] = ho[...].astype(F32)
    over(F, lambda k: send(ho_s, ho_r.at[f], (r, (f + k) % F), "head_out"), 1)
    ho_r[f] = ho_s[...]
    def pack_head():
        wide = -(-rows // LANES) * LANES
        tall = jnp.concatenate([hw[...].astype(F32), jnp.zeros((LANES - d.HC, rows), F32)], axis=0)
        if wide > rows:
            tall = jnp.concatenate([tall, jnp.zeros((LANES, wide - rows), F32)], axis=1)
        tall = jnp.transpose(tall)
        if wide < 2 * half:
            tall = jnp.concatenate([tall, jnp.zeros((2 * half - wide, LANES), F32)], axis=0)
        hw_s[...] = (tall[0:half] + pltpu.roll(tall[half : 2 * half], d.HC, 1)).astype(hw_s.dtype)

    bits = W.bit_length() - 1

    def places(axis, shape):
        q = lax.broadcasted_iota(jnp.int32, shape, axis)
        image = jnp.zeros(shape, jnp.int32)
        for i in range(1, M // PIX):
            image = image + jnp.where(q >= i * PIX, 1, 0)
        q = q - image * PIX
        window = image * (PIX // 4) + (q >> (bits + 1)) * (W // 2) + ((q & (W - 1)) >> 1)
        position = 2 * ((q >> bits) & 1) + (q & 1)
        return window, position.astype(F32)

    def windows(rows_first):
        shape = (M, PW) if rows_first else (PW, M)
        window, position = places(0 if rows_first else 1, shape)
        other = lax.broadcasted_iota(jnp.int32, shape, 1 if rows_first else 0)
        return window == other, position

    def pixel_columns():
        feat[...] = jnp.zeros_like(feat)
        feat[0:1, 0:PD] = labels
        feat[1:4, 0:PD] = masks
        feat[4:8, 0:PD] = wanted
        columns_s[...] = jnp.transpose(feat[...])[0:PD, 0:LANES]

    def pool_matrices():
        feat[...] = jnp.zeros_like(feat)
        for i in range(R):
            feat[0:1, i * (PW // R) : (i + 1) * (PW // R)] = start_r[i, 1:2, 0 : PW // R]
        picked_row = feat[0:1, 0:PW]
        picked_col = jnp.transpose(feat[...])[0:PW, 0:1]
        inside, position = windows(True)
        u_sel[...] = jnp.where(inside & (position == picked_row), 1.0, 0.0).astype(BF16)
        inside, position = windows(False)
        ut_sel[...] = jnp.where(inside & (position == picked_col), 1.0, 0.0).astype(BF16)

    def image_rows(i):
        return pl.ds(pl.multiple_of(i * PIX, PIX), PIX)

    def per_image(count, body, init):
        return lax.fori_loop(0, count, body, init)

    def column_of(shape):
        return lax.broadcasted_iota(jnp.int32, shape, 0) & (W - 1)

    blank = jnp.zeros((W, CR), F32)

    def conv(src, count, l, out):
        height = count * PIX
        for kx in range(3):
            taps = [wf[l, (3 * ky + kx) * C : (3 * ky + kx + 1) * C, :].astype(BF16) for ky in range(3)]
            y[0:height, kx * 3 * CR : (kx + 1) * 3 * CR] = jnp.dot(
                src[...], jnp.concatenate(taps, axis=1), preferred_element_type=F32
            )

        def body(i, summed):
            at = image_rows(i)
            col = column_of((PIX, CR))
            parts = []
            for kx in range(3):
                up, mid, down = (y[at, (kx * 3 + ky) * CR : (kx * 3 + ky + 1) * CR] for ky in range(3))
                parts.append(
                    mid
                    + jnp.concatenate([blank, up[: PIX - W]], axis=0)
                    + jnp.concatenate([down[W:], blank], axis=0)
                )
            z = (
                parts[1]
                + jnp.where(col > 0, pltpu.roll(parts[0], 1, 0), 0.0)
                + jnp.where(col < W - 1, pltpu.roll(parts[2], PIX - 1, 0), 0.0)
            )
            out[at, :] = z
            return summed + jnp.sum(z, axis=0, keepdims=True)

        return per_image(count, body, jnp.zeros((1, CR), F32))

    def spread_taps(i, grad):
        at = image_rows(i)
        col = column_of((PIX, CR))
        moved = (
            jnp.where(col < W - 1, pltpu.roll(grad, PIX - 1, 0), 0.0),
            grad,
            jnp.where(col > 0, pltpu.roll(grad, 1, 0), 0.0),
        )
        low_blank = blank.astype(BF16)
        for kx in range(3):
            low = moved[kx].astype(BF16)
            nine = (
                jnp.concatenate([low[W:], low_blank], axis=0),
                low,
                jnp.concatenate([low_blank, low[: PIX - W]], axis=0),
            )
            for ky in range(3):
                d9[at, (kx * 3 + ky) * CR : (kx * 3 + ky + 1) * CR] = nine[ky]

    def data_grad(l, height, write):
        step = 2 * CR
        for half in range(C // step):
            taps = [
                wf[l, t * C + half * step : t * C + (half + 1) * step, :].astype(BF16)
                for t in (3 * ky + kx for kx in range(3) for ky in range(3))
            ]
            part = lax.dot_general(
                d9[0:height, :],
                jnp.concatenate(taps, axis=1),
                (((1,), (1,)), ((), ())),
                preferred_element_type=F32,
            )
            write(half, part)

    def lanes_of(owner):
        return pl.ds(pl.multiple_of(owner * CR, CR), CR)

    def gather_start(name, piece):
        send(piece(r, 0), piece(r, 0), at_one, f"{name}x0")
        send(piece(r, 1), piece(r, 1), at_two, f"{name}y1")
        send(piece(r, 1), piece(r, 1), at_one, f"{name}x1")
        send(piece(r, 0), piece(r, 0), at_two, f"{name}y0")

    def gather_forward(name, piece):
        wait_recv(f"{name}x0")
        send(piece(one, 0), piece(one, 0), at_two, f"{name}f0")
        wait_recv(f"{name}y1")
        send(piece(two, 1), piece(two, 1), at_one, f"{name}f1")

    def await_rest(name):
        for way in ("x1", "y0", "f0", "f1"):
            wait_recv(f"{name}{way}")

    def scatter_start(name, piece, land):
        send(piece(both, 0), land(0), at_one, f"{name}x0")
        send(piece(both, 1), land(2), at_two, f"{name}y1")
        send(piece(one, 0), land(1), at_one, f"{name}x1")
        send(piece(two, 1), land(3), at_two, f"{name}y0")

    def scatter_forward(name, piece, land):
        for way, ref, came, dst, to, group in (
            ("x0", piece(two, 0), land(0), land(4), at_two, "f0"),
            ("y1", piece(one, 1), land(2), land(5), at_one, "f1"),
        ):
            wait_recv(f"{name}{way}")
            ref[...] = (ref[...].astype(F32) + came[...].astype(F32)).astype(ref.dtype)
            send(ref, dst, to, f"{name}{group}")

    def ag_piece(j):
        return lambda owner, h: zg.at[j, pl.ds(h * (M // 2), M // 2), lanes_of(owner)]

    def rows_piece(l):
        return lambda owner, h: gather.at[l, pl.ds(h * half, half if h == 0 else rows - half), lanes_of(owner)]

    def rs_piece(j):
        return lambda owner, h: rs_s.at[j, owner, pl.ds(h * (M // 2), M // 2)]

    def rs_land(j):
        return lambda i: rs_l.at[j, i]

    def gi_piece(owner, h):
        return gi_s.at[owner, pl.ds(h * (PD // 2), PD // 2)]

    def gi_land(i):
        return gi_l.at[i]

    def sigmoid(v):
        return 0.5 * jnp.tanh(0.5 * v) + 0.5

    def g_block(l, owner):
        return gf.at[l, block(owner)] if l < 4 else hg.at[owner]

    def from_core(l):
        return cr.at[l] if l < 4 else hcr

    def from_z(l, i, h):
        return zr.at[l, i, cut_at(l, h)] if l < 4 else hzr.at[i, cut_at(l, h)]

    def g_piece(l, owner, h):
        first, size = cut(l, h)
        if l < 4:
            return gf.at[l, pl.ds(pl.multiple_of(owner * rows + first, d.row_tile), size)]
        return hg.at[owner, pl.ds(first, size)]

    def weight_grad(l, src, height):
        for kx in range(3):
            part = lax.dot_general(
                src[...],
                d9[0:height, kx * 3 * CR : (kx + 1) * 3 * CR],
                (((0,), (0,)), ((), ())),
                preferred_element_type=F32,
            )
            for ky in range(3):
                t = 3 * ky + kx
                gf[l % 4, t * C : (t + 1) * C, :] = part[:, ky * CR : (ky + 1) * CR].astype(gf.dtype)
        if l == 4:

            def pack(i, carry):
                at = i * rows
                low = gf[0, pl.ds(pl.multiple_of(at, d.row_tile), half), :].astype(F32)
                high = gf[0, pl.ds(pl.multiple_of(at + half, d.row_tile), rows - half), :].astype(F32)
                if rows < 2 * half:
                    high = jnp.concatenate([high, jnp.zeros((2 * half - rows, CR), F32)], axis=0)
                hg[i] = (low + pltpu.roll(high, d.HC, 1)).astype(hg.dtype)
                return carry

            lax.fori_loop(0, F, pack, 0)
        over(Z, lambda k: send(g_block(l, 2 * k + 1 - core), from_core(l).at[k], sib, f"core{l}"))

    def core_sum(l):
        wait_recv(f"core{l}")

        def step(k):
            ref = g_block(l, 2 * k + core)
            ref[...] = (ref[...].astype(F32) + from_core(l)[k].astype(F32)).astype(ref.dtype)

        over(Z, step)

    def z_push(l):
        for h in pieces:
            z_push_middle(l, h)
        for h in pieces:
            z_push_piece(l, h)

    def z_push_middle(l, h):
        if line:

            def to_middle():
                through, owner = jnp.where(zc == 0, 1, Z - 2), Z - 1 - zc
                send(g_piece(l, 2 * owner + core, h), from_z(l, through, h), (r, 2 * through + core), f"mid{l}.{h}")

            when(is_end, to_middle)
            g = GROUP[f"mid{l}.{h}"]
            arriving[f"mid{l}.{h}"] = lambda: when(
                jnp.logical_not(is_end), lambda: wait_for(from_z(l, 0, h), rsem.at[g])
            )
            leaving[f"mid{l}.{h}"] = lambda: when(is_end, lambda: wait_for(from_z(l, 0, h), ssem.at[g]))

    def z_push_piece(l, h):
        def push(k):
            to = (zc + k) % Z
            send(g_piece(l, 2 * to + core, h), from_z(l, zc, h), (r, 2 * to + core), f"z{l}.{h}")

        for k in range(1, Z) if Z <= 8 else ():
            if line and k == 2:
                when(is_end, lambda: push(2))
            else:
                direct(k, lambda: push(k))
        if Z > 8:
            over(Z, push, 1)
        arriving[f"z{l}.{h}"] = lambda: z_wait(l, h, rsem.at[GROUP[f"z{l}.{h}"]])
        leaving[f"z{l}.{h}"] = lambda: z_wait(l, h, ssem.at[GROUP[f"z{l}.{h}"]])

    def z_middle(l):
        for h in pieces:
            z_middle_piece(l, h)

    def z_middle_piece(l, h):
        if line:
            wait_recv(f"mid{l}.{h}")

            def hand_on():
                owner = (Z - 1) * (Z - 2 - zc)
                ref = g_piece(l, 2 * owner + core, h)
                ref[...] = (ref[...].astype(F32) + from_z(l, zc, h)[...].astype(F32)).astype(ref.dtype)
                send(ref, from_z(l, zc, h), (r, 2 * owner + core), f"z{l}.{h}")

            when(jnp.logical_not(is_end), hand_on)

    def z_wait(l, h, sem):
        first, size = cut(l, h)
        many = lambda count: (zr.at[l, pl.ds(0, count), cut_at(l, h)] if l < 4 else hzr.at[pl.ds(0, count), cut_at(l, h)])
        if line:
            when(is_end, lambda: wait_for(many(Z - 2), sem))
            when(jnp.logical_not(is_end), lambda: wait_for(many(Z - 1), sem))
        else:
            wait_for(many(Z - 1), sem)

    def z_sum(l):
        for h in pieces:
            z_sum_piece(l, h)
        if l < 4:
            gather_start(f"rows{l}", rows_piece(l))
        else:
            over(R, lambda k: send(hr.at[r], hr.at[r], rep_peer(k), "rows4"), 1)

    def z_sum_piece(l, h):
        wait_recv(f"z{l}.{h}")
        read = lambda i: from_z(l, i, h)[...].astype(F32)
        summed = g_piece(l, f, h)[...].astype(F32)
        if line:
            one_side = jnp.where(zc == 0, 1, jnp.where(zc == Z - 1, Z - 2, zc - 1))
            other_side = jnp.where(zc == 0, 2, jnp.where(zc == Z - 1, 1, zc + 1))
            opposite = jnp.where(zc == 1, Z - 1, 0)
            summed = summed + read(one_side) + read(other_side) + jnp.where(is_end, 0.0, read(opposite))
        else:
            summed = lax.fori_loop(1, Z, lambda k, so_far: so_far + read((zc + k) % Z), summed)
        summed = summed * (1.0 / root)
        if l < 4:
            gather[l, cut_at(l, h), my_lanes] = summed.astype(gather.dtype)
        else:
            hr[r, cut_at(l, h)] = summed.astype(hr.dtype)

    def rows_done(l):
        if l < 4:
            await_rest(f"rows{l}")
            copy_here(gather.at[l], gw[l], f"out{l}")
        else:
            wait_recv("rows4")
            summed = sum(hr[i].astype(F32) for i in range(R))
            wide = -(-half // LANES) * LANES
            if wide > half:
                summed = jnp.concatenate([summed, jnp.zeros((wide - half, LANES), F32)], axis=0)
            summed = jnp.transpose(summed)
            ghc[:, 0:half] = summed[0 : d.HC, 0:half]
            ghc[:, half:rows] = summed[d.HC : 2 * d.HC, 0 : rows - half]

    def exchange(e):
        over(F, lambda k: send(st_s.at[e], st_r.at[e, f], (r, (f + k) % F), f"stat{e}"), 1)
        st_r[e, f] = st_s[e]

    def exchanged(e):
        wait_recv(f"stat{e}")
        return st_r[e]

    st_s[...] = jnp.zeros_like(st_s)
    w_relay_rest(0)
    w_relay_near(0)
    w_far(0)
    w_push_rest(1, who=at_ends)
    wait_recv("images")
    wait_recv("own_image")
    wait_recv("start")

    rep_all = lambda src, dst, group: over(R, lambda k: send(src, dst, rep_peer(k), group), 1)
    images_here = M // PIX
    inverse_of, counts = [], None

    def widened(j, i, b):
        value = zg[j, image_rows(i), b * CR : (b + 1) * CR].astype(F32)
        return value, [nrm_r[j, b, k : k + 1, :] for k in range(4)]

    def slopes_of(j):
        def body(i, carry):
            for b in range(R):
                value, (a, o, inverse, off) = widened(j, i, b)
                shaped = value * a + o
                squashed = sigmoid(shaped)
                steep = squashed + shaped * squashed * (1.0 - squashed)
                slope[j, image_rows(i), b * CR : (b + 1) * CR] = steep.astype(BF16)
                slope_z[j, image_rows(i), b * CR : (b + 1) * CR] = (steep * (value * inverse + off)).astype(BF16)
            return carry

        per_image(images_here, body, 0)

    for l in range(4):
        w_finish(l)
        if l == 2:
            wait_recv("pool")
            s[2] = jnp.dot(u_sel[...], pool_all[...], preferred_element_type=F32).astype(BF16)
        first = conv(s.at[l], images_here, l, zb)
        mean_here = first * (1.0 / M)
        j = l // 2
        gathers = l in (0, 2)

        def squares(i, so_far):
            apart = zb[image_rows(i), :] - mean_here
            if gathers:
                zg[j, image_rows(i), my_lanes] = apart.astype(BF16)
            return so_far + jnp.sum(jnp.square(apart), axis=0, keepdims=True)

        squared = per_image(images_here, squares, jnp.zeros((1, CR), F32))
        if gathers:
            gather_start(f"ag{l}", ag_piece(j))
        st_s[l, 0:1, :] = first
        st_s[l, 1:2, :] = squared
        if l == 0:
            st_s[l, 2:3, :] = sum(start_r[i, 0:1, :] for i in range(R))
        exchange(l)
        if l == 0:
            w_push_rest(1, who=between)
            w_push_near(1)
            w_relay_rest(1)
        elif l < 3:
            w_push_rest(l + 1, pieces[1:])
            w_push_near(l + 1)
            w_relay_rest(l + 1, pieces[:1])
        else:
            w_push_near(4)
            w_relay_rest(4)
        if gathers:
            gather_forward(f"ag{l}", ag_piece(j))
        elif l == 1:
            pixel_columns()
        else:
            slopes_of(1)
        parts = exchanged(l)
        tot = jnp.sum(parts, axis=0)
        mean = tot[0:1] * (1.0 / total)
        apart = jnp.sum(jnp.square(parts * (1.0 / M) - mean[None]), axis=0)[0:1] * float(M)
        inverse = lax.rsqrt((tot[1:2] + apart) * (1.0 / total) + EPS)
        inverse_of.append(inverse)
        if l == 0:
            counts = tot[2:3]
        g_row, b_row = gain[l : l + 1, my_lanes], shift[l : l + 1, my_lanes]
        if gathers:
            off = (mean_here - mean) * inverse
            nrm_s[j, 0:1, :] = inverse * g_row
            nrm_s[j, 1:2, :] = off * g_row + b_row
            nrm_s[j, 2:3, :] = inverse
            nrm_s[j, 3:4, :] = off
            rep_all(nrm_s.at[j], nrm_r.at[j, r], f"norm{j}")
            nrm_r[j, r] = nrm_s[j]

        def activate(i, carry):
            at = image_rows(i)
            normed = (zb[at, :] - mean) * inverse
            zhat[l, at, :] = normed
            shaped = normed * g_row + b_row
            hidden = shaped * sigmoid(shaped)
            if l == 1:
                zb[at, :] = hidden
            else:
                a2a_s[i] = hidden.astype(BF16)
            return carry

        def keep_normed(i, carry):
            zhat[l, image_rows(i), :] = (zb[image_rows(i), :] - mean) * inverse
            return carry

        def activate_all(i, carry):
            for b in range(R):
                value, (a, o, unused, also) = widened(j, i, b)
                shaped = value * a + o
                s[l + 1, image_rows(i), b * CR : (b + 1) * CR] = (shaped * sigmoid(shaped)).astype(BF16)
            return carry

        per_image(images_here, keep_normed if gathers else activate, 0)
        if l == 1:
            inside, unused = windows(False)
            pooled = jnp.dot(
                jnp.where(inside, 0.25, 0.0), zb[...], precision=EXACT, preferred_element_type=F32
            )
            pool_own[...] = pooled.astype(BF16)
            pool_all[:, my_lanes] = pooled.astype(BF16)
            rep_all(pool_own, pool_all.at[:, my_lanes], "pool")
            w_relay_rest(2, pieces[1:])
            slopes_of(0)
        elif l == 3:
            over(R, lambda k: send(a2a_s.at[(r + k) % R], s4.at[:, my_lanes], rep_peer(k), "a2a"), 1)
            s4[:, my_lanes] = a2a_s[r]
        elif l == 0:
            pool_matrices()
        else:
            w_relay_rest(3, pieces[1:])
            pack_head()
        w_relay_near(l + 1)
        if l < 2:
            w_push_rest(l + 2, pieces[:1])
        elif l == 2:
            w_push_rest(4)
        w_far(l + 1)
        if gathers:
            wait_recv(f"norm{j}")
            await_rest(f"ag{l}")
            per_image(images_here, activate_all, 0)

    w_finish(4)
    low_lanes = lax.broadcasted_iota(jnp.int32, (half, LANES), 1) < d.HC

    def unpack(i, carry):
        both = hp[i].astype(F32)
        at = i * rows
        wf[4, pl.ds(pl.multiple_of(at, d.row_tile), half), :] = jnp.where(low_lanes, both, 0.0).astype(wf.dtype)
        high = jnp.where(low_lanes, pltpu.roll(both, d.HC, 1), 0.0).astype(wf.dtype)
        wf[4, pl.ds(pl.multiple_of(at + half, d.row_tile), rows - half), :] = high[0 : rows - half]
        return carry

    lax.fori_loop(0, F, unpack, 0)
    wait_recv("a2a")
    wait_recv("head_out")
    conv(s4, PD // PIX, 4, zb)
    head_bias = jnp.concatenate([hb[...], jnp.zeros((1, CR - d.HC), F32)], axis=1)
    out_bias = jnp.concatenate([ob[...], jnp.zeros((1, CR - d.OC), F32)], axis=1)
    head_raw = zb[0:PD, :] + head_bias
    squashed = sigmoid(head_raw)
    head_act = head_raw * squashed
    project = jnp.concatenate([ho_r[i][0 : d.q] for i in range(F)] + [jnp.zeros((LANES - d.HC, LANES), F32)], axis=0)
    out = jnp.dot(head_act, project, precision=EXACT, preferred_element_type=F32) + out_bias
    lane = lax.broadcasted_iota(jnp.int32, (PD, LANES), 1)
    classes = d.OC - 4
    factor = total * jnp.concatenate([tw[...], jnp.zeros((1, LANES - 3), F32)], axis=1) / jnp.maximum(counts, 1.0)
    pixel = [columns_s[:, i : i + 1] for i in range(8)]
    is_class = lane < classes
    top = jnp.max(jnp.where(is_class, out, -jnp.inf), axis=1, keepdims=True)
    grown = jnp.where(is_class, jnp.exp(jnp.where(is_class, out - top, 0.0)), 0.0)
    likely = grown / jnp.sum(grown, axis=1, keepdims=True)
    onehot = jnp.where(lane.astype(F32) == pixel[0], 1.0, 0.0)
    grad_class = factor[:, 0:1] * pixel[1] * (likely - onehot)
    misfit = out - pixel[4]
    grad_depth = factor[:, 1:2] * pixel[2] * misfit / jnp.sqrt(misfit * misfit + 1.0)
    is_normal = (lane > classes) & (lane < d.OC)
    predicted = jnp.where(is_normal, out, 0.0)
    wanted = sum(jnp.where(lane == classes + 1 + i, pixel[5 + i], 0.0) for i in range(3))
    radius = jnp.sqrt(jnp.sum(predicted * predicted, axis=1, keepdims=True) + 1.0)
    aligned = jnp.sum(predicted * wanted, axis=1, keepdims=True)
    grad_normal = -(factor[:, 2:3] * pixel[3]) * (wanted / radius - aligned / (radius * radius * radius) * predicted)
    grad_out = jnp.where(
        is_class, grad_class, jnp.where(lane == classes, grad_depth, jnp.where(is_normal, grad_normal, 0.0))
    )
    grad_act = lax.dot_general(
        grad_out, project, (((1,), (1,)), ((), ())), precision=EXACT, preferred_element_type=F32
    )
    grad_head = (grad_act * (squashed + head_raw * squashed * (1.0 - squashed))).astype(BF16).astype(F32)
    zb[0:PD, :] = grad_head
    y[0:PD, 0:CR] = head_act
    y[0:PD, CR : 2 * CR] = grad_out

    def spread_head(i, carry):
        spread_taps(i, zb[image_rows(i), :])
        return carry

    per_image(PD // PIX, spread_head, 0)

    def write_dh3(half, part):
        a2a_s[2 * half] = part[:, 0:CR].astype(BF16)
        a2a_s[2 * half + 1] = part[:, CR : 2 * CR].astype(BF16)

    wait_send("a2a")
    data_grad(4, PD, write_dh3)
    over(R, lambda k: send(a2a_s.at[(r + k) % R], a2a_r.at[r], rep_peer(k), "dh3"), 1)
    a2a_r[r] = a2a_s[r]
    weight_grad(4, s4, PD)
    head_act, grad_out = y[0:PD, 0:CR], y[0:PD, CR : 2 * CR]
    pad = jnp.zeros((2 * LANES - PD, LANES), F32)
    act_t = jnp.transpose(jnp.concatenate([head_act, pad], axis=0))[:, 0:PD]
    rep_s[0 : d.HC, :] = jnp.dot(act_t, grad_out, precision=EXACT, preferred_element_type=F32)[0 : d.HC]
    rep_s[d.HC : d.HC + 8, :] = jnp.zeros((8, LANES), F32)
    rep_s[d.HC : d.HC + 1, :] = jnp.sum(zb[0:PD, :], axis=0, keepdims=True)
    rep_s[d.HC + 1 : d.HC + 2, :] = jnp.sum(grad_out, axis=0, keepdims=True)
    over(R, lambda k: send(rep_s, rep_r.at[r], rep_peer(k), "small_rep"), 1)
    rep_r[r] = rep_s[...]

    def head_small():
        wait_recv("small_rep")
        summed = sum(rep_r[i] for i in range(R))
        for i in range(F):
            all_s[i, 0 : d.q, :] = summed[i * d.q : (i + 1) * d.q]
            if d.q < 8:
                all_s[i, d.q : 8, :] = jnp.zeros((8 - d.q, LANES), F32)
            all_s[i, 8:16, :] = summed[d.HC : d.HC + 8]
        over(F, lambda k: send(all_s.at[(f + k) % F], all_r.at[f], (r, (f + k) % F), "small_all"), 1)
        all_r[f] = all_s[f]

    def rows_of(l):
        return gain[l : l + 1, my_lanes], shift[l : l + 1, my_lanes]

    def slope_here(l, at):
        g_row, b_row = rows_of(l)
        normed = zhat[l, at, :]
        shaped = normed * g_row + b_row
        squashed = sigmoid(shaped)
        return normed, squashed + shaped * squashed * (1.0 - squashed)

    def enter(l, entering):
        def body(i, so_far):
            at = image_rows(i)
            normed, steep = slope_here(l, at)
            grad = entering(i, at) * steep
            zb[at, :] = grad
            return (
                so_far[0] + jnp.sum(grad, axis=0, keepdims=True),
                so_far[1] + jnp.sum(grad * normed, axis=0, keepdims=True),
            )

        none = jnp.zeros((1, CR), F32)
        part_bias, part_gain = per_image(images_here, body, (none, none))
        st_s[7 - l, 0:1, :] = part_bias
        st_s[7 - l, 1:2, :] = part_gain
        exchange(7 - l)

    def through_norm(l, grad_of):
        tot = jnp.sum(exchanged(7 - l), axis=0)
        bias_sum, gain_sum = tot[0:1], tot[1:2]
        norm_s[l : l + 1, :] = gain_sum * (1.0 / root)
        norm_s[4 + l : 5 + l, :] = bias_sum * (1.0 / root)
        scale = inverse_of[l] * rows_of(l)[0]
        if l in (0, 2):
            await_rest(f"rs{l + 1}")

        def body(i, carry):
            at = image_rows(i)
            normed, grad = grad_of(i, at)
            spread_taps(i, scale * (grad - bias_sum * (1.0 / total) - normed * (gain_sum * (1.0 / total))))
            return carry

        per_image(images_here, body, 0)

    def from_zb(l):
        return lambda i, at: (zhat[l, at, :], zb[at, :])

    def from_scatter(l):
        j = l // 2
        here = images_here // 2

        def grad_of(i, at):
            normed, steep = slope_here(l, at)
            h = i // here
            local = image_rows(i - h * here)
            grad = (
                rs_s[j, r, at, :].astype(F32)
                + rs_l[j, 1 + 2 * h, local, :].astype(F32)
                + rs_l[j, 4 + h, local, :].astype(F32)
            )
            return normed, grad * steep

        return grad_of

    def layer_down(l):
        j = (l - 1) // 2

        def write(part_at, part):
            for b in range(2):
                n = 2 * part_at + b
                grad = part[:, b * CR : (b + 1) * CR]
                rs_s[j, n] = grad.astype(BF16)
                cols = slice(n * CR, (n + 1) * CR)
                sums_s[j, n, 0:1, :] = jnp.sum(grad * slope[j, :, cols].astype(F32), axis=0, keepdims=True)
                sums_s[j, n, 1:2, :] = jnp.sum(grad * slope_z[j, :, cols].astype(F32), axis=0, keepdims=True)

        data_grad(l, M, write)
        over(R, lambda k: send(sums_s.at[j, (r + k) % R], sums_r.at[j, r], rep_peer(k), f"sums{j}"), 1)
        scatter_start(f"rs{l}", rs_piece(j), rs_land(j))
        sums_r[j, r] = sums_s[j, r]
        z_middle_piece(l + 1, 0)
        weight_grad(l, s.at[l], M)
        wait_recv(f"sums{j}")
        e = 7 - (l - 1)
        st_s[e, 0:2, :] = sum(sums_r[j, i, 0:2, :] for i in range(R))
        exchange(e)
        scatter_forward(f"rs{l}", rs_piece(j), rs_land(j))
        for h in pieces[1:]:
            z_middle_piece(l + 1, h)

    wait_recv("dh3")
    enter(3, lambda i, at: a2a_r[i].astype(F32))
    core_sum(4)
    z_push(4)
    head_small()
    through_norm(3, from_zb(3))
    layer_down(3)
    core_sum(3)
    z_push(3)

    through_norm(2, from_scatter(2))

    def write_pooled(part_at, part):
        chosen = jnp.dot(ut_sel[...], part.astype(BF16), preferred_element_type=F32).astype(BF16)
        ps_s[2 * part_at] = chosen[:, 0:CR]
        ps_s[2 * part_at + 1] = chosen[:, CR : 2 * CR]

    z_middle(3)
    data_grad(2, M, write_pooled)
    over(R, lambda k: send(ps_s.at[(r + k) % R], ps_r.at[r], rep_peer(k), "rs2"), 1)
    ps_r[r] = ps_s[r]
    weight_grad(2, s.at[2], M)
    wait_recv("rs2")
    pooled = sum(ps_r[i].astype(F32) for i in range(R))
    inside, unused = windows(True)
    zb[...] = jnp.dot(jnp.where(inside, 0.25, 0.0), pooled, precision=EXACT, preferred_element_type=F32)
    enter(1, lambda i, at: zb[at, :])
    core_sum(2)
    z_push(2)
    z_sum(4)
    z_sum(3)
    through_norm(1, from_zb(1))
    gather_forward("rows3", rows_piece(3))
    layer_down(1)
    core_sum(1)
    z_push(1)
    z_sum(2)

    through_norm(0, from_scatter(0))
    weight_grad(0, s.at[0], M)
    gather_forward("rows2", rows_piece(2))

    def write_images(part_at, part):
        for i in range(R):
            gi_s[i, :, part_at * 2 * CR : (part_at + 1) * 2 * CR] = part[i * PD : (i + 1) * PD].astype(BF16)

    data_grad(0, M, write_images)
    scatter_start("rs0", gi_piece, gi_land)
    z_middle(1)
    core_sum(0)
    z_push(0)

    gnorm[:, my_lanes] = norm_s[...]
    rep_all(norm_s, gnorm.at[:, my_lanes], "norms")
    z_middle(0)
    scatter_forward("rs0", gi_piece, gi_land)
    z_sum(1)
    wait_recv("small_all")
    gsmall[...] = jnp.sum(all_r[...], axis=0) * (1.0 / root)
    rows_done(4)
    rows_done(3)
    gather_forward("rows1", rows_piece(1))
    rows_done(2)
    await_rest("rs0")
    for h in range(2):
        at = slice(h * (PD // 2), (h + 1) * (PD // 2))
        gi[at, :] = gi_s[r, at, :].astype(F32) + gi_l[1 + 2 * h].astype(F32) + gi_l[4 + h].astype(F32)
    last = rows_piece(0)
    if d.pieces == 2:
        z_sum_piece(0, 0)
        send(last(r, 0), last(r, 0), at_one, "rows0x0")
        send(last(r, 0), last(r, 0), at_two, "rows0y0")
        send(last(r, 0), last(r, 0), (both, f), "rows0f0")
        rows_done(1)
        z_sum_piece(0, 1)
        send(last(r, 1), last(r, 1), at_one, "rows0x1")
        send(last(r, 1), last(r, 1), at_two, "rows0y1")
        send(last(r, 1), last(r, 1), (both, f), "rows0f1")
        wait_recv("rows0x0")
        wait_recv("rows0y1")
    else:
        z_sum(0)
        rows_done(1)
        gather_forward("rows0", last)
    wait_recv("norms")
    rows_done(0)

    drain()


def finish(gi, gw0, gw1, gw2, gw3, ghc, gnorm, gsmall, *outs):
    out_gi, out0, out1, out2, out3, out_hc, out_ho, out_gain, out_bias, out_hb, out_ob = outs
    out_gi[...] = gi[...]
    for src, dst in ((gw0, out0), (gw1, out1), (gw2, out2), (gw3, out3)):
        dst[...] = src[...].astype(F32)

    @pl.when(pl.program_id(0) == 0)
    def _():
        out_hc[...] = ghc[...]
        out_ho[...] = gsmall[0 : out_ho.shape[0], 0 : out_ho.shape[1]]
        out_gain[...] = gnorm[0:4, :]
        out_bias[...] = gnorm[4:8, :]
        out_hb[...] = gsmall[8:9, 0 : out_hb.shape[1]]
        out_ob[...] = gsmall[9:10, 0 : out_ob.shape[1]]


def per_device(
    R, F,
    images, enc_first, enc_second, dec_first, dec_second, head_conv, head_out, norm_gain, norm_bias, head_bias, out_bias,
    task_weights, pool_index, labels, task_masks, targets,
):
    n, height, breadth, channels = images.shape
    rows, hidden = head_conv.shape
    q, out_ch = head_out.shape
    d = types.SimpleNamespace(
        n=n, R=R, F=F, Z=F // 2, rows=rows, C=channels, CR=channels // R, W=breadth, PIX=height * breadth,
        PD=n * height * breadth, HC=hidden, OC=out_ch, q=q,
    )
    d.M = R * d.PD
    d.pieces = 2 if d.Z == 4 else 1
    d.PW = d.M // 4
    wire = BF16 if rows % 16 == 0 else F32
    d.row_tile = 16 if rows % 16 == 0 else 8
    d.half = -(-rows // (2 * d.row_tile)) * d.row_tile
    vm = pltpu.VMEM
    patch = 9 * channels
    scratch = [
        vm((4, rows, d.C), wire),
        vm((d.PD, LANES), F32),
        vm((4, d.M, d.C), BF16),
        vm((d.PD, d.C), BF16),
        vm((5, patch, d.CR), wire),
        vm((d.M, 9 * d.CR), F32),
        vm((d.M, d.CR), F32),
        vm((4, d.M, d.CR), F32),
        vm((d.M, 9 * d.CR), BF16),
        vm((d.M, d.PW), BF16),
        vm((d.PW, d.M), BF16),
        vm((R, d.PD, d.CR), BF16),
        vm((R, d.PD, d.CR), BF16),
        vm((2, R, d.M, d.CR), BF16),
        vm((2, 6, d.M // 2, d.CR), BF16),
        vm((d.PW, d.CR), BF16),
        vm((d.PW, d.C), BF16),
        vm((R, d.PW, d.CR), BF16),
        vm((R, d.PW, d.CR), BF16),
        vm((R, d.PD, d.C), BF16),
        vm((6, d.PD // 2, d.C), BF16),
        vm((2, d.M, d.C), BF16),
        vm((2, d.M, d.C), BF16),
        vm((2, d.M, d.C), BF16),
        vm((2, 8, LANES), F32),
        vm((2, R, 8, LANES), F32),
        vm((2, R, 8, LANES), F32),
        vm((2, R, 8, LANES), F32),
        vm((4, patch, d.CR), wire),
        vm((4, d.Z, rows, d.CR), wire),
        vm((4, d.Z, rows, d.CR), wire),
        vm((d.half, LANES), wire),
        vm((F, d.half, LANES), wire),
        vm((F, d.half, LANES), wire),
        vm((d.Z, d.half, LANES), wire),
        vm((d.Z, d.half, LANES), wire),
        vm((R, d.half, LANES), wire),
        vm((8, 8, LANES), F32),
        vm((8, F, 8, LANES), F32),
        vm((8, LANES), F32),
        vm((R, 8, LANES), F32),
        vm((8, LANES), F32),
        vm((F, 8, LANES), F32),
        vm((hidden + 8, LANES), F32),
        vm((R, hidden + 8, LANES), F32),
        vm((F, 16, LANES), F32),
        vm((F, 16, LANES), F32),
        vm((8, LANES), F32),
        vm((LANES, 2 * LANES), F32),
        pltpu.SemaphoreType.DMA((len(GROUPS),)),
        pltpu.SemaphoreType.DMA((len(GROUPS),)),
        pltpu.SemaphoreType.DMA((5 * d.pieces, d.Z)),
        pltpu.SemaphoreType.DMA((5 * d.pieces, d.Z)),
        pltpu.SemaphoreType.DMA((5 * d.pieces, d.Z)),
        pltpu.SemaphoreType.DMA((5 * d.pieces, d.Z)),
    ]
    here, there = pl.BlockSpec(memory_space=pltpu.VMEM), pl.BlockSpec(memory_space=pl.ANY)
    shape = jax.ShapeDtypeStruct
    kept = pl.pallas_call(
        functools.partial(kernel, d),
        out_shape=[shape((d.PD, d.C), F32)]
        + [shape((rows, d.C), wire)] * 4
        + [shape((hidden, rows), F32), shape((8, d.C), F32), shape((16, LANES), F32)],
        in_specs=[there] * 5 + [here] * 11,
        out_specs=[here] + [there] * 4 + [here] * 3,
        scratch_shapes=scratch,
        compiler_params=pltpu.CompilerParams(collective_id=0, has_side_effects=True, vmem_limit_bytes=60 * 2**20),
    )(
        images.reshape(d.PD, channels),
        *(w.astype(wire) for w in (enc_first, enc_second, dec_first, dec_second)),
        head_conv.T, head_out, norm_gain, norm_bias, head_bias.reshape(1, hidden), out_bias.reshape(1, out_ch),
        task_weights.reshape(1, 3), pool_index, labels, jnp.transpose(task_masks, (1, 0, 2)), targets,
    )
    steps = next(count for count in (2, 1) if rows % (count * d.row_tile) == 0 and d.PD % (count * 8) == 0)
    part = lambda height, width: pl.BlockSpec((height // steps, width), lambda i: (i, 0))
    all_of = lambda height, width: pl.BlockSpec((height, width), lambda i: (0, 0))
    rest = ((q, out_ch), (4, channels), (4, channels), (1, hidden), (1, out_ch))
    gi, gw0, gw1, gw2, gw3, ghc, gq, gain, bias, ghb, gob = pl.pallas_call(
        finish,
        grid=(steps,),
        out_shape=[shape((d.PD, channels), F32)]
        + [shape((rows, channels), F32)] * 4
        + [shape((hidden, rows), F32)]
        + [shape(size, F32) for size in rest],
        in_specs=[part(d.PD, channels)]
        + [part(rows, channels)] * 4
        + [all_of(hidden, rows), all_of(8, channels), all_of(16, LANES)],
        out_specs=[part(d.PD, channels)]
        + [part(rows, channels)] * 4
        + [all_of(hidden, rows)]
        + [all_of(*size) for size in rest],
    )(*kept)
    return (
        gi.reshape(images.shape), gw0, gw1, gw2, gw3, ghc.T, gq, gain, bias, ghb.reshape(hidden), gob.reshape(out_ch),
    )


def solution(mesh):
    split = ("rep", "fsdp")
    rows = P("fsdp", None)
    return jax.shard_map(
        functools.partial(per_device, mesh.shape["rep"], mesh.shape["fsdp"]),
        mesh=mesh,
        in_specs=(P(split, None, None, None),)
        + (rows,) * 6
        + (P(),) * 5
        + (P(split, None), P(split, None), P(split, None, None), P(split, None, None)),
        out_specs=(P(split, None, None, None),) + (rows,) * 6 + (P(),) * 4,
        check_vma=False,
    )
```

```python
import functools
import math
import types

import jax
import jax.numpy as jnp
from jax import lax
from jax.experimental import pallas as pl
from jax.experimental.pallas import tpu as pltpu
from jax.sharding import PartitionSpec as P

MESH = pl.DeviceIdType.MESH
F32, BF16 = jnp.float32, jnp.bfloat16
EPS = 1e-05
LANES = 128
EXACT = lax.Precision.HIGHEST

GROUPS = (
    ["images", "start", "head_out", "a2a", "pool", "dh3", "rs2", "norms", "small_rep", "small_all"]
    + [f"sums{i}" for i in range(4)]
    + ["pool_slope"]
    + [f"norm{i}" for i in range(3)]
    + [
        f"{name}{way}"
        for name in ("ag0", "ag2", "rs3", "rs1", "rs0", "rows0", "rows1", "rows2", "rows3")
        for way in ("x0", "x1", "y0", "y1", "f0", "f1")
    ]
    + [f"stat{i}" for i in range(8)]
    + [f"core{i}" for i in range(5)]
    + [f"z{i}.{h}" for i in range(5) for h in range(2)]
    + [f"mid{i}.{h}" for i in range(5) for h in range(2)]
    + ["rows4"]
    + [f"own{i}" for i in range(5)]
    + [f"out{i}" for i in range(4)]
    + [f"in{i}" for i in range(11)]
    + ["own_image", "out_gi", "out_ghc", "out_gnorm", "out_gsmall"]
)
GROUP = {name: number for number, name in enumerate(GROUPS)}


def kernel(d, *refs):
    it = iter(refs)
    take = lambda count: [next(it) for _ in range(count)]
    images, w0, w1, w2, w3, *small_in = take(16)
    gi_out, gw0, gw1, gw2, gw3, *small_out = take(8)
    small = hw, ho, gain, shift, hb, ob, tw, pidx, lab, msk, tgt = take(11)
    gi, ghc, gnorm, gsmall = take(4)
    gather, columns_s = take(2)
    (s, s4, wf, y, zb, zhat, d9, u_sel, ut_sel, a2a_s, a2a_r, rs_s, rs_l, pool_own, pool_all, ps_s, ps_r, gi_s, gi_l) = take(19)
    (zg, slope, slope_z, nrm_s, nrm_r, sums_s, sums_r, z4, slope4, slope_z4, sp_own, sp_all) = take(12)
    (gf, cr, zr, hw_s, hp, hg, hcr, hzr, hr, st_s, st_r, start_s, start_r, ho_s, ho_r, rep_s, rep_r, all_s, all_r, norm_s, feat) = take(21)
    ssem, rsem, wsz, wrz, wsf, wrf = take(6)
    w_in, gw = (w0, w1, w2, w3, hw_s), (gw0, gw1, gw2, gw3)
    R, F, Z, rows, half, C, CR, W, PIX, PD, M, PW = d.R, d.F, d.Z, d.rows, d.half, d.C, d.CR, d.W, d.PIX, d.PD, d.M, d.PW
    total = float(M * F)
    root = math.sqrt(total)

    r, f = lax.axis_index("rep"), lax.axis_index("fsdp")
    zc, core = f // 2, f % 2
    sib = (r, zc * 2 + (1 - core))
    rep_peer = lambda k: ((r + k) % R, f)
    one, two = r + 1 - 2 * (r % 2), (r + 2) % R
    both = (one + 2) % R
    at_one, at_two = (one, f), (two, f)
    z_peer = lambda k: (r, ((zc + k) % Z) * 2 + core)
    line = Z == 4
    is_end = (zc == 0) | (zc == Z - 1)
    is_far = lambda k: (zc + k) % Z - zc == Z - 1
    is_far_back = lambda k: zc - (zc + k) % Z == Z - 1
    ends_apart = lambda k: is_far(k) | is_far_back(k)
    my_lanes = pl.ds(pl.multiple_of(r * CR, CR), CR)

    def block(owner):
        return pl.ds(pl.multiple_of(owner * rows, d.row_tile), rows)

    arriving, leaving = {}, {}

    def first_of(ref, count):
        return lambda: ref.at[pl.ds(0, count)]

    volume = {
        "images": first_of(s.at[0], (R - 1) * PD),
        "own_image": first_of(s.at[0], PD),
        "start": first_of(start_r, R - 1),
        "head_out": first_of(ho_r, F - 1),
        "a2a": lambda: z4.at[:, pl.ds(0, (R - 1) * CR)],
        "pool_slope": lambda: sp_all.at[:, :, pl.ds(0, (R - 1) * CR)],
        "pool": lambda: pool_all.at[:, pl.ds(0, (R - 1) * CR)],
        "dh3": first_of(a2a_r, R - 1),
        "rs2": first_of(ps_r, R - 1),
        "norms": lambda: gnorm.at[:, pl.ds(0, (R - 1) * CR)],
        "small_rep": first_of(rep_r, R - 1),
        "small_all": first_of(all_r, F - 1),
        "rows4": first_of(hr, R - 1),
        "core4": lambda: hcr,
    }
    for way in ("x", "y", "f"):
        for h in range(2):
            for j in range(2):
                volume[f"ag{2 * j}{way}{h}"] = lambda j=j: zg.at[j, pl.ds(0, M // 2), pl.ds(0, CR)]
                volume[f"rs{2 * j + 1}{way}{h}"] = lambda j=j: rs_l.at[j, 0]
            volume[f"rs0{way}{h}"] = lambda: gi_l.at[0]
            size = half if h == 0 else rows - half
            for l in range(4):
                volume[f"rows{l}{way}{h}"] = lambda l=l, size=size: gather.at[l, pl.ds(0, size), pl.ds(0, CR)]
    for j in range(4):
        volume[f"sums{j}"] = first_of(sums_r.at[j], R - 1)
    for j in range(3):
        volume[f"norm{j}"] = first_of(nrm_r.at[j], R - 1)
    for e in range(8):
        volume[f"stat{e}"] = first_of(st_r.at[e], F - 1)
    for l in range(4):
        volume[f"core{l}"] = lambda l=l: cr.at[l]

    def wait_for(ref, sem):
        pltpu.make_async_copy(ref, ref, sem).wait()

    def wait_recv(group):
        arriving.pop(group)()

    def wait_send(group):
        leaving.pop(group)()

    def copy_here(src, dst, group):
        g = GROUP[group]
        arriving[group] = lambda: wait_for(dst, rsem.at[g])
        pltpu.make_async_copy(src, dst, rsem.at[g]).start()

    def send(src, dst, to, group):
        g = GROUP[group]
        if group in volume:
            arriving[group] = lambda: wait_for(volume[group](), rsem.at[g])
            leaving[group] = lambda: wait_for(volume[group](), ssem.at[g])
        pltpu.make_async_remote_copy(
            src_ref=src, dst_ref=dst, send_sem=ssem.at[g], recv_sem=rsem.at[g], device_id=to, device_id_type=MESH
        ).start()

    def over(count, body, first=0):
        if count <= 8:
            for i in range(first, count):
                body(i)
            return

        def step(i, carry):
            body(i)
            return carry

        lax.fori_loop(first, count, step, 0)

    def when(condition, body):
        pl.when(condition)(body)

    def direct(k, body):
        if line and k in (1, Z - 1):
            when(jnp.logical_not(ends_apart(k)), body)
        else:
            body()

    def drain():
        for waits in (arriving, leaving):
            for wait in list(waits.values()):
                wait()

    for i, (src, dst) in enumerate(zip(small_in, small)):
        copy_here(src, dst, f"in{i}")

    barrier = pltpu.get_barrier_semaphore()
    over(R, lambda k: pl.semaphore_signal(barrier, inc=1, device_id=rep_peer(k), device_id_type=MESH), 1)
    over(F, lambda k: pl.semaphore_signal(barrier, inc=1, device_id=(r, (f + k) % F), device_id_type=MESH), 1)
    pl.semaphore_wait(barrier, R + F - 2)

    pieces = range(d.pieces)

    def cut(l, h):
        size = rows if l < 4 else half
        first = -(-size // (d.pieces * d.row_tile)) * d.row_tile
        return (0, first) if h == 0 else (first, size - first)

    def cut_at(l, h):
        first, size = cut(l, h)
        return pl.ds(first, size)

    near = sorted({1, Z - 1})
    beyond = list(range(2, Z - 1))

    def w_block(l, owner, h):
        first, size = cut(l, h)
        if l < 4:
            return wf.at[l, pl.ds(pl.multiple_of(owner * rows + first, d.row_tile), size)]
        return hp.at[owner, pl.ds(first, size)]

    def w_copy(l, h, src, owner, to, send_sem, recv_sem):
        return pltpu.make_async_remote_copy(
            src_ref=src, dst_ref=w_block(l, owner, h), send_sem=send_sem, recv_sem=recv_sem, device_id=to, device_id_type=MESH
        )

    def w_src(l, h):
        return w_in[l].at[cut_at(l, h), my_lanes] if l < 4 else hw_s.at[cut_at(l, h)]

    def w_wait(l, h, sem):
        wait_for(w_block(l, f, h), sem)

    def w_send(l, h, k, who=lambda body: body()):
        u = l * d.pieces + h
        arriving["z", l, h, k] = lambda: direct(Z - k, lambda: w_wait(l, h, wrz.at[u, k]))
        leaving["z", l, h, k] = lambda: direct(k, lambda: w_wait(l, h, wsz.at[u, k]))
        start = lambda: w_copy(l, h, w_src(l, h), f, z_peer(k), wsz.at[u, k], wrz.at[u, k]).start()
        who(lambda: direct(k, start))

    def w_relayed(l, h, k):
        u = l * d.pieces + h
        arriving["core", l, h, k] = lambda: w_wait(l, h, wrf.at[u, k])
        leaving["core", l, h, k] = lambda: w_wait(l, h, wsf.at[u, k])

    def w_push_near(l):
        for h in pieces:
            u = l * d.pieces + h
            for k in near:
                w_send(l, h, k)
            w_copy(l, h, w_src(l, h), f, sib, wsf.at[u, 0], wrf.at[u, 0]).start()
            w_relayed(l, h, 0)
        copy_here(w_in[l].at[:, my_lanes] if l < 4 else hw_s, wf.at[l, block(f)] if l < 4 else hp.at[f], f"own{l}")

    def w_push_rest(l, hs=pieces, who=lambda body: body()):
        for h in hs:
            for k in beyond:
                w_send(l, h, k, who)

    def at_ends(body):
        if line:
            when(is_end, body)
        else:
            body()

    def between(body):
        if line:
            when(jnp.logical_not(is_end), body)

    def w_arrived(l, h, k):
        u = l * d.pieces + h
        owner = ((zc + Z - k) % Z) * 2 + core
        w_wait(l, h, wrz.at[u, k])
        w_copy(l, h, w_block(l, owner, h), owner, sib, wsf.at[u, k], wrf.at[u, k]).start()

    def w_relay_rest(l, hs=pieces):
        for h in hs:
            u = l * d.pieces + h
            for k in beyond:
                arriving.pop(("z", l, h, k))
                w_arrived(l, h, k)
                w_relayed(l, h, k)
            if line:

                def hand_on():
                    to = (Z - 1) * (zc - 1)
                    owner = (Z - 1 - to) * 2 + core
                    slot = jnp.where(zc == 1, 1, Z - 1)
                    w_copy(
                        l, h, w_block(l, owner, h), owner, (r, to * 2 + core), wsz.at[u, 0], wrz.at[u, slot]
                    ).start()

                when(jnp.logical_not(is_end), hand_on)
                leaving["far", l, h] = lambda u=u, h=h: when(
                    jnp.logical_not(is_end), lambda: w_wait(l, h, wsz.at[u, 0])
                )

    def w_relay_near(l):
        for h in pieces:
            for k in near:
                arriving.pop(("z", l, h, k))
                direct(Z - k, lambda: w_arrived(l, h, k))
                if not line:
                    w_relayed(l, h, k)

    def w_far(l):
        if line:
            for h in pieces:
                for k in near:
                    w_relayed(l, h, k)
                when(zc == 0, lambda: w_arrived(l, h, 1))
                when(zc == Z - 1, lambda: w_arrived(l, h, Z - 1))

    def w_finish(l):
        for h in pieces:
            for k in range(Z):
                wait_recv(("core", l, h, k))
        wait_recv(f"own{l}")

    w_push_rest(0)
    w_push_near(0)
    over(R, lambda k: send(images, s.at[0, pl.ds(pl.multiple_of(r * PD, PD), PD)], rep_peer(k), "images"), 1)
    own_rows = s.at[0, pl.ds(pl.multiple_of(r * PD, PD), PD)]
    copy_here(images, own_rows, "own_image")

    for i in range(len(small)):
        wait_recv(f"in{i}")
    start_s[...] = jnp.zeros_like(start_s)
    masks = jnp.concatenate([msk[:, i, :] for i in range(d.n)], axis=1).astype(F32)
    labels = jnp.concatenate([lab[i : i + 1, :] for i in range(d.n)], axis=1).astype(F32)
    wanted = jnp.concatenate([tgt[i] for i in range(d.n)], axis=1)
    pools = jnp.concatenate([pidx[i : i + 1, :] for i in range(d.n)], axis=1).astype(F32)
    counted = jnp.sum(masks, axis=1, keepdims=True)
    lane = lax.broadcasted_iota(jnp.int32, (1, LANES), 1)
    start_s[0:1, :] = sum(jnp.where(lane == t, counted[t : t + 1, :], 0.0) for t in range(3))
    start_s[1:2, 0 : PW // R] = pools
    over(R, lambda k: send(start_s, start_r.at[r], rep_peer(k), "start"), 1)
    start_r[r] = start_s[...]
    ho_s[...] = jnp.zeros_like(ho_s)
    ho_s[0 : d.q, 0 : d.OC] = ho[...].astype(F32)
    over(F, lambda k: send(ho_s, ho_r.at[f], (r, (f + k) % F), "head_out"), 1)
    ho_r[f] = ho_s[...]
    def pack_head():
        wide = -(-rows // LANES) * LANES
        tall = jnp.concatenate([hw[...].astype(F32), jnp.zeros((LANES - d.HC, rows), F32)], axis=0)
        if wide > rows:
            tall = jnp.concatenate([tall, jnp.zeros((LANES, wide - rows), F32)], axis=1)
        tall = jnp.transpose(tall)
        if wide < 2 * half:
            tall = jnp.concatenate([tall, jnp.zeros((2 * half - wide, LANES), F32)], axis=0)
        hw_s[...] = (tall[0:half] + pltpu.roll(tall[half : 2 * half], d.HC, 1)).astype(hw_s.dtype)

    bits = W.bit_length() - 1

    def places(axis, shape):
        q = lax.broadcasted_iota(jnp.int32, shape, axis)
        image = jnp.zeros(shape, jnp.int32)
        for i in range(1, M // PIX):
            image = image + jnp.where(q >= i * PIX, 1, 0)
        q = q - image * PIX
        window = image * (PIX // 4) + (q >> (bits + 1)) * (W // 2) + ((q & (W - 1)) >> 1)
        position = 2 * ((q >> bits) & 1) + (q & 1)
        return window, position.astype(F32)

    def windows(rows_first):
        shape = (M, PW) if rows_first else (PW, M)
        window, position = places(0 if rows_first else 1, shape)
        other = lax.broadcasted_iota(jnp.int32, shape, 1 if rows_first else 0)
        return window == other, position

    def pixel_columns():
        feat[...] = jnp.zeros_like(feat)
        feat[0:1, 0:PD] = labels
        feat[1:4, 0:PD] = masks
        feat[4:8, 0:PD] = wanted
        columns_s[...] = jnp.transpose(feat[...])[0:PD, 0:LANES]

    def pool_matrices():
        feat[...] = jnp.zeros_like(feat)
        for i in range(R):
            feat[0:1, i * (PW // R) : (i + 1) * (PW // R)] = start_r[i, 1:2, 0 : PW // R]
        picked_row = feat[0:1, 0:PW]
        picked_col = jnp.transpose(feat[...])[0:PW, 0:1]
        inside, position = windows(True)
        u_sel[...] = jnp.where(inside & (position == picked_row), 1.0, 0.0).astype(BF16)
        inside, position = windows(False)
        ut_sel[...] = jnp.where(inside & (position == picked_col), 1.0, 0.0).astype(BF16)

    def image_rows(i):
        return pl.ds(pl.multiple_of(i * PIX, PIX), PIX)

    def per_image(count, body, init):
        return lax.fori_loop(0, count, body, init)

    def column_of(shape):
        return lax.broadcasted_iota(jnp.int32, shape, 0) & (W - 1)

    blank = jnp.zeros((W, CR), F32)

    def conv(src, count, l, out):
        height = count * PIX
        for kx in range(3):
            taps = [wf[l, (3 * ky + kx) * C : (3 * ky + kx + 1) * C, :].astype(BF16) for ky in range(3)]
            y[0:height, kx * 3 * CR : (kx + 1) * 3 * CR] = jnp.dot(
                src[...], jnp.concatenate(taps, axis=1), preferred_element_type=F32
            )

        def body(i, summed):
            at = image_rows(i)
            col = column_of((PIX, CR))
            parts = []
            for kx in range(3):
                up, mid, down = (y[at, (kx * 3 + ky) * CR : (kx * 3 + ky + 1) * CR] for ky in range(3))
                parts.append(
                    mid
                    + jnp.concatenate([blank, up[: PIX - W]], axis=0)
                    + jnp.concatenate([down[W:], blank], axis=0)
                )
            z = (
                parts[1]
                + jnp.where(col > 0, pltpu.roll(parts[0], 1, 0), 0.0)
                + jnp.where(col < W - 1, pltpu.roll(parts[2], PIX - 1, 0), 0.0)
            )
            out[at, :] = z
            return summed + jnp.sum(z, axis=0, keepdims=True)

        return per_image(count, body, jnp.zeros((1, CR), F32))

    def spread_taps(i, grad):
        at = image_rows(i)
        col = column_of((PIX, CR))
        moved = (
            jnp.where(col < W - 1, pltpu.roll(grad, PIX - 1, 0), 0.0),
            grad,
            jnp.where(col > 0, pltpu.roll(grad, 1, 0), 0.0),
        )
        low_blank = blank.astype(BF16)
        for kx in range(3):
            low = moved[kx].astype(BF16)
            nine = (
                jnp.concatenate([low[W:], low_blank], axis=0),
                low,
                jnp.concatenate([low_blank, low[: PIX - W]], axis=0),
            )
            for ky in range(3):
                d9[at, (kx * 3 + ky) * CR : (kx * 3 + ky + 1) * CR] = nine[ky]

    def data_grad(l, height, write):
        step = 2 * CR
        for half in range(C // step):
            taps = [
                wf[l, t * C + half * step : t * C + (half + 1) * step, :].astype(BF16)
                for t in (3 * ky + kx for kx in range(3) for ky in range(3))
            ]
            part = lax.dot_general(
                d9[0:height, :],
                jnp.concatenate(taps, axis=1),
                (((1,), (1,)), ((), ())),
                preferred_element_type=F32,
            )
            write(half, part)

    def lanes_of(owner):
        return pl.ds(pl.multiple_of(owner * CR, CR), CR)

    def gather_start(name, piece):
        send(piece(r, 0), piece(r, 0), at_one, f"{name}x0")
        send(piece(r, 1), piece(r, 1), at_two, f"{name}y1")
        send(piece(r, 1), piece(r, 1), at_one, f"{name}x1")
        send(piece(r, 0), piece(r, 0), at_two, f"{name}y0")

    def gather_forward(name, piece):
        wait_recv(f"{name}x0")
        send(piece(one, 0), piece(one, 0), at_two, f"{name}f0")
        wait_recv(f"{name}y1")
        send(piece(two, 1), piece(two, 1), at_one, f"{name}f1")

    def await_rest(name):
        for way in ("x1", "y0", "f0", "f1"):
            wait_recv(f"{name}{way}")

    def scatter_start(name, piece, land):
        send(piece(both, 0), land(0), at_one, f"{name}x0")
        send(piece(both, 1), land(2), at_two, f"{name}y1")
        send(piece(one, 0), land(1), at_one, f"{name}x1")
        send(piece(two, 1), land(3), at_two, f"{name}y0")

    def scatter_forward(name, piece, land):
        for way, ref, came, dst, to, group in (
            ("x0", piece(two, 0), land(0), land(4), at_two, "f0"),
            ("y1", piece(one, 1), land(2), land(5), at_one, "f1"),
        ):
            wait_recv(f"{name}{way}")
            ref[...] = (ref[...].astype(F32) + came[...].astype(F32)).astype(ref.dtype)
            send(ref, dst, to, f"{name}{group}")

    def ag_piece(j):
        return lambda owner, h: zg.at[j, pl.ds(h * (M // 2), M // 2), lanes_of(owner)]

    def rows_piece(l):
        return lambda owner, h: gather.at[l, pl.ds(h * half, half if h == 0 else rows - half), lanes_of(owner)]

    def rs_piece(j):
        return lambda owner, h: rs_s.at[j, owner, pl.ds(h * (M // 2), M // 2)]

    def rs_land(j):
        return lambda i: rs_l.at[j, i]

    def gi_piece(owner, h):
        return gi_s.at[owner, pl.ds(h * (PD // 2), PD // 2)]

    def gi_land(i):
        return gi_l.at[i]

    def sigmoid(v):
        return 0.5 * jnp.tanh(0.5 * v) + 0.5

    def g_block(l, owner):
        return gf.at[l, block(owner)] if l < 4 else hg.at[owner]

    def from_core(l):
        return cr.at[l] if l < 4 else hcr

    def from_z(l, i, h):
        return zr.at[l, i, cut_at(l, h)] if l < 4 else hzr.at[i, cut_at(l, h)]

    def g_piece(l, owner, h):
        first, size = cut(l, h)
        if l < 4:
            return gf.at[l, pl.ds(pl.multiple_of(owner * rows + first, d.row_tile), size)]
        return hg.at[owner, pl.ds(first, size)]

    def weight_grad(l, src, height):
        for kx in range(3):
            part = lax.dot_general(
                src[...],
                d9[0:height, kx * 3 * CR : (kx + 1) * 3 * CR],
                (((0,), (0,)), ((), ())),
                preferred_element_type=F32,
            )
            for ky in range(3):
                t = 3 * ky + kx
                gf[l % 4, t * C : (t + 1) * C, :] = part[:, ky * CR : (ky + 1) * CR].astype(gf.dtype)
        if l == 4:

            def pack(i, carry):
                at = i * rows
                low = gf[0, pl.ds(pl.multiple_of(at, d.row_tile), half), :].astype(F32)
                high = gf[0, pl.ds(pl.multiple_of(at + half, d.row_tile), rows - half), :].astype(F32)
                if rows < 2 * half:
                    high = jnp.concatenate([high, jnp.zeros((2 * half - rows, CR), F32)], axis=0)
                hg[i] = (low + pltpu.roll(high, d.HC, 1)).astype(hg.dtype)
                return carry

            lax.fori_loop(0, F, pack, 0)
        over(Z, lambda k: send(g_block(l, 2 * k + 1 - core), from_core(l).at[k], sib, f"core{l}"))

    def core_sum(l):
        wait_recv(f"core{l}")

        def step(k):
            ref = g_block(l, 2 * k + core)
            ref[...] = (ref[...].astype(F32) + from_core(l)[k].astype(F32)).astype(ref.dtype)

        over(Z, step)

    def z_push(l):
        for h in pieces:
            z_push_middle(l, h)
        for h in pieces:
            z_push_piece(l, h)

    def z_push_middle(l, h):
        if line:

            def to_middle():
                through, owner = jnp.where(zc == 0, 1, Z - 2), Z - 1 - zc
                send(g_piece(l, 2 * owner + core, h), from_z(l, through, h), (r, 2 * through + core), f"mid{l}.{h}")

            when(is_end, to_middle)
            g = GROUP[f"mid{l}.{h}"]
            arriving[f"mid{l}.{h}"] = lambda: when(
                jnp.logical_not(is_end), lambda: wait_for(from_z(l, 0, h), rsem.at[g])
            )
            leaving[f"mid{l}.{h}"] = lambda: when(is_end, lambda: wait_for(from_z(l, 0, h), ssem.at[g]))

    def z_push_piece(l, h):
        def push(k):
            to = (zc + k) % Z
            send(g_piece(l, 2 * to + core, h), from_z(l, zc, h), (r, 2 * to + core), f"z{l}.{h}")

        for k in range(1, Z) if Z <= 8 else ():
            if line and k == 2:
                when(is_end, lambda: push(2))
            else:
                direct(k, lambda: push(k))
        if Z > 8:
            over(Z, push, 1)
        arriving[f"z{l}.{h}"] = lambda: z_wait(l, h, rsem.at[GROUP[f"z{l}.{h}"]])
        leaving[f"z{l}.{h}"] = lambda: z_wait(l, h, ssem.at[GROUP[f"z{l}.{h}"]])

    def z_middle(l):
        for h in pieces:
            z_middle_piece(l, h)

    def z_middle_piece(l, h):
        if line:
            wait_recv(f"mid{l}.{h}")

            def hand_on():
                owner = (Z - 1) * (Z - 2 - zc)
                ref = g_piece(l, 2 * owner + core, h)
                ref[...] = (ref[...].astype(F32) + from_z(l, zc, h)[...].astype(F32)).astype(ref.dtype)
                send(ref, from_z(l, zc, h), (r, 2 * owner + core), f"z{l}.{h}")

            when(jnp.logical_not(is_end), hand_on)

    def z_wait(l, h, sem):
        first, size = cut(l, h)
        many = lambda count: (zr.at[l, pl.ds(0, count), cut_at(l, h)] if l < 4 else hzr.at[pl.ds(0, count), cut_at(l, h)])
        if line:
            when(is_end, lambda: wait_for(many(Z - 2), sem))
            when(jnp.logical_not(is_end), lambda: wait_for(many(Z - 1), sem))
        else:
            wait_for(many(Z - 1), sem)

    def z_sum(l):
        for h in pieces:
            z_sum_piece(l, h)
        if l < 4:
            gather_start(f"rows{l}", rows_piece(l))
        else:
            over(R, lambda k: send(hr.at[r], hr.at[r], rep_peer(k), "rows4"), 1)

    def z_sum_piece(l, h):
        wait_recv(f"z{l}.{h}")
        read = lambda i: from_z(l, i, h)[...].astype(F32)
        summed = g_piece(l, f, h)[...].astype(F32)
        if line:
            one_side = jnp.where(zc == 0, 1, jnp.where(zc == Z - 1, Z - 2, zc - 1))
            other_side = jnp.where(zc == 0, 2, jnp.where(zc == Z - 1, 1, zc + 1))
            opposite = jnp.where(zc == 1, Z - 1, 0)
            summed = summed + read(one_side) + read(other_side) + jnp.where(is_end, 0.0, read(opposite))
        else:
            summed = lax.fori_loop(1, Z, lambda k, so_far: so_far + read((zc + k) % Z), summed)
        summed = summed * (1.0 / root)
        if l < 4:
            gather[l, cut_at(l, h), my_lanes] = summed.astype(gather.dtype)
        else:
            hr[r, cut_at(l, h)] = summed.astype(hr.dtype)

    def rows_done(l):
        if l < 4:
            await_rest(f"rows{l}")
            copy_here(gather.at[l], gw[l], f"out{l}")
        else:
            wait_recv("rows4")
            summed = sum(hr[i].astype(F32) for i in range(R))
            wide = -(-half // LANES) * LANES
            if wide > half:
                summed = jnp.concatenate([summed, jnp.zeros((wide - half, LANES), F32)], axis=0)
            summed = jnp.transpose(summed)
            ghc[:, 0:half] = summed[0 : d.HC, 0:half]
            ghc[:, half:rows] = summed[d.HC : 2 * d.HC, 0 : rows - half]

    def exchange(e):
        over(F, lambda k: send(st_s.at[e], st_r.at[e, f], (r, (f + k) % F), f"stat{e}"), 1)
        st_r[e, f] = st_s[e]

    def exchanged(e):
        wait_recv(f"stat{e}")
        return st_r[e]

    st_s[...] = jnp.zeros_like(st_s)
    w_relay_rest(0)
    w_relay_near(0)
    w_far(0)
    w_push_rest(1, who=at_ends)
    wait_recv("images")
    wait_recv("own_image")
    wait_recv("start")

    rep_all = lambda src, dst, group: over(R, lambda k: send(src, dst, rep_peer(k), group), 1)
    images_here = M // PIX
    inverse_of, counts = [], None

    def widened(j, i, b):
        value = zg[j, image_rows(i), b * CR : (b + 1) * CR].astype(F32)
        return value, [nrm_r[j, b, k : k + 1, :] for k in range(4)]

    def slopes_of(j):
        def body(i, carry):
            for b in range(R):
                value, (a, o, inverse, off) = widened(j, i, b)
                shaped = value * a + o
                squashed = sigmoid(shaped)
                steep = squashed + shaped * squashed * (1.0 - squashed)
                slope[j, image_rows(i), b * CR : (b + 1) * CR] = steep.astype(BF16)
                slope_z[j, image_rows(i), b * CR : (b + 1) * CR] = (steep * (value * inverse + off)).astype(BF16)
            return carry

        per_image(images_here, body, 0)

    def rows_of(l):
        return gain[l : l + 1, my_lanes], shift[l : l + 1, my_lanes]

    def slope_here(l, at):
        g_row, b_row = rows_of(l)
        normed = zhat[l, at, :]
        shaped = normed * g_row + b_row
        squashed = sigmoid(shaped)
        return normed, squashed + shaped * squashed * (1.0 - squashed)

    def pool_slopes():
        def body(i, carry):
            at = image_rows(i)
            normed, steep = slope_here(1, at)
            y[at, 0:CR] = steep
            y[at, CR : 2 * CR] = steep * normed
            return carry

        per_image(images_here, body, 0)
        inside, unused = windows(False)
        averaged = jnp.dot(
            jnp.where(inside, 0.25, 0.0), y[:, 0 : 2 * CR], precision=EXACT, preferred_element_type=F32
        ).astype(BF16)
        for k in range(2):
            sp_own[k] = averaged[:, k * CR : (k + 1) * CR]
            sp_all[k, :, my_lanes] = averaged[:, k * CR : (k + 1) * CR]
        rep_all(sp_own, sp_all.at[:, :, my_lanes], "pool_slope")

    for l in range(4):
        w_finish(l)
        if l == 2:
            wait_recv("pool")
            s[2] = jnp.dot(u_sel[...], pool_all[...], preferred_element_type=F32).astype(BF16)
        first = conv(s.at[l], images_here, l, zb)
        mean_here = first * (1.0 / M)
        gathers = l in (0, 2)
        ahead = l != 1
        j = 2 if l == 3 else l // 2

        def squares(i, so_far):
            apart = zb[image_rows(i), :] - mean_here
            if gathers:
                zg[j, image_rows(i), my_lanes] = apart.astype(BF16)
            elif l == 3:
                a2a_s[i] = apart.astype(BF16)
            return so_far + jnp.sum(jnp.square(apart), axis=0, keepdims=True)

        squared = per_image(images_here, squares, jnp.zeros((1, CR), F32))
        if gathers:
            gather_start(f"ag{l}", ag_piece(j))
        elif l == 3:
            over(R, lambda k: send(a2a_s.at[(r + k) % R], z4.at[:, my_lanes], rep_peer(k), "a2a"), 1)
            z4[:, my_lanes] = a2a_s[r]
        st_s[l, 0:1, :] = first
        st_s[l, 1:2, :] = squared
        if l == 0:
            st_s[l, 2:3, :] = sum(start_r[i, 0:1, :] for i in range(R))
        exchange(l)
        if l == 0:
            w_push_rest(1, who=between)
            w_push_near(1)
            w_relay_rest(1)
        elif l < 3:
            w_push_rest(l + 1, pieces[1:])
            w_push_near(l + 1)
            w_relay_rest(l + 1, pieces[:1])
        else:
            w_push_near(4)
            w_relay_rest(4)
        if gathers:
            gather_forward(f"ag{l}", ag_piece(j))
        elif l == 1:
            pixel_columns()
        else:
            slopes_of(1)
        parts = exchanged(l)
        tot = jnp.sum(parts, axis=0)
        mean = tot[0:1] * (1.0 / total)
        apart = jnp.sum(jnp.square(parts * (1.0 / M) - mean[None]), axis=0)[0:1] * float(M)
        inverse = lax.rsqrt((tot[1:2] + apart) * (1.0 / total) + EPS)
        inverse_of.append(inverse)
        if l == 0:
            counts = tot[2:3]
        g_row, b_row = gain[l : l + 1, my_lanes], shift[l : l + 1, my_lanes]
        if ahead:
            off = (mean_here - mean) * inverse
            nrm_s[j, 0:1, :] = inverse * g_row
            nrm_s[j, 1:2, :] = off * g_row + b_row
            nrm_s[j, 2:3, :] = inverse
            nrm_s[j, 3:4, :] = off
            rep_all(nrm_s.at[j], nrm_r.at[j, r], f"norm{j}")
            nrm_r[j, r] = nrm_s[j]

        def activate(i, carry):
            at = image_rows(i)
            normed = (zb[at, :] - mean) * inverse
            zhat[l, at, :] = normed
            shaped = normed * g_row + b_row
            hidden = shaped * sigmoid(shaped)
            zb[at, :] = hidden
            return carry

        def keep_normed(i, carry):
            zhat[l, image_rows(i), :] = (zb[image_rows(i), :] - mean) * inverse
            return carry

        def activate_all(i, carry):
            for b in range(R):
                value, (a, o, unused, also) = widened(j, i, b)
                shaped = value * a + o
                s[l + 1, image_rows(i), b * CR : (b + 1) * CR] = (shaped * sigmoid(shaped)).astype(BF16)
            return carry

        per_image(images_here, keep_normed if ahead else activate, 0)
        if l == 1:
            inside, unused = windows(False)
            pooled = jnp.dot(
                jnp.where(inside, 0.25, 0.0), zb[...], precision=EXACT, preferred_element_type=F32
            )
            pool_own[...] = pooled.astype(BF16)
            pool_all[:, my_lanes] = pooled.astype(BF16)
            rep_all(pool_own, pool_all.at[:, my_lanes], "pool")
            w_relay_rest(2, pieces[1:])
            pool_slopes()
            slopes_of(0)
        elif l == 0:
            pool_matrices()
        elif l == 2:
            w_relay_rest(3, pieces[1:])
            pack_head()
        w_relay_near(l + 1)
        if l < 2:
            w_push_rest(l + 2, pieces[:1])
        elif l == 2:
            w_push_rest(4)
        w_far(l + 1)
        if gathers:
            wait_recv(f"norm{j}")
            await_rest(f"ag{l}")
            per_image(images_here, activate_all, 0)

    w_finish(4)
    low_lanes = lax.broadcasted_iota(jnp.int32, (half, LANES), 1) < d.HC

    def unpack(i, carry):
        both = hp[i].astype(F32)
        at = i * rows
        wf[4, pl.ds(pl.multiple_of(at, d.row_tile), half), :] = jnp.where(low_lanes, both, 0.0).astype(wf.dtype)
        high = jnp.where(low_lanes, pltpu.roll(both, d.HC, 1), 0.0).astype(wf.dtype)
        wf[4, pl.ds(pl.multiple_of(at + half, d.row_tile), rows - half), :] = high[0 : rows - half]
        return carry

    lax.fori_loop(0, F, unpack, 0)
    wait_recv("norm2")
    wait_recv("a2a")

    def activate_own(i, carry):
        at = image_rows(i)
        for b in range(R):
            lanes = slice(b * CR, (b + 1) * CR)
            value = z4[at, lanes].astype(F32)
            a, o, inverse, off = [nrm_r[2, b, k : k + 1, :] for k in range(4)]
            shaped = value * a + o
            squashed = sigmoid(shaped)
            s4[at, lanes] = (shaped * squashed).astype(BF16)
            steep = squashed + shaped * squashed * (1.0 - squashed)
            slope4[at, lanes] = steep.astype(BF16)
            slope_z4[at, lanes] = (steep * (value * inverse + off)).astype(BF16)
        return carry

    per_image(PD // PIX, activate_own, 0)
    wait_recv("head_out")
    conv(s4, PD // PIX, 4, zb)
    head_bias = jnp.concatenate([hb[...], jnp.zeros((1, CR - d.HC), F32)], axis=1)
    out_bias = jnp.concatenate([ob[...], jnp.zeros((1, CR - d.OC), F32)], axis=1)
    head_raw = zb[0:PD, :] + head_bias
    squashed = sigmoid(head_raw)
    head_act = head_raw * squashed
    project = jnp.concatenate([ho_r[i][0 : d.q] for i in range(F)] + [jnp.zeros((LANES - d.HC, LANES), F32)], axis=0)
    out = jnp.dot(head_act, project, precision=EXACT, preferred_element_type=F32) + out_bias
    lane = lax.broadcasted_iota(jnp.int32, (PD, LANES), 1)
    classes = d.OC - 4
    factor = total * jnp.concatenate([tw[...], jnp.zeros((1, LANES - 3), F32)], axis=1) / jnp.maximum(counts, 1.0)
    pixel = [columns_s[:, i : i + 1] for i in range(8)]
    is_class = lane < classes
    top = jnp.max(jnp.where(is_class, out, -jnp.inf), axis=1, keepdims=True)
    grown = jnp.where(is_class, jnp.exp(jnp.where(is_class, out - top, 0.0)), 0.0)
    likely = grown / jnp.sum(grown, axis=1, keepdims=True)
    onehot = jnp.where(lane.astype(F32) == pixel[0], 1.0, 0.0)
    grad_class = factor[:, 0:1] * pixel[1] * (likely - onehot)
    misfit = out - pixel[4]
    grad_depth = factor[:, 1:2] * pixel[2] * misfit / jnp.sqrt(misfit * misfit + 1.0)
    is_normal = (lane > classes) & (lane < d.OC)
    predicted = jnp.where(is_normal, out, 0.0)
    wanted = sum(jnp.where(lane == classes + 1 + i, pixel[5 + i], 0.0) for i in range(3))
    radius = jnp.sqrt(jnp.sum(predicted * predicted, axis=1, keepdims=True) + 1.0)
    aligned = jnp.sum(predicted * wanted, axis=1, keepdims=True)
    grad_normal = -(factor[:, 2:3] * pixel[3]) * (wanted / radius - aligned / (radius * radius * radius) * predicted)
    grad_out = jnp.where(
        is_class, grad_class, jnp.where(lane == classes, grad_depth, jnp.where(is_normal, grad_normal, 0.0))
    )
    grad_act = lax.dot_general(
        grad_out, project, (((1,), (1,)), ((), ())), precision=EXACT, preferred_element_type=F32
    )
    grad_head = (grad_act * (squashed + head_raw * squashed * (1.0 - squashed))).astype(BF16).astype(F32)
    zb[0:PD, :] = grad_head
    y[0:PD, 0:CR] = head_act
    y[0:PD, CR : 2 * CR] = grad_out

    def spread_head(i, carry):
        spread_taps(i, zb[image_rows(i), :])
        return carry

    per_image(PD // PIX, spread_head, 0)

    def put_sums(j, n, grad, steep, steep_z):
        sums_s[j, n, 0:1, :] = jnp.sum(grad * steep.astype(F32), axis=0, keepdims=True)
        sums_s[j, n, 1:2, :] = jnp.sum(grad * steep_z.astype(F32), axis=0, keepdims=True)

    def send_sums(j):
        over(R, lambda k: send(sums_s.at[j, (r + k) % R], sums_r.at[j, r], rep_peer(k), f"sums{j}"), 1)
        sums_r[j, r] = sums_s[j, r]

    def pass_sums(j, e):
        wait_recv(f"sums{j}")
        st_s[e, 0:2, :] = sum(sums_r[j, i, 0:2, :] for i in range(R))
        exchange(e)

    def write_dh3(part_at, part):
        for b in range(2):
            n = 2 * part_at + b
            grad = part[:, b * CR : (b + 1) * CR]
            cols = slice(n * CR, (n + 1) * CR)
            a2a_s[n] = grad.astype(BF16)
            put_sums(2, n, grad, slope4[:, cols], slope_z4[:, cols])

    wait_send("a2a")
    data_grad(4, PD, write_dh3)
    send_sums(2)
    over(R, lambda k: send(a2a_s.at[(r + k) % R], a2a_r.at[r], rep_peer(k), "dh3"), 1)
    a2a_r[r] = a2a_s[r]
    weight_grad(4, s4, PD)
    head_act, grad_out = y[0:PD, 0:CR], y[0:PD, CR : 2 * CR]
    pad = jnp.zeros((2 * LANES - PD, LANES), F32)
    act_t = jnp.transpose(jnp.concatenate([head_act, pad], axis=0))[:, 0:PD]
    rep_s[0 : d.HC, :] = jnp.dot(act_t, grad_out, precision=EXACT, preferred_element_type=F32)[0 : d.HC]
    rep_s[d.HC : d.HC + 8, :] = jnp.zeros((8, LANES), F32)
    rep_s[d.HC : d.HC + 1, :] = jnp.sum(zb[0:PD, :], axis=0, keepdims=True)
    rep_s[d.HC + 1 : d.HC + 2, :] = jnp.sum(grad_out, axis=0, keepdims=True)
    over(R, lambda k: send(rep_s, rep_r.at[r], rep_peer(k), "small_rep"), 1)
    rep_r[r] = rep_s[...]

    def head_small():
        wait_recv("small_rep")
        summed = sum(rep_r[i] for i in range(R))
        for i in range(F):
            all_s[i, 0 : d.q, :] = summed[i * d.q : (i + 1) * d.q]
            if d.q < 8:
                all_s[i, d.q : 8, :] = jnp.zeros((8 - d.q, LANES), F32)
            all_s[i, 8:16, :] = summed[d.HC : d.HC + 8]
        over(F, lambda k: send(all_s.at[(f + k) % F], all_r.at[f], (r, (f + k) % F), "small_all"), 1)
        all_r[f] = all_s[f]

    def through_norm(l, grad_of):
        tot = jnp.sum(exchanged(7 - l), axis=0)
        bias_sum, gain_sum = tot[0:1], tot[1:2]
        norm_s[l : l + 1, :] = gain_sum * (1.0 / root)
        norm_s[4 + l : 5 + l, :] = bias_sum * (1.0 / root)
        scale = inverse_of[l] * rows_of(l)[0]
        if l in (0, 2):
            await_rest(f"rs{l + 1}")
        elif l == 3:
            wait_recv("dh3")

        def body(i, carry):
            at = image_rows(i)
            normed, grad = grad_of(i, at)
            spread_taps(i, scale * (grad - bias_sum * (1.0 / total) - normed * (gain_sum * (1.0 / total))))
            return carry

        per_image(images_here, body, 0)

    def from_scatter(l):
        j = l // 2
        here = images_here // 2

        def grad_of(i, at):
            normed, steep = slope_here(l, at)
            h = i // here
            local = image_rows(i - h * here)
            grad = (
                rs_s[j, r, at, :].astype(F32)
                + rs_l[j, 1 + 2 * h, local, :].astype(F32)
                + rs_l[j, 4 + h, local, :].astype(F32)
            )
            return normed, grad * steep

        return grad_of

    def layer_down(l):
        j = (l - 1) // 2

        def write(part_at, part):
            for b in range(2):
                n = 2 * part_at + b
                grad = part[:, b * CR : (b + 1) * CR]
                rs_s[j, n] = grad.astype(BF16)
                cols = slice(n * CR, (n + 1) * CR)
                put_sums(j, n, grad, slope[j, :, cols], slope_z[j, :, cols])

        data_grad(l, M, write)
        send_sums(j)
        scatter_start(f"rs{l}", rs_piece(j), rs_land(j))
        z_middle_piece(l + 1, 0)
        weight_grad(l, s.at[l], M)
        pass_sums(j, 7 - (l - 1))
        scatter_forward(f"rs{l}", rs_piece(j), rs_land(j))
        for h in pieces[1:]:
            z_middle_piece(l + 1, h)

    def from_head(i, at):
        normed, steep = slope_here(3, at)
        return normed, a2a_r[i].astype(F32) * steep

    pass_sums(2, 4)
    core_sum(4)
    z_push(4)
    head_small()
    through_norm(3, from_head)
    layer_down(3)
    core_sum(3)
    z_push(3)
    z_sum(4)

    through_norm(2, from_scatter(2))

    def write_pooled(part_at, part):
        chosen = jnp.dot(ut_sel[...], part.astype(BF16), preferred_element_type=F32)
        for b in range(2):
            n = 2 * part_at + b
            grad = chosen[:, b * CR : (b + 1) * CR]
            cols = slice(n * CR, (n + 1) * CR)
            ps_s[n] = grad.astype(BF16)
            put_sums(3, n, grad, sp_all[0, :, cols], sp_all[1, :, cols])

    z_middle(3)
    wait_recv("pool_slope")
    data_grad(2, M, write_pooled)
    send_sums(3)
    over(R, lambda k: send(ps_s.at[(r + k) % R], ps_r.at[r], rep_peer(k), "rs2"), 1)
    ps_r[r] = ps_s[r]
    weight_grad(2, s.at[2], M)
    pass_sums(3, 6)
    core_sum(2)
    z_push(2)
    wait_recv("rs2")
    pooled = sum(ps_r[i].astype(F32) for i in range(R))
    inside, unused = windows(True)
    zb[...] = jnp.dot(jnp.where(inside, 0.25, 0.0), pooled, precision=EXACT, preferred_element_type=F32)

    def from_pool(i, at):
        normed, steep = slope_here(1, at)
        return normed, zb[at, :] * steep

    through_norm(1, from_pool)
    layer_down(1)
    z_sum(3)
    core_sum(1)
    z_push(1)
    gather_forward("rows3", rows_piece(3))
    z_sum(2)

    through_norm(0, from_scatter(0))
    def write_images(part_at, part):
        for i in range(R):
            gi_s[i, :, part_at * 2 * CR : (part_at + 1) * 2 * CR] = part[i * PD : (i + 1) * PD].astype(BF16)

    data_grad(0, M, write_images)
    scatter_start("rs0", gi_piece, gi_land)
    weight_grad(0, s.at[0], M)
    gather_forward("rows2", rows_piece(2))
    z_middle(1)
    core_sum(0)
    z_push(0)

    gnorm[:, my_lanes] = norm_s[...]
    rep_all(norm_s, gnorm.at[:, my_lanes], "norms")
    z_middle(0)
    scatter_forward("rs0", gi_piece, gi_land)
    z_sum(1)
    wait_recv("small_all")
    gsmall[...] = jnp.sum(all_r[...], axis=0) * (1.0 / root)
    rows_done(4)
    copy_here(ghc, small_out[0], "out_ghc")
    copy_here(gsmall, small_out[2], "out_gsmall")
    rows_done(3)
    gather_forward("rows1", rows_piece(1))
    rows_done(2)
    await_rest("rs0")
    for h in range(2):
        at = slice(h * (PD // 2), (h + 1) * (PD // 2))
        gi[at, :] = gi_s[r, at, :].astype(F32) + gi_l[1 + 2 * h].astype(F32) + gi_l[4 + h].astype(F32)
    copy_here(gi, gi_out, "out_gi")
    wait_recv("norms")
    copy_here(gnorm, small_out[1], "out_gnorm")
    last = rows_piece(0)
    if d.pieces == 2:
        z_sum_piece(0, 0)
        send(last(r, 0), last(r, 0), at_one, "rows0x0")
        send(last(r, 0), last(r, 0), at_two, "rows0y0")
        send(last(r, 0), last(r, 0), (both, f), "rows0f0")
        rows_done(1)
        z_sum_piece(0, 1)
        send(last(r, 1), last(r, 1), at_one, "rows0x1")
        send(last(r, 1), last(r, 1), at_two, "rows0y1")
        send(last(r, 1), last(r, 1), (both, f), "rows0f1")
        wait_recv("rows0x0")
        wait_recv("rows0y1")
    else:
        z_sum(0)
        rows_done(1)
        gather_forward("rows0", last)
    rows_done(0)

    drain()


def finish(gi, gw0, gw1, gw2, gw3, ghc, gnorm, gsmall, *outs):
    out_gi, out0, out1, out2, out3, out_hc, out_ho, out_gain, out_bias, out_hb, out_ob = outs
    out_gi[...] = gi[...]
    for src, dst in ((gw0, out0), (gw1, out1), (gw2, out2), (gw3, out3)):
        dst[...] = src[...].astype(F32)

    @pl.when(pl.program_id(0) == 0)
    def _():
        out_hc[...] = ghc[...]
        out_ho[...] = gsmall[0 : out_ho.shape[0], 0 : out_ho.shape[1]]
        out_gain[...] = gnorm[0:4, :]
        out_bias[...] = gnorm[4:8, :]
        out_hb[...] = gsmall[8:9, 0 : out_hb.shape[1]]
        out_ob[...] = gsmall[9:10, 0 : out_ob.shape[1]]


def per_device(
    R, F,
    images, enc_first, enc_second, dec_first, dec_second, head_conv, head_out, norm_gain, norm_bias, head_bias, out_bias,
    task_weights, pool_index, labels, task_masks, targets,
):
    n, height, breadth, channels = images.shape
    rows, hidden = head_conv.shape
    q, out_ch = head_out.shape
    d = types.SimpleNamespace(
        n=n, R=R, F=F, Z=F // 2, rows=rows, C=channels, CR=channels // R, W=breadth, PIX=height * breadth,
        PD=n * height * breadth, HC=hidden, OC=out_ch, q=q,
    )
    d.M = R * d.PD
    d.pieces = 2 if d.Z == 4 else 1
    d.PW = d.M // 4
    wire = BF16 if rows % 16 == 0 else F32
    d.row_tile = 16 if rows % 16 == 0 else 8
    d.half = -(-rows // (2 * d.row_tile)) * d.row_tile
    vm = pltpu.VMEM
    patch = 9 * channels
    smalls = (
        head_conv.T, head_out, norm_gain, norm_bias, head_bias.reshape(1, hidden), out_bias.reshape(1, out_ch),
        task_weights.reshape(1, 3), pool_index, labels, jnp.transpose(task_masks, (1, 0, 2)), targets,
    )
    smalls = (smalls[0].astype(wire),) + smalls[1:]
    scratch = [vm(value.shape, value.dtype) for value in smalls] + [
        vm((d.PD, d.C), F32),
        vm((hidden, rows), F32),
        vm((8, d.C), F32),
        vm((16, LANES), F32),
        vm((4, rows, d.C), wire),
        vm((d.PD, LANES), F32),
        vm((4, d.M, d.C), BF16),
        vm((d.PD, d.C), BF16),
        vm((5, patch, d.CR), wire),
        vm((d.M, 9 * d.CR), F32),
        vm((d.M, d.CR), F32),
        vm((4, d.M, d.CR), F32),
        vm((d.M, 9 * d.CR), BF16),
        vm((d.M, d.PW), BF16),
        vm((d.PW, d.M), BF16),
        vm((R, d.PD, d.CR), BF16),
        vm((R, d.PD, d.CR), BF16),
        vm((2, R, d.M, d.CR), BF16),
        vm((2, 6, d.M // 2, d.CR), BF16),
        vm((d.PW, d.CR), BF16),
        vm((d.PW, d.C), BF16),
        vm((R, d.PW, d.CR), BF16),
        vm((R, d.PW, d.CR), BF16),
        vm((R, d.PD, d.C), BF16),
        vm((6, d.PD // 2, d.C), BF16),
        vm((2, d.M, d.C), BF16),
        vm((2, d.M, d.C), BF16),
        vm((2, d.M, d.C), BF16),
        vm((3, 8, LANES), F32),
        vm((3, R, 8, LANES), F32),
        vm((4, R, 8, LANES), F32),
        vm((4, R, 8, LANES), F32),
        vm((d.PD, d.C), BF16),
        vm((d.PD, d.C), BF16),
        vm((d.PD, d.C), BF16),
        vm((2, d.PW, d.CR), BF16),
        vm((2, d.PW, d.C), BF16),
        vm((4, patch, d.CR), wire),
        vm((4, d.Z, rows, d.CR), wire),
        vm((4, d.Z, rows, d.CR), wire),
        vm((d.half, LANES), wire),
        vm((F, d.half, LANES), wire),
        vm((F, d.half, LANES), wire),
        vm((d.Z, d.half, LANES), wire),
        vm((d.Z, d.half, LANES), wire),
        vm((R, d.half, LANES), wire),
        vm((8, 8, LANES), F32),
        vm((8, F, 8, LANES), F32),
        vm((8, LANES), F32),
        vm((R, 8, LANES), F32),
        vm((8, LANES), F32),
        vm((F, 8, LANES), F32),
        vm((hidden + 8, LANES), F32),
        vm((R, hidden + 8, LANES), F32),
        vm((F, 16, LANES), F32),
        vm((F, 16, LANES), F32),
        vm((8, LANES), F32),
        vm((LANES, 2 * LANES), F32),
        pltpu.SemaphoreType.DMA((len(GROUPS),)),
        pltpu.SemaphoreType.DMA((len(GROUPS),)),
        pltpu.SemaphoreType.DMA((5 * d.pieces, d.Z)),
        pltpu.SemaphoreType.DMA((5 * d.pieces, d.Z)),
        pltpu.SemaphoreType.DMA((5 * d.pieces, d.Z)),
        pltpu.SemaphoreType.DMA((5 * d.pieces, d.Z)),
    ]
    there = pl.BlockSpec(memory_space=pl.ANY)
    shape = jax.ShapeDtypeStruct
    kept = pl.pallas_call(
        functools.partial(kernel, d),
        out_shape=[shape((d.PD, d.C), F32)]
        + [shape((rows, d.C), wire)] * 4
        + [shape((hidden, rows), F32), shape((8, d.C), F32), shape((16, LANES), F32)],
        in_specs=[there] * 16,
        out_specs=[there] * 8,
        scratch_shapes=scratch,
        compiler_params=pltpu.CompilerParams(collective_id=0, has_side_effects=True, vmem_limit_bytes=63 * 2**20),
    )(
        images.reshape(d.PD, channels),
        *(w.astype(wire) for w in (enc_first, enc_second, dec_first, dec_second)),
        *smalls,
    )
    steps = next(count for count in (2, 1) if rows % (count * d.row_tile) == 0 and d.PD % (count * 8) == 0)
    part = lambda height, width: pl.BlockSpec((height // steps, width), lambda i: (i, 0))
    all_of = lambda height, width: pl.BlockSpec((height, width), lambda i: (0, 0))
    rest = ((q, out_ch), (4, channels), (4, channels), (1, hidden), (1, out_ch))
    gi, gw0, gw1, gw2, gw3, ghc, gq, gain, bias, ghb, gob = pl.pallas_call(
        finish,
        grid=(steps,),
        out_shape=[shape((d.PD, channels), F32)]
        + [shape((rows, channels), F32)] * 4
        + [shape((hidden, rows), F32)]
        + [shape(size, F32) for size in rest],
        in_specs=[part(d.PD, channels)]
        + [part(rows, channels)] * 4
        + [all_of(hidden, rows), all_of(8, channels), all_of(16, LANES)],
        out_specs=[part(d.PD, channels)]
        + [part(rows, channels)] * 4
        + [all_of(hidden, rows)]
        + [all_of(*size) for size in rest],
    )(*kept)
    return (
        gi.reshape(images.shape), gw0, gw1, gw2, gw3, ghc.T, gq, gain, bias, ghb.reshape(hidden), gob.reshape(out_ch),
    )


def solution(mesh):
    split = ("rep", "fsdp")
    rows = P("fsdp", None)
    return jax.shard_map(
        functools.partial(per_device, mesh.shape["rep"], mesh.shape["fsdp"]),
        mesh=mesh,
        in_specs=(P(split, None, None, None),)
        + (rows,) * 6
        + (P(),) * 5
        + (P(split, None), P(split, None), P(split, None, None), P(split, None, None)),
        out_specs=(P(split, None, None, None),) + (rows,) * 6 + (P(),) * 4,
        check_vma=False,
    )
```

```python
import functools
import math
import types

import jax
import jax.numpy as jnp
from jax import lax
from jax.experimental import pallas as pl
from jax.experimental.pallas import tpu as pltpu
from jax.sharding import PartitionSpec as P

MESH = pl.DeviceIdType.MESH
F32, BF16 = jnp.float32, jnp.bfloat16
EPS = 1e-05
LANES = 128
EXACT = lax.Precision.HIGHEST

GROUPS = (
    ["images", "start", "head_out", "a2a", "pool", "dh3", "rs2", "norms", "small_rep", "small_all"]
    + [f"sums{i}" for i in range(4)]
    + ["pool_slope"]
    + [f"norm{i}" for i in range(3)]
    + [
        f"{name}{way}"
        for name in ("ag0", "ag2", "rs3", "rs1", "rs0", "rows0", "rows1", "rows2", "rows3")
        for way in ("x0", "y1", "r")
    ]
    + [f"stat{i}" for i in range(8)]
    + [f"core{i}" for i in range(5)]
    + [f"weights{i}" for i in range(5)]
    + [f"z{i}.{h}" for i in range(5) for h in range(2)]
    + [f"mid{i}.{h}" for i in range(5) for h in range(2)]
    + ["rows4"]
    + [f"own{i}" for i in range(5)]
    + [f"out{i}" for i in range(4)]
    + [f"in{i}" for i in range(11)]
    + ["own_image", "out_gi", "out_ghc", "out_gnorm", "out_gsmall"]
)
GROUP = {name: number for number, name in enumerate(GROUPS)}

CLASSES = [
    "images", "start", "head_out", "a2a", "pool", "dh3", "rs2", "norms", "small_rep", "small_all", "pool_slope",
    "rows4", "weights", "weights4", "core", "core4", "z", "z4", "ag", "rs", "rs0", "rows", "sums", "norm", "stat",
]
CLASS = {name: number for number, name in enumerate(CLASSES)}


def class_of(group):
    if group in CLASS:
        return CLASS[group]
    if group.startswith("rs0"):
        return CLASS["rs0"]
    name = group.rstrip("xyr0123456789.")
    if name in ("mid", "z"):
        name = "z"
        return CLASS["z4" if group[len(group.split(".")[0]) - 1] == "4" else "z"]
    return CLASS[name]


def kernel(d, *refs):
    it = iter(refs)
    take = lambda count: [next(it) for _ in range(count)]
    images, w0, w1, w2, w3, *small_in = take(16)
    gi_out, gw0, gw1, gw2, gw3, *small_out = take(8)
    small = hw, ho, gain, shift, hb, ob, tw, pidx, lab, msk, tgt = take(11)
    gi, ghc, gnorm, gsmall = take(4)
    gather, columns_s = take(2)
    (s, s4, wf, y, zb, zhat, d9, u_sel, ut_sel, a2a_s, a2a_r, rs_s, rs_l, pool_own, pool_all, ps_s, ps_r, gi_s, gi_l) = take(19)
    (zg, slope, slope_z, nrm_s, nrm_r, sums_s, sums_r, z4, slope4, slope_z4, sp_own, sp_all) = take(12)
    (gf, cr, zr, hw_s, hp, hg, hcr, hzr, hr, st_s, st_r, start_s, start_r, ho_s, ho_r, rep_s, rep_r, all_s, all_r, norm_s, feat) = take(21)
    ssem, rsem, wrz = take(3)
    w_in, gw = (w0, w1, w2, w3, hw_s), (gw0, gw1, gw2, gw3)
    R, F, Z, rows, half, C, CR, W, PIX, PD, M, PW = d.R, d.F, d.Z, d.rows, d.half, d.C, d.CR, d.W, d.PIX, d.PD, d.M, d.PW
    total = float(M * F)
    root = math.sqrt(total)

    r, f = lax.axis_index("rep"), lax.axis_index("fsdp")
    zc, core = f // 2, f % 2
    sib = (r, zc * 2 + (1 - core))
    rep_peer = lambda k: ((r + k) % R, f)
    one, two = r + 1 - 2 * (r % 2), (r + 2) % R
    both = (one + 2) % R
    at_one, at_two = (one, f), (two, f)
    z_peer = lambda k: (r, ((zc + k) % Z) * 2 + core)
    line = Z == 4
    is_end = (zc == 0) | (zc == Z - 1)
    is_far = lambda k: (zc + k) % Z - zc == Z - 1
    is_far_back = lambda k: zc - (zc + k) % Z == Z - 1
    ends_apart = lambda k: is_far(k) | is_far_back(k)
    my_lanes = pl.ds(pl.multiple_of(r * CR, CR), CR)

    def block(owner):
        return pl.ds(pl.multiple_of(owner * rows, d.row_tile), rows)

    arriving, leaving = {}, {}

    def first_of(ref, count):
        return lambda: ref.at[pl.ds(0, count)]

    volume = {
        "images": first_of(s.at[0], (R - 1) * PD),
        "own_image": first_of(s.at[0], PD),
        "start": first_of(start_r, R - 1),
        "head_out": first_of(ho_r, F - 1),
        "a2a": lambda: z4.at[:, pl.ds(0, (R - 1) * CR)],
        "pool_slope": lambda: sp_all.at[:, :, pl.ds(0, (R - 1) * CR)],
        "pool": lambda: pool_all.at[:, pl.ds(0, (R - 1) * CR)],
        "dh3": first_of(a2a_r, R - 1),
        "rs2": first_of(ps_r, R - 1),
        "norms": lambda: gnorm.at[:, pl.ds(0, (R - 1) * CR)],
        "small_rep": first_of(rep_r, R - 1),
        "small_all": first_of(all_r, F - 1),
        "rows4": first_of(hr, R - 1),
        "core4": lambda: hcr,
    }
    for j in range(2):
        for way in ("x0", "y1"):
            volume[f"ag{2 * j}{way}"] = lambda j=j: zg.at[j, pl.ds(0, M // 2), pl.ds(0, CR)]
            volume[f"rs{2 * j + 1}{way}"] = lambda j=j: rs_l.at[j, 0]
        volume[f"ag{2 * j}r"] = lambda j=j: zg.at[j, :, pl.ds(0, 2 * CR)]
        volume[f"rs{2 * j + 1}r"] = lambda j=j: rs_l.at[j, pl.ds(0, 4)]
    volume["rs0x0"] = volume["rs0y1"] = lambda: gi_l.at[0]
    volume["rs0r"] = lambda: gi_l.at[pl.ds(0, 4)]
    for l in range(4):
        volume[f"rows{l}x0"] = lambda l=l: gather.at[l, pl.ds(0, half), pl.ds(0, CR)]
        volume[f"rows{l}y1"] = lambda l=l: gather.at[l, pl.ds(half, rows - half), pl.ds(0, CR)]
        volume[f"rows{l}r"] = lambda l=l: gather.at[l, :, pl.ds(0, (3 if l == 0 and line else 2) * CR)]
    for j in range(4):
        volume[f"sums{j}"] = first_of(sums_r.at[j], R - 1)
    for j in range(3):
        volume[f"norm{j}"] = first_of(nrm_r.at[j], R - 1)
    for e in range(8):
        volume[f"stat{e}"] = first_of(st_r.at[e], F - 1)
    for l in range(4):
        volume[f"core{l}"] = lambda l=l: cr.at[l]

    def wait_for(ref, sem):
        pltpu.make_async_copy(ref, ref, sem).wait()

    def wait_recv(group):
        arriving.pop(group)()

    def wait_send(group):
        leaving.pop(CLASS[group])()

    def when_line(at_end, inside, otherwise):
        if line:
            when(is_end, at_end)
            when(jnp.logical_not(is_end), inside)
        else:
            otherwise()

    def departed(number):
        name = CLASSES[number]
        whole = {
            "core": lambda: cr,
            "core4": lambda: hcr,
            "z": lambda: zr.at[:, pl.ds(0, Z - 1)],
            "z4": lambda: hzr.at[pl.ds(0, Z - 1)],
            "ag": lambda: zg.at[:, :, pl.ds(0, 3 * CR)],
            "rs": lambda: rs_l,
            "rs0": lambda: gi_l,
            "rows": lambda: gather.at[:, :, pl.ds(0, 3 * CR)],
            "sums": lambda: sums_r.at[:, pl.ds(0, R - 1)],
            "norm": lambda: nrm_r.at[:, pl.ds(0, R - 1)],
            "stat": lambda: st_r.at[:, pl.ds(0, F - 1)],
        }
        sem = ssem.at[number]
        if name == "weights":
            many = lambda count: lambda: wait_for(wf.at[pl.ds(0, 4), pl.ds(0, count * rows)], sem)
            when_line(many(6), many(8), many(2 * Z - 1))
        elif name == "weights4":
            many = lambda count: lambda: wait_for(hp.at[pl.ds(0, count)], sem)
            when_line(many(6), many(8), many(2 * Z - 1))
        else:
            wait_for((whole[name] if name in whole else volume[name])(), sem)

    def copy_here(src, dst, group):
        g = GROUP[group]
        arriving[group] = lambda: wait_for(dst, rsem.at[g])
        pltpu.make_async_copy(src, dst, rsem.at[g]).start()

    def send(src, dst, to, group):
        g, out = GROUP[group], class_of(group)
        if group in volume:
            arriving[group] = lambda: wait_for(volume[group](), rsem.at[g])
        leaving[out] = lambda: departed(out)
        pltpu.make_async_remote_copy(
            src_ref=src, dst_ref=dst, send_sem=ssem.at[out], recv_sem=rsem.at[g], device_id=to, device_id_type=MESH
        ).start()

    def over(count, body, first=0):
        if count <= 8:
            for i in range(first, count):
                body(i)
            return

        def step(i, carry):
            body(i)
            return carry

        lax.fori_loop(first, count, step, 0)

    def when(condition, body):
        pl.when(condition)(body)

    def direct(k, body):
        if line and k in (1, Z - 1):
            when(jnp.logical_not(ends_apart(k)), body)
        else:
            body()

    def drain():
        for waits in (arriving, leaving):
            for wait in list(waits.values()):
                wait()

    for i, (src, dst) in enumerate(zip(small_in, small)):
        copy_here(src, dst, f"in{i}")

    barrier = pltpu.get_barrier_semaphore()
    over(R, lambda k: pl.semaphore_signal(barrier, inc=1, device_id=rep_peer(k), device_id_type=MESH), 1)
    over(F, lambda k: pl.semaphore_signal(barrier, inc=1, device_id=(r, (f + k) % F), device_id_type=MESH), 1)
    pl.semaphore_wait(barrier, R + F - 2)

    pieces = range(d.pieces)

    def cut(l, h):
        size = rows if l < 4 else half
        first = -(-size // (d.pieces * d.row_tile)) * d.row_tile
        return (0, first) if h == 0 else (first, size - first)

    def cut_at(l, h):
        first, size = cut(l, h)
        return pl.ds(first, size)

    near = sorted({1, Z - 1})
    beyond = list(range(2, Z - 1))

    def w_block(l, owner, h):
        first, size = cut(l, h)
        if l < 4:
            return wf.at[l, pl.ds(pl.multiple_of(owner * rows + first, d.row_tile), size)]
        return hp.at[owner, pl.ds(first, size)]

    def w_copy(l, h, src, owner, to, recv_sem):
        out = CLASS["weights" if l < 4 else "weights4"]
        leaving[out] = lambda: departed(out)
        return pltpu.make_async_remote_copy(
            src_ref=src, dst_ref=w_block(l, owner, h), send_sem=ssem.at[out], recv_sem=recv_sem, device_id=to,
            device_id_type=MESH,
        )

    def w_to_core(l, h, src, owner):
        w_copy(l, h, src, owner, sib, rsem.at[GROUP[f"weights{l}"]]).start()

    def w_src(l, h):
        return w_in[l].at[cut_at(l, h), my_lanes] if l < 4 else hw_s.at[cut_at(l, h)]

    def w_wait(l, h, sem):
        wait_for(w_block(l, f, h), sem)

    def w_send(l, h, k, who=lambda body: body()):
        u = l * d.pieces + h
        arriving["z", l, h, k] = lambda: direct(Z - k, lambda: w_wait(l, h, wrz.at[u, k]))
        start = lambda: w_copy(l, h, w_src(l, h), f, z_peer(k), wrz.at[u, k]).start()
        who(lambda: direct(k, start))

    def w_push_near(l):
        for h in pieces:
            for k in near:
                w_send(l, h, k)
            w_to_core(l, h, w_src(l, h), f)
        copy_here(w_in[l].at[:, my_lanes] if l < 4 else hw_s, wf.at[l, block(f)] if l < 4 else hp.at[f], f"own{l}")

    def w_push_rest(l, hs=pieces, who=lambda body: body()):
        for h in hs:
            for k in beyond:
                w_send(l, h, k, who)

    def at_ends(body):
        if line:
            when(is_end, body)
        else:
            body()

    def between(body):
        if line:
            when(jnp.logical_not(is_end), body)

    def w_arrived(l, h, k):
        u = l * d.pieces + h
        owner = ((zc + Z - k) % Z) * 2 + core
        w_wait(l, h, wrz.at[u, k])
        w_to_core(l, h, w_block(l, owner, h), owner)

    def w_relay_rest(l, hs=pieces):
        for h in hs:
            u = l * d.pieces + h
            for k in beyond:
                arriving.pop(("z", l, h, k))
                w_arrived(l, h, k)
            if line:

                def hand_on():
                    to = (Z - 1) * (zc - 1)
                    owner = (Z - 1 - to) * 2 + core
                    slot = jnp.where(zc == 1, 1, Z - 1)
                    w_copy(l, h, w_block(l, owner, h), owner, (r, to * 2 + core), wrz.at[u, slot]).start()

                when(jnp.logical_not(is_end), hand_on)

    def w_relay_near(l):
        for h in pieces:
            for k in near:
                arriving.pop(("z", l, h, k))
                direct(Z - k, lambda: w_arrived(l, h, k))

    def w_far(l):
        if line:
            for h in pieces:
                when(zc == 0, lambda: w_arrived(l, h, 1))
                when(zc == Z - 1, lambda: w_arrived(l, h, Z - 1))

    def w_finish(l):
        one = GROUP[f"weights{l}"]
        wait_for(wf.at[l, pl.ds(0, Z * rows)] if l < 4 else hp.at[pl.ds(0, Z)], rsem.at[one])
        wait_recv(f"own{l}")

    w_push_rest(0)
    w_push_near(0)
    over(R, lambda k: send(images, s.at[0, pl.ds(pl.multiple_of(r * PD, PD), PD)], rep_peer(k), "images"), 1)
    own_rows = s.at[0, pl.ds(pl.multiple_of(r * PD, PD), PD)]
    copy_here(images, own_rows, "own_image")

    for i in range(len(small)):
        wait_recv(f"in{i}")
    start_s[...] = jnp.zeros_like(start_s)
    masks = jnp.concatenate([msk[:, i, :] for i in range(d.n)], axis=1).astype(F32)
    labels = jnp.concatenate([lab[i : i + 1, :] for i in range(d.n)], axis=1).astype(F32)
    wanted = jnp.concatenate([tgt[i] for i in range(d.n)], axis=1)
    pools = jnp.concatenate([pidx[i : i + 1, :] for i in range(d.n)], axis=1).astype(F32)
    counted = jnp.sum(masks, axis=1, keepdims=True)
    lane = lax.broadcasted_iota(jnp.int32, (1, LANES), 1)
    start_s[0:1, :] = sum(jnp.where(lane == t, counted[t : t + 1, :], 0.0) for t in range(3))
    start_s[1:2, 0 : PW // R] = pools
    over(R, lambda k: send(start_s, start_r.at[r], rep_peer(k), "start"), 1)
    start_r[r] = start_s[...]
    ho_s[...] = jnp.zeros_like(ho_s)
    ho_s[0 : d.q, 0 : d.OC] = ho[...].astype(F32)
    over(F, lambda k: send(ho_s, ho_r.at[f], (r, (f + k) % F), "head_out"), 1)
    ho_r[f] = ho_s[...]
    def pack_head():
        wide = -(-rows // LANES) * LANES
        tall = jnp.concatenate([hw[...].astype(F32), jnp.zeros((LANES - d.HC, rows), F32)], axis=0)
        if wide > rows:
            tall = jnp.concatenate([tall, jnp.zeros((LANES, wide - rows), F32)], axis=1)
        tall = jnp.transpose(tall)
        if wide < 2 * half:
            tall = jnp.concatenate([tall, jnp.zeros((2 * half - wide, LANES), F32)], axis=0)
        hw_s[...] = (tall[0:half] + pltpu.roll(tall[half : 2 * half], d.HC, 1)).astype(hw_s.dtype)

    bits = W.bit_length() - 1

    def places(axis, shape):
        q = lax.broadcasted_iota(jnp.int32, shape, axis)
        image = jnp.zeros(shape, jnp.int32)
        for i in range(1, M // PIX):
            image = image + jnp.where(q >= i * PIX, 1, 0)
        q = q - image * PIX
        window = image * (PIX // 4) + (q >> (bits + 1)) * (W // 2) + ((q & (W - 1)) >> 1)
        position = 2 * ((q >> bits) & 1) + (q & 1)
        return window, position.astype(F32)

    def windows(rows_first):
        shape = (M, PW) if rows_first else (PW, M)
        window, position = places(0 if rows_first else 1, shape)
        other = lax.broadcasted_iota(jnp.int32, shape, 1 if rows_first else 0)
        return window == other, position

    def pixel_columns():
        feat[...] = jnp.zeros_like(feat)
        feat[0:1, 0:PD] = labels
        feat[1:4, 0:PD] = masks
        feat[4:8, 0:PD] = wanted
        columns_s[...] = jnp.transpose(feat[...])[0:PD, 0:LANES]

    def pool_matrices():
        feat[...] = jnp.zeros_like(feat)
        for i in range(R):
            feat[0:1, i * (PW // R) : (i + 1) * (PW // R)] = start_r[i, 1:2, 0 : PW // R]
        picked_row = feat[0:1, 0:PW]
        picked_col = jnp.transpose(feat[...])[0:PW, 0:1]
        inside, position = windows(True)
        u_sel[...] = jnp.where(inside & (position == picked_row), 1.0, 0.0).astype(BF16)
        inside, position = windows(False)
        ut_sel[...] = jnp.where(inside & (position == picked_col), 1.0, 0.0).astype(BF16)

    def image_rows(i):
        return pl.ds(pl.multiple_of(i * PIX, PIX), PIX)

    def per_image(count, body, init):
        return lax.fori_loop(0, count, body, init)

    def column_of(shape):
        return lax.broadcasted_iota(jnp.int32, shape, 0) & (W - 1)

    blank = jnp.zeros((W, CR), F32)

    def conv(src, count, l, out):
        height = count * PIX
        for kx in range(3):
            taps = [wf[l, (3 * ky + kx) * C : (3 * ky + kx + 1) * C, :].astype(BF16) for ky in range(3)]
            y[0:height, kx * 3 * CR : (kx + 1) * 3 * CR] = jnp.dot(
                src[...], jnp.concatenate(taps, axis=1), preferred_element_type=F32
            )

        def body(i, summed):
            at = image_rows(i)
            col = column_of((PIX, CR))
            parts = []
            for kx in range(3):
                up, mid, down = (y[at, (kx * 3 + ky) * CR : (kx * 3 + ky + 1) * CR] for ky in range(3))
                parts.append(
                    mid
                    + jnp.concatenate([blank, up[: PIX - W]], axis=0)
                    + jnp.concatenate([down[W:], blank], axis=0)
                )
            z = (
                parts[1]
                + jnp.where(col > 0, pltpu.roll(parts[0], 1, 0), 0.0)
                + jnp.where(col < W - 1, pltpu.roll(parts[2], PIX - 1, 0), 0.0)
            )
            out[at, :] = z
            return summed + jnp.sum(z, axis=0, keepdims=True)

        return per_image(count, body, jnp.zeros((1, CR), F32))

    def spread_taps(i, grad):
        at = image_rows(i)
        col = column_of((PIX, CR))
        moved = (
            jnp.where(col < W - 1, pltpu.roll(grad, PIX - 1, 0), 0.0),
            grad,
            jnp.where(col > 0, pltpu.roll(grad, 1, 0), 0.0),
        )
        low_blank = blank.astype(BF16)
        for kx in range(3):
            low = moved[kx].astype(BF16)
            nine = (
                jnp.concatenate([low[W:], low_blank], axis=0),
                low,
                jnp.concatenate([low_blank, low[: PIX - W]], axis=0),
            )
            for ky in range(3):
                d9[at, (kx * 3 + ky) * CR : (kx * 3 + ky + 1) * CR] = nine[ky]

    def data_grad(l, height, write):
        step = 2 * CR
        for half in range(C // step):
            taps = [
                wf[l, t * C + half * step : t * C + (half + 1) * step, :].astype(BF16)
                for t in (3 * ky + kx for kx in range(3) for ky in range(3))
            ]
            part = lax.dot_general(
                d9[0:height, :],
                jnp.concatenate(taps, axis=1),
                (((1,), (1,)), ((), ())),
                preferred_element_type=F32,
            )
            write(half, part)

    def lanes_of(owner):
        return pl.ds(pl.multiple_of(owner * CR, CR), CR)

    def gather_start(name, piece):
        send(piece(r, 0), piece(r, 0), at_one, f"{name}x0")
        send(piece(r, 1), piece(r, 1), at_two, f"{name}y1")
        send(piece(r, 1), piece(r, 1), at_one, f"{name}r")
        send(piece(r, 0), piece(r, 0), at_two, f"{name}r")

    def gather_forward(name, piece):
        wait_recv(f"{name}x0")
        send(piece(one, 0), piece(one, 0), at_two, f"{name}r")
        wait_recv(f"{name}y1")
        send(piece(two, 1), piece(two, 1), at_one, f"{name}r")

    def await_rest(name):
        wait_recv(f"{name}r")

    def scatter_start(name, piece, land):
        send(piece(both, 0), land(0), at_one, f"{name}x0")
        send(piece(both, 1), land(2), at_two, f"{name}y1")
        send(piece(one, 0), land(1), at_one, f"{name}r")
        send(piece(two, 1), land(3), at_two, f"{name}r")

    def scatter_forward(name, piece, land):
        for way, ref, came, dst, to in (
            ("x0", piece(two, 0), land(0), land(4), at_two),
            ("y1", piece(one, 1), land(2), land(5), at_one),
        ):
            wait_recv(f"{name}{way}")
            ref[...] = (ref[...].astype(F32) + came[...].astype(F32)).astype(ref.dtype)
            send(ref, dst, to, f"{name}r")

    def ag_piece(j):
        return lambda owner, h: zg.at[j, pl.ds(h * (M // 2), M // 2), lanes_of(owner)]

    def rows_piece(l):
        return lambda owner, h: gather.at[l, pl.ds(h * half, half if h == 0 else rows - half), lanes_of(owner)]

    def rs_piece(j):
        return lambda owner, h: rs_s.at[j, owner, pl.ds(h * (M // 2), M // 2)]

    def rs_land(j):
        return lambda i: rs_l.at[j, i]

    def gi_piece(owner, h):
        return gi_s.at[owner, pl.ds(h * (PD // 2), PD // 2)]

    def gi_land(i):
        return gi_l.at[i]

    def sigmoid(v):
        return 0.5 * jnp.tanh(0.5 * v) + 0.5

    def g_block(l, owner):
        return gf.at[l, block(owner)] if l < 4 else hg.at[owner]

    def from_core(l):
        return cr.at[l] if l < 4 else hcr

    def from_z(l, i, h):
        return zr.at[l, i, cut_at(l, h)] if l < 4 else hzr.at[i, cut_at(l, h)]

    def g_piece(l, owner, h):
        first, size = cut(l, h)
        if l < 4:
            return gf.at[l, pl.ds(pl.multiple_of(owner * rows + first, d.row_tile), size)]
        return hg.at[owner, pl.ds(first, size)]

    def weight_grad(l, src, height):
        for kx in range(3):
            part = lax.dot_general(
                src[...],
                d9[0:height, kx * 3 * CR : (kx + 1) * 3 * CR],
                (((0,), (0,)), ((), ())),
                preferred_element_type=F32,
            )
            for ky in range(3):
                t = 3 * ky + kx
                gf[l % 4, t * C : (t + 1) * C, :] = part[:, ky * CR : (ky + 1) * CR].astype(gf.dtype)
        if l == 4:

            def pack(i, carry):
                at = i * rows
                low = gf[0, pl.ds(pl.multiple_of(at, d.row_tile), half), :].astype(F32)
                high = gf[0, pl.ds(pl.multiple_of(at + half, d.row_tile), rows - half), :].astype(F32)
                if rows < 2 * half:
                    high = jnp.concatenate([high, jnp.zeros((2 * half - rows, CR), F32)], axis=0)
                hg[i] = (low + pltpu.roll(high, d.HC, 1)).astype(hg.dtype)
                return carry

            lax.fori_loop(0, F, pack, 0)
        over(Z, lambda k: send(g_block(l, 2 * k + 1 - core), from_core(l).at[k], sib, f"core{l}"))

    def core_sum(l):
        wait_recv(f"core{l}")

        def step(k):
            ref = g_block(l, 2 * k + core)
            ref[...] = (ref[...].astype(F32) + from_core(l)[k].astype(F32)).astype(ref.dtype)

        over(Z, step)

    def z_push(l):
        for h in pieces:
            z_push_middle(l, h)
        for h in pieces:
            z_push_piece(l, h)

    def z_push_middle(l, h):
        if line:

            def to_middle():
                through, owner = jnp.where(zc == 0, 1, Z - 2), Z - 1 - zc
                send(g_piece(l, 2 * owner + core, h), from_z(l, through, h), (r, 2 * through + core), f"mid{l}.{h}")

            when(is_end, to_middle)
            g = GROUP[f"mid{l}.{h}"]
            arriving[f"mid{l}.{h}"] = lambda: when(
                jnp.logical_not(is_end), lambda: wait_for(from_z(l, 0, h), rsem.at[g])
            )

    def z_push_piece(l, h):
        def push(k):
            to = (zc + k) % Z
            send(g_piece(l, 2 * to + core, h), from_z(l, zc, h), (r, 2 * to + core), f"z{l}.{h}")

        for k in range(1, Z) if Z <= 8 else ():
            if line and k == 2:
                when(is_end, lambda: push(2))
            else:
                direct(k, lambda: push(k))
        if Z > 8:
            over(Z, push, 1)
        arriving[f"z{l}.{h}"] = lambda: z_wait(l, h, rsem.at[GROUP[f"z{l}.{h}"]])

    def z_middle(l):
        for h in pieces:
            z_middle_piece(l, h)

    def z_middle_piece(l, h):
        if line:
            wait_recv(f"mid{l}.{h}")

            def hand_on():
                owner = (Z - 1) * (Z - 2 - zc)
                ref = g_piece(l, 2 * owner + core, h)
                ref[...] = (ref[...].astype(F32) + from_z(l, zc, h)[...].astype(F32)).astype(ref.dtype)
                send(ref, from_z(l, zc, h), (r, 2 * owner + core), f"z{l}.{h}")

            when(jnp.logical_not(is_end), hand_on)

    def z_wait(l, h, sem):
        first, size = cut(l, h)
        many = lambda count: (zr.at[l, pl.ds(0, count), cut_at(l, h)] if l < 4 else hzr.at[pl.ds(0, count), cut_at(l, h)])
        if line:
            when(is_end, lambda: wait_for(many(Z - 2), sem))
            when(jnp.logical_not(is_end), lambda: wait_for(many(Z - 1), sem))
        else:
            wait_for(many(Z - 1), sem)

    def z_sum(l):
        for h in pieces:
            z_sum_piece(l, h)
        if l < 4:
            gather_start(f"rows{l}", rows_piece(l))
        else:
            over(R, lambda k: send(hr.at[r], hr.at[r], rep_peer(k), "rows4"), 1)

    def z_sum_piece(l, h):
        wait_recv(f"z{l}.{h}")
        read = lambda i: from_z(l, i, h)[...].astype(F32)
        summed = g_piece(l, f, h)[...].astype(F32)
        if line:
            one_side = jnp.where(zc == 0, 1, jnp.where(zc == Z - 1, Z - 2, zc - 1))
            other_side = jnp.where(zc == 0, 2, jnp.where(zc == Z - 1, 1, zc + 1))
            opposite = jnp.where(zc == 1, Z - 1, 0)
            summed = summed + read(one_side) + read(other_side) + jnp.where(is_end, 0.0, read(opposite))
        else:
            summed = lax.fori_loop(1, Z, lambda k, so_far: so_far + read((zc + k) % Z), summed)
        summed = summed * (1.0 / root)
        if l < 4:
            gather[l, cut_at(l, h), my_lanes] = summed.astype(gather.dtype)
        else:
            hr[r, cut_at(l, h)] = summed.astype(hr.dtype)

    def rows_done(l):
        if l < 4:
            await_rest(f"rows{l}")
            copy_here(gather.at[l], gw[l], f"out{l}")
        else:
            wait_recv("rows4")
            summed = sum(hr[i].astype(F32) for i in range(R))
            wide = -(-half // LANES) * LANES
            if wide > half:
                summed = jnp.concatenate([summed, jnp.zeros((wide - half, LANES), F32)], axis=0)
            summed = jnp.transpose(summed)
            ghc[:, 0:half] = summed[0 : d.HC, 0:half]
            ghc[:, half:rows] = summed[d.HC : 2 * d.HC, 0 : rows - half]

    def exchange(e):
        over(F, lambda k: send(st_s.at[e], st_r.at[e, f], (r, (f + k) % F), f"stat{e}"), 1)
        st_r[e, f] = st_s[e]

    def exchanged(e):
        wait_recv(f"stat{e}")
        return st_r[e]

    st_s[...] = jnp.zeros_like(st_s)
    w_relay_rest(0)
    w_relay_near(0)
    w_far(0)
    w_push_rest(1, who=at_ends)
    wait_recv("images")
    wait_recv("own_image")
    wait_recv("start")

    rep_all = lambda src, dst, group: over(R, lambda k: send(src, dst, rep_peer(k), group), 1)
    images_here = M // PIX
    inverse_of, counts = [], None

    def widened(j, i, b):
        value = zg[j, image_rows(i), b * CR : (b + 1) * CR].astype(F32)
        return value, [nrm_r[j, b, k : k + 1, :] for k in range(4)]

    def slopes_of(j):
        def body(i, carry):
            for b in range(R):
                value, (a, o, inverse, off) = widened(j, i, b)
                shaped = value * a + o
                squashed = sigmoid(shaped)
                steep = squashed + shaped * squashed * (1.0 - squashed)
                slope[j, image_rows(i), b * CR : (b + 1) * CR] = steep.astype(BF16)
                slope_z[j, image_rows(i), b * CR : (b + 1) * CR] = (steep * (value * inverse + off)).astype(BF16)
            return carry

        per_image(images_here, body, 0)

    def rows_of(l):
        return gain[l : l + 1, my_lanes], shift[l : l + 1, my_lanes]

    def slope_here(l, at):
        g_row, b_row = rows_of(l)
        normed = zhat[l, at, :]
        shaped = normed * g_row + b_row
        squashed = sigmoid(shaped)
        return normed, squashed + shaped * squashed * (1.0 - squashed)

    def pool_slopes():
        def body(i, carry):
            at = image_rows(i)
            normed, steep = slope_here(1, at)
            y[at, 0:CR] = steep
            y[at, CR : 2 * CR] = steep * normed
            return carry

        per_image(images_here, body, 0)
        inside, unused = windows(False)
        averaged = jnp.dot(
            jnp.where(inside, 0.25, 0.0), y[:, 0 : 2 * CR], precision=EXACT, preferred_element_type=F32
        ).astype(BF16)
        for k in range(2):
            sp_own[k] = averaged[:, k * CR : (k + 1) * CR]
            sp_all[k, :, my_lanes] = averaged[:, k * CR : (k + 1) * CR]
        rep_all(sp_own, sp_all.at[:, :, my_lanes], "pool_slope")

    for l in range(4):
        w_finish(l)
        if l == 2:
            wait_recv("pool")
            s[2] = jnp.dot(u_sel[...], pool_all[...], preferred_element_type=F32).astype(BF16)
        first = conv(s.at[l], images_here, l, zb)
        mean_here = first * (1.0 / M)
        gathers = l in (0, 2)
        ahead = l != 1
        j = 2 if l == 3 else l // 2

        def squares(i, so_far):
            apart = zb[image_rows(i), :] - mean_here
            if gathers:
                zg[j, image_rows(i), my_lanes] = apart.astype(BF16)
            elif l == 3:
                a2a_s[i] = apart.astype(BF16)
            return so_far + jnp.sum(jnp.square(apart), axis=0, keepdims=True)

        squared = per_image(images_here, squares, jnp.zeros((1, CR), F32))
        if gathers:
            gather_start(f"ag{l}", ag_piece(j))
        elif l == 3:
            over(R, lambda k: send(a2a_s.at[(r + k) % R], z4.at[:, my_lanes], rep_peer(k), "a2a"), 1)
            z4[:, my_lanes] = a2a_s[r]
        st_s[l, 0:1, :] = first
        st_s[l, 1:2, :] = squared
        if l == 0:
            st_s[l, 2:3, :] = sum(start_r[i, 0:1, :] for i in range(R))
        exchange(l)
        if l == 0:
            w_push_rest(1, who=between)
            w_push_near(1)
            w_relay_rest(1)
        elif l < 3:
            w_push_rest(l + 1, pieces[1:])
            w_push_near(l + 1)
            w_relay_rest(l + 1, pieces[:1])
        else:
            w_push_near(4)
            w_relay_rest(4)
        if gathers:
            gather_forward(f"ag{l}", ag_piece(j))
        elif l == 1:
            pixel_columns()
        else:
            slopes_of(1)
        parts = exchanged(l)
        tot = jnp.sum(parts, axis=0)
        mean = tot[0:1] * (1.0 / total)
        apart = jnp.sum(jnp.square(parts * (1.0 / M) - mean[None]), axis=0)[0:1] * float(M)
        inverse = lax.rsqrt((tot[1:2] + apart) * (1.0 / total) + EPS)
        inverse_of.append(inverse)
        if l == 0:
            counts = tot[2:3]
        g_row, b_row = gain[l : l + 1, my_lanes], shift[l : l + 1, my_lanes]
        if ahead:
            off = (mean_here - mean) * inverse
            nrm_s[j, 0:1, :] = inverse * g_row
            nrm_s[j, 1:2, :] = off * g_row + b_row
            nrm_s[j, 2:3, :] = inverse
            nrm_s[j, 3:4, :] = off
            rep_all(nrm_s.at[j], nrm_r.at[j, r], f"norm{j}")
            nrm_r[j, r] = nrm_s[j]

        def activate(i, carry):
            at = image_rows(i)
            normed = (zb[at, :] - mean) * inverse
            zhat[l, at, :] = normed
            shaped = normed * g_row + b_row
            hidden = shaped * sigmoid(shaped)
            zb[at, :] = hidden
            return carry

        def keep_normed(i, carry):
            zhat[l, image_rows(i), :] = (zb[image_rows(i), :] - mean) * inverse
            return carry

        def activate_all(i, carry):
            for b in range(R):
                value, (a, o, unused, also) = widened(j, i, b)
                shaped = value * a + o
                s[l + 1, image_rows(i), b * CR : (b + 1) * CR] = (shaped * sigmoid(shaped)).astype(BF16)
            return carry

        per_image(images_here, keep_normed if ahead else activate, 0)
        if l == 1:
            inside, unused = windows(False)
            pooled = jnp.dot(
                jnp.where(inside, 0.25, 0.0), zb[...], precision=EXACT, preferred_element_type=F32
            )
            pool_own[...] = pooled.astype(BF16)
            pool_all[:, my_lanes] = pooled.astype(BF16)
            rep_all(pool_own, pool_all.at[:, my_lanes], "pool")
            w_relay_rest(2, pieces[1:])
            pool_slopes()
            slopes_of(0)
        elif l == 0:
            pool_matrices()
        elif l == 2:
            w_relay_rest(3, pieces[1:])
            pack_head()
        w_relay_near(l + 1)
        if l < 2:
            w_push_rest(l + 2, pieces[:1])
        elif l == 2:
            w_push_rest(4)
        w_far(l + 1)
        if gathers:
            wait_recv(f"norm{j}")
            await_rest(f"ag{l}")
            per_image(images_here, activate_all, 0)

    w_finish(4)
    low_lanes = lax.broadcasted_iota(jnp.int32, (half, LANES), 1) < d.HC

    def unpack(i, carry):
        both = hp[i].astype(F32)
        at = i * rows
        wf[4, pl.ds(pl.multiple_of(at, d.row_tile), half), :] = jnp.where(low_lanes, both, 0.0).astype(wf.dtype)
        high = jnp.where(low_lanes, pltpu.roll(both, d.HC, 1), 0.0).astype(wf.dtype)
        wf[4, pl.ds(pl.multiple_of(at + half, d.row_tile), rows - half), :] = high[0 : rows - half]
        return carry

    lax.fori_loop(0, F, unpack, 0)
    wait_recv("norm2")
    wait_recv("a2a")

    def activate_own(i, carry):
        at = image_rows(i)
        for b in range(R):
            lanes = slice(b * CR, (b + 1) * CR)
            value = z4[at, lanes].astype(F32)
            a, o, inverse, off = [nrm_r[2, b, k : k + 1, :] for k in range(4)]
            shaped = value * a + o
            squashed = sigmoid(shaped)
            s4[at, lanes] = (shaped * squashed).astype(BF16)
            steep = squashed + shaped * squashed * (1.0 - squashed)
            slope4[at, lanes] = steep.astype(BF16)
            slope_z4[at, lanes] = (steep * (value * inverse + off)).astype(BF16)
        return carry

    per_image(PD // PIX, activate_own, 0)
    wait_recv("head_out")
    conv(s4, PD // PIX, 4, zb)
    head_bias = jnp.concatenate([hb[...], jnp.zeros((1, CR - d.HC), F32)], axis=1)
    out_bias = jnp.concatenate([ob[...], jnp.zeros((1, CR - d.OC), F32)], axis=1)
    head_raw = zb[0:PD, :] + head_bias
    squashed = sigmoid(head_raw)
    head_act = head_raw * squashed
    project = jnp.concatenate([ho_r[i][0 : d.q] for i in range(F)] + [jnp.zeros((LANES - d.HC, LANES), F32)], axis=0)
    out = jnp.dot(head_act, project, precision=EXACT, preferred_element_type=F32) + out_bias
    lane = lax.broadcasted_iota(jnp.int32, (PD, LANES), 1)
    classes = d.OC - 4
    factor = total * jnp.concatenate([tw[...], jnp.zeros((1, LANES - 3), F32)], axis=1) / jnp.maximum(counts, 1.0)
    pixel = [columns_s[:, i : i + 1] for i in range(8)]
    is_class = lane < classes
    top = jnp.max(jnp.where(is_class, out, -jnp.inf), axis=1, keepdims=True)
    grown = jnp.where(is_class, jnp.exp(jnp.where(is_class, out - top, 0.0)), 0.0)
    likely = grown / jnp.sum(grown, axis=1, keepdims=True)
    onehot = jnp.where(lane.astype(F32) == pixel[0], 1.0, 0.0)
    grad_class = factor[:, 0:1] * pixel[1] * (likely - onehot)
    misfit = out - pixel[4]
    grad_depth = factor[:, 1:2] * pixel[2] * misfit / jnp.sqrt(misfit * misfit + 1.0)
    is_normal = (lane > classes) & (lane < d.OC)
    predicted = jnp.where(is_normal, out, 0.0)
    wanted = sum(jnp.where(lane == classes + 1 + i, pixel[5 + i], 0.0) for i in range(3))
    radius = jnp.sqrt(jnp.sum(predicted * predicted, axis=1, keepdims=True) + 1.0)
    aligned = jnp.sum(predicted * wanted, axis=1, keepdims=True)
    grad_normal = -(factor[:, 2:3] * pixel[3]) * (wanted / radius - aligned / (radius * radius * radius) * predicted)
    grad_out = jnp.where(
        is_class, grad_class, jnp.where(lane == classes, grad_depth, jnp.where(is_normal, grad_normal, 0.0))
    )
    grad_act = lax.dot_general(
        grad_out, project, (((1,), (1,)), ((), ())), precision=EXACT, preferred_element_type=F32
    )
    grad_head = (grad_act * (squashed + head_raw * squashed * (1.0 - squashed))).astype(BF16).astype(F32)
    zb[0:PD, :] = grad_head
    y[0:PD, 0:CR] = head_act
    y[0:PD, CR : 2 * CR] = grad_out

    def spread_head(i, carry):
        spread_taps(i, zb[image_rows(i), :])
        return carry

    per_image(PD // PIX, spread_head, 0)

    def put_sums(j, n, grad, steep, steep_z):
        sums_s[j, n, 0:1, :] = jnp.sum(grad * steep.astype(F32), axis=0, keepdims=True)
        sums_s[j, n, 1:2, :] = jnp.sum(grad * steep_z.astype(F32), axis=0, keepdims=True)

    def send_sums(j):
        over(R, lambda k: send(sums_s.at[j, (r + k) % R], sums_r.at[j, r], rep_peer(k), f"sums{j}"), 1)
        sums_r[j, r] = sums_s[j, r]

    def pass_sums(j, e):
        wait_recv(f"sums{j}")
        st_s[e, 0:2, :] = sum(sums_r[j, i, 0:2, :] for i in range(R))
        exchange(e)

    def write_dh3(part_at, part):
        for b in range(2):
            n = 2 * part_at + b
            grad = part[:, b * CR : (b + 1) * CR]
            cols = slice(n * CR, (n + 1) * CR)
            a2a_s[n] = grad.astype(BF16)
            put_sums(2, n, grad, slope4[:, cols], slope_z4[:, cols])

    wait_send("a2a")
    data_grad(4, PD, write_dh3)
    send_sums(2)
    over(R, lambda k: send(a2a_s.at[(r + k) % R], a2a_r.at[r], rep_peer(k), "dh3"), 1)
    a2a_r[r] = a2a_s[r]
    weight_grad(4, s4, PD)
    head_act, grad_out = y[0:PD, 0:CR], y[0:PD, CR : 2 * CR]
    pad = jnp.zeros((2 * LANES - PD, LANES), F32)
    act_t = jnp.transpose(jnp.concatenate([head_act, pad], axis=0))[:, 0:PD]
    rep_s[0 : d.HC, :] = jnp.dot(act_t, grad_out, precision=EXACT, preferred_element_type=F32)[0 : d.HC]
    rep_s[d.HC : d.HC + 8, :] = jnp.zeros((8, LANES), F32)
    rep_s[d.HC : d.HC + 1, :] = jnp.sum(zb[0:PD, :], axis=0, keepdims=True)
    rep_s[d.HC + 1 : d.HC + 2, :] = jnp.sum(grad_out, axis=0, keepdims=True)
    over(R, lambda k: send(rep_s, rep_r.at[r], rep_peer(k), "small_rep"), 1)
    rep_r[r] = rep_s[...]

    def head_small():
        wait_recv("small_rep")
        summed = sum(rep_r[i] for i in range(R))
        for i in range(F):
            all_s[i, 0 : d.q, :] = summed[i * d.q : (i + 1) * d.q]
            if d.q < 8:
                all_s[i, d.q : 8, :] = jnp.zeros((8 - d.q, LANES), F32)
            all_s[i, 8:16, :] = summed[d.HC : d.HC + 8]
        over(F, lambda k: send(all_s.at[(f + k) % F], all_r.at[f], (r, (f + k) % F), "small_all"), 1)
        all_r[f] = all_s[f]

    def through_norm(l, grad_of):
        tot = jnp.sum(exchanged(7 - l), axis=0)
        bias_sum, gain_sum = tot[0:1], tot[1:2]
        norm_s[l : l + 1, :] = gain_sum * (1.0 / root)
        norm_s[4 + l : 5 + l, :] = bias_sum * (1.0 / root)
        scale = inverse_of[l] * rows_of(l)[0]
        if l in (0, 2):
            await_rest(f"rs{l + 1}")
        elif l == 3:
            wait_recv("dh3")

        def body(i, carry):
            at = image_rows(i)
            normed, grad = grad_of(i, at)
            spread_taps(i, scale * (grad - bias_sum * (1.0 / total) - normed * (gain_sum * (1.0 / total))))
            return carry

        per_image(images_here, body, 0)

    def from_scatter(l):
        j = l // 2
        here = images_here // 2

        def grad_of(i, at):
            normed, steep = slope_here(l, at)
            h = i // here
            local = image_rows(i - h * here)
            grad = (
                rs_s[j, r, at, :].astype(F32)
                + rs_l[j, 1 + 2 * h, local, :].astype(F32)
                + rs_l[j, 4 + h, local, :].astype(F32)
            )
            return normed, grad * steep

        return grad_of

    def layer_down(l):
        j = (l - 1) // 2

        def write(part_at, part):
            for b in range(2):
                n = 2 * part_at + b
                grad = part[:, b * CR : (b + 1) * CR]
                rs_s[j, n] = grad.astype(BF16)
                cols = slice(n * CR, (n + 1) * CR)
                put_sums(j, n, grad, slope[j, :, cols], slope_z[j, :, cols])

        data_grad(l, M, write)
        send_sums(j)
        scatter_start(f"rs{l}", rs_piece(j), rs_land(j))
        z_middle_piece(l + 1, 0)
        weight_grad(l, s.at[l], M)
        pass_sums(j, 7 - (l - 1))
        scatter_forward(f"rs{l}", rs_piece(j), rs_land(j))
        for h in pieces[1:]:
            z_middle_piece(l + 1, h)

    def from_head(i, at):
        normed, steep = slope_here(3, at)
        return normed, a2a_r[i].astype(F32) * steep

    pass_sums(2, 4)
    core_sum(4)
    z_push(4)
    head_small()
    through_norm(3, from_head)
    layer_down(3)
    core_sum(3)
    z_push(3)
    z_sum(4)

    through_norm(2, from_scatter(2))

    def write_pooled(part_at, part):
        chosen = jnp.dot(ut_sel[...], part.astype(BF16), preferred_element_type=F32)
        for b in range(2):
            n = 2 * part_at + b
            grad = chosen[:, b * CR : (b + 1) * CR]
            cols = slice(n * CR, (n + 1) * CR)
            ps_s[n] = grad.astype(BF16)
            put_sums(3, n, grad, sp_all[0, :, cols], sp_all[1, :, cols])

    z_middle(3)
    wait_recv("pool_slope")
    data_grad(2, M, write_pooled)
    send_sums(3)
    over(R, lambda k: send(ps_s.at[(r + k) % R], ps_r.at[r], rep_peer(k), "rs2"), 1)
    ps_r[r] = ps_s[r]
    weight_grad(2, s.at[2], M)
    pass_sums(3, 6)
    core_sum(2)
    z_push(2)
    wait_recv("rs2")
    pooled = sum(ps_r[i].astype(F32) for i in range(R))
    inside, unused = windows(True)
    zb[...] = jnp.dot(jnp.where(inside, 0.25, 0.0), pooled, precision=EXACT, preferred_element_type=F32)

    def from_pool(i, at):
        normed, steep = slope_here(1, at)
        return normed, zb[at, :] * steep

    through_norm(1, from_pool)
    layer_down(1)
    z_sum(3)
    core_sum(1)
    z_push(1)
    gather_forward("rows3", rows_piece(3))
    z_sum(2)

    through_norm(0, from_scatter(0))
    def write_images(part_at, part):
        for i in range(R):
            gi_s[i, :, part_at * 2 * CR : (part_at + 1) * 2 * CR] = part[i * PD : (i + 1) * PD].astype(BF16)

    data_grad(0, M, write_images)
    scatter_start("rs0", gi_piece, gi_land)
    weight_grad(0, s.at[0], M)
    gather_forward("rows2", rows_piece(2))
    z_middle(1)
    core_sum(0)
    z_push(0)

    gnorm[:, my_lanes] = norm_s[...]
    rep_all(norm_s, gnorm.at[:, my_lanes], "norms")
    z_middle(0)
    scatter_forward("rs0", gi_piece, gi_land)
    z_sum(1)
    wait_recv("small_all")
    gsmall[...] = jnp.sum(all_r[...], axis=0) * (1.0 / root)
    rows_done(4)
    copy_here(ghc, small_out[0], "out_ghc")
    copy_here(gsmall, small_out[2], "out_gsmall")
    rows_done(3)
    gather_forward("rows1", rows_piece(1))
    rows_done(2)
    await_rest("rs0")
    for h in range(2):
        at = slice(h * (PD // 2), (h + 1) * (PD // 2))
        gi[at, :] = gi_s[r, at, :].astype(F32) + gi_l[1 + 2 * h].astype(F32) + gi_l[4 + h].astype(F32)
    copy_here(gi, gi_out, "out_gi")
    wait_recv("norms")
    copy_here(gnorm, small_out[1], "out_gnorm")
    last = rows_piece(0)
    if d.pieces == 2:
        z_sum_piece(0, 0)
        send(last(r, 0), last(r, 0), at_one, "rows0r")
        send(last(r, 0), last(r, 0), at_two, "rows0r")
        send(last(r, 0), last(r, 0), (both, f), "rows0r")
        rows_done(1)
        z_sum_piece(0, 1)
        send(last(r, 1), last(r, 1), at_one, "rows0r")
        send(last(r, 1), last(r, 1), at_two, "rows0r")
        send(last(r, 1), last(r, 1), (both, f), "rows0r")
    else:
        z_sum(0)
        rows_done(1)
        gather_forward("rows0", last)
    rows_done(0)

    drain()


def finish(gi, gw0, gw1, gw2, gw3, ghc, gnorm, gsmall, *outs):
    out_gi, out0, out1, out2, out3, out_hc, out_ho, out_gain, out_bias, out_hb, out_ob = outs
    out_gi[...] = gi[...]
    for src, dst in ((gw0, out0), (gw1, out1), (gw2, out2), (gw3, out3)):
        dst[...] = src[...].astype(F32)

    @pl.when(pl.program_id(0) == 0)
    def _():
        out_hc[...] = ghc[...]
        out_ho[...] = gsmall[0 : out_ho.shape[0], 0 : out_ho.shape[1]]
        out_gain[...] = gnorm[0:4, :]
        out_bias[...] = gnorm[4:8, :]
        out_hb[...] = gsmall[8:9, 0 : out_hb.shape[1]]
        out_ob[...] = gsmall[9:10, 0 : out_ob.shape[1]]


def per_device(
    R, F,
    images, enc_first, enc_second, dec_first, dec_second, head_conv, head_out, norm_gain, norm_bias, head_bias, out_bias,
    task_weights, pool_index, labels, task_masks, targets,
):
    n, height, breadth, channels = images.shape
    rows, hidden = head_conv.shape
    q, out_ch = head_out.shape
    d = types.SimpleNamespace(
        n=n, R=R, F=F, Z=F // 2, rows=rows, C=channels, CR=channels // R, W=breadth, PIX=height * breadth,
        PD=n * height * breadth, HC=hidden, OC=out_ch, q=q,
    )
    d.M = R * d.PD
    d.pieces = 2 if d.Z == 4 else 1
    d.PW = d.M // 4
    wire = BF16 if rows % 16 == 0 else F32
    d.row_tile = 16 if rows % 16 == 0 else 8
    d.half = -(-rows // (2 * d.row_tile)) * d.row_tile
    vm = pltpu.VMEM
    patch = 9 * channels
    smalls = (
        head_conv.T, head_out, norm_gain, norm_bias, head_bias.reshape(1, hidden), out_bias.reshape(1, out_ch),
        task_weights.reshape(1, 3), pool_index, labels, jnp.transpose(task_masks, (1, 0, 2)), targets,
    )
    smalls = (smalls[0].astype(wire),) + smalls[1:]
    scratch = [vm(value.shape, value.dtype) for value in smalls] + [
        vm((d.PD, d.C), F32),
        vm((hidden, rows), F32),
        vm((8, d.C), F32),
        vm((16, LANES), F32),
        vm((4, rows, d.C), wire),
        vm((d.PD, LANES), F32),
        vm((4, d.M, d.C), BF16),
        vm((d.PD, d.C), BF16),
        vm((5, patch, d.CR), wire),
        vm((d.M, 9 * d.CR), F32),
        vm((d.M, d.CR), F32),
        vm((4, d.M, d.CR), F32),
        vm((d.M, 9 * d.CR), BF16),
        vm((d.M, d.PW), BF16),
        vm((d.PW, d.M), BF16),
        vm((R, d.PD, d.CR), BF16),
        vm((R, d.PD, d.CR), BF16),
        vm((2, R, d.M, d.CR), BF16),
        vm((2, 6, d.M // 2, d.CR), BF16),
        vm((d.PW, d.CR), BF16),
        vm((d.PW, d.C), BF16),
        vm((R, d.PW, d.CR), BF16),
        vm((R, d.PW, d.CR), BF16),
        vm((R, d.PD, d.C), BF16),
        vm((6, d.PD // 2, d.C), BF16),
        vm((2, d.M, d.C), BF16),
        vm((2, d.M, d.C), BF16),
        vm((2, d.M, d.C), BF16),
        vm((3, 8, LANES), F32),
        vm((3, R, 8, LANES), F32),
        vm((4, R, 8, LANES), F32),
        vm((4, R, 8, LANES), F32),
        vm((d.PD, d.C), BF16),
        vm((d.PD, d.C), BF16),
        vm((d.PD, d.C), BF16),
        vm((2, d.PW, d.CR), BF16),
        vm((2, d.PW, d.C), BF16),
        vm((4, patch, d.CR), wire),
        vm((4, d.Z, rows, d.CR), wire),
        vm((4, d.Z, rows, d.CR), wire),
        vm((d.half, LANES), wire),
        vm((F, d.half, LANES), wire),
        vm((F, d.half, LANES), wire),
        vm((d.Z, d.half, LANES), wire),
        vm((d.Z, d.half, LANES), wire),
        vm((R, d.half, LANES), wire),
        vm((8, 8, LANES), F32),
        vm((8, F, 8, LANES), F32),
        vm((8, LANES), F32),
        vm((R, 8, LANES), F32),
        vm((8, LANES), F32),
        vm((F, 8, LANES), F32),
        vm((hidden + 8, LANES), F32),
        vm((R, hidden + 8, LANES), F32),
        vm((F, 16, LANES), F32),
        vm((F, 16, LANES), F32),
        vm((8, LANES), F32),
        vm((LANES, 2 * LANES), F32),
        pltpu.SemaphoreType.DMA((len(CLASSES),)),
        pltpu.SemaphoreType.DMA((len(GROUPS),)),
        pltpu.SemaphoreType.DMA((5 * d.pieces, d.Z)),
    ]
    there = pl.BlockSpec(memory_space=pl.ANY)
    shape = jax.ShapeDtypeStruct
    kept = pl.pallas_call(
        functools.partial(kernel, d),
        out_shape=[shape((d.PD, d.C), F32)]
        + [shape((rows, d.C), wire)] * 4
        + [shape((hidden, rows), F32), shape((8, d.C), F32), shape((16, LANES), F32)],
        in_specs=[there] * 16,
        out_specs=[there] * 8,
        scratch_shapes=scratch,
        compiler_params=pltpu.CompilerParams(collective_id=0, has_side_effects=True, vmem_limit_bytes=63 * 2**20),
    )(
        images.reshape(d.PD, channels),
        *(w.astype(wire) for w in (enc_first, enc_second, dec_first, dec_second)),
        *smalls,
    )
    steps = next(count for count in (2, 1) if rows % (count * d.row_tile) == 0 and d.PD % (count * 8) == 0)
    part = lambda height, width: pl.BlockSpec((height // steps, width), lambda i: (i, 0))
    all_of = lambda height, width: pl.BlockSpec((height, width), lambda i: (0, 0))
    rest = ((q, out_ch), (4, channels), (4, channels), (1, hidden), (1, out_ch))
    gi, gw0, gw1, gw2, gw3, ghc, gq, gain, bias, ghb, gob = pl.pallas_call(
        finish,
        grid=(steps,),
        out_shape=[shape((d.PD, channels), F32)]
        + [shape((rows, channels), F32)] * 4
        + [shape((hidden, rows), F32)]
        + [shape(size, F32) for size in rest],
        in_specs=[part(d.PD, channels)]
        + [part(rows, channels)] * 4
        + [all_of(hidden, rows), all_of(8, channels), all_of(16, LANES)],
        out_specs=[part(d.PD, channels)]
        + [part(rows, channels)] * 4
        + [all_of(hidden, rows)]
        + [all_of(*size) for size in rest],
    )(*kept)
    return (
        gi.reshape(images.shape), gw0, gw1, gw2, gw3, ghc.T, gq, gain, bias, ghb.reshape(hidden), gob.reshape(out_ch),
    )


def solution(mesh):
    split = ("rep", "fsdp")
    rows = P("fsdp", None)
    return jax.shard_map(
        functools.partial(per_device, mesh.shape["rep"], mesh.shape["fsdp"]),
        mesh=mesh,
        in_specs=(P(split, None, None, None),)
        + (rows,) * 6
        + (P(),) * 5
        + (P(split, None), P(split, None), P(split, None, None), P(split, None, None)),
        out_specs=(P(split, None, None, None),) + (rows,) * 6 + (P(),) * 4,
        check_vma=False,
    )
```

```python
import functools
import math
import types

import jax
import jax.numpy as jnp
from jax import lax
from jax.experimental import pallas as pl
from jax.experimental.pallas import tpu as pltpu
from jax.sharding import PartitionSpec as P

MESH = pl.DeviceIdType.MESH
F32, BF16 = jnp.float32, jnp.bfloat16
EPS = 1e-05
LANES = 128
EXACT = lax.Precision.HIGHEST

GROUPS = (
    ["images", "start", "head_out", "a2a", "pool", "dh3", "rs2", "norms", "small_rep", "small_all"]
    + [f"sums{i}" for i in range(4)]
    + ["pool_slope"]
    + [f"norm{i}" for i in range(3)]
    + [
        f"{name}{way}"
        for name in ("ag0", "ag2", "rs3", "rs1", "rs0", "rows0", "rows1", "rows2", "rows3")
        for way in ("x0", "y1", "r")
    ]
    + [f"stat{i}" for i in range(8)]
    + [f"core{i}" for i in range(5)]
    + [f"weights{i}" for i in range(5)]
    + [f"z{i}.{h}" for i in range(5) for h in range(2)]
    + [f"mid{i}.{h}" for i in range(5) for h in range(2)]
    + ["rows4"]
    + [f"own{i}" for i in range(5)]
    + [f"out{i}" for i in range(4)]
    + [f"in{i}" for i in range(11)]
    + ["own_image", "out_gi", "out_ghc", "out_gnorm", "out_gsmall"]
)
GROUP = {name: number for number, name in enumerate(GROUPS)}

CLASSES = [
    "images", "start", "head_out", "a2a", "pool", "dh3", "rs2", "norms", "small_rep", "small_all", "pool_slope",
    "rows4", "weights", "weights4", "core", "core4", "z", "z4", "ag", "rs", "rs0", "rows", "sums", "norm", "stat",
]
CLASS = {name: number for number, name in enumerate(CLASSES)}


def class_of(group):
    if group in CLASS:
        return CLASS[group]
    if group.startswith("rs0"):
        return CLASS["rs0"]
    name = group.rstrip("xyr0123456789.")
    if name in ("mid", "z"):
        name = "z"
        return CLASS["z4" if group[len(group.split(".")[0]) - 1] == "4" else "z"]
    return CLASS[name]


def kernel(d, *refs):
    it = iter(refs)
    take = lambda count: [next(it) for _ in range(count)]
    images, w0, w1, w2, w3, *small_in = take(16)
    gi_out, gw0, gw1, gw2, gw3, *small_out = take(8)
    small = hw, ho, gain, shift, hb, ob, tw, pidx, lab, msk, tgt = take(11)
    gi, ghc, gnorm, gsmall = take(4)
    gather, columns_s = take(2)
    (s, s4, wf, y, zb, zhat, d9, u_sel, ut_sel, a2a_s, a2a_r, rs_s, rs_l, pool_own, pool_all, ps_s, ps_r, gi_s, gi_l) = take(19)
    (zg, slope, slope_z, nrm_s, nrm_r, sums_s, sums_r, z4, slope4, slope_z4, sp_own, sp_all) = take(12)
    (gf, cr, zr, hw_s, hp, hg, hcr, hzr, hr, st_s, st_r, start_s, start_r, ho_s, ho_r, rep_s, rep_r, all_s, all_r, norm_s, feat) = take(21)
    ssem, rsem, wrz = take(3)
    w_in, gw = (w0, w1, w2, w3, hw_s), (gw0, gw1, gw2, gw3)
    R, F, Z, rows, half, C, CR, W, PIX, PD, M, PW = d.R, d.F, d.Z, d.rows, d.half, d.C, d.CR, d.W, d.PIX, d.PD, d.M, d.PW
    total = float(M * F)
    root = math.sqrt(total)

    r, f = lax.axis_index("rep"), lax.axis_index("fsdp")
    zc, core = f // 2, f % 2
    sib = (r, zc * 2 + (1 - core))
    rep_peer = lambda k: ((r + k) % R, f)
    one, two = r + 1 - 2 * (r % 2), (r + 2) % R
    both = (one + 2) % R
    at_one, at_two = (one, f), (two, f)
    z_peer = lambda k: (r, ((zc + k) % Z) * 2 + core)
    line = Z == 4
    is_end = (zc == 0) | (zc == Z - 1)
    is_far = lambda k: (zc + k) % Z - zc == Z - 1
    is_far_back = lambda k: zc - (zc + k) % Z == Z - 1
    ends_apart = lambda k: is_far(k) | is_far_back(k)
    my_lanes = pl.ds(pl.multiple_of(r * CR, CR), CR)

    def block(owner):
        return pl.ds(pl.multiple_of(owner * rows, d.row_tile), rows)

    arriving, leaving = {}, {}

    def first_of(ref, count):
        return lambda: ref.at[pl.ds(0, count)]

    volume = {
        "images": first_of(s.at[0], (R - 1) * PD),
        "own_image": first_of(s.at[0], PD),
        "start": first_of(start_r, R - 1),
        "head_out": first_of(ho_r, F - 1),
        "a2a": lambda: z4.at[:, pl.ds(0, (R - 1) * CR)],
        "pool_slope": lambda: sp_all.at[:, :, pl.ds(0, (R - 1) * CR)],
        "pool": lambda: pool_all.at[:, pl.ds(0, (R - 1) * CR)],
        "dh3": first_of(a2a_r, R - 1),
        "rs2": first_of(ps_r, R - 1),
        "norms": lambda: gnorm.at[:, pl.ds(0, (R - 1) * CR)],
        "small_rep": first_of(rep_r, R - 1),
        "small_all": first_of(all_r, F - 1),
        "rows4": first_of(hr, R - 1),
        "core4": lambda: hcr,
    }
    for j in range(2):
        for way in ("x0", "y1"):
            volume[f"ag{2 * j}{way}"] = lambda j=j: zg.at[j, pl.ds(0, M // 2), pl.ds(0, CR)]
            volume[f"rs{2 * j + 1}{way}"] = lambda j=j: rs_l.at[j, 0]
        volume[f"ag{2 * j}r"] = lambda j=j: zg.at[j, :, pl.ds(0, 2 * CR)]
        volume[f"rs{2 * j + 1}r"] = lambda j=j: rs_l.at[j, pl.ds(0, 4)]
    volume["rs0x0"] = volume["rs0y1"] = lambda: gi_l.at[0]
    volume["rs0r"] = lambda: gi_l.at[pl.ds(0, 4)]
    for l in range(4):
        volume[f"rows{l}x0"] = lambda l=l: gather.at[l, pl.ds(0, half), pl.ds(0, CR)]
        volume[f"rows{l}y1"] = lambda l=l: gather.at[l, pl.ds(half, rows - half), pl.ds(0, CR)]
        volume[f"rows{l}r"] = lambda l=l: gather.at[l, :, pl.ds(0, (3 if l == 0 and line else 2) * CR)]
    for j in range(4):
        volume[f"sums{j}"] = first_of(sums_r.at[j], R - 1)
    for j in range(3):
        volume[f"norm{j}"] = first_of(nrm_r.at[j], R - 1)
    for e in range(8):
        volume[f"stat{e}"] = first_of(st_r.at[e], F - 1)
    for l in range(4):
        volume[f"core{l}"] = lambda l=l: cr.at[l]

    def wait_for(ref, sem):
        pltpu.make_async_copy(ref, ref, sem).wait()

    def wait_recv(group):
        arriving.pop(group)()

    def wait_send(group):
        leaving.pop(CLASS[group])()

    def when_line(at_end, inside, otherwise):
        if line:
            when(is_end, at_end)
            when(jnp.logical_not(is_end), inside)
        else:
            otherwise()

    def departed(number):
        name = CLASSES[number]
        whole = {
            "core": lambda: cr,
            "core4": lambda: hcr,
            "z": lambda: zr.at[:, pl.ds(0, Z - 1)],
            "z4": lambda: hzr.at[pl.ds(0, Z - 1)],
            "ag": lambda: zg.at[:, :, pl.ds(0, 3 * CR)],
            "rs": lambda: rs_l,
            "rs0": lambda: gi_l,
            "rows": lambda: gather.at[:, :, pl.ds(0, 3 * CR)],
            "sums": lambda: sums_r.at[:, pl.ds(0, R - 1)],
            "norm": lambda: nrm_r.at[:, pl.ds(0, R - 1)],
            "stat": lambda: st_r.at[:, pl.ds(0, F - 1)],
        }
        sem = ssem.at[number]
        if name == "weights":
            many = lambda count: lambda: wait_for(wf.at[pl.ds(0, 4), pl.ds(0, count * rows)], sem)
            when_line(many(6), many(8), many(2 * Z - 1))
        elif name == "weights4":
            many = lambda count: lambda: wait_for(hp.at[pl.ds(0, count)], sem)
            when_line(many(6), many(8), many(2 * Z - 1))
        else:
            wait_for((whole[name] if name in whole else volume[name])(), sem)

    def copy_here(src, dst, group):
        g = GROUP[group]
        arriving[group] = lambda: wait_for(dst, rsem.at[g])
        pltpu.make_async_copy(src, dst, rsem.at[g]).start()

    def send(src, dst, to, group):
        g, out = GROUP[group], class_of(group)
        if group in volume:
            arriving[group] = lambda: wait_for(volume[group](), rsem.at[g])
        leaving[out] = lambda: departed(out)
        pltpu.make_async_remote_copy(
            src_ref=src, dst_ref=dst, send_sem=ssem.at[out], recv_sem=rsem.at[g], device_id=to, device_id_type=MESH
        ).start()

    def over(count, body, first=0):
        if count <= 8:
            for i in range(first, count):
                body(i)
            return

        def step(i, carry):
            body(i)
            return carry

        lax.fori_loop(first, count, step, 0)

    def when(condition, body):
        pl.when(condition)(body)

    def direct(k, body):
        if line and k in (1, Z - 1):
            when(jnp.logical_not(ends_apart(k)), body)
        else:
            body()

    def drain():
        for waits in (arriving, leaving):
            for wait in list(waits.values()):
                wait()

    for i, (src, dst) in enumerate(zip(small_in, small)):
        copy_here(src, dst, f"in{i}")

    barrier = pltpu.get_barrier_semaphore()
    over(R, lambda k: pl.semaphore_signal(barrier, inc=1, device_id=rep_peer(k), device_id_type=MESH), 1)
    over(F, lambda k: pl.semaphore_signal(barrier, inc=1, device_id=(r, (f + k) % F), device_id_type=MESH), 1)
    pl.semaphore_wait(barrier, R + F - 2)

    pieces = range(d.pieces)

    def cut(l, h):
        size = rows if l < 4 else half
        first = -(-size // (d.pieces * d.row_tile)) * d.row_tile
        return (0, first) if h == 0 else (first, size - first)

    def cut_at(l, h):
        first, size = cut(l, h)
        return pl.ds(first, size)

    near = sorted({1, Z - 1})
    beyond = list(range(2, Z - 1))

    def w_block(l, owner, h):
        first, size = cut(l, h)
        if l < 4:
            return wf.at[l, pl.ds(pl.multiple_of(owner * rows + first, d.row_tile), size)]
        return hp.at[owner, pl.ds(first, size)]

    def w_copy(l, h, src, owner, to, recv_sem):
        out = CLASS["weights" if l < 4 else "weights4"]
        leaving[out] = lambda: departed(out)
        return pltpu.make_async_remote_copy(
            src_ref=src, dst_ref=w_block(l, owner, h), send_sem=ssem.at[out], recv_sem=recv_sem, device_id=to,
            device_id_type=MESH,
        )

    def w_to_core(l, h, src, owner):
        w_copy(l, h, src, owner, sib, rsem.at[GROUP[f"weights{l}"]]).start()

    def w_src(l, h):
        return w_in[l].at[cut_at(l, h), my_lanes] if l < 4 else hw_s.at[cut_at(l, h)]

    def w_wait(l, h, sem):
        wait_for(w_block(l, f, h), sem)

    def w_send(l, h, k, who=lambda body: body()):
        u = l * d.pieces + h
        arriving["z", l, h, k] = lambda: direct(Z - k, lambda: w_wait(l, h, wrz.at[u, k]))
        start = lambda: w_copy(l, h, w_src(l, h), f, z_peer(k), wrz.at[u, k]).start()
        who(lambda: direct(k, start))

    def w_push_near(l):
        for h in pieces:
            for k in near:
                w_send(l, h, k)
            w_to_core(l, h, w_src(l, h), f)
        copy_here(w_in[l].at[:, my_lanes] if l < 4 else hw_s, wf.at[l, block(f)] if l < 4 else hp.at[f], f"own{l}")

    def w_push_rest(l, hs=pieces, who=lambda body: body()):
        for h in hs:
            for k in beyond:
                w_send(l, h, k, who)

    def at_ends(body):
        if line:
            when(is_end, body)
        else:
            body()

    def between(body):
        if line:
            when(jnp.logical_not(is_end), body)

    def w_arrived(l, h, k):
        u = l * d.pieces + h
        owner = ((zc + Z - k) % Z) * 2 + core
        w_wait(l, h, wrz.at[u, k])
        w_to_core(l, h, w_block(l, owner, h), owner)

    def w_relay_rest(l, hs=pieces):
        for h in hs:
            u = l * d.pieces + h
            for k in beyond:
                arriving.pop(("z", l, h, k))
                w_arrived(l, h, k)
            if line:

                def hand_on():
                    to = (Z - 1) * (zc - 1)
                    owner = (Z - 1 - to) * 2 + core
                    slot = jnp.where(zc == 1, 1, Z - 1)
                    w_copy(l, h, w_block(l, owner, h), owner, (r, to * 2 + core), wrz.at[u, slot]).start()

                when(jnp.logical_not(is_end), hand_on)

    def w_relay_near(l):
        for h in pieces:
            for k in near:
                arriving.pop(("z", l, h, k))
                direct(Z - k, lambda: w_arrived(l, h, k))

    def w_far(l):
        if line:
            for h in pieces:
                when(zc == 0, lambda: w_arrived(l, h, 1))
                when(zc == Z - 1, lambda: w_arrived(l, h, Z - 1))

    def w_finish(l):
        one = GROUP[f"weights{l}"]
        wait_for(wf.at[l, pl.ds(0, Z * rows)] if l < 4 else hp.at[pl.ds(0, Z)], rsem.at[one])
        wait_recv(f"own{l}")

    w_push_rest(0)
    w_push_near(0)
    over(R, lambda k: send(images, s.at[0, pl.ds(pl.multiple_of(r * PD, PD), PD)], rep_peer(k), "images"), 1)
    own_rows = s.at[0, pl.ds(pl.multiple_of(r * PD, PD), PD)]
    copy_here(images, own_rows, "own_image")

    for i in range(len(small)):
        wait_recv(f"in{i}")
    start_s[...] = jnp.zeros_like(start_s)
    masks = jnp.concatenate([msk[:, i, :] for i in range(d.n)], axis=1).astype(F32)
    labels = jnp.concatenate([lab[i : i + 1, :] for i in range(d.n)], axis=1).astype(F32)
    wanted = jnp.concatenate([tgt[i] for i in range(d.n)], axis=1)
    pools = jnp.concatenate([pidx[i : i + 1, :] for i in range(d.n)], axis=1).astype(F32)
    counted = jnp.sum(masks, axis=1, keepdims=True)
    lane = lax.broadcasted_iota(jnp.int32, (1, LANES), 1)
    start_s[0:1, :] = sum(jnp.where(lane == t, counted[t : t + 1, :], 0.0) for t in range(3))
    start_s[1:2, 0 : PW // R] = pools
    over(R, lambda k: send(start_s, start_r.at[r], rep_peer(k), "start"), 1)
    start_r[r] = start_s[...]
    ho_s[...] = jnp.zeros_like(ho_s)
    ho_s[0 : d.q, 0 : d.OC] = ho[...].astype(F32)
    over(F, lambda k: send(ho_s, ho_r.at[f], (r, (f + k) % F), "head_out"), 1)
    ho_r[f] = ho_s[...]
    def pack_head():
        wide = -(-rows // LANES) * LANES
        tall = jnp.concatenate([hw[...].astype(F32), jnp.zeros((LANES - d.HC, rows), F32)], axis=0)
        if wide > rows:
            tall = jnp.concatenate([tall, jnp.zeros((LANES, wide - rows), F32)], axis=1)
        tall = jnp.transpose(tall)
        if wide < 2 * half:
            tall = jnp.concatenate([tall, jnp.zeros((2 * half - wide, LANES), F32)], axis=0)
        hw_s[...] = (tall[0:half] + pltpu.roll(tall[half : 2 * half], d.HC, 1)).astype(hw_s.dtype)

    bits = W.bit_length() - 1

    def places(axis, shape):
        q = lax.broadcasted_iota(jnp.int32, shape, axis)
        image = jnp.zeros(shape, jnp.int32)
        for i in range(1, M // PIX):
            image = image + jnp.where(q >= i * PIX, 1, 0)
        q = q - image * PIX
        window = image * (PIX // 4) + (q >> (bits + 1)) * (W // 2) + ((q & (W - 1)) >> 1)
        position = 2 * ((q >> bits) & 1) + (q & 1)
        return window, position.astype(F32)

    def windows(rows_first):
        shape = (M, PW) if rows_first else (PW, M)
        window, position = places(0 if rows_first else 1, shape)
        other = lax.broadcasted_iota(jnp.int32, shape, 1 if rows_first else 0)
        return window == other, position

    def pixel_columns():
        feat[...] = jnp.zeros_like(feat)
        feat[0:1, 0:PD] = labels
        feat[1:4, 0:PD] = masks
        feat[4:8, 0:PD] = wanted
        columns_s[...] = jnp.transpose(feat[...])[0:PD, 0:LANES]

    def pool_matrices():
        feat[...] = jnp.zeros_like(feat)
        for i in range(R):
            feat[0:1, i * (PW // R) : (i + 1) * (PW // R)] = start_r[i, 1:2, 0 : PW // R]
        picked_row = feat[0:1, 0:PW]
        picked_col = jnp.transpose(feat[...])[0:PW, 0:1]
        inside, position = windows(True)
        u_sel[...] = jnp.where(inside & (position == picked_row), 1.0, 0.0).astype(BF16)
        inside, position = windows(False)
        ut_sel[...] = jnp.where(inside & (position == picked_col), 1.0, 0.0).astype(BF16)

    def image_rows(i):
        return pl.ds(pl.multiple_of(i * PIX, PIX), PIX)

    def per_image(count, body, init):
        return lax.fori_loop(0, count, body, init)

    def column_of(shape):
        return lax.broadcasted_iota(jnp.int32, shape, 0) & (W - 1)

    blank = jnp.zeros((W, CR), F32)

    def conv(src, count, l, out):
        height = count * PIX
        for kx in range(3):
            taps = [wf[l, (3 * ky + kx) * C : (3 * ky + kx + 1) * C, :].astype(BF16) for ky in range(3)]
            y[0:height, kx * 3 * CR : (kx + 1) * 3 * CR] = jnp.dot(
                src[...], jnp.concatenate(taps, axis=1), preferred_element_type=F32
            )

        def body(i, summed):
            at = image_rows(i)
            col = column_of((PIX, CR))
            parts = []
            for kx in range(3):
                up, mid, down = (y[at, (kx * 3 + ky) * CR : (kx * 3 + ky + 1) * CR] for ky in range(3))
                parts.append(
                    mid
                    + jnp.concatenate([blank, up[: PIX - W]], axis=0)
                    + jnp.concatenate([down[W:], blank], axis=0)
                )
            z = (
                parts[1]
                + jnp.where(col > 0, pltpu.roll(parts[0], 1, 0), 0.0)
                + jnp.where(col < W - 1, pltpu.roll(parts[2], PIX - 1, 0), 0.0)
            )
            out[at, :] = z
            return summed + jnp.sum(z, axis=0, keepdims=True)

        return per_image(count, body, jnp.zeros((1, CR), F32))

    def spread_taps(i, grad):
        at = image_rows(i)
        col = column_of((PIX, CR))
        moved = (
            jnp.where(col < W - 1, pltpu.roll(grad, PIX - 1, 0), 0.0),
            grad,
            jnp.where(col > 0, pltpu.roll(grad, 1, 0), 0.0),
        )
        low_blank = blank.astype(BF16)
        for kx in range(3):
            low = moved[kx].astype(BF16)
            nine = (
                jnp.concatenate([low[W:], low_blank], axis=0),
                low,
                jnp.concatenate([low_blank, low[: PIX - W]], axis=0),
            )
            for ky in range(3):
                d9[at, (ky * 3 + kx) * CR : (ky * 3 + kx + 1) * CR] = nine[ky]

    def data_grad(l, height, write):
        step = 2 * CR
        for half in range(C // step):
            taps = [
                wf[l, t * C + half * step : t * C + (half + 1) * step, :].astype(BF16)
                for t in range(9)
            ]
            part = lax.dot_general(
                d9[0:height, :],
                jnp.concatenate(taps, axis=1),
                (((1,), (1,)), ((), ())),
                preferred_element_type=F32,
            )
            write(half, part)

    def lanes_of(owner):
        return pl.ds(pl.multiple_of(owner * CR, CR), CR)

    def gather_start(name, piece):
        send(piece(r, 0), piece(r, 0), at_one, f"{name}x0")
        send(piece(r, 1), piece(r, 1), at_two, f"{name}y1")
        send(piece(r, 1), piece(r, 1), at_one, f"{name}r")
        send(piece(r, 0), piece(r, 0), at_two, f"{name}r")

    def gather_forward(name, piece):
        wait_recv(f"{name}x0")
        send(piece(one, 0), piece(one, 0), at_two, f"{name}r")
        wait_recv(f"{name}y1")
        send(piece(two, 1), piece(two, 1), at_one, f"{name}r")

    def await_rest(name):
        wait_recv(f"{name}r")

    def scatter_start(name, piece, land):
        send(piece(both, 0), land(0), at_one, f"{name}x0")
        send(piece(both, 1), land(2), at_two, f"{name}y1")
        send(piece(one, 0), land(1), at_one, f"{name}r")
        send(piece(two, 1), land(3), at_two, f"{name}r")

    def scatter_forward(name, piece, land):
        for way, ref, came, dst, to in (
            ("x0", piece(two, 0), land(0), land(4), at_two),
            ("y1", piece(one, 1), land(2), land(5), at_one),
        ):
            wait_recv(f"{name}{way}")
            ref[...] = (ref[...].astype(F32) + came[...].astype(F32)).astype(ref.dtype)
            send(ref, dst, to, f"{name}r")

    def ag_piece(j):
        return lambda owner, h: zg.at[j, pl.ds(h * (M // 2), M // 2), lanes_of(owner)]

    def rows_piece(l):
        return lambda owner, h: gather.at[l, pl.ds(h * half, half if h == 0 else rows - half), lanes_of(owner)]

    def rs_piece(j):
        return lambda owner, h: rs_s.at[j, owner, pl.ds(h * (M // 2), M // 2)]

    def rs_land(j):
        return lambda i: rs_l.at[j, i]

    def gi_piece(owner, h):
        return gi_s.at[owner, pl.ds(h * (PD // 2), PD // 2)]

    def gi_land(i):
        return gi_l.at[i]

    def sigmoid(v):
        return 0.5 * jnp.tanh(0.5 * v) + 0.5

    def g_block(l, owner):
        return gf.at[l, block(owner)] if l < 4 else hg.at[owner]

    def from_core(l):
        return cr.at[l] if l < 4 else hcr

    def from_z(l, i, h):
        return zr.at[l, i, cut_at(l, h)] if l < 4 else hzr.at[i, cut_at(l, h)]

    def g_piece(l, owner, h):
        first, size = cut(l, h)
        if l < 4:
            return gf.at[l, pl.ds(pl.multiple_of(owner * rows + first, d.row_tile), size)]
        return hg.at[owner, pl.ds(first, size)]

    def weight_grad(l, src, height):
        to_core = lambda k: send(g_block(l, 2 * k + 1 - core), from_core(l).at[k], sib, f"core{l}")
        sent = 0
        for ky in range(3):
            part = lax.dot_general(
                src[...],
                d9[0:height, ky * 3 * CR : (ky + 1) * 3 * CR],
                (((0,), (0,)), ((), ())),
                preferred_element_type=F32,
            )
            for kx in range(3):
                t = 3 * ky + kx
                gf[l % 4, t * C : (t + 1) * C, :] = part[:, kx * CR : (kx + 1) * CR].astype(gf.dtype)
            while l < 4 and sent < Z and 2 * (sent + 1) * rows <= (ky + 1) * 3 * C:
                to_core(sent)
                sent += 1
        if l == 4:

            def pack(i, carry):
                at = i * rows
                low = gf[0, pl.ds(pl.multiple_of(at, d.row_tile), half), :].astype(F32)
                high = gf[0, pl.ds(pl.multiple_of(at + half, d.row_tile), rows - half), :].astype(F32)
                if rows < 2 * half:
                    high = jnp.concatenate([high, jnp.zeros((2 * half - rows, CR), F32)], axis=0)
                hg[i] = (low + pltpu.roll(high, d.HC, 1)).astype(hg.dtype)
                return carry

            lax.fori_loop(0, F, pack, 0)
            over(Z, to_core)

    def core_sum(l):
        wait_recv(f"core{l}")

        def step(k):
            ref = g_block(l, 2 * k + core)
            ref[...] = (ref[...].astype(F32) + from_core(l)[k].astype(F32)).astype(ref.dtype)

        over(Z, step)

    def z_push(l):
        for h in pieces:
            z_push_middle(l, h)
        for h in pieces:
            z_push_piece(l, h)

    def z_push_middle(l, h):
        if line:

            def to_middle():
                through, owner = jnp.where(zc == 0, 1, Z - 2), Z - 1 - zc
                send(g_piece(l, 2 * owner + core, h), from_z(l, through, h), (r, 2 * through + core), f"mid{l}.{h}")

            when(is_end, to_middle)
            g = GROUP[f"mid{l}.{h}"]
            arriving[f"mid{l}.{h}"] = lambda: when(
                jnp.logical_not(is_end), lambda: wait_for(from_z(l, 0, h), rsem.at[g])
            )

    def z_push_piece(l, h):
        def push(k):
            to = (zc + k) % Z
            send(g_piece(l, 2 * to + core, h), from_z(l, zc, h), (r, 2 * to + core), f"z{l}.{h}")

        for k in range(1, Z) if Z <= 8 else ():
            if line and k == 2:
                when(is_end, lambda: push(2))
            else:
                direct(k, lambda: push(k))
        if Z > 8:
            over(Z, push, 1)
        arriving[f"z{l}.{h}"] = lambda: z_wait(l, h, rsem.at[GROUP[f"z{l}.{h}"]])

    def z_middle(l):
        for h in pieces:
            z_middle_piece(l, h)

    def z_middle_piece(l, h):
        if line:
            wait_recv(f"mid{l}.{h}")

            def hand_on():
                owner = (Z - 1) * (Z - 2 - zc)
                ref = g_piece(l, 2 * owner + core, h)
                ref[...] = (ref[...].astype(F32) + from_z(l, zc, h)[...].astype(F32)).astype(ref.dtype)
                send(ref, from_z(l, zc, h), (r, 2 * owner + core), f"z{l}.{h}")

            when(jnp.logical_not(is_end), hand_on)

    def z_wait(l, h, sem):
        first, size = cut(l, h)
        many = lambda count: (zr.at[l, pl.ds(0, count), cut_at(l, h)] if l < 4 else hzr.at[pl.ds(0, count), cut_at(l, h)])
        if line:
            when(is_end, lambda: wait_for(many(Z - 2), sem))
            when(jnp.logical_not(is_end), lambda: wait_for(many(Z - 1), sem))
        else:
            wait_for(many(Z - 1), sem)

    def z_sum(l):
        for h in pieces:
            z_sum_piece(l, h)
        if l < 4:
            gather_start(f"rows{l}", rows_piece(l))
        else:
            over(R, lambda k: send(hr.at[r], hr.at[r], rep_peer(k), "rows4"), 1)

    def z_sum_piece(l, h):
        wait_recv(f"z{l}.{h}")
        read = lambda i: from_z(l, i, h)[...].astype(F32)
        summed = g_piece(l, f, h)[...].astype(F32)
        if line:
            one_side = jnp.where(zc == 0, 1, jnp.where(zc == Z - 1, Z - 2, zc - 1))
            other_side = jnp.where(zc == 0, 2, jnp.where(zc == Z - 1, 1, zc + 1))
            opposite = jnp.where(zc == 1, Z - 1, 0)
            summed = summed + read(one_side) + read(other_side) + jnp.where(is_end, 0.0, read(opposite))
        else:
            summed = lax.fori_loop(1, Z, lambda k, so_far: so_far + read((zc + k) % Z), summed)
        summed = summed * (1.0 / root)
        if l < 4:
            gather[l, cut_at(l, h), my_lanes] = summed.astype(gather.dtype)
        else:
            hr[r, cut_at(l, h)] = summed.astype(hr.dtype)

    def rows_done(l):
        if l < 4:
            await_rest(f"rows{l}")
            copy_here(gather.at[l], gw[l], f"out{l}")
        else:
            wait_recv("rows4")
            summed = sum(hr[i].astype(F32) for i in range(R))
            wide = -(-half // LANES) * LANES
            if wide > half:
                summed = jnp.concatenate([summed, jnp.zeros((wide - half, LANES), F32)], axis=0)
            summed = jnp.transpose(summed)
            ghc[:, 0:half] = summed[0 : d.HC, 0:half]
            ghc[:, half:rows] = summed[d.HC : 2 * d.HC, 0 : rows - half]

    def exchange(e):
        over(F, lambda k: send(st_s.at[e], st_r.at[e, f], (r, (f + k) % F), f"stat{e}"), 1)
        st_r[e, f] = st_s[e]

    def exchanged(e):
        wait_recv(f"stat{e}")
        return st_r[e]

    st_s[...] = jnp.zeros_like(st_s)
    w_relay_rest(0)
    w_relay_near(0)
    w_far(0)
    w_push_rest(1, who=at_ends)
    wait_recv("images")
    wait_recv("own_image")
    wait_recv("start")

    rep_all = lambda src, dst, group: over(R, lambda k: send(src, dst, rep_peer(k), group), 1)
    images_here = M // PIX
    inverse_of, counts = [], None

    def widened(j, i, b):
        value = zg[j, image_rows(i), b * CR : (b + 1) * CR].astype(F32)
        return value, [nrm_r[j, b, k : k + 1, :] for k in range(4)]

    def slopes_of(j):
        def body(i, carry):
            for b in range(R):
                value, (a, o, inverse, off) = widened(j, i, b)
                shaped = value * a + o
                squashed = sigmoid(shaped)
                steep = squashed + shaped * squashed * (1.0 - squashed)
                slope[j, image_rows(i), b * CR : (b + 1) * CR] = steep.astype(BF16)
                slope_z[j, image_rows(i), b * CR : (b + 1) * CR] = (steep * (value * inverse + off)).astype(BF16)
            return carry

        per_image(images_here, body, 0)

    def rows_of(l):
        return gain[l : l + 1, my_lanes], shift[l : l + 1, my_lanes]

    def slope_here(l, at):
        g_row, b_row = rows_of(l)
        normed = zhat[l, at, :]
        shaped = normed * g_row + b_row
        squashed = sigmoid(shaped)
        return normed, squashed + shaped * squashed * (1.0 - squashed)

    def pool_slopes():
        def body(i, carry):
            at = image_rows(i)
            normed, steep = slope_here(1, at)
            y[at, 0:CR] = steep
            y[at, CR : 2 * CR] = steep * normed
            return carry

        per_image(images_here, body, 0)
        inside, unused = windows(False)
        averaged = jnp.dot(
            jnp.where(inside, 0.25, 0.0), y[:, 0 : 2 * CR], precision=EXACT, preferred_element_type=F32
        ).astype(BF16)
        for k in range(2):
            sp_own[k] = averaged[:, k * CR : (k + 1) * CR]
            sp_all[k, :, my_lanes] = averaged[:, k * CR : (k + 1) * CR]
        rep_all(sp_own, sp_all.at[:, :, my_lanes], "pool_slope")

    for l in range(4):
        w_finish(l)
        if l == 2:
            wait_recv("pool")
            s[2] = jnp.dot(u_sel[...], pool_all[...], preferred_element_type=F32).astype(BF16)
        first = conv(s.at[l], images_here, l, zb)
        mean_here = first * (1.0 / M)
        gathers = l in (0, 2)
        ahead = l != 1
        j = 2 if l == 3 else l // 2

        def squares(i, so_far):
            apart = zb[image_rows(i), :] - mean_here
            if gathers:
                zg[j, image_rows(i), my_lanes] = apart.astype(BF16)
            elif l == 3:
                a2a_s[i] = apart.astype(BF16)
            return so_far + jnp.sum(jnp.square(apart), axis=0, keepdims=True)

        squared = per_image(images_here, squares, jnp.zeros((1, CR), F32))
        if gathers:
            gather_start(f"ag{l}", ag_piece(j))
        elif l == 3:
            over(R, lambda k: send(a2a_s.at[(r + k) % R], z4.at[:, my_lanes], rep_peer(k), "a2a"), 1)
            z4[:, my_lanes] = a2a_s[r]
        st_s[l, 0:1, :] = first
        st_s[l, 1:2, :] = squared
        if l == 0:
            st_s[l, 2:3, :] = sum(start_r[i, 0:1, :] for i in range(R))
        exchange(l)
        if l == 0:
            w_push_rest(1, who=between)
            w_push_near(1)
            w_relay_rest(1)
        elif l < 3:
            w_push_rest(l + 1, pieces[1:])
            w_push_near(l + 1)
            w_relay_rest(l + 1, pieces[:1])
        else:
            w_push_near(4)
            w_relay_rest(4)
        if gathers:
            gather_forward(f"ag{l}", ag_piece(j))
        elif l == 1:
            pixel_columns()
        else:
            slopes_of(1)
        parts = exchanged(l)
        tot = jnp.sum(parts, axis=0)
        mean = tot[0:1] * (1.0 / total)
        apart = jnp.sum(jnp.square(parts * (1.0 / M) - mean[None]), axis=0)[0:1] * float(M)
        inverse = lax.rsqrt((tot[1:2] + apart) * (1.0 / total) + EPS)
        inverse_of.append(inverse)
        if l == 0:
            counts = tot[2:3]
        g_row, b_row = gain[l : l + 1, my_lanes], shift[l : l + 1, my_lanes]
        if ahead:
            off = (mean_here - mean) * inverse
            nrm_s[j, 0:1, :] = inverse * g_row
            nrm_s[j, 1:2, :] = off * g_row + b_row
            nrm_s[j, 2:3, :] = inverse
            nrm_s[j, 3:4, :] = off
            rep_all(nrm_s.at[j], nrm_r.at[j, r], f"norm{j}")
            nrm_r[j, r] = nrm_s[j]

        def activate(i, carry):
            at = image_rows(i)
            normed = (zb[at, :] - mean) * inverse
            zhat[l, at, :] = normed
            shaped = normed * g_row + b_row
            hidden = shaped * sigmoid(shaped)
            zb[at, :] = hidden
            return carry

        def keep_normed(i, carry):
            zhat[l, image_rows(i), :] = (zb[image_rows(i), :] - mean) * inverse
            return carry

        def activate_all(i, carry):
            for b in range(R):
                value, (a, o, unused, also) = widened(j, i, b)
                shaped = value * a + o
                s[l + 1, image_rows(i), b * CR : (b + 1) * CR] = (shaped * sigmoid(shaped)).astype(BF16)
            return carry

        per_image(images_here, keep_normed if ahead else activate, 0)
        if l == 1:
            inside, unused = windows(False)
            pooled = jnp.dot(
                jnp.where(inside, 0.25, 0.0), zb[...], precision=EXACT, preferred_element_type=F32
            )
            pool_own[...] = pooled.astype(BF16)
            pool_all[:, my_lanes] = pooled.astype(BF16)
            rep_all(pool_own, pool_all.at[:, my_lanes], "pool")
            w_relay_rest(2, pieces[1:])
            pool_slopes()
            slopes_of(0)
        elif l == 0:
            pool_matrices()
        elif l == 2:
            w_relay_rest(3, pieces[1:])
            pack_head()
        w_relay_near(l + 1)
        if l < 2:
            w_push_rest(l + 2, pieces[:1])
        elif l == 2:
            w_push_rest(4)
        w_far(l + 1)
        if gathers:
            wait_recv(f"norm{j}")
            await_rest(f"ag{l}")
            per_image(images_here, activate_all, 0)

    w_finish(4)
    low_lanes = lax.broadcasted_iota(jnp.int32, (half, LANES), 1) < d.HC

    def unpack(i, carry):
        both = hp[i].astype(F32)
        at = i * rows
        wf[4, pl.ds(pl.multiple_of(at, d.row_tile), half), :] = jnp.where(low_lanes, both, 0.0).astype(wf.dtype)
        high = jnp.where(low_lanes, pltpu.roll(both, d.HC, 1), 0.0).astype(wf.dtype)
        wf[4, pl.ds(pl.multiple_of(at + half, d.row_tile), rows - half), :] = high[0 : rows - half]
        return carry

    lax.fori_loop(0, F, unpack, 0)
    wait_recv("norm2")
    wait_recv("a2a")

    def activate_own(i, carry):
        at = image_rows(i)
        for b in range(R):
            lanes = slice(b * CR, (b + 1) * CR)
            value = z4[at, lanes].astype(F32)
            a, o, inverse, off = [nrm_r[2, b, k : k + 1, :] for k in range(4)]
            shaped = value * a + o
            squashed = sigmoid(shaped)
            s4[at, lanes] = (shaped * squashed).astype(BF16)
            steep = squashed + shaped * squashed * (1.0 - squashed)
            slope4[at, lanes] = steep.astype(BF16)
            slope_z4[at, lanes] = (steep * (value * inverse + off)).astype(BF16)
        return carry

    per_image(PD // PIX, activate_own, 0)
    wait_recv("head_out")
    conv(s4, PD // PIX, 4, zb)
    head_bias = jnp.concatenate([hb[...], jnp.zeros((1, CR - d.HC), F32)], axis=1)
    out_bias = jnp.concatenate([ob[...], jnp.zeros((1, CR - d.OC), F32)], axis=1)
    head_raw = zb[0:PD, :] + head_bias
    squashed = sigmoid(head_raw)
    head_act = head_raw * squashed
    project = jnp.concatenate([ho_r[i][0 : d.q] for i in range(F)] + [jnp.zeros((LANES - d.HC, LANES), F32)], axis=0)
    out = jnp.dot(head_act, project, precision=EXACT, preferred_element_type=F32) + out_bias
    lane = lax.broadcasted_iota(jnp.int32, (PD, LANES), 1)
    classes = d.OC - 4
    factor = total * jnp.concatenate([tw[...], jnp.zeros((1, LANES - 3), F32)], axis=1) / jnp.maximum(counts, 1.0)
    pixel = [columns_s[:, i : i + 1] for i in range(8)]
    is_class = lane < classes
    top = jnp.max(jnp.where(is_class, out, -jnp.inf), axis=1, keepdims=True)
    grown = jnp.where(is_class, jnp.exp(jnp.where(is_class, out - top, 0.0)), 0.0)
    likely = grown / jnp.sum(grown, axis=1, keepdims=True)
    onehot = jnp.where(lane.astype(F32) == pixel[0], 1.0, 0.0)
    grad_class = factor[:, 0:1] * pixel[1] * (likely - onehot)
    misfit = out - pixel[4]
    grad_depth = factor[:, 1:2] * pixel[2] * misfit / jnp.sqrt(misfit * misfit + 1.0)
    is_normal = (lane > classes) & (lane < d.OC)
    predicted = jnp.where(is_normal, out, 0.0)
    wanted = sum(jnp.where(lane == classes + 1 + i, pixel[5 + i], 0.0) for i in range(3))
    radius = jnp.sqrt(jnp.sum(predicted * predicted, axis=1, keepdims=True) + 1.0)
    aligned = jnp.sum(predicted * wanted, axis=1, keepdims=True)
    grad_normal = -(factor[:, 2:3] * pixel[3]) * (wanted / radius - aligned / (radius * radius * radius) * predicted)
    grad_out = jnp.where(
        is_class, grad_class, jnp.where(lane == classes, grad_depth, jnp.where(is_normal, grad_normal, 0.0))
    )
    grad_act = lax.dot_general(
        grad_out, project, (((1,), (1,)), ((), ())), precision=EXACT, preferred_element_type=F32
    )
    grad_head = (grad_act * (squashed + head_raw * squashed * (1.0 - squashed))).astype(BF16).astype(F32)
    zb[0:PD, :] = grad_head
    y[0:PD, 0:CR] = head_act
    y[0:PD, CR : 2 * CR] = grad_out

    def spread_head(i, carry):
        spread_taps(i, zb[image_rows(i), :])
        return carry

    per_image(PD // PIX, spread_head, 0)

    def put_sums(j, n, grad, steep, steep_z):
        sums_s[j, n, 0:1, :] = jnp.sum(grad * steep.astype(F32), axis=0, keepdims=True)
        sums_s[j, n, 1:2, :] = jnp.sum(grad * steep_z.astype(F32), axis=0, keepdims=True)

    def send_sums(j):
        over(R, lambda k: send(sums_s.at[j, (r + k) % R], sums_r.at[j, r], rep_peer(k), f"sums{j}"), 1)
        sums_r[j, r] = sums_s[j, r]

    def pass_sums(j, e):
        wait_recv(f"sums{j}")
        st_s[e, 0:2, :] = sum(sums_r[j, i, 0:2, :] for i in range(R))
        exchange(e)

    def write_dh3(part_at, part):
        for b in range(2):
            n = 2 * part_at + b
            grad = part[:, b * CR : (b + 1) * CR]
            cols = slice(n * CR, (n + 1) * CR)
            a2a_s[n] = grad.astype(BF16)
            put_sums(2, n, grad, slope4[:, cols], slope_z4[:, cols])

    wait_send("a2a")
    data_grad(4, PD, write_dh3)
    send_sums(2)
    over(R, lambda k: send(a2a_s.at[(r + k) % R], a2a_r.at[r], rep_peer(k), "dh3"), 1)
    a2a_r[r] = a2a_s[r]
    weight_grad(4, s4, PD)
    head_act, grad_out = y[0:PD, 0:CR], y[0:PD, CR : 2 * CR]
    pad = jnp.zeros((2 * LANES - PD, LANES), F32)
    act_t = jnp.transpose(jnp.concatenate([head_act, pad], axis=0))[:, 0:PD]
    rep_s[0 : d.HC, :] = jnp.dot(act_t, grad_out, precision=EXACT, preferred_element_type=F32)[0 : d.HC]
    rep_s[d.HC : d.HC + 8, :] = jnp.zeros((8, LANES), F32)
    rep_s[d.HC : d.HC + 1, :] = jnp.sum(zb[0:PD, :], axis=0, keepdims=True)
    rep_s[d.HC + 1 : d.HC + 2, :] = jnp.sum(grad_out, axis=0, keepdims=True)
    over(R, lambda k: send(rep_s, rep_r.at[r], rep_peer(k), "small_rep"), 1)
    rep_r[r] = rep_s[...]

    def head_small():
        wait_recv("small_rep")
        summed = sum(rep_r[i] for i in range(R))
        for i in range(F):
            all_s[i, 0 : d.q, :] = summed[i * d.q : (i + 1) * d.q]
            if d.q < 8:
                all_s[i, d.q : 8, :] = jnp.zeros((8 - d.q, LANES), F32)
            all_s[i, 8:16, :] = summed[d.HC : d.HC + 8]
        over(F, lambda k: send(all_s.at[(f + k) % F], all_r.at[f], (r, (f + k) % F), "small_all"), 1)
        all_r[f] = all_s[f]

    def through_norm(l, grad_of):
        tot = jnp.sum(exchanged(7 - l), axis=0)
        bias_sum, gain_sum = tot[0:1], tot[1:2]
        norm_s[l : l + 1, :] = gain_sum * (1.0 / root)
        norm_s[4 + l : 5 + l, :] = bias_sum * (1.0 / root)
        scale = inverse_of[l] * rows_of(l)[0]
        if l in (0, 2):
            await_rest(f"rs{l + 1}")
        elif l == 3:
            wait_recv("dh3")

        def body(i, carry):
            at = image_rows(i)
            normed, grad = grad_of(i, at)
            spread_taps(i, scale * (grad - bias_sum * (1.0 / total) - normed * (gain_sum * (1.0 / total))))
            return carry

        per_image(images_here, body, 0)

    def from_scatter(l):
        j = l // 2
        here = images_here // 2

        def grad_of(i, at):
            normed, steep = slope_here(l, at)
            h = i // here
            local = image_rows(i - h * here)
            grad = (
                rs_s[j, r, at, :].astype(F32)
                + rs_l[j, 1 + 2 * h, local, :].astype(F32)
                + rs_l[j, 4 + h, local, :].astype(F32)
            )
            return normed, grad * steep

        return grad_of

    def layer_down(l):
        j = (l - 1) // 2

        def write(part_at, part):
            for b in range(2):
                n = 2 * part_at + b
                grad = part[:, b * CR : (b + 1) * CR]
                rs_s[j, n] = grad.astype(BF16)
                cols = slice(n * CR, (n + 1) * CR)
                put_sums(j, n, grad, slope[j, :, cols], slope_z[j, :, cols])

        data_grad(l, M, write)
        send_sums(j)
        scatter_start(f"rs{l}", rs_piece(j), rs_land(j))
        z_middle_piece(l + 1, 0)
        weight_grad(l, s.at[l], M)
        pass_sums(j, 7 - (l - 1))
        scatter_forward(f"rs{l}", rs_piece(j), rs_land(j))
        for h in pieces[1:]:
            z_middle_piece(l + 1, h)

    def from_head(i, at):
        normed, steep = slope_here(3, at)
        return normed, a2a_r[i].astype(F32) * steep

    pass_sums(2, 4)
    core_sum(4)
    z_push(4)
    head_small()
    through_norm(3, from_head)
    layer_down(3)
    core_sum(3)
    z_push(3)
    z_sum(4)

    through_norm(2, from_scatter(2))

    def write_pooled(part_at, part):
        chosen = jnp.dot(ut_sel[...], part.astype(BF16), preferred_element_type=F32)
        for b in range(2):
            n = 2 * part_at + b
            grad = chosen[:, b * CR : (b + 1) * CR]
            cols = slice(n * CR, (n + 1) * CR)
            ps_s[n] = grad.astype(BF16)
            put_sums(3, n, grad, sp_all[0, :, cols], sp_all[1, :, cols])

    wait_recv("pool_slope")
    data_grad(2, M, write_pooled)
    send_sums(3)
    z_middle(3)
    over(R, lambda k: send(ps_s.at[(r + k) % R], ps_r.at[r], rep_peer(k), "rs2"), 1)
    ps_r[r] = ps_s[r]
    weight_grad(2, s.at[2], M)
    pass_sums(3, 6)
    core_sum(2)
    z_push(2)
    wait_recv("rs2")
    pooled = sum(ps_r[i].astype(F32) for i in range(R))
    inside, unused = windows(True)
    zb[...] = jnp.dot(jnp.where(inside, 0.25, 0.0), pooled, precision=EXACT, preferred_element_type=F32)

    def from_pool(i, at):
        normed, steep = slope_here(1, at)
        return normed, zb[at, :] * steep

    through_norm(1, from_pool)
    layer_down(1)
    z_sum(3)
    core_sum(1)
    z_push(1)
    gather_forward("rows3", rows_piece(3))
    z_sum(2)

    through_norm(0, from_scatter(0))
    def write_images(part_at, part):
        for i in range(R):
            gi_s[i, :, part_at * 2 * CR : (part_at + 1) * 2 * CR] = part[i * PD : (i + 1) * PD].astype(BF16)

    data_grad(0, M, write_images)
    scatter_start("rs0", gi_piece, gi_land)
    weight_grad(0, s.at[0], M)
    gather_forward("rows2", rows_piece(2))
    z_middle(1)
    core_sum(0)
    z_push(0)

    gnorm[:, my_lanes] = norm_s[...]
    rep_all(norm_s, gnorm.at[:, my_lanes], "norms")
    z_middle(0)
    scatter_forward("rs0", gi_piece, gi_land)
    z_sum(1)
    wait_recv("small_all")
    gsmall[...] = jnp.sum(all_r[...], axis=0) * (1.0 / root)
    rows_done(4)
    copy_here(ghc, small_out[0], "out_ghc")
    copy_here(gsmall, small_out[2], "out_gsmall")
    rows_done(3)
    gather_forward("rows1", rows_piece(1))
    rows_done(2)
    await_rest("rs0")
    for h in range(2):
        at = slice(h * (PD // 2), (h + 1) * (PD // 2))
        gi[at, :] = gi_s[r, at, :].astype(F32) + gi_l[1 + 2 * h].astype(F32) + gi_l[4 + h].astype(F32)
    copy_here(gi, gi_out, "out_gi")
    wait_recv("norms")
    copy_here(gnorm, small_out[1], "out_gnorm")
    last = rows_piece(0)
    if d.pieces == 2:
        z_sum_piece(0, 0)
        send(last(r, 0), last(r, 0), at_one, "rows0r")
        send(last(r, 0), last(r, 0), at_two, "rows0r")
        send(last(r, 0), last(r, 0), (both, f), "rows0r")
        rows_done(1)
        z_sum_piece(0, 1)
        send(last(r, 1), last(r, 1), at_one, "rows0r")
        send(last(r, 1), last(r, 1), at_two, "rows0r")
        send(last(r, 1), last(r, 1), (both, f), "rows0r")
    else:
        z_sum(0)
        rows_done(1)
        gather_forward("rows0", last)
    rows_done(0)

    drain()


def finish(gi, gw0, gw1, gw2, gw3, ghc, gnorm, gsmall, *outs):
    out_gi, out0, out1, out2, out3, out_hc, out_ho, out_gain, out_bias, out_hb, out_ob = outs
    out_gi[...] = gi[...]
    for src, dst in ((gw0, out0), (gw1, out1), (gw2, out2), (gw3, out3)):
        dst[...] = src[...].astype(F32)

    @pl.when(pl.program_id(0) == 0)
    def _():
        out_hc[...] = ghc[...]
        out_ho[...] = gsmall[0 : out_ho.shape[0], 0 : out_ho.shape[1]]
        out_gain[...] = gnorm[0:4, :]
        out_bias[...] = gnorm[4:8, :]
        out_hb[...] = gsmall[8:9, 0 : out_hb.shape[1]]
        out_ob[...] = gsmall[9:10, 0 : out_ob.shape[1]]


def per_device(
    R, F,
    images, enc_first, enc_second, dec_first, dec_second, head_conv, head_out, norm_gain, norm_bias, head_bias, out_bias,
    task_weights, pool_index, labels, task_masks, targets,
):
    n, height, breadth, channels = images.shape
    rows, hidden = head_conv.shape
    q, out_ch = head_out.shape
    d = types.SimpleNamespace(
        n=n, R=R, F=F, Z=F // 2, rows=rows, C=channels, CR=channels // R, W=breadth, PIX=height * breadth,
        PD=n * height * breadth, HC=hidden, OC=out_ch, q=q,
    )
    d.M = R * d.PD
    d.pieces = 2 if d.Z == 4 else 1
    d.PW = d.M // 4
    wire = BF16 if rows % 16 == 0 else F32
    d.row_tile = 16 if rows % 16 == 0 else 8
    d.half = -(-rows // (2 * d.row_tile)) * d.row_tile
    vm = pltpu.VMEM
    patch = 9 * channels
    smalls = (
        head_conv.T, head_out, norm_gain, norm_bias, head_bias.reshape(1, hidden), out_bias.reshape(1, out_ch),
        task_weights.reshape(1, 3), pool_index, labels, jnp.transpose(task_masks, (1, 0, 2)), targets,
    )
    smalls = (smalls[0].astype(wire),) + smalls[1:]
    scratch = [vm(value.shape, value.dtype) for value in smalls] + [
        vm((d.PD, d.C), F32),
        vm((hidden, rows), F32),
        vm((8, d.C), F32),
        vm((16, LANES), F32),
        vm((4, rows, d.C), wire),
        vm((d.PD, LANES), F32),
        vm((4, d.M, d.C), BF16),
        vm((d.PD, d.C), BF16),
        vm((5, patch, d.CR), wire),
        vm((d.M, 9 * d.CR), F32),
        vm((d.M, d.CR), F32),
        vm((4, d.M, d.CR), F32),
        vm((d.M, 9 * d.CR), BF16),
        vm((d.M, d.PW), BF16),
        vm((d.PW, d.M), BF16),
        vm((R, d.PD, d.CR), BF16),
        vm((R, d.PD, d.CR), BF16),
        vm((2, R, d.M, d.CR), BF16),
        vm((2, 6, d.M // 2, d.CR), BF16),
        vm((d.PW, d.CR), BF16),
        vm((d.PW, d.C), BF16),
        vm((R, d.PW, d.CR), BF16),
        vm((R, d.PW, d.CR), BF16),
        vm((R, d.PD, d.C), BF16),
        vm((6, d.PD // 2, d.C), BF16),
        vm((2, d.M, d.C), BF16),
        vm((2, d.M, d.C), BF16),
        vm((2, d.M, d.C), BF16),
        vm((3, 8, LANES), F32),
        vm((3, R, 8, LANES), F32),
        vm((4, R, 8, LANES), F32),
        vm((4, R, 8, LANES), F32),
        vm((d.PD, d.C), BF16),
        vm((d.PD, d.C), BF16),
        vm((d.PD, d.C), BF16),
        vm((2, d.PW, d.CR), BF16),
        vm((2, d.PW, d.C), BF16),
        vm((4, patch, d.CR), wire),
        vm((4, d.Z, rows, d.CR), wire),
        vm((4, d.Z, rows, d.CR), wire),
        vm((d.half, LANES), wire),
        vm((F, d.half, LANES), wire),
        vm((F, d.half, LANES), wire),
        vm((d.Z, d.half, LANES), wire),
        vm((d.Z, d.half, LANES), wire),
        vm((R, d.half, LANES), wire),
        vm((8, 8, LANES), F32),
        vm((8, F, 8, LANES), F32),
        vm((8, LANES), F32),
        vm((R, 8, LANES), F32),
        vm((8, LANES), F32),
        vm((F, 8, LANES), F32),
        vm((hidden + 8, LANES), F32),
        vm((R, hidden + 8, LANES), F32),
        vm((F, 16, LANES), F32),
        vm((F, 16, LANES), F32),
        vm((8, LANES), F32),
        vm((LANES, 2 * LANES), F32),
        pltpu.SemaphoreType.DMA((len(CLASSES),)),
        pltpu.SemaphoreType.DMA((len(GROUPS),)),
        pltpu.SemaphoreType.DMA((5 * d.pieces, d.Z)),
    ]
    there = pl.BlockSpec(memory_space=pl.ANY)
    shape = jax.ShapeDtypeStruct
    kept = pl.pallas_call(
        functools.partial(kernel, d),
        out_shape=[shape((d.PD, d.C), F32)]
        + [shape((rows, d.C), wire)] * 4
        + [shape((hidden, rows), F32), shape((8, d.C), F32), shape((16, LANES), F32)],
        in_specs=[there] * 16,
        out_specs=[there] * 8,
        scratch_shapes=scratch,
        compiler_params=pltpu.CompilerParams(collective_id=0, has_side_effects=True, vmem_limit_bytes=63 * 2**20),
    )(
        images.reshape(d.PD, channels),
        *(w.astype(wire) for w in (enc_first, enc_second, dec_first, dec_second)),
        *smalls,
    )
    steps = next(count for count in (2, 1) if rows % (count * d.row_tile) == 0 and d.PD % (count * 8) == 0)
    part = lambda height, width: pl.BlockSpec((height // steps, width), lambda i: (i, 0))
    all_of = lambda height, width: pl.BlockSpec((height, width), lambda i: (0, 0))
    rest = ((q, out_ch), (4, channels), (4, channels), (1, hidden), (1, out_ch))
    gi, gw0, gw1, gw2, gw3, ghc, gq, gain, bias, ghb, gob = pl.pallas_call(
        finish,
        grid=(steps,),
        out_shape=[shape((d.PD, channels), F32)]
        + [shape((rows, channels), F32)] * 4
        + [shape((hidden, rows), F32)]
        + [shape(size, F32) for size in rest],
        in_specs=[part(d.PD, channels)]
        + [part(rows, channels)] * 4
        + [all_of(hidden, rows), all_of(8, channels), all_of(16, LANES)],
        out_specs=[part(d.PD, channels)]
        + [part(rows, channels)] * 4
        + [all_of(hidden, rows)]
        + [all_of(*size) for size in rest],
    )(*kept)
    return (
        gi.reshape(images.shape), gw0, gw1, gw2, gw3, ghc.T, gq, gain, bias, ghb.reshape(hidden), gob.reshape(out_ch),
    )


def solution(mesh):
    split = ("rep", "fsdp")
    rows = P("fsdp", None)
    return jax.shard_map(
        functools.partial(per_device, mesh.shape["rep"], mesh.shape["fsdp"]),
        mesh=mesh,
        in_specs=(P(split, None, None, None),)
        + (rows,) * 6
        + (P(),) * 5
        + (P(split, None), P(split, None), P(split, None, None), P(split, None, None)),
        out_specs=(P(split, None, None, None),) + (rows,) * 6 + (P(),) * 4,
        check_vma=False,
    )
```

```python
import functools
import math
import types

import jax
import jax.numpy as jnp
from jax import lax
from jax.experimental import pallas as pl
from jax.experimental.pallas import tpu as pltpu
from jax.sharding import PartitionSpec as P

MESH = pl.DeviceIdType.MESH
F32, BF16 = jnp.float32, jnp.bfloat16
EPS = 1e-05
LANES = 128
EXACT = lax.Precision.HIGHEST

GROUPS = (
    ["im", "st", "ho", "a2a", "pl", "d3", "rs2", "ns", "sp", "sa"]
    + [f"s{i}" for i in range(4)]
    + ["ps"]
    + [f"n{i}" for i in range(3)]
    + [
        f"{name}{way}"
        for name in ("ag0", "ag2", "rs3", "rs1", "rs0", "w0", "w1", "w2", "w3")
        for way in ("x0", "y1", "r")
    ]
    + [f"t{i}" for i in range(8)]
    + [f"c{i}" for i in range(5)]
    + [f"k{i}" for i in range(5)]
    + [f"z{i}.{h}" for i in range(5) for h in range(2)]
    + [f"m{i}.{h}" for i in range(5) for h in range(2)]
    + ["w4"]
    + [f"o{i}" for i in range(5)]
    + [f"u{i}" for i in range(4)]
    + [f"in{i}" for i in range(11)]
    + ["oi", "og", "oh", "on", "os"]
)
GROUP = {name: number for number, name in enumerate(GROUPS)}

CLASSES = [
    "im", "st", "ho", "a2a", "pl", "d3", "rs2", "ns", "sp", "sa", "ps",
    "w4", "k", "k4", "c", "c4", "z", "z4", "ag", "rs", "rs0", "w", "s", "n", "t",
]
CLASS = {name: number for number, name in enumerate(CLASSES)}


def class_of(group):
    if group in CLASS:
        return CLASS[group]
    if group.startswith("rs0"):
        return CLASS["rs0"]
    name = group.rstrip("xyr0123456789.")
    if name in ("m", "z"):
        name = "z"
        return CLASS["z4" if group[len(group.split(".")[0]) - 1] == "4" else "z"]
    return CLASS[name]


def kernel(d, *refs):
    it = iter(refs)
    take = lambda count: [next(it) for _ in range(count)]
    images, w0, w1, w2, w3, *small_in = take(16)
    gi_out, gw0, gw1, gw2, gw3, *small_out = take(8)
    small = hw, ho, gain, shift, hb, ob, tw, pidx, lab, msk, tgt = take(11)
    gi, ghc, gnorm, gsmall = take(4)
    gather, columns_s = take(2)
    (s, s4, wf, y, zb, zhat, d9, u_sel, ut_sel, a2a_s, a2a_r, rs_s, rs_l, pool_own, pool_all, ps_s, ps_r, gi_s, gi_l) = take(19)
    (zg, slope, slope_z, nrm_s, nrm_r, sums_s, sums_r, z4, slope4, slope_z4, sp_own, sp_all) = take(12)
    (gf, cr, zr, hw_s, hp, hg, hcr, hzr, hr, st_s, st_r, start_s, start_r, ho_s, ho_r, rep_s, rep_r, all_s, all_r, norm_s, feat) = take(21)
    ssem, rsem, wrz = take(3)
    w_in, gw = (w0, w1, w2, w3, hw_s), (gw0, gw1, gw2, gw3)
    R, F, Z, rows, half, C, CR, W, PIX, PD, M, PW = d.R, d.F, d.Z, d.rows, d.half, d.C, d.CR, d.W, d.PIX, d.PD, d.M, d.PW
    total = float(M * F)
    root = math.sqrt(total)

    r, f = lax.axis_index("rep"), lax.axis_index("fsdp")
    zc, core = f // 2, f % 2
    sib = (r, zc * 2 + (1 - core))
    rep_peer = lambda k: ((r + k) % R, f)
    one, two = r + 1 - 2 * (r % 2), (r + 2) % R
    both = (one + 2) % R
    at_one, at_two = (one, f), (two, f)
    z_peer = lambda k: (r, ((zc + k) % Z) * 2 + core)
    line = Z == 4
    is_end = (zc == 0) | (zc == Z - 1)
    is_far = lambda k: (zc + k) % Z - zc == Z - 1
    is_far_back = lambda k: zc - (zc + k) % Z == Z - 1
    ends_apart = lambda k: is_far(k) | is_far_back(k)
    my_lanes = pl.ds(pl.multiple_of(r * CR, CR), CR)

    def block(owner):
        return pl.ds(pl.multiple_of(owner * rows, d.row_tile), rows)

    arriving, leaving = {}, {}

    def first_of(ref, count):
        return lambda: ref.at[pl.ds(0, count)]

    volume = {
        "im": first_of(s.at[0], (R - 1) * PD),
        "oi": first_of(s.at[0], PD),
        "st": first_of(start_r, R - 1),
        "ho": first_of(ho_r, F - 1),
        "a2a": lambda: z4.at[:, pl.ds(0, (R - 1) * CR)],
        "ps": lambda: sp_all.at[:, :, pl.ds(0, (R - 1) * CR)],
        "pl": lambda: pool_all.at[:, pl.ds(0, (R - 1) * CR)],
        "d3": first_of(a2a_r, R - 1),
        "rs2": first_of(ps_r, R - 1),
        "ns": lambda: gnorm.at[:, pl.ds(0, (R - 1) * CR)],
        "sp": first_of(rep_r, R - 1),
        "sa": first_of(all_r, F - 1),
        "w4": first_of(hr, R - 1),
        "c4": lambda: hcr,
    }
    for j in range(2):
        for way in ("x0", "y1"):
            volume[f"ag{2 * j}{way}"] = lambda j=j: zg.at[j, pl.ds(0, M // 2), pl.ds(0, CR)]
            volume[f"rs{2 * j + 1}{way}"] = lambda j=j: rs_l.at[j, 0]
        volume[f"ag{2 * j}r"] = lambda j=j: zg.at[j, :, pl.ds(0, 2 * CR)]
        volume[f"rs{2 * j + 1}r"] = lambda j=j: rs_l.at[j, pl.ds(0, 4)]
    volume["rs0x0"] = volume["rs0y1"] = lambda: gi_l.at[0]
    volume["rs0r"] = lambda: gi_l.at[pl.ds(0, 4)]
    for l in range(4):
        volume[f"w{l}x0"] = lambda l=l: gather.at[l, pl.ds(0, half), pl.ds(0, CR)]
        volume[f"w{l}y1"] = lambda l=l: gather.at[l, pl.ds(half, rows - half), pl.ds(0, CR)]
        volume[f"w{l}r"] = lambda l=l: gather.at[l, :, pl.ds(0, (3 if l == 0 and line else 2) * CR)]
    for j in range(4):
        volume[f"s{j}"] = first_of(sums_r.at[j], R - 1)
    for j in range(3):
        volume[f"n{j}"] = first_of(nrm_r.at[j], R - 1)
    for e in range(8):
        volume[f"t{e}"] = first_of(st_r.at[e], F - 1)
    for l in range(4):
        volume[f"c{l}"] = lambda l=l: cr.at[l]

    def wait_for(ref, sem):
        pltpu.make_async_copy(ref, ref, sem).wait()

    def wait_recv(group):
        arriving.pop(group)()

    def wait_send(group):
        leaving.pop(CLASS[group])()

    def when_line(at_end, inside, otherwise):
        if line:
            when(is_end, at_end)
            when(jnp.logical_not(is_end), inside)
        else:
            otherwise()

    def departed(number):
        name = CLASSES[number]
        whole = {
            "c": lambda: cr,
            "c4": lambda: hcr,
            "z": lambda: zr.at[:, pl.ds(0, Z - 1)],
            "z4": lambda: hzr.at[pl.ds(0, Z - 1)],
            "ag": lambda: zg.at[:, :, pl.ds(0, 3 * CR)],
            "rs": lambda: rs_l,
            "rs0": lambda: gi_l,
            "w": lambda: gather.at[:, :, pl.ds(0, 3 * CR)],
            "s": lambda: sums_r.at[:, pl.ds(0, R - 1)],
            "n": lambda: nrm_r.at[:, pl.ds(0, R - 1)],
            "t": lambda: st_r.at[:, pl.ds(0, F - 1)],
        }
        sem = ssem.at[number]
        if name == "k":
            many = lambda count: lambda: wait_for(wf.at[pl.ds(0, 4), pl.ds(0, count * rows)], sem)
            when_line(many(6), many(8), many(2 * Z - 1))
        elif name == "k4":
            many = lambda count: lambda: wait_for(hp.at[pl.ds(0, count)], sem)
            when_line(many(6), many(8), many(2 * Z - 1))
        else:
            wait_for((whole[name] if name in whole else volume[name])(), sem)

    def copy_here(src, dst, group):
        g = GROUP[group]
        arriving[group] = lambda: wait_for(dst, rsem.at[g])
        pltpu.make_async_copy(src, dst, rsem.at[g]).start()

    def send(src, dst, to, group):
        g, out = GROUP[group], class_of(group)
        if group in volume:
            arriving[group] = lambda: wait_for(volume[group](), rsem.at[g])
        leaving[out] = lambda: departed(out)
        pltpu.make_async_remote_copy(
            src_ref=src, dst_ref=dst, send_sem=ssem.at[out], recv_sem=rsem.at[g], device_id=to, device_id_type=MESH
        ).start()

    def over(count, body, first=0):
        if count <= 8:
            for i in range(first, count):
                body(i)
            return

        def step(i, carry):
            body(i)
            return carry

        lax.fori_loop(first, count, step, 0)

    def when(condition, body):
        pl.when(condition)(body)

    def direct(k, body):
        if line and k in (1, Z - 1):
            when(jnp.logical_not(ends_apart(k)), body)
        else:
            body()

    def drain():
        for waits in (arriving, leaving):
            for wait in list(waits.values()):
                wait()

    for i, (src, dst) in enumerate(zip(small_in, small)):
        copy_here(src, dst, f"in{i}")

    barrier = pltpu.get_barrier_semaphore()
    over(R, lambda k: pl.semaphore_signal(barrier, inc=1, device_id=rep_peer(k), device_id_type=MESH), 1)
    over(F, lambda k: pl.semaphore_signal(barrier, inc=1, device_id=(r, (f + k) % F), device_id_type=MESH), 1)
    pl.semaphore_wait(barrier, R + F - 2)

    pieces = range(d.pieces)

    def cut(l, h):
        size = rows if l < 4 else half
        first = -(-size // (d.pieces * d.row_tile)) * d.row_tile
        return (0, first) if h == 0 else (first, size - first)

    def cut_at(l, h):
        first, size = cut(l, h)
        return pl.ds(first, size)

    near = sorted({1, Z - 1})
    beyond = list(range(2, Z - 1))

    def w_block(l, owner, h):
        first, size = cut(l, h)
        if l < 4:
            return wf.at[l, pl.ds(pl.multiple_of(owner * rows + first, d.row_tile), size)]
        return hp.at[owner, pl.ds(first, size)]

    def w_copy(l, h, src, owner, to, recv_sem):
        out = CLASS["k" if l < 4 else "k4"]
        leaving[out] = lambda: departed(out)
        return pltpu.make_async_remote_copy(
            src_ref=src, dst_ref=w_block(l, owner, h), send_sem=ssem.at[out], recv_sem=recv_sem, device_id=to,
            device_id_type=MESH,
        )

    def w_to_core(l, h, src, owner):
        w_copy(l, h, src, owner, sib, rsem.at[GROUP[f"k{l}"]]).start()

    def w_src(l, h):
        return w_in[l].at[cut_at(l, h), my_lanes] if l < 4 else hw_s.at[cut_at(l, h)]

    def w_wait(l, h, sem):
        wait_for(w_block(l, f, h), sem)

    def w_send(l, h, k, who=lambda body: body()):
        u = l * d.pieces + h
        arriving["z", l, h, k] = lambda: direct(Z - k, lambda: w_wait(l, h, wrz.at[u, k]))
        start = lambda: w_copy(l, h, w_src(l, h), f, z_peer(k), wrz.at[u, k]).start()
        who(lambda: direct(k, start))

    def w_push_near(l):
        for h in pieces:
            for k in near:
                w_send(l, h, k)
            w_to_core(l, h, w_src(l, h), f)
        copy_here(w_in[l].at[:, my_lanes] if l < 4 else hw_s, wf.at[l, block(f)] if l < 4 else hp.at[f], f"o{l}")

    def w_push_rest(l, hs=pieces, who=lambda body: body()):
        for h in hs:
            for k in beyond:
                w_send(l, h, k, who)

    def at_ends(body):
        if line:
            when(is_end, body)
        else:
            body()

    def between(body):
        if line:
            when(jnp.logical_not(is_end), body)

    def w_arrived(l, h, k):
        u = l * d.pieces + h
        owner = ((zc + Z - k) % Z) * 2 + core
        w_wait(l, h, wrz.at[u, k])
        w_to_core(l, h, w_block(l, owner, h), owner)

    def w_relay_rest(l, hs=pieces):
        for h in hs:
            u = l * d.pieces + h
            for k in beyond:
                arriving.pop(("z", l, h, k))
                w_arrived(l, h, k)
            if line:

                def hand_on():
                    to = (Z - 1) * (zc - 1)
                    owner = (Z - 1 - to) * 2 + core
                    slot = jnp.where(zc == 1, 1, Z - 1)
                    w_copy(l, h, w_block(l, owner, h), owner, (r, to * 2 + core), wrz.at[u, slot]).start()

                when(jnp.logical_not(is_end), hand_on)

    def w_relay_near(l):
        for h in pieces:
            for k in near:
                arriving.pop(("z", l, h, k))
                direct(Z - k, lambda: w_arrived(l, h, k))

    def w_far(l):
        if line:
            for h in pieces:
                when(zc == 0, lambda: w_arrived(l, h, 1))
                when(zc == Z - 1, lambda: w_arrived(l, h, Z - 1))

    def w_finish(l):
        one = GROUP[f"k{l}"]
        wait_for(wf.at[l, pl.ds(0, Z * rows)] if l < 4 else hp.at[pl.ds(0, Z)], rsem.at[one])
        wait_recv(f"o{l}")

    w_push_rest(0)
    w_push_near(0)
    over(R, lambda k: send(images, s.at[0, pl.ds(pl.multiple_of(r * PD, PD), PD)], rep_peer(k), "im"), 1)
    own_rows = s.at[0, pl.ds(pl.multiple_of(r * PD, PD), PD)]
    copy_here(images, own_rows, "oi")

    for i in range(len(small)):
        wait_recv(f"in{i}")
    start_s[...] = jnp.zeros_like(start_s)
    masks = jnp.concatenate([msk[:, i, :] for i in range(d.n)], axis=1).astype(F32)
    labels = jnp.concatenate([lab[i : i + 1, :] for i in range(d.n)], axis=1).astype(F32)
    wanted = jnp.concatenate([tgt[i] for i in range(d.n)], axis=1)
    pools = jnp.concatenate([pidx[i : i + 1, :] for i in range(d.n)], axis=1).astype(F32)
    counted = jnp.sum(masks, axis=1, keepdims=True)
    lane = lax.broadcasted_iota(jnp.int32, (1, LANES), 1)
    start_s[0:1, :] = sum(jnp.where(lane == t, counted[t : t + 1, :], 0.0) for t in range(3))
    start_s[1:2, 0 : PW // R] = pools
    over(R, lambda k: send(start_s, start_r.at[r], rep_peer(k), "st"), 1)
    start_r[r] = start_s[...]
    ho_s[...] = jnp.zeros_like(ho_s)
    ho_s[0 : d.q, 0 : d.OC] = ho[...].astype(F32)
    over(F, lambda k: send(ho_s, ho_r.at[f], (r, (f + k) % F), "ho"), 1)
    ho_r[f] = ho_s[...]
    def pack_head():
        wide = -(-rows // LANES) * LANES
        tall = jnp.concatenate([hw[...].astype(F32), jnp.zeros((LANES - d.HC, rows), F32)], axis=0)
        if wide > rows:
            tall = jnp.concatenate([tall, jnp.zeros((LANES, wide - rows), F32)], axis=1)
        tall = jnp.transpose(tall)
        if wide < 2 * half:
            tall = jnp.concatenate([tall, jnp.zeros((2 * half - wide, LANES), F32)], axis=0)
        hw_s[...] = (tall[0:half] + pltpu.roll(tall[half : 2 * half], d.HC, 1)).astype(hw_s.dtype)

    bits = W.bit_length() - 1

    def places(axis, shape):
        q = lax.broadcasted_iota(jnp.int32, shape, axis)
        image = jnp.zeros(shape, jnp.int32)
        for i in range(1, M // PIX):
            image = image + jnp.where(q >= i * PIX, 1, 0)
        q = q - image * PIX
        window = image * (PIX // 4) + (q >> (bits + 1)) * (W // 2) + ((q & (W - 1)) >> 1)
        position = 2 * ((q >> bits) & 1) + (q & 1)
        return window, position.astype(F32)

    def windows(rows_first):
        shape = (M, PW) if rows_first else (PW, M)
        window, position = places(0 if rows_first else 1, shape)
        other = lax.broadcasted_iota(jnp.int32, shape, 1 if rows_first else 0)
        return window == other, position

    def pixel_columns():
        feat[...] = jnp.zeros_like(feat)
        feat[0:1, 0:PD] = labels
        feat[1:4, 0:PD] = masks
        feat[4:8, 0:PD] = wanted
        columns_s[...] = jnp.transpose(feat[...])[0:PD, 0:LANES]

    def pool_matrices():
        feat[...] = jnp.zeros_like(feat)
        for i in range(R):
            feat[0:1, i * (PW // R) : (i + 1) * (PW // R)] = start_r[i, 1:2, 0 : PW // R]
        picked_row = feat[0:1, 0:PW]
        picked_col = jnp.transpose(feat[...])[0:PW, 0:1]
        inside, position = windows(True)
        u_sel[...] = jnp.where(inside & (position == picked_row), 1.0, 0.0).astype(BF16)
        inside, position = windows(False)
        ut_sel[...] = jnp.where(inside & (position == picked_col), 1.0, 0.0).astype(BF16)

    def image_rows(i):
        return pl.ds(pl.multiple_of(i * PIX, PIX), PIX)

    def per_image(count, body, init):
        return lax.fori_loop(0, count, body, init, unroll=True)

    def column_of(shape):
        return lax.broadcasted_iota(jnp.int32, shape, 0) & (W - 1)

    blank = jnp.zeros((W, CR), F32)

    def conv(src, count, l, out):
        height = count * PIX
        for kx in range(3):
            taps = [wf[l, (3 * ky + kx) * C : (3 * ky + kx + 1) * C, :].astype(BF16) for ky in range(3)]
            y[0:height, kx * 3 * CR : (kx + 1) * 3 * CR] = jnp.dot(
                src[...], jnp.concatenate(taps, axis=1), preferred_element_type=F32
            )

        def body(i, summed):
            at = image_rows(i)
            col = column_of((PIX, CR))
            parts = []
            for kx in range(3):
                up, mid, down = (y[at, (kx * 3 + ky) * CR : (kx * 3 + ky + 1) * CR] for ky in range(3))
                parts.append(
                    mid
                    + jnp.concatenate([blank, up[: PIX - W]], axis=0)
                    + jnp.concatenate([down[W:], blank], axis=0)
                )
            z = (
                parts[1]
                + jnp.where(col > 0, pltpu.roll(parts[0], 1, 0), 0.0)
                + jnp.where(col < W - 1, pltpu.roll(parts[2], PIX - 1, 0), 0.0)
            )
            out[at, :] = z
            return summed + jnp.sum(z, axis=0, keepdims=True)

        return per_image(count, body, jnp.zeros((1, CR), F32))

    def spread_taps(i, grad):
        at = image_rows(i)
        col = column_of((PIX, CR))
        moved = (
            jnp.where(col < W - 1, pltpu.roll(grad, PIX - 1, 0), 0.0),
            grad,
            jnp.where(col > 0, pltpu.roll(grad, 1, 0), 0.0),
        )
        low_blank = blank.astype(BF16)
        for kx in range(3):
            low = moved[kx].astype(BF16)
            nine = (
                jnp.concatenate([low[W:], low_blank], axis=0),
                low,
                jnp.concatenate([low_blank, low[: PIX - W]], axis=0),
            )
            for ky in range(3):
                d9[at, (ky * 3 + kx) * CR : (ky * 3 + kx + 1) * CR] = nine[ky]

    def data_grad(l, height, write):
        step = 2 * CR
        for half in range(C // step):
            taps = [
                wf[l, t * C + half * step : t * C + (half + 1) * step, :].astype(BF16)
                for t in range(9)
            ]
            part = lax.dot_general(
                d9[0:height, :],
                jnp.concatenate(taps, axis=1),
                (((1,), (1,)), ((), ())),
                preferred_element_type=F32,
            )
            write(half, part)

    def lanes_of(owner):
        return pl.ds(pl.multiple_of(owner * CR, CR), CR)

    def gather_start(name, piece):
        send(piece(r, 0), piece(r, 0), at_one, f"{name}x0")
        send(piece(r, 1), piece(r, 1), at_two, f"{name}y1")
        send(piece(r, 1), piece(r, 1), at_one, f"{name}r")
        send(piece(r, 0), piece(r, 0), at_two, f"{name}r")

    def gather_forward(name, piece):
        wait_recv(f"{name}x0")
        send(piece(one, 0), piece(one, 0), at_two, f"{name}r")
        wait_recv(f"{name}y1")
        send(piece(two, 1), piece(two, 1), at_one, f"{name}r")

    def await_rest(name):
        wait_recv(f"{name}r")

    def scatter_start(name, piece, land):
        send(piece(both, 0), land(0), at_one, f"{name}x0")
        send(piece(both, 1), land(2), at_two, f"{name}y1")
        send(piece(one, 0), land(1), at_one, f"{name}r")
        send(piece(two, 1), land(3), at_two, f"{name}r")

    def scatter_forward(name, piece, land):
        for way, ref, came, dst, to in (
            ("x0", piece(two, 0), land(0), land(4), at_two),
            ("y1", piece(one, 1), land(2), land(5), at_one),
        ):
            wait_recv(f"{name}{way}")
            ref[...] = (ref[...].astype(F32) + came[...].astype(F32)).astype(ref.dtype)
            send(ref, dst, to, f"{name}r")

    def ag_piece(j):
        return lambda owner, h: zg.at[j, pl.ds(h * (M // 2), M // 2), lanes_of(owner)]

    def rows_piece(l):
        return lambda owner, h: gather.at[l, pl.ds(h * half, half if h == 0 else rows - half), lanes_of(owner)]

    def rs_piece(j):
        return lambda owner, h: rs_s.at[j, owner, pl.ds(h * (M // 2), M // 2)]

    def rs_land(j):
        return lambda i: rs_l.at[j, i]

    def gi_piece(owner, h):
        return gi_s.at[owner, pl.ds(h * (PD // 2), PD // 2)]

    def gi_land(i):
        return gi_l.at[i]

    def sigmoid(v):
        return 0.5 * jnp.tanh(0.5 * v) + 0.5

    def g_block(l, owner):
        return gf.at[l, block(owner)] if l < 4 else hg.at[owner]

    def from_core(l):
        return cr.at[l] if l < 4 else hcr

    def from_z(l, i, h):
        return zr.at[l, i, cut_at(l, h)] if l < 4 else hzr.at[i, cut_at(l, h)]

    def g_piece(l, owner, h):
        first, size = cut(l, h)
        if l < 4:
            return gf.at[l, pl.ds(pl.multiple_of(owner * rows + first, d.row_tile), size)]
        return hg.at[owner, pl.ds(first, size)]

    def weight_grad(l, src, height):
        to_core = lambda k: send(g_block(l, 2 * k + 1 - core), from_core(l).at[k], sib, f"c{l}")
        sent = 0
        for ky in range(3):
            part = lax.dot_general(
                src[...],
                d9[0:height, ky * 3 * CR : (ky + 1) * 3 * CR],
                (((0,), (0,)), ((), ())),
                preferred_element_type=F32,
            )
            for kx in range(3):
                t = 3 * ky + kx
                gf[l % 4, t * C : (t + 1) * C, :] = part[:, kx * CR : (kx + 1) * CR].astype(gf.dtype)
            while l < 4 and sent < Z and 2 * (sent + 1) * rows <= (ky + 1) * 3 * C:
                to_core(sent)
                sent += 1
        if l == 4:

            def pack(i, carry):
                at = i * rows
                low = gf[0, pl.ds(pl.multiple_of(at, d.row_tile), half), :].astype(F32)
                high = gf[0, pl.ds(pl.multiple_of(at + half, d.row_tile), rows - half), :].astype(F32)
                if rows < 2 * half:
                    high = jnp.concatenate([high, jnp.zeros((2 * half - rows, CR), F32)], axis=0)
                hg[i] = (low + pltpu.roll(high, d.HC, 1)).astype(hg.dtype)
                return carry

            lax.fori_loop(0, F, pack, 0)
            over(Z, to_core)

    def core_sum(l):
        wait_recv(f"c{l}")

        def step(k):
            ref = g_block(l, 2 * k + core)
            ref[...] = (ref[...].astype(F32) + from_core(l)[k].astype(F32)).astype(ref.dtype)

        over(Z, step)

    def z_push(l):
        for h in pieces:
            z_push_middle(l, h)
        for h in pieces:
            z_push_piece(l, h)

    def z_push_middle(l, h):
        if line:

            def to_middle():
                through, owner = jnp.where(zc == 0, 1, Z - 2), Z - 1 - zc
                send(g_piece(l, 2 * owner + core, h), from_z(l, through, h), (r, 2 * through + core), f"m{l}.{h}")

            when(is_end, to_middle)
            g = GROUP[f"m{l}.{h}"]
            arriving[f"m{l}.{h}"] = lambda: when(
                jnp.logical_not(is_end), lambda: wait_for(from_z(l, 0, h), rsem.at[g])
            )

    def z_push_piece(l, h):
        def push(k):
            to = (zc + k) % Z
            send(g_piece(l, 2 * to + core, h), from_z(l, zc, h), (r, 2 * to + core), f"z{l}.{h}")

        for k in range(1, Z) if Z <= 8 else ():
            if line and k == 2:
                when(is_end, lambda: push(2))
            else:
                direct(k, lambda: push(k))
        if Z > 8:
            over(Z, push, 1)
        arriving[f"z{l}.{h}"] = lambda: z_wait(l, h, rsem.at[GROUP[f"z{l}.{h}"]])

    def z_middle(l):
        for h in pieces:
            z_middle_piece(l, h)

    def z_middle_piece(l, h):
        if line:
            wait_recv(f"m{l}.{h}")

            def hand_on():
                owner = (Z - 1) * (Z - 2 - zc)
                ref = g_piece(l, 2 * owner + core, h)
                ref[...] = (ref[...].astype(F32) + from_z(l, zc, h)[...].astype(F32)).astype(ref.dtype)
                send(ref, from_z(l, zc, h), (r, 2 * owner + core), f"z{l}.{h}")

            when(jnp.logical_not(is_end), hand_on)

    def z_wait(l, h, sem):
        first, size = cut(l, h)
        many = lambda count: (zr.at[l, pl.ds(0, count), cut_at(l, h)] if l < 4 else hzr.at[pl.ds(0, count), cut_at(l, h)])
        if line:
            when(is_end, lambda: wait_for(many(Z - 2), sem))
            when(jnp.logical_not(is_end), lambda: wait_for(many(Z - 1), sem))
        else:
            wait_for(many(Z - 1), sem)

    def z_sum(l):
        for h in pieces:
            z_sum_piece(l, h)
        if l < 4:
            gather_start(f"w{l}", rows_piece(l))
        else:
            over(R, lambda k: send(hr.at[r], hr.at[r], rep_peer(k), "w4"), 1)

    def z_sum_piece(l, h):
        wait_recv(f"z{l}.{h}")
        read = lambda i: from_z(l, i, h)[...].astype(F32)
        summed = g_piece(l, f, h)[...].astype(F32)
        if line:
            one_side = jnp.where(zc == 0, 1, jnp.where(zc == Z - 1, Z - 2, zc - 1))
            other_side = jnp.where(zc == 0, 2, jnp.where(zc == Z - 1, 1, zc + 1))
            opposite = jnp.where(zc == 1, Z - 1, 0)
            summed = summed + read(one_side) + read(other_side) + jnp.where(is_end, 0.0, read(opposite))
        else:
            summed = lax.fori_loop(1, Z, lambda k, so_far: so_far + read((zc + k) % Z), summed)
        summed = summed * (1.0 / root)
        if l < 4:
            gather[l, cut_at(l, h), my_lanes] = summed.astype(gather.dtype)
        else:
            hr[r, cut_at(l, h)] = summed.astype(hr.dtype)

    def rows_done(l):
        if l < 4:
            await_rest(f"w{l}")
            copy_here(gather.at[l], gw[l], f"u{l}")
        else:
            wait_recv("w4")
            summed = sum(hr[i].astype(F32) for i in range(R))
            wide = -(-half // LANES) * LANES
            if wide > half:
                summed = jnp.concatenate([summed, jnp.zeros((wide - half, LANES), F32)], axis=0)
            summed = jnp.transpose(summed)
            ghc[:, 0:half] = summed[0 : d.HC, 0:half]
            ghc[:, half:rows] = summed[d.HC : 2 * d.HC, 0 : rows - half]

    def exchange(e):
        over(F, lambda k: send(st_s.at[e], st_r.at[e, f], (r, (f + k) % F), f"t{e}"), 1)
        st_r[e, f] = st_s[e]

    def exchanged(e):
        wait_recv(f"t{e}")
        return st_r[e]

    st_s[...] = jnp.zeros_like(st_s)
    w_relay_rest(0)
    w_relay_near(0)
    w_far(0)
    w_push_rest(1, who=at_ends)
    wait_recv("im")
    wait_recv("oi")
    wait_recv("st")

    rep_all = lambda src, dst, group: over(R, lambda k: send(src, dst, rep_peer(k), group), 1)
    images_here = M // PIX
    inverse_of, counts = [], None

    def widened(j, i, b):
        value = zg[j, image_rows(i), b * CR : (b + 1) * CR].astype(F32)
        return value, [nrm_r[j, b, k : k + 1, :] for k in range(4)]

    def slopes_of(j):
        def body(i, carry):
            for b in range(R):
                value, (a, o, inverse, off) = widened(j, i, b)
                shaped = value * a + o
                squashed = sigmoid(shaped)
                steep = squashed + shaped * squashed * (1.0 - squashed)
                slope[j, image_rows(i), b * CR : (b + 1) * CR] = steep.astype(BF16)
                slope_z[j, image_rows(i), b * CR : (b + 1) * CR] = (steep * (value * inverse + off)).astype(BF16)
            return carry

        per_image(images_here, body, 0)

    def rows_of(l):
        return gain[l : l + 1, my_lanes], shift[l : l + 1, my_lanes]

    def slope_here(l, at):
        g_row, b_row = rows_of(l)
        normed = zhat[l, at, :]
        shaped = normed * g_row + b_row
        squashed = sigmoid(shaped)
        return normed, squashed + shaped * squashed * (1.0 - squashed)

    def pool_slopes():
        def body(i, carry):
            at = image_rows(i)
            normed, steep = slope_here(1, at)
            y[at, 0:CR] = steep
            y[at, CR : 2 * CR] = steep * normed
            return carry

        per_image(images_here, body, 0)
        inside, unused = windows(False)
        averaged = jnp.dot(
            jnp.where(inside, 0.25, 0.0), y[:, 0 : 2 * CR], precision=EXACT, preferred_element_type=F32
        ).astype(BF16)
        for k in range(2):
            sp_own[k] = averaged[:, k * CR : (k + 1) * CR]
            sp_all[k, :, my_lanes] = averaged[:, k * CR : (k + 1) * CR]
        rep_all(sp_own, sp_all.at[:, :, my_lanes], "ps")

    for l in range(4):
        w_finish(l)
        if l == 2:
            wait_recv("pl")
            s[2] = jnp.dot(u_sel[...], pool_all[...], preferred_element_type=F32).astype(BF16)
        first = conv(s.at[l], images_here, l, zb)
        mean_here = first * (1.0 / M)
        gathers = l in (0, 2)
        ahead = l != 1
        j = 2 if l == 3 else l // 2

        def squares(i, so_far):
            apart = zb[image_rows(i), :] - mean_here
            if gathers:
                zg[j, image_rows(i), my_lanes] = apart.astype(BF16)
            elif l == 3:
                a2a_s[i] = apart.astype(BF16)
            return so_far + jnp.sum(jnp.square(apart), axis=0, keepdims=True)

        squared = per_image(images_here, squares, jnp.zeros((1, CR), F32))
        if gathers:
            gather_start(f"ag{l}", ag_piece(j))
        elif l == 3:
            over(R, lambda k: send(a2a_s.at[(r + k) % R], z4.at[:, my_lanes], rep_peer(k), "a2a"), 1)
            z4[:, my_lanes] = a2a_s[r]
        st_s[l, 0:1, :] = first
        st_s[l, 1:2, :] = squared
        if l == 0:
            st_s[l, 2:3, :] = sum(start_r[i, 0:1, :] for i in range(R))
        exchange(l)
        if l == 0:
            w_push_rest(1, who=between)
            w_push_near(1)
            w_relay_rest(1)
        elif l < 3:
            w_push_rest(l + 1, pieces[1:])
            w_push_near(l + 1)
            w_relay_rest(l + 1, pieces[:1])
        else:
            w_push_near(4)
            w_relay_rest(4)
        if gathers:
            gather_forward(f"ag{l}", ag_piece(j))
        elif l == 1:
            pixel_columns()
        else:
            slopes_of(1)
        parts = exchanged(l)
        tot = jnp.sum(parts, axis=0)
        mean = tot[0:1] * (1.0 / total)
        apart = jnp.sum(jnp.square(parts * (1.0 / M) - mean[None]), axis=0)[0:1] * float(M)
        inverse = lax.rsqrt((tot[1:2] + apart) * (1.0 / total) + EPS)
        inverse_of.append(inverse)
        if l == 0:
            counts = tot[2:3]
        g_row, b_row = gain[l : l + 1, my_lanes], shift[l : l + 1, my_lanes]
        if ahead:
            off = (mean_here - mean) * inverse
            nrm_s[j, 0:1, :] = inverse * g_row
            nrm_s[j, 1:2, :] = off * g_row + b_row
            nrm_s[j, 2:3, :] = inverse
            nrm_s[j, 3:4, :] = off
            rep_all(nrm_s.at[j], nrm_r.at[j, r], f"n{j}")
            nrm_r[j, r] = nrm_s[j]

        def activate(i, carry):
            at = image_rows(i)
            normed = (zb[at, :] - mean) * inverse
            zhat[l, at, :] = normed
            shaped = normed * g_row + b_row
            hidden = shaped * sigmoid(shaped)
            zb[at, :] = hidden
            return carry

        def keep_normed(i, carry):
            zhat[l, image_rows(i), :] = (zb[image_rows(i), :] - mean) * inverse
            return carry

        def activate_all(i, carry):
            for b in range(R):
                value, (a, o, unused, also) = widened(j, i, b)
                shaped = value * a + o
                s[l + 1, image_rows(i), b * CR : (b + 1) * CR] = (shaped * sigmoid(shaped)).astype(BF16)
            return carry

        per_image(images_here, keep_normed if ahead else activate, 0)
        if l == 1:
            inside, unused = windows(False)
            pooled = jnp.dot(
                jnp.where(inside, 0.25, 0.0), zb[...], precision=EXACT, preferred_element_type=F32
            )
            pool_own[...] = pooled.astype(BF16)
            pool_all[:, my_lanes] = pooled.astype(BF16)
            rep_all(pool_own, pool_all.at[:, my_lanes], "pl")
            w_relay_rest(2, pieces[1:])
            pool_slopes()
            slopes_of(0)
        elif l == 0:
            pool_matrices()
        elif l == 2:
            w_relay_rest(3, pieces[1:])
            pack_head()
        w_relay_near(l + 1)
        if l < 2:
            w_push_rest(l + 2, pieces[:1])
        elif l == 2:
            w_push_rest(4)
        w_far(l + 1)
        if gathers:
            wait_recv(f"n{j}")
            await_rest(f"ag{l}")
            per_image(images_here, activate_all, 0)

    w_finish(4)
    low_lanes = lax.broadcasted_iota(jnp.int32, (half, LANES), 1) < d.HC

    def unpack(i, carry):
        both = hp[i].astype(F32)
        at = i * rows
        wf[4, pl.ds(pl.multiple_of(at, d.row_tile), half), :] = jnp.where(low_lanes, both, 0.0).astype(wf.dtype)
        high = jnp.where(low_lanes, pltpu.roll(both, d.HC, 1), 0.0).astype(wf.dtype)
        wf[4, pl.ds(pl.multiple_of(at + half, d.row_tile), rows - half), :] = high[0 : rows - half]
        return carry

    lax.fori_loop(0, F, unpack, 0)
    wait_recv("n2")
    wait_recv("a2a")

    def activate_own(i, carry):
        at = image_rows(i)
        for b in range(R):
            lanes = slice(b * CR, (b + 1) * CR)
            value = z4[at, lanes].astype(F32)
            a, o, inverse, off = [nrm_r[2, b, k : k + 1, :] for k in range(4)]
            shaped = value * a + o
            squashed = sigmoid(shaped)
            s4[at, lanes] = (shaped * squashed).astype(BF16)
            steep = squashed + shaped * squashed * (1.0 - squashed)
            slope4[at, lanes] = steep.astype(BF16)
            slope_z4[at, lanes] = (steep * (value * inverse + off)).astype(BF16)
        return carry

    per_image(PD // PIX, activate_own, 0)
    wait_recv("ho")
    conv(s4, PD // PIX, 4, zb)
    head_bias = jnp.concatenate([hb[...], jnp.zeros((1, CR - d.HC), F32)], axis=1)
    out_bias = jnp.concatenate([ob[...], jnp.zeros((1, CR - d.OC), F32)], axis=1)
    head_raw = zb[0:PD, :] + head_bias
    squashed = sigmoid(head_raw)
    head_act = head_raw * squashed
    project = jnp.concatenate([ho_r[i][0 : d.q] for i in range(F)] + [jnp.zeros((LANES - d.HC, LANES), F32)], axis=0)
    out = jnp.dot(head_act, project, precision=EXACT, preferred_element_type=F32) + out_bias
    lane = lax.broadcasted_iota(jnp.int32, (PD, LANES), 1)
    classes = d.OC - 4
    factor = total * jnp.concatenate([tw[...], jnp.zeros((1, LANES - 3), F32)], axis=1) / jnp.maximum(counts, 1.0)
    pixel = [columns_s[:, i : i + 1] for i in range(8)]
    is_class = lane < classes
    top = jnp.max(jnp.where(is_class, out, -jnp.inf), axis=1, keepdims=True)
    grown = jnp.where(is_class, jnp.exp(jnp.where(is_class, out - top, 0.0)), 0.0)
    likely = grown / jnp.sum(grown, axis=1, keepdims=True)
    onehot = jnp.where(lane.astype(F32) == pixel[0], 1.0, 0.0)
    grad_class = factor[:, 0:1] * pixel[1] * (likely - onehot)
    misfit = out - pixel[4]
    grad_depth = factor[:, 1:2] * pixel[2] * misfit / jnp.sqrt(misfit * misfit + 1.0)
    is_normal = (lane > classes) & (lane < d.OC)
    predicted = jnp.where(is_normal, out, 0.0)
    wanted = sum(jnp.where(lane == classes + 1 + i, pixel[5 + i], 0.0) for i in range(3))
    radius = jnp.sqrt(jnp.sum(predicted * predicted, axis=1, keepdims=True) + 1.0)
    aligned = jnp.sum(predicted * wanted, axis=1, keepdims=True)
    grad_normal = -(factor[:, 2:3] * pixel[3]) * (wanted / radius - aligned / (radius * radius * radius) * predicted)
    grad_out = jnp.where(
        is_class, grad_class, jnp.where(lane == classes, grad_depth, jnp.where(is_normal, grad_normal, 0.0))
    )
    grad_act = lax.dot_general(
        grad_out, project, (((1,), (1,)), ((), ())), precision=EXACT, preferred_element_type=F32
    )
    grad_head = (grad_act * (squashed + head_raw * squashed * (1.0 - squashed))).astype(BF16).astype(F32)
    zb[0:PD, :] = grad_head
    y[0:PD, 0:CR] = head_act
    y[0:PD, CR : 2 * CR] = grad_out

    def spread_head(i, carry):
        spread_taps(i, zb[image_rows(i), :])
        return carry

    per_image(PD // PIX, spread_head, 0)

    def put_sums(j, n, grad, steep, steep_z):
        sums_s[j, n, 0:1, :] = jnp.sum(grad * steep.astype(F32), axis=0, keepdims=True)
        sums_s[j, n, 1:2, :] = jnp.sum(grad * steep_z.astype(F32), axis=0, keepdims=True)

    def send_sums(j):
        over(R, lambda k: send(sums_s.at[j, (r + k) % R], sums_r.at[j, r], rep_peer(k), f"s{j}"), 1)
        sums_r[j, r] = sums_s[j, r]

    def pass_sums(j, e):
        wait_recv(f"s{j}")
        st_s[e, 0:2, :] = sum(sums_r[j, i, 0:2, :] for i in range(R))
        exchange(e)

    def write_dh3(part_at, part):
        for b in range(2):
            n = 2 * part_at + b
            grad = part[:, b * CR : (b + 1) * CR]
            cols = slice(n * CR, (n + 1) * CR)
            a2a_s[n] = grad.astype(BF16)
            put_sums(2, n, grad, slope4[:, cols], slope_z4[:, cols])

    wait_send("a2a")
    data_grad(4, PD, write_dh3)
    send_sums(2)
    over(R, lambda k: send(a2a_s.at[(r + k) % R], a2a_r.at[r], rep_peer(k), "d3"), 1)
    a2a_r[r] = a2a_s[r]
    weight_grad(4, s4, PD)
    head_act, grad_out = y[0:PD, 0:CR], y[0:PD, CR : 2 * CR]
    pad = jnp.zeros((2 * LANES - PD, LANES), F32)
    act_t = jnp.transpose(jnp.concatenate([head_act, pad], axis=0))[:, 0:PD]
    rep_s[0 : d.HC, :] = jnp.dot(act_t, grad_out, precision=EXACT, preferred_element_type=F32)[0 : d.HC]
    rep_s[d.HC : d.HC + 8, :] = jnp.zeros((8, LANES), F32)
    rep_s[d.HC : d.HC + 1, :] = jnp.sum(zb[0:PD, :], axis=0, keepdims=True)
    rep_s[d.HC + 1 : d.HC + 2, :] = jnp.sum(grad_out, axis=0, keepdims=True)
    over(R, lambda k: send(rep_s, rep_r.at[r], rep_peer(k), "sp"), 1)
    rep_r[r] = rep_s[...]

    def head_small():
        wait_recv("sp")
        summed = sum(rep_r[i] for i in range(R))
        for i in range(F):
            all_s[i, 0 : d.q, :] = summed[i * d.q : (i + 1) * d.q]
            if d.q < 8:
                all_s[i, d.q : 8, :] = jnp.zeros((8 - d.q, LANES), F32)
            all_s[i, 8:16, :] = summed[d.HC : d.HC + 8]
        over(F, lambda k: send(all_s.at[(f + k) % F], all_r.at[f], (r, (f + k) % F), "sa"), 1)
        all_r[f] = all_s[f]

    def through_norm(l, grad_of):
        tot = jnp.sum(exchanged(7 - l), axis=0)
        bias_sum, gain_sum = tot[0:1], tot[1:2]
        norm_s[l : l + 1, :] = gain_sum * (1.0 / root)
        norm_s[4 + l : 5 + l, :] = bias_sum * (1.0 / root)
        scale = inverse_of[l] * rows_of(l)[0]
        if l in (0, 2):
            await_rest(f"rs{l + 1}")
        elif l == 3:
            wait_recv("d3")

        def body(i, carry):
            at = image_rows(i)
            normed, grad = grad_of(i, at)
            spread_taps(i, scale * (grad - bias_sum * (1.0 / total) - normed * (gain_sum * (1.0 / total))))
            return carry

        per_image(images_here, body, 0)

    def from_scatter(l):
        j = l // 2
        here = images_here // 2

        def grad_of(i, at):
            normed, steep = slope_here(l, at)
            h = i // here
            local = image_rows(i - h * here)
            grad = (
                rs_s[j, r, at, :].astype(F32)
                + rs_l[j, 1 + 2 * h, local, :].astype(F32)
                + rs_l[j, 4 + h, local, :].astype(F32)
            )
            return normed, grad * steep

        return grad_of

    def layer_down(l):
        j = (l - 1) // 2

        def write(part_at, part):
            for b in range(2):
                n = 2 * part_at + b
                grad = part[:, b * CR : (b + 1) * CR]
                rs_s[j, n] = grad.astype(BF16)
                cols = slice(n * CR, (n + 1) * CR)
                put_sums(j, n, grad, slope[j, :, cols], slope_z[j, :, cols])

        data_grad(l, M, write)
        send_sums(j)
        scatter_start(f"rs{l}", rs_piece(j), rs_land(j))
        z_middle_piece(l + 1, 0)
        weight_grad(l, s.at[l], M)
        pass_sums(j, 7 - (l - 1))
        scatter_forward(f"rs{l}", rs_piece(j), rs_land(j))
        for h in pieces[1:]:
            z_middle_piece(l + 1, h)

    def from_head(i, at):
        normed, steep = slope_here(3, at)
        return normed, a2a_r[i].astype(F32) * steep

    pass_sums(2, 4)
    core_sum(4)
    z_push(4)
    head_small()
    through_norm(3, from_head)
    layer_down(3)
    core_sum(3)
    z_push(3)
    z_sum(4)

    through_norm(2, from_scatter(2))

    def write_pooled(part_at, part):
        chosen = jnp.dot(ut_sel[...], part.astype(BF16), preferred_element_type=F32)
        for b in range(2):
            n = 2 * part_at + b
            grad = chosen[:, b * CR : (b + 1) * CR]
            cols = slice(n * CR, (n + 1) * CR)
            ps_s[n] = grad.astype(BF16)
            put_sums(3, n, grad, sp_all[0, :, cols], sp_all[1, :, cols])

    wait_recv("ps")
    data_grad(2, M, write_pooled)
    send_sums(3)
    z_middle(3)
    over(R, lambda k: send(ps_s.at[(r + k) % R], ps_r.at[r], rep_peer(k), "rs2"), 1)
    ps_r[r] = ps_s[r]
    weight_grad(2, s.at[2], M)
    pass_sums(3, 6)
    core_sum(2)
    z_push(2)
    wait_recv("rs2")
    pooled = sum(ps_r[i].astype(F32) for i in range(R))
    inside, unused = windows(True)
    zb[...] = jnp.dot(jnp.where(inside, 0.25, 0.0), pooled, precision=EXACT, preferred_element_type=F32)

    def from_pool(i, at):
        normed, steep = slope_here(1, at)
        return normed, zb[at, :] * steep

    through_norm(1, from_pool)
    layer_down(1)
    z_sum(3)
    core_sum(1)
    z_push(1)
    gather_forward("w3", rows_piece(3))
    z_sum(2)

    through_norm(0, from_scatter(0))
    def write_images(part_at, part):
        for i in range(R):
            gi_s[i, :, part_at * 2 * CR : (part_at + 1) * 2 * CR] = part[i * PD : (i + 1) * PD].astype(BF16)

    data_grad(0, M, write_images)
    scatter_start("rs0", gi_piece, gi_land)
    weight_grad(0, s.at[0], M)
    gather_forward("w2", rows_piece(2))
    z_middle(1)
    core_sum(0)
    z_push(0)

    gnorm[:, my_lanes] = norm_s[...]
    rep_all(norm_s, gnorm.at[:, my_lanes], "ns")
    z_middle(0)
    scatter_forward("rs0", gi_piece, gi_land)
    z_sum(1)
    wait_recv("sa")
    gsmall[...] = jnp.sum(all_r[...], axis=0) * (1.0 / root)
    rows_done(4)
    copy_here(ghc, small_out[0], "oh")
    copy_here(gsmall, small_out[2], "os")
    rows_done(3)
    gather_forward("w1", rows_piece(1))
    rows_done(2)
    await_rest("rs0")
    for h in range(2):
        at = slice(h * (PD // 2), (h + 1) * (PD // 2))
        gi[at, :] = gi_s[r, at, :].astype(F32) + gi_l[1 + 2 * h].astype(F32) + gi_l[4 + h].astype(F32)
    copy_here(gi, gi_out, "og")
    wait_recv("ns")
    copy_here(gnorm, small_out[1], "on")
    last = rows_piece(0)
    if d.pieces == 2:
        z_sum_piece(0, 0)
        send(last(r, 0), last(r, 0), at_one, "w0r")
        send(last(r, 0), last(r, 0), at_two, "w0r")
        send(last(r, 0), last(r, 0), (both, f), "w0r")
        rows_done(1)
        z_sum_piece(0, 1)
        send(last(r, 1), last(r, 1), at_one, "w0r")
        send(last(r, 1), last(r, 1), at_two, "w0r")
        send(last(r, 1), last(r, 1), (both, f), "w0r")
    else:
        z_sum(0)
        rows_done(1)
        gather_forward("w0", last)
    rows_done(0)

    drain()


def finish(gi, gw0, gw1, gw2, gw3, ghc, gnorm, gsmall, *outs):
    out_gi, out0, out1, out2, out3, out_hc, out_ho, out_gain, out_bias, out_hb, out_ob = outs
    out_gi[...] = gi[...]
    for src, dst in ((gw0, out0), (gw1, out1), (gw2, out2), (gw3, out3)):
        dst[...] = src[...].astype(F32)

    @pl.when(pl.program_id(0) == 0)
    def _():
        out_hc[...] = ghc[...]
        out_ho[...] = gsmall[0 : out_ho.shape[0], 0 : out_ho.shape[1]]
        out_gain[...] = gnorm[0:4, :]
        out_bias[...] = gnorm[4:8, :]
        out_hb[...] = gsmall[8:9, 0 : out_hb.shape[1]]
        out_ob[...] = gsmall[9:10, 0 : out_ob.shape[1]]


def per_device(
    R, F,
    images, enc_first, enc_second, dec_first, dec_second, head_conv, head_out, norm_gain, norm_bias, head_bias, out_bias,
    task_weights, pool_index, labels, task_masks, targets,
):
    n, height, breadth, channels = images.shape
    rows, hidden = head_conv.shape
    q, out_ch = head_out.shape
    d = types.SimpleNamespace(
        n=n, R=R, F=F, Z=F // 2, rows=rows, C=channels, CR=channels // R, W=breadth, PIX=height * breadth,
        PD=n * height * breadth, HC=hidden, OC=out_ch, q=q,
    )
    d.M = R * d.PD
    d.pieces = 2 if d.Z == 4 else 1
    d.PW = d.M // 4
    wire = BF16 if rows % 16 == 0 else F32
    d.row_tile = 16 if rows % 16 == 0 else 8
    d.half = -(-rows // (2 * d.row_tile)) * d.row_tile
    vm = pltpu.VMEM
    patch = 9 * channels
    smalls = (
        head_conv.T, head_out, norm_gain, norm_bias, head_bias.reshape(1, hidden), out_bias.reshape(1, out_ch),
        task_weights.reshape(1, 3), pool_index, labels, jnp.transpose(task_masks, (1, 0, 2)), targets,
    )
    smalls = (smalls[0].astype(wire),) + smalls[1:]
    scratch = [vm(value.shape, value.dtype) for value in smalls] + [
        vm((d.PD, d.C), F32),
        vm((hidden, rows), F32),
        vm((8, d.C), F32),
        vm((16, LANES), F32),
        vm((4, rows, d.C), wire),
        vm((d.PD, LANES), F32),
        vm((4, d.M, d.C), BF16),
        vm((d.PD, d.C), BF16),
        vm((5, patch, d.CR), wire),
        vm((d.M, 9 * d.CR), F32),
        vm((d.M, d.CR), F32),
        vm((4, d.M, d.CR), F32),
        vm((d.M, 9 * d.CR), BF16),
        vm((d.M, d.PW), BF16),
        vm((d.PW, d.M), BF16),
        vm((R, d.PD, d.CR), BF16),
        vm((R, d.PD, d.CR), BF16),
        vm((2, R, d.M, d.CR), BF16),
        vm((2, 6, d.M // 2, d.CR), BF16),
        vm((d.PW, d.CR), BF16),
        vm((d.PW, d.C), BF16),
        vm((R, d.PW, d.CR), BF16),
        vm((R, d.PW, d.CR), BF16),
        vm((R, d.PD, d.C), BF16),
        vm((6, d.PD // 2, d.C), BF16),
        vm((2, d.M, d.C), BF16),
        vm((2, d.M, d.C), BF16),
        vm((2, d.M, d.C), BF16),
        vm((3, 8, LANES), F32),
        vm((3, R, 8, LANES), F32),
        vm((4, R, 8, LANES), F32),
        vm((4, R, 8, LANES), F32),
        vm((d.PD, d.C), BF16),
        vm((d.PD, d.C), BF16),
        vm((d.PD, d.C), BF16),
        vm((2, d.PW, d.CR), BF16),
        vm((2, d.PW, d.C), BF16),
        vm((4, patch, d.CR), wire),
        vm((4, d.Z, rows, d.CR), wire),
        vm((4, d.Z, rows, d.CR), wire),
        vm((d.half, LANES), wire),
        vm((F, d.half, LANES), wire),
        vm((F, d.half, LANES), wire),
        vm((d.Z, d.half, LANES), wire),
        vm((d.Z, d.half, LANES), wire),
        vm((R, d.half, LANES), wire),
        vm((8, 8, LANES), F32),
        vm((8, F, 8, LANES), F32),
        vm((8, LANES), F32),
        vm((R, 8, LANES), F32),
        vm((8, LANES), F32),
        vm((F, 8, LANES), F32),
        vm((hidden + 8, LANES), F32),
        vm((R, hidden + 8, LANES), F32),
        vm((F, 16, LANES), F32),
        vm((F, 16, LANES), F32),
        vm((8, LANES), F32),
        vm((LANES, 2 * LANES), F32),
        pltpu.SemaphoreType.DMA((len(CLASSES),)),
        pltpu.SemaphoreType.DMA((len(GROUPS),)),
        pltpu.SemaphoreType.DMA((5 * d.pieces, d.Z)),
    ]
    there = pl.BlockSpec(memory_space=pl.ANY)
    shape = jax.ShapeDtypeStruct
    kept = pl.pallas_call(
        functools.partial(kernel, d),
        out_shape=[shape((d.PD, d.C), F32)]
        + [shape((rows, d.C), wire)] * 4
        + [shape((hidden, rows), F32), shape((8, d.C), F32), shape((16, LANES), F32)],
        in_specs=[there] * 16,
        out_specs=[there] * 8,
        scratch_shapes=scratch,
        compiler_params=pltpu.CompilerParams(collective_id=0, has_side_effects=True, vmem_limit_bytes=63 * 2**20),
    )(
        images.reshape(d.PD, channels),
        *(w.astype(wire) for w in (enc_first, enc_second, dec_first, dec_second)),
        *smalls,
    )
    steps = next(count for count in (2, 1) if rows % (count * d.row_tile) == 0 and d.PD % (count * 8) == 0)
    part = lambda height, width: pl.BlockSpec((height // steps, width), lambda i: (i, 0))
    all_of = lambda height, width: pl.BlockSpec((height, width), lambda i: (0, 0))
    rest = ((q, out_ch), (4, channels), (4, channels), (1, hidden), (1, out_ch))
    gi, gw0, gw1, gw2, gw3, ghc, gq, gain, bias, ghb, gob = pl.pallas_call(
        finish,
        grid=(steps,),
        out_shape=[shape((d.PD, channels), F32)]
        + [shape((rows, channels), F32)] * 4
        + [shape((hidden, rows), F32)]
        + [shape(size, F32) for size in rest],
        in_specs=[part(d.PD, channels)]
        + [part(rows, channels)] * 4
        + [all_of(hidden, rows), all_of(8, channels), all_of(16, LANES)],
        out_specs=[part(d.PD, channels)]
        + [part(rows, channels)] * 4
        + [all_of(hidden, rows)]
        + [all_of(*size) for size in rest],
    )(*kept)
    return (
        gi.reshape(images.shape), gw0, gw1, gw2, gw3, ghc.T, gq, gain, bias, ghb.reshape(hidden), gob.reshape(out_ch),
    )


def solution(mesh):
    split = ("rep", "fsdp")
    rows = P("fsdp", None)
    return jax.shard_map(
        functools.partial(per_device, mesh.shape["rep"], mesh.shape["fsdp"]),
        mesh=mesh,
        in_specs=(P(split, None, None, None),)
        + (rows,) * 6
        + (P(),) * 5
        + (P(split, None), P(split, None), P(split, None, None), P(split, None, None)),
        out_specs=(P(split, None, None, None),) + (rows,) * 6 + (P(),) * 4,
        check_vma=False,
    )
```
